128 devices in a mesh: sp: 64 (over y, x_hi, z, core), tp: 2 (over x_lo).
Axes of the slice: x: 4 (x_hi: 2, x_lo: 2; x = x_hi * 2 + x_lo), y: 4, z: 4, core: 2. Of those that a mesh axis runs over, the one named last changes fastest.
Arguments:
- layer_input: bfloat16 [16384, 1152], P(('sp', 'tp')), may hold values from -6 to 6
- segment_ids: int32 [16384], replicated, may hold values from 0 to 3, as said below
- positions: int32 [16384], replicated, may hold values from 0 to 16383, as said below
- w_query: bfloat16 [1152, 1024], P(None, 'tp'), may hold values from -0.1875 to 0.1875
- w_key: bfloat16 [1152, 256], replicated, may hold values from -0.1875 to 0.1875
- w_value: bfloat16 [1152, 256], replicated, may hold values from -0.1875 to 0.1875
- w_out: bfloat16 [1024, 1152], P('tp'), may hold values from -0.1875 to 0.1875
- w_gate: bfloat16 [1152, 6912], P(None, 'tp'), may hold values from -0.1875 to 0.1875
- w_up: bfloat16 [1152, 6912], P(None, 'tp'), may hold values from -0.1875 to 0.1875
- w_down: bfloat16 [6912, 1152], P('tp'), may hold values from -0.078125 to 0.078125
- norm_attn: float32 [1152], replicated, may hold values from 0.5 to 1.5
- norm_query: float32 [256], replicated, may hold values from 0.1 to 1.9
- norm_key: float32 [256], replicated, may hold values from 0.1 to 1.9
- norm_post: float32 [1152], replicated, may hold values from 0.5 to 1.5
- norm_ffn: float32 [1152], replicated, may hold values from 0.5 to 1.5
- norm_out: float32 [1152], replicated, may hold values from 0.5 to 1.5
- cotangent: bfloat16 [16384, 1152], P(('sp', 'tp')), may hold values from -6 to 6
Outputs:
- layer_output: bfloat16 [16384, 1152], P(('sp', 'tp'))
- d_input: bfloat16 [16384, 1152], P(('sp', 'tp'))
- d_w_query: float32 [1152, 1024], P('sp', 'tp')
- d_w_key: float32 [1152, 256], replicated
- d_w_value: float32 [1152, 256], replicated
- d_w_out: float32 [1024, 1152], P('tp', 'sp')
- d_w_gate: float32 [1152, 6912], P('sp', 'tp')
- d_w_up: float32 [1152, 6912], P('sp', 'tp')
- d_w_down: float32 [6912, 1152], P('tp', 'sp')
- d_norm_attn: float32 [1152], replicated
- d_norm_query: float32 [256], replicated
- d_norm_key: float32 [256], replicated
- d_norm_post: float32 [1152], replicated
- d_norm_ffn: float32 [1152], replicated
- d_norm_out: float32 [1152], replicated
The draws below stay inside these ranges and needn't reach their ends.
Inputs may be any that keep to these rules, and one draw needn't show every extreme that they name: `segment_ids`: segment numbers never fall along the tokens and every number names at least one token; one document, whose number varies, covers all but at most (3) * (32) tokens. The first token of every document has position 0, and positions rise by 1 or 2 from one token to the next within a document.
All inputs are finite; a program needn't handle non-finite values.
Results may differ from the reference program's by a relative error of at most 0.02.
Values may be sent and summed in bfloat16 or wider, within the bound.
A program may use at most 448 MiB of HBM per device.

```python
import math
import jax
import jax.numpy as jnp
from jax import lax

D = 1152
HEADS = 4
HD = 256
FF = 6912
TOK_DEV = 128
SEQS = 4
TOKENS = 16384


def pack_layout(key):
    choose_key, length_key, step_key, order_key = jax.random.split(key, 4)
    long_index = jax.random.randint(choose_key, (), 0, SEQS)
    shorts = jax.random.randint(length_key, (SEQS,), 1, TOK_DEV // SEQS + 1)
    ordinal = jnp.arange(SEQS)
    is_long = ordinal == long_index
    others = jnp.sum(jnp.where(is_long, 0, shorts))
    lengths = jnp.where(is_long, TOKENS - others, shorts)
    starts = jnp.cumsum(lengths) - lengths
    places = jnp.arange(TOKENS)
    segments = jnp.sum((places[:, None] >= starts[None, 1:]).astype(jnp.int32), axis=1).astype(jnp.int32)
    long_length = TOKENS - others
    long_start = starts[long_index]
    long_step = (segments == long_index) & (places != long_start)
    twos = TOKENS - long_length
    shuffled = jax.random.permutation(order_key, TOKENS)
    scores = jnp.where(long_step, shuffled, TOKENS + shuffled)
    order = jnp.argsort(scores, stable=True)
    rank = jnp.argsort(order, stable=True)
    long_strides = 1 + (rank < twos).astype(jnp.int32)
    random_strides = jax.random.randint(step_key, (TOKENS,), 1, 3)
    strides = jnp.where(long_step, long_strides, random_strides)
    climbed = jnp.cumsum(strides)
    firsts = climbed[starts]
    token_pos = climbed - firsts[segments]
    return (segments, token_pos.astype(jnp.int32))


def draw_segment_ids(key, part):
    layout = pack_layout(key)
    return layout[0]


def draw_positions(key, part):
    layout = pack_layout(key)
    return layout[1]


def block_scale(rng, dims, cuts, least, largest):
    def one(axis_at, shards_of):
        draws = jax.random.uniform(jax.random.fold_in(jax.random.fold_in(rng, 6), axis_at), (shards_of,), jnp.float32, least / len(cuts), largest / len(cuts))
        return jnp.repeat(jnp.exp(draws), dims[axis_at] // shards_of).reshape((-1,) + (1,) * (len(dims) - axis_at - 1))

    loudness = one(*cuts[0])
    for cut in cuts[1:]:
        loudness = loudness * one(*cut)
    return loudness


def noise(own_key, extent, scale, most, cuts=(), held_as=jnp.bfloat16):
    loudness = block_scale(own_key, extent, cuts, -0.22, 0.18) if cuts else 1.0
    values = jax.random.normal(own_key, extent, jnp.float32) * scale * loudness
    return jnp.minimum(jnp.maximum(values, -most), most).astype(held_as)


def setup_inputs(seed: int = 0) -> dict:
    key_list = jax.random.split(jax.random.key(seed), 18)
    layer_input = noise(key_list[0], (TOKENS, D), 1.0, 6.0, ((0, 128),))
    segment_ids = draw_segment_ids(jax.random.fold_in(key_list[17], 71), 0)
    positions = draw_positions(jax.random.fold_in(key_list[17], 71), 0)
    w_query = noise(key_list[3], (D, HEADS * HD), D ** -0.5, 0.1875, ((1, 2),))
    w_key = noise(key_list[4], (D, HD), D ** -0.5, 0.1875)
    w_value = noise(key_list[5], (D, HD), D ** -0.5, 0.1875)
    w_out = noise(key_list[6], (HEADS * HD, D), (HEADS * HD) ** -0.5, 0.1875, ((0, 2),))
    w_gate = noise(key_list[7], (D, FF), D ** -0.5, 0.1875, ((1, 2),))
    w_up = noise(key_list[8], (D, FF), D ** -0.5, 0.1875, ((1, 2),))
    w_down = noise(key_list[9], (FF, D), FF ** -0.5, 0.078125, ((0, 2),))
    norm_attn = jnp.clip(1.0 + 0.1 * jax.random.normal(key_list[10], (D,), jnp.float32), 0.5, 1.5)
    norm_query = jnp.clip(1.0 + 0.18 * jax.random.normal(key_list[11], (HD,), jnp.float32), 0.1, 1.9)
    norm_key = jnp.clip(1.0 + 0.18 * jax.random.normal(key_list[12], (HD,), jnp.float32), 0.1, 1.9)
    norm_post = jnp.clip(1.0 + 0.1 * jax.random.normal(key_list[13], (D,), jnp.float32), 0.5, 1.5)
    norm_ffn = jnp.clip(1.0 + 0.1 * jax.random.normal(key_list[14], (D,), jnp.float32), 0.5, 1.5)
    norm_out = jnp.clip(1.0 + 0.1 * jax.random.normal(key_list[15], (D,), jnp.float32), 0.5, 1.5)
    cotangent = noise(key_list[16], (TOKENS, D), 1.0, 6.0, ((0, 128),))
    return dict(layer_input=layer_input, segment_ids=segment_ids, positions=positions, w_query=w_query, w_key=w_key, w_value=w_value, w_out=w_out, w_gate=w_gate, w_up=w_up, w_down=w_down, norm_attn=norm_attn, norm_query=norm_query, norm_key=norm_key, norm_post=norm_post, norm_ffn=norm_ffn, norm_out=norm_out, cotangent=cotangent)


@jax.custom_vjp
def low(v):
    return lax.optimization_barrier(v.astype(jnp.bfloat16)).astype(jnp.float32)

@jax.custom_vjp
def low_back(v):
    return v

def low_keep(v):
    return (low(v), None)

def low_pass(kept, grad):
    return (grad,)

def back_keep(v):
    return (v, None)

def back_low(kept, grad):
    return (low(grad),)
low.defvjp(low_keep, low_pass)
low_back.defvjp(back_keep, back_low)
EPS = 1e-06
THETA = 1000000.0
NEG = -1e+30
HIGH = lax.Precision.HIGHEST

def rms_scale(tensor, scaling):
    return tensor * lax.rsqrt(lax.optimization_barrier(jnp.mean(tensor * tensor, axis=-1, keepdims=True)) + EPS) * scaling

def angles(token_pos, head_size):
    middle = head_size // 2
    frequency = THETA ** (-2.0 * jnp.arange(middle, dtype=jnp.float32) / head_size)
    turned = token_pos.astype(jnp.float32)[:, None] * frequency[None, :]
    return (jnp.cos(turned), jnp.sin(turned))

def rotary(tensor, cosine, sine):
    middle = tensor.shape[-1] // 2
    lower_half = tensor[..., :middle]
    upper_half = tensor[..., middle:]
    return jnp.concatenate([lower_half * cosine - upper_half * sine, upper_half * cosine + lower_half * sine], axis=-1)

def attend(queries, keys, values, segment_ids):
    count = queries.shape[0]
    block = math.gcd(count, 512)
    blocks = count // block
    row_index = jnp.arange(count, dtype=jnp.int32)
    scale_factor = HD ** (-0.5)

    def one_block(inputs):
        query_block, seg_block, row_block = inputs
        raw = low_back(jnp.einsum('qhd,kd->hqk', query_block, keys, precision=HIGH)) * scale_factor
        allowed = (seg_block[:, None] == segment_ids[None, :]) & (row_block[:, None] >= row_index[None, :])
        scores = jnp.where(allowed[None], raw, NEG)
        top = lax.optimization_barrier(jnp.max(scores, axis=-1, keepdims=True))
        weights = jnp.exp(scores - top)
        probs = weights / lax.optimization_barrier(jnp.sum(weights, axis=-1, keepdims=True))
        return jnp.einsum('hqk,kd->qhd', low(probs), values, precision=HIGH)
    pieces = lax.map(jax.checkpoint(one_block), (queries.reshape(blocks, block, HEADS, HD), segment_ids.reshape(blocks, block), row_index.reshape(blocks, block)))
    return pieces.reshape(count, HEADS, HD)

def reference(layer_input, segment_ids, positions, w_query, w_key, w_value, w_out, w_gate, w_up, w_down, norm_attn, norm_query, norm_key, norm_post, norm_ffn, norm_out, cotangent):
    cosine, sine = angles(positions, HD)

    def layer(input_f, wq, wk, wv, wo, wg, wu, wd, g_attn, g_query, g_key, g_post, g_ffn, g_out):
        count = input_f.shape[0]
        h_attn = low(rms_scale(input_f, g_attn))
        q_pre = low_back(jnp.dot(h_attn, wq, precision=HIGH)).reshape(count, HEADS, HD)
        queries = low(low_back(rotary(rms_scale(q_pre, g_query), cosine[:, None, :], sine[:, None, :])))
        k_pre = low_back(jnp.dot(h_attn, wk, precision=HIGH))
        keys = low(low_back(rotary(rms_scale(k_pre, g_key), cosine, sine)))
        values = low(low_back(jnp.dot(h_attn, wv, precision=HIGH)))
        attended = attend(queries, keys, values, segment_ids)
        outputs = low(low_back(attended)).reshape(count, HEADS * HD)
        projected = low_back(jnp.dot(outputs, wo, precision=HIGH))
        mid = input_f + rms_scale(projected, g_post)
        rows = math.gcd(count, 4096)

        def ffn_block(mid_block):
            h_ffn = low(rms_scale(mid_block, g_ffn))
            gate = low_back(jnp.dot(h_ffn, wg, precision=HIGH))
            upper = low_back(jnp.dot(h_ffn, wu, precision=HIGH))
            act = low(jax.nn.gelu(gate, approximate=True) * upper)
            ffn_out = low_back(jnp.dot(act, wd, precision=HIGH))
            return mid_block + rms_scale(ffn_out, g_out)
        result = lax.map(jax.checkpoint(ffn_block), mid.reshape(count // rows, rows, mid.shape[1]))
        return result.reshape(count, mid.shape[1])
    floats = tuple((array_in.astype(jnp.float32) for array_in in (layer_input, w_query, w_key, w_value, w_out, w_gate, w_up, w_down, norm_attn, norm_query, norm_key, norm_post, norm_ffn, norm_out)))
    result, pull = jax.vjp(layer, *floats)
    grads = pull(cotangent.astype(jnp.float32))
    return (result.astype(jnp.bfloat16), grads[0].astype(jnp.bfloat16), grads[1], grads[2], grads[3], grads[4], grads[5], grads[6], grads[7], grads[8], grads[9], grads[10], grads[11], grads[12], grads[13])
```

```python
import jax
import jax.numpy as jnp
import numpy as np
from jax import lax
from jax.experimental import pallas as pl
from jax.experimental.pallas import tpu as pltpu
from jax.sharding import PartitionSpec as P

EPS = 1e-06
THETA = 1000000.0
BF = jnp.bfloat16
F32 = jnp.float32
MESH = pl.DeviceIdType.MESH
IN_VMEM = pl.BlockSpec(memory_space=pltpu.VMEM)
VMEM_BYTES = 58 * 1024 * 1024

TOK = 128
D = 1152
HD = 256
HEADS = 4
ROWS = 2 * TOK
HID = 1728
HID_PAD = 1792
HALF = 1408
CUT = 768
CHUNK = 256


class Place:
    def __init__(self):
        sp = lax.axis_index("sp")
        self.core = lax.rem(sp, 2)
        self.z = lax.rem(lax.div(sp, 2), 4)
        self.y = lax.div(sp, 16)
        self.x = lax.rem(lax.div(sp, 8), 2) * 2 + lax.axis_index("tp")

    def device(self, **moved):
        x, y, z, core = (moved.get(name, getattr(self, name)) for name in ("x", "y", "z", "core"))
        return (((y * 2 + lax.div(x, 2)) * 4 + z) * 2 + core, lax.rem(x, 2))

    def step(self, axis, by):
        return lax.rem(getattr(self, axis) + by, 4)

    def toward(self, axis, by):
        return self.device(**{axis: self.step(axis, by)})

    def partner(self):
        return self.device(core=1 - self.core)


class Net:
    def __init__(self, send, recv):
        self.send, self.recv, self.used, self.started = send, recv, 0, []

    def copy(self, source, target, device):
        at = self.used
        self.used += 1
        return pltpu.make_async_remote_copy(
            src_ref=source,
            dst_ref=target,
            send_sem=self.send.at[at],
            recv_sem=self.recv.at[at],
            device_id=device,
            device_id_type=MESH,
        )

    def go(self, copy):
        copy.start()
        self.started.append(copy)

    def drain(self):
        for copy in self.started:
            copy.wait_send()
        self.started = []


def greet(devices):
    barrier = pltpu.get_barrier_semaphore()
    for device in devices:
        pl.semaphore_signal(barrier, inc=1, device_id=device, device_id_type=MESH)
    pl.semaphore_wait(barrier, len(devices))


def ring(place, axis):
    return [place.toward(axis, 1), place.toward(axis, 3)]


class RingGather:
    def __init__(self, net, place, axis, view, lo, hi):
        self.net = net
        me, nxt, prev = getattr(place, axis), place.step(axis, 1), place.step(axis, 3)
        right, left = ring(place, axis)
        self.to_right = net.copy(view(me), view(me), right)
        self.to_left = net.copy(view(me), view(me), left)
        self.on_right = net.copy(lo(prev), lo(prev), right)
        self.on_left = net.copy(hi(nxt), hi(nxt), left)

    def start(self):
        self.net.go(self.to_right)
        self.net.go(self.to_left)

    def forward(self):
        self.to_right.wait_recv()
        self.net.go(self.on_right)
        self.to_left.wait_recv()
        self.net.go(self.on_left)

    def finish(self):
        self.on_right.wait_recv()
        self.on_left.wait_recv()


def by_rows(ref, act, most=16):
    *lead, rows, _ = ref.shape
    block = most
    for spot in np.ndindex(*lead):

        def one(i, carry, spot=spot):
            act(spot, pl.ds(pl.multiple_of(i * block, block), block))
            return carry

        lax.fori_loop(0, rows // block, one, 0)


def add_to(target, other):
    def act(spot, rows):
        at = (*spot, rows, slice(None))
        target[at] = (target[at].astype(F32) + other[at].astype(F32)).astype(target.dtype)

    by_rows(target, act)


def sum_to(target, others):
    def act(spot, rows):
        at = (*spot, rows, slice(None))
        total = others[0][at].astype(F32)
        for other in others[1:]:
            total = total + other[at].astype(F32)
        target[at] = total.astype(target.dtype)

    by_rows(target, act)


class RingScatter:
    def __init__(self, net, place, axis, lo, hi, room):
        self.net, self.lo, self.hi = net, lo, hi
        self.me, self.nxt, self.opp, self.prev = (place.step(axis, by) for by in range(4))
        right, left = ring(place, axis)
        self.lo1, self.lo_l, self.lo_r, self.hi1, self.hi_l, self.hi_r = room
        self.a = net.copy(lo(self.opp), self.lo1, right)
        self.b = net.copy(hi(self.opp), self.hi1, left)
        self.c_hi = net.copy(hi(self.nxt), self.hi_l, right)
        self.d_lo = net.copy(lo(self.prev), self.lo_r, left)
        self.c_lo = net.copy(self.lo1, self.lo_l, right)
        self.d_hi = net.copy(self.hi1, self.hi_r, left)

    def start_far(self):
        self.net.go(self.a)
        self.net.go(self.b)

    def start_near(self):
        self.net.go(self.c_hi)
        self.net.go(self.d_lo)

    def middle(self):
        self.a.wait_recv()
        add_to(self.lo1, self.lo(self.nxt))
        self.net.go(self.c_lo)
        self.b.wait_recv()
        add_to(self.hi1, self.hi(self.prev))
        self.net.go(self.d_hi)

    def finish(self, lo_out, hi_out):
        self.c_hi.wait_recv()
        self.d_hi.wait_recv()
        sum_to(hi_out, [self.hi(self.me), self.hi_l, self.hi_r])
        self.d_lo.wait_recv()
        self.c_lo.wait_recv()
        sum_to(lo_out, [self.lo(self.me), self.lo_l, self.lo_r])

    @staticmethod
    def room_shapes(lo_shape, hi_shape):
        return [pltpu.VMEM(lo_shape, BF)] * 3 + [pltpu.VMEM(hi_shape, BF)] * 3


def params(call_id):
    return pltpu.CompilerParams(
        collective_id=call_id, has_side_effects=True, vmem_limit_bytes=VMEM_BYTES
    )


def sems(count):
    return [pltpu.SemaphoreType.DMA((count,)), pltpu.SemaphoreType.DMA((count,))]


def weight_kernel(w_ref, other_ref, send, recv):
    place, net = Place(), Net(send, recv)
    right, left = ring(place, "x")
    quarter = w_ref.shape[0] // 4
    greet([right, left, place.partner()])
    finish = swap_weight(place, net, w_ref, other_ref, quarter)
    finish()
    net.drain()


def swap_weight(place, net, w_ref, other_ref, quarter):
    right, left = ring(place, "x")
    core = place.core

    def rows(side):
        return pl.ds(pl.multiple_of((2 * side + core) * quarter, 16), quarter)

    def cores_rows(side):
        return other_ref.at[rows(side)]

    one = net.copy(w_ref.at[rows(0)], cores_rows(0), left)
    two = net.copy(w_ref.at[rows(1)], cores_rows(1), right)
    trades = [net.copy(cores_rows(side), cores_rows(side), place.partner()) for side in (0, 1)]
    net.go(one)
    net.go(two)

    def finish():
        for first, trade in zip((one, two), trades):
            first.wait_recv()
            net.go(trade)
        for trade in trades:
            trade.wait_recv()

    return finish


def fetch_weight(w, call_id):
    return pl.pallas_call(
        weight_kernel,
        out_shape=jax.ShapeDtypeStruct(w.shape, w.dtype),
        in_specs=[IN_VMEM],
        out_specs=IN_VMEM,
        scratch_shapes=sems(4),
        compiler_params=params(call_id),
    )(w)


PARTS = (
    (0, 48, 0, ("x", "y", "z")),
    (48, 48, 768, ("z", "x", "y")),
    (96, 32, 1536, ("y", "z", "x")),
)


def part_views(place, buf, part):
    _, rows, base, (first, second, third) = part
    at1, at2, at3 = (getattr(place, axis) for axis in (first, second, third))

    def block(lead, start, size):
        return buf.at[lead, pl.ds(pl.multiple_of(base + start, 16), size)]

    return (
        (first, lambda j: block(at3, (at2 * 4 + j) * rows, rows)),
        (second, lambda j: block(at3, j * 4 * rows, 4 * rows)),
        (third, lambda j: block(j, 0, 16 * rows)),
    )


def halves(view):
    return (lambda j: view(j).at[:, pl.ds(0, HD)]), (lambda j: view(j).at[:, pl.ds(HD, HD)])


def key_tokens():
    out = np.zeros((4, 2048), np.int32)
    for skip, rows, base, axes in PARTS:
        for j in range(4):
            for r in range(16 * rows):
                spot = {axes[2]: j, axes[1]: r // (4 * rows), axes[0]: (r // rows) % 4}
                x, y, z = spot["x"], spot["y"], spot["z"]
                token = ((y * 2 + x // 2) * 4 + z) * 512 + (x % 2) * 128 + skip + r % rows
                out[j, base + r] = token
    order = np.zeros((8, CHUNK), np.int64)
    for c in range(8):
        for i in range(4):
            start = 256 * c + 64 * i if c < 6 else 1536 + 128 * i + 64 * (c - 6)
            order[c, 64 * i : 64 * i + 64] = np.arange(start, start + 64)
    return out[:, order]


KEY_TOKENS = key_tokens()


def chunk_at(place, n, by):
    lead = jnp.where(
        n < 3, place.step("z", by), jnp.where(n < 6, place.step("y", by), place.step("x", by))
    )
    first_y = jnp.where(n < 3, n, jnp.where(n < 6, lead, (n - 6) * 2))
    last_y = jnp.where(n < 3, n + 1, jnp.where(n < 6, lead, (n - 6) * 2 + 1))
    start = jnp.where(n < 6, n * 256, 1536 + 64 * (n - 6))
    stride = jnp.where(n < 6, 64, 128)
    starts = [pl.multiple_of(start + stride * i, 16) for i in range(4)]
    skip = first_y > place.y
    holds_first = (lead == 0) & ((n == 0) | (n == 3) | (n == 6))
    final = (place.x == 3) & (place.y == 3) & (place.z == 3)
    plain = (last_y < place.y) & jnp.logical_not(holds_first) & jnp.logical_not(final)
    return lead, starts, skip, plain


def read_chunk(buf, lead, starts, column):
    return jnp.concatenate(
        [buf[lead, pl.ds(start, 64), pl.ds(column, HD)] for start in starts], axis=0
    )


def contract(left, right, left_dim, right_dim):
    return lax.dot_general(
        left, right, (((left_dim,), (right_dim,)), ((), ())), preferred_element_type=F32
    )


def forward_kernel(
    kv_ref,
    q_ref,
    w_ref,
    key_ref,
    last_ref,
    first_ref,
    buf,
    q_all,
    w_other,
    o_out,
    inv_out,
    o_sum,
    l_sum,
    o_got,
    l_got,
    send,
    recv,
):
    place, net = Place(), Net(send, recv)
    core = place.core
    partner = place.partner()
    greet(ring(place, "x") + ring(place, "y") + ring(place, "z") + [partner])
    mine = pl.ds(pl.multiple_of(core * TOK, TOK), TOK)
    theirs = pl.ds(pl.multiple_of((1 - core) * TOK, TOK), TOK)
    q_all[:, mine] = q_ref[...]
    stages = []
    for part in PARTS:
        skip, rows, _, _ = part
        views = part_views(place, buf, part)
        axis, view = views[0]
        own = view(getattr(place, axis))
        own[...] = kv_ref[pl.ds(skip, rows)]
        stages.append([RingGather(net, place, axis, view, *halves(view)) for axis, view in views])
    for rings in stages:
        rings[0].start()
    swap_q = net.copy(q_all.at[:, mine], q_all.at[:, mine], partner)
    net.go(swap_q)
    for h in range(HEADS):
        o_sum[h] = jnp.zeros((ROWS, HD), F32)
        l_sum[h] = jnp.zeros((ROWS, 128), F32)
    for level in (0, 1):
        for rings in stages:
            rings[level].forward()
        for rings in stages:
            rings[level].finish()
            rings[level + 1].start()
    finish_w = swap_weight(place, net, w_ref, w_other, w_ref.shape[0] // 4)
    swap_q.wait_recv()

    def attend(n, by):
        lead, starts, skip, plain = chunk_at(place, n, by)

        def run(masked):
            keys = read_chunk(buf, lead, starts, 0)
            values = read_chunk(buf, lead, starts, HD)
            if masked:
                token = key_ref[lead, pl.ds(n, 1)]
                allowed = (token <= last_ref[...]) & (token >= first_ref[...])
            for h in range(HEADS):
                weights = jnp.exp(contract(q_all[h], keys, 1, 1))
                if masked:
                    weights = jnp.where(allowed, weights, 0.0)
                l_sum[h] += weights[:, :128] + weights[:, 128:]
                o_sum[h] += jnp.dot(weights.astype(BF), values, preferred_element_type=F32)

        @pl.when(plain)
        def _():
            run(False)

        @pl.when(jnp.logical_not(plain) & jnp.logical_not(skip))
        def _():
            run(True)

    def visit(by):
        lax.fori_loop(0, 8, lambda n, c: (attend(n, by), c)[1], 0)

    visit(0)
    for rings in stages:
        rings[2].forward()
    finish_w()
    lax.fori_loop(0, 16, lambda n, c: (attend(lax.rem(n, 8), 1 + 2 * lax.div(n, 8)), c)[1], 0)
    for rings in stages:
        rings[2].finish()
    visit(2)
    swap_o = net.copy(o_sum.at[:, theirs], o_got, partner)
    swap_l = net.copy(l_sum.at[:, theirs], l_got, partner)
    net.go(swap_l)
    net.go(swap_o)
    swap_l.wait_recv()
    swap_o.wait_recv()
    for h in range(HEADS):
        total = jnp.sum(l_sum[h, mine] + l_got[h], axis=1, keepdims=True)
        inverse = 1.0 / total
        o_out[h] = (o_sum[h, mine] + o_got[h]) * inverse
        inv_out[h] = jnp.broadcast_to(inverse, (TOK, 128))
    net.drain()


def attention_forward(kv, q, w_out, key_rows, last, first, call_id):
    shape = jax.ShapeDtypeStruct
    return pl.pallas_call(
        forward_kernel,
        out_shape=(
            shape((4, 2048, 2 * HD), BF),
            shape((HEADS, ROWS, HD), BF),
            shape(w_out.shape, BF),
            shape((HEADS, TOK, HD), F32),
            shape((HEADS, TOK, 128), F32),
        ),
        in_specs=[IN_VMEM] * 6,
        out_specs=[IN_VMEM] * 5,
        scratch_shapes=[
            pltpu.VMEM((HEADS, ROWS, HD), F32),
            pltpu.VMEM((HEADS, ROWS, 128), F32),
            pltpu.VMEM((HEADS, TOK, HD), F32),
            pltpu.VMEM((HEADS, TOK, 128), F32),
            *sems(48),
        ],
        compiler_params=params(call_id),
    )(kv, q, w_out, key_rows, last, first)


def backward_kernel(
    buf,
    q_all,
    do_ref,
    delta_ref,
    key_ref,
    last_ref,
    first_ref,
    dq_out,
    dkv_out,
    do_all,
    delta_all,
    grads,
    dq_sum,
    dq_got,
    *rest,
):
    *rooms, send, recv = rest
    place, net = Place(), Net(send, recv)
    core, partner = place.core, place.partner()
    greet(ring(place, "x") + ring(place, "y") + ring(place, "z") + [partner])
    mine = pl.ds(pl.multiple_of(core * TOK, TOK), TOK)
    theirs = pl.ds(pl.multiple_of((1 - core) * TOK, TOK), TOK)
    do_all[:, mine] = do_ref[...]
    delta_all[core] = delta_ref[...]
    swap_do = net.copy(do_all.at[:, mine], do_all.at[:, mine], partner)
    swap_delta = net.copy(delta_all.at[core], delta_all.at[core], partner)
    net.go(swap_do)
    net.go(swap_delta)
    for h in range(HEADS):
        dq_sum[h] = jnp.zeros((HD, ROWS), F32)
    stages = []
    for i, part in enumerate(PARTS):
        views = part_views(place, grads, part)
        rings = []
        for level, (axis, view) in enumerate(views):
            at = 6 * (3 * i + level)
            rings.append(RingScatter(net, place, axis, *halves(view), rooms[at : at + 6]))
        stages.append((rings, views))
    swap_do.wait_recv()
    swap_delta.wait_recv()

    def differ(n, by):
        lead, starts, skip, plain = chunk_at(place, n, by)

        def store(column, value):
            value = value.astype(BF)
            for i, start in enumerate(starts):
                grads[lead, pl.ds(start, 64), pl.ds(column, HD)] = value[64 * i : 64 * i + 64]

        def run(masked):
            keys = read_chunk(buf, lead, starts, 0)
            values = read_chunk(buf, lead, starts, HD)
            if masked:
                token = key_ref[lead, n]
                allowed = (token <= last_ref[...]) & (token >= first_ref[...])
            d_keys = d_values = None
            for h in range(HEADS):
                probs = jnp.exp(contract(keys, q_all[h], 1, 1))
                if masked:
                    probs = jnp.where(allowed, probs, 0.0)
                delta = jnp.concatenate(
                    [delta_all[0, pl.ds(h, 1)], delta_all[1, pl.ds(h, 1)]], axis=1
                )
                d_scores = (probs * (contract(values, do_all[h], 1, 1) - delta)).astype(BF)
                value_term = jnp.dot(probs.astype(BF), do_all[h], preferred_element_type=F32)
                key_term = jnp.dot(d_scores, q_all[h], preferred_element_type=F32)
                d_values = value_term if h == 0 else d_values + value_term
                d_keys = key_term if h == 0 else d_keys + key_term
                dq_sum[h] += contract(keys, d_scores, 0, 0)
            store(0, d_keys)
            store(HD, d_values)

        @pl.when(plain)
        def _():
            run(False)

        @pl.when(jnp.logical_not(plain) & jnp.logical_not(skip))
        def _():
            run(True)

        @pl.when(skip)
        def _():
            for start in starts:
                grads[lead, pl.ds(start, 64)] = jnp.zeros((64, 2 * HD), BF)

    def visit(by):
        lax.fori_loop(0, 8, lambda n, c: (differ(n, by), c)[1], 0)

    visit(2)
    for rings, _ in stages:
        rings[2].start_far()
    lax.fori_loop(0, 16, lambda n, c: (differ(lax.rem(n, 8), 1 + 2 * lax.div(n, 8)), c)[1], 0)
    for rings, _ in stages:
        rings[2].start_near()
    for rings, _ in stages:
        rings[2].middle()
    visit(0)
    swap_dq = net.copy(dq_sum.at[:, :, theirs], dq_got, partner)
    net.go(swap_dq)
    for level in (2, 1, 0):
        for (rings, views), part in zip(stages, PARTS):
            axis, view = views[level]
            lo, hi = halves(view)
            me = getattr(place, axis)
            skip, rows, _, _ = part
            if level:
                rings[level].finish(lo(me), hi(me))
                rings[level - 1].start_far()
                rings[level - 1].start_near()
            else:
                out = dkv_out.at[pl.ds(skip, rows)]
                rings[level].finish(out.at[:, pl.ds(0, HD)], out.at[:, pl.ds(HD, HD)])
        if level:
            for rings, _ in stages:
                rings[level - 1].middle()
    swap_dq.wait_recv()
    for h in range(HEADS):
        dq_out[h] = dq_sum[h, :, mine] + dq_got[h]
    net.drain()


def attention_backward(kv_all, q_all, d_heads, delta, key_columns, last, first, call_id):
    shape = jax.ShapeDtypeStruct
    rooms = []
    for _, rows, _, _ in PARTS:
        for blocks in (1, 4, 16):
            rooms += RingScatter.room_shapes((blocks * rows, HD), (blocks * rows, HD))
    return pl.pallas_call(
        backward_kernel,
        out_shape=(shape((HEADS, HD, TOK), F32), shape((TOK, 2 * HD), F32)),
        in_specs=[IN_VMEM] * 7,
        out_specs=[IN_VMEM] * 2,
        scratch_shapes=[
            pltpu.VMEM((HEADS, ROWS, HD), BF),
            pltpu.VMEM((2, 8, TOK), F32),
            pltpu.VMEM((4, 2048, 2 * HD), BF),
            pltpu.VMEM((HEADS, HD, ROWS), F32),
            pltpu.VMEM((HEADS, HD, TOK), F32),
            *rooms,
            *sems(64),
        ],
        compiler_params=params(call_id),
    )(kv_all, q_all, d_heads, delta, key_columns, last, first)


def x_gather_kernel(rows_ref, out_ref, send, recv):
    place, net = Place(), Net(send, recv)
    greet(ring(place, "x"))
    out_ref[place.x] = rows_ref[...]
    line = RingGather(
        net,
        place,
        "x",
        lambda j: out_ref.at[j],
        lambda j: out_ref.at[j, pl.ds(0, TOK // 2)],
        lambda j: out_ref.at[j, pl.ds(TOK // 2, TOK // 2)],
    )
    line.start()
    line.forward()
    line.finish()
    net.drain()


def x_gather(rows, call_id):
    return pl.pallas_call(
        x_gather_kernel,
        out_shape=jax.ShapeDtypeStruct((4, TOK, D), BF),
        in_specs=[IN_VMEM],
        out_specs=IN_VMEM,
        scratch_shapes=sems(4),
        compiler_params=params(call_id),
    )(rows)


def x_scatter_kernel(terms_ref, out_ref, *rest):
    *room, send, recv = rest
    place, net = Place(), Net(send, recv)
    greet(ring(place, "x"))
    half = TOK // 2
    line = RingScatter(
        net,
        place,
        "x",
        lambda j: terms_ref.at[j, pl.ds(0, half)],
        lambda j: terms_ref.at[j, pl.ds(half, half)],
        room,
    )
    line.start_far()
    line.start_near()
    line.middle()
    line.finish(out_ref.at[pl.ds(0, half)], out_ref.at[pl.ds(half, half)])
    net.drain()


def x_scatter(terms, call_id):
    half = (TOK // 2, D)
    return pl.pallas_call(
        x_scatter_kernel,
        out_shape=jax.ShapeDtypeStruct((TOK, D), F32),
        in_specs=[IN_VMEM],
        out_specs=IN_VMEM,
        scratch_shapes=[*RingScatter.room_shapes(half, half), *sems(6)],
        compiler_params=params(call_id),
    )(terms)


def ffn_grads_kernel(terms_ref, out_ref, got, snd, rcv, *rest):
    *rooms, send, recv, send2, recv2, here = rest
    place, net = Place(), Net(send, recv)
    core, partner = place.core, place.partner()
    x_hi, x_lo = lax.div(place.x, 2), lax.rem(place.x, 2)
    r, c = lax.div(place.z, 2), lax.rem(place.z, 2)
    friends = []
    for k in range(1, 16):
        spot = lax.rem(x_hi * 8 + place.z * 2 + core + k, 16)
        friends.append(
            place.device(
                x=lax.div(spot, 8) * 2 + x_lo, z=lax.rem(lax.div(spot, 2), 4), core=lax.rem(spot, 2)
            )
        )
    greet(friends + ring(place, "y"))
    swaps = [net.copy(terms_ref.at[1 - core, y], got.at[y], partner) for y in range(4)]
    for swap in swaps:
        net.go(swap)

    def left(lead):
        return lead.at[..., pl.ds(0, CUT)]

    def right(lead):
        return lead.at[..., pl.ds(CUT, HALF - CUT)]

    y_first = RingScatter(
        net, place, "y", lambda j: left(got.at[j, 0]), lambda j: left(got.at[j, 1]), rooms[0:6]
    )

    def z_spot(j):
        return got.at[:, lax.div(j, 2), lax.rem(j, 2)]

    z_first = RingScatter(
        net,
        place,
        "z",
        lambda j: right(z_spot(j).at[pl.ds(0, 2)]),
        lambda j: right(z_spot(j).at[pl.ds(2, 2)]),
        rooms[6:12],
    )

    def then_z(j):
        return got.at[place.y, lax.div(j, 2), lax.rem(j, 2)]

    z_second = RingScatter(
        net,
        place,
        "z",
        lambda j: then_z(j).at[:, pl.ds(0, 384)],
        lambda j: then_z(j).at[:, pl.ds(384, 384)],
        rooms[12:18],
    )

    def then_y(j):
        return got.at[j, r, c]

    y_second = RingScatter(
        net,
        place,
        "y",
        lambda j: then_y(j).at[:, pl.ds(768, 384)],
        lambda j: then_y(j).at[:, pl.ds(1152, 256)],
        rooms[18:24],
    )
    for y, swap in enumerate(swaps):
        swap.wait_recv()
        add_to(got.at[y], terms_ref.at[core, y])
    first, second = (y_first, z_first), (z_second, y_second)
    for line in first:
        line.start_far()
        line.start_near()
    for line in first:
        line.middle()
    me = place.y
    y_first.finish(left(got.at[me, 0]), left(got.at[me, 1]))
    z_second.start_far()
    z_second.start_near()
    own = z_spot(place.z)
    z_first.finish(right(own.at[pl.ds(0, 2)]), right(own.at[pl.ds(2, 2)]))
    y_second.start_far()
    y_second.start_near()
    for line in second:
        line.middle()
    done = got.at[place.y, r, c]
    z_second.finish(done.at[:, pl.ds(0, 384)], done.at[:, pl.ds(384, 384)])
    y_second.finish(done.at[:, pl.ds(768, 384)], done.at[:, pl.ds(1152, 256)])
    total = done[...].astype(F32)
    rest_rows = jnp.zeros((14, HALF), F32)
    for k in range(8):
        snd[k] = jnp.concatenate([total[18 * k : 18 * k + 18], rest_rows], axis=0).astype(BF)
    slot = x_hi * 4 + core * 2 + c
    own_spot = place.z * 2 + core
    stays = r == x_hi
    for k in range(8):
        copy = pltpu.make_async_remote_copy(
            src_ref=snd.at[k],
            dst_ref=rcv.at[slot],
            send_sem=send2.at[k],
            recv_sem=recv2.at[slot],
            device_id=place.device(x=r * 2 + x_lo, z=k // 2, core=k % 2),
            device_id_type=MESH,
        )
        is_here = stays & (own_spot == k)

        @pl.when(jnp.logical_not(is_here))
        def _(copy=copy):
            copy.start()

        @pl.when(is_here)
        def _(k=k):
            keep = pltpu.make_async_copy(snd.at[k], rcv.at[slot], here.at[0])
            keep.start()
            keep.wait()

    for m in range(8):
        arrival = pltpu.make_async_remote_copy(
            src_ref=snd.at[m],
            dst_ref=rcv.at[m],
            send_sem=send2.at[m],
            recv_sem=recv2.at[m],
            device_id=partner,
            device_id_type=MESH,
        )

        @pl.when(jnp.logical_not(stays & (slot == m)))
        def _(arrival=arrival):
            arrival.wait_recv()

        @pl.when(jnp.logical_not(stays & (own_spot == m)))
        def _(arrival=arrival):
            arrival.wait_send()

    out_ref[...] = rcv[...]
    net.drain()


def ffn_grads(terms, call_id):
    rooms = [
        *RingScatter.room_shapes((2, 144, CUT), (2, 144, CUT)),
        *RingScatter.room_shapes((2, 144, HALF - CUT), (2, 144, HALF - CUT)),
        *RingScatter.room_shapes((144, 384), (144, 384)),
        *RingScatter.room_shapes((144, 384), (144, 256)),
    ]
    return pl.pallas_call(
        ffn_grads_kernel,
        out_shape=jax.ShapeDtypeStruct((8, 32, HALF), BF),
        in_specs=[IN_VMEM],
        out_specs=IN_VMEM,
        scratch_shapes=[
            pltpu.VMEM((4, 2, 2, 144, HALF), BF),
            pltpu.VMEM((8, 32, HALF), BF),
            pltpu.VMEM((8, 32, HALF), BF),
            *rooms,
            *sems(32),
            *sems(8),
            pltpu.SemaphoreType.DMA((1,)),
        ],
        compiler_params=params(call_id),
    )(terms)


LANES = 384
ORDERS = (("x", "y", "z"), ("y", "z", "x"), ("z", "x", "y"))


def small_grads_kernel(terms_ref, gains_ref, out_ref, gains_out, got, sums, gain_got, *rest):
    *rooms, send, recv = rest
    place, net = Place(), Net(send, recv)
    core, partner = place.core, place.partner()
    greet(ring(place, "x") + ring(place, "y") + ring(place, "z") + [partner])
    swap = net.copy(terms_ref.at[1 - core], got, partner)
    gain_got[0, core] = gains_ref[...]
    gain_swap = net.copy(gain_got.at[0, core], gain_got.at[0, core], partner)
    net.go(gain_swap)
    net.go(swap)

    def gain_ring(level, axis):
        return RingGather(
            net,
            place,
            axis,
            lambda j: gain_got.at[level, j],
            lambda j: gain_got.at[level, j, :, pl.ds(0, 512)],
            lambda j: gain_got.at[level, j, :, pl.ds(512, 640)],
        )

    gain_lines = [gain_ring(1, "x"), gain_ring(2, "y"), gain_ring(3, "z")]
    gain_swap.wait_recv()
    gain_got[1, place.x] = gain_got[0, 0] + gain_got[0, 1]
    gain_lines[0].start()

    rows = out_ref.at[core]
    scatters, gathers = [], []
    for p, (first, second, third) in enumerate(ORDERS):
        lanes = pl.ds(LANES * p, LANES)
        at1, at2, at3 = (getattr(place, axis) for axis in (first, second, third))

        def views(ref, lanes=lanes, at1=at1):
            def piece(start, size):
                return ref.at[pl.ds(pl.multiple_of(start, 16), size), lanes]

            return (
                lambda j: piece(320 * j, 320),
                lambda j: piece(320 * j, 160),
                lambda j: piece(320 * j + 160, 160),
                lambda j: piece(320 * at1 + 80 * j, 80),
                lambda j: piece(320 * at1 + 80 * j, 48),
                lambda j: piece(320 * at1 + 80 * j + 48, 32),
            )

        _, lo1, hi1, term2, lo2, hi2 = views(got)
        room = rooms[12 * p : 12 * p + 12]
        scatters.append(
            (
                (RingScatter(net, place, first, lo1, hi1, room[:6]), lo1, hi1, at1),
                (RingScatter(net, place, second, lo2, hi2, room[6:]), lo2, hi2, at2),
            )
        )
        spot = sums.at[p]
        last = RingGather(
            net,
            place,
            third,
            lambda j, spot=spot: spot.at[j],
            lambda j, spot=spot: spot.at[j, pl.ds(0, 48)],
            lambda j, spot=spot: spot.at[j, pl.ds(48, 32)],
        )
        whole1, whole_lo1, whole_hi1, whole2, whole_lo2, whole_hi2 = views(rows)
        gathers.append(
            (
                last,
                RingGather(net, place, second, whole2, whole_lo2, whole_hi2),
                RingGather(net, place, first, whole1, whole_lo1, whole_hi1),
                term2(at2),
                whole2(at2),
                at3,
            )
        )
    swap.wait_recv()
    add_to(got, terms_ref.at[core])
    for level in (0, 1):
        for pair in scatters:
            pair[level][0].start_far()
            pair[level][0].start_near()
        for pair in scatters:
            pair[level][0].middle()
        gain_lines[level].forward()
        for pair in scatters:
            line, lo, hi, at = pair[level]
            line.finish(lo(at), hi(at))
        gain_lines[level].finish()
        nxt = place.y if level == 0 else place.z
        gain_got[level + 2, nxt] = (gain_got[level + 1, 0] + gain_got[level + 1, 1]) + (
            gain_got[level + 1, 2] + gain_got[level + 1, 3]
        )
        gain_lines[level + 1].start()
    for p, (last, _, _, term, _, at3) in enumerate(gathers):
        sums[p, at3] = term[...]
        last.start()
    for last, *_ in gathers:
        last.forward()
    gain_lines[2].forward()
    for p, (last, second, _, _, own, _) in enumerate(gathers):
        last.finish()
        sum_to(own, [sums.at[p, j] for j in range(4)])
        second.start()
    for _, second, *_ in gathers:
        second.forward()
    for _, second, first, *_ in gathers:
        second.finish()
        first.start()
    for _, _, first, *_ in gathers:
        first.forward()
    gain_lines[2].finish()
    gains_out[...] = (gain_got[3, 0] + gain_got[3, 1]) + (gain_got[3, 2] + gain_got[3, 3])
    for _, _, first, *_ in gathers:
        first.finish()
    final = net.copy(rows, rows, partner)
    net.go(final)
    final.wait_recv()
    net.drain()


def small_grads(terms, gains, call_id):
    shape = jax.ShapeDtypeStruct
    rooms = []
    for _ in ORDERS:
        rooms += RingScatter.room_shapes((160, LANES), (160, LANES))
        rooms += RingScatter.room_shapes((48, LANES), (32, LANES))
    return pl.pallas_call(
        small_grads_kernel,
        out_shape=(shape(terms.shape, BF), shape(gains.shape, F32)),
        in_specs=[IN_VMEM] * 2,
        out_specs=[IN_VMEM] * 2,
        scratch_shapes=[
            pltpu.VMEM((1280, D), BF),
            pltpu.VMEM((3, 4, 80, LANES), BF),
            pltpu.VMEM((4, 4, 8, D), F32),
            *rooms,
            *sems(96),
        ],
        compiler_params=params(call_id),
    )(terms, gains)


def rms_scale(tensor, scaling):
    return tensor * lax.rsqrt(jnp.mean(tensor * tensor, axis=-1, keepdims=True) + EPS) * scaling


def angles(token_pos):
    middle = HD // 2
    frequency = THETA ** (-2.0 * jnp.arange(middle, dtype=F32) / HD)
    turned = token_pos.astype(F32)[:, None] * frequency[None, :]
    return (jnp.cos(turned), jnp.sin(turned))


def rotary(tensor, cosine, sine):
    middle = tensor.shape[-1] // 2
    lower_half = tensor[..., :middle]
    upper_half = tensor[..., middle:]
    return jnp.concatenate(
        [lower_half * cosine - upper_half * sine, upper_half * cosine + lower_half * sine], axis=-1
    )


def glu_piece(gate_in, up_in):
    return jax.nn.gelu(gate_in, approximate=True) * up_in


def shards(
    layer_input,
    segment_ids,
    positions,
    w_query,
    w_key,
    w_value,
    w_out,
    w_gate,
    w_up,
    w_down,
    norm_attn,
    norm_query,
    norm_key,
    norm_post,
    norm_ffn,
    norm_out,
    cotangent,
):
    sp, tp = lax.axis_index("sp"), lax.axis_index("tp")
    core, x_hi = lax.rem(sp, 2), lax.rem(lax.div(sp, 8), 2)
    own_start = (sp * 2 + tp) * TOK
    chip_start = lax.div(sp, 2) * 512 + tp * TOK

    firsts = jnp.sum(
        (segment_ids[None, :] < jnp.arange(4, dtype=jnp.int32)[:, None]).astype(jnp.int32), axis=1
    )
    row_token = chip_start + jnp.concatenate([jnp.arange(TOK), 256 + jnp.arange(TOK)]).astype(
        jnp.int32
    )
    row_segs = jnp.concatenate(
        [
            lax.dynamic_slice_in_dim(segment_ids, chip_start, TOK),
            lax.dynamic_slice_in_dim(segment_ids, chip_start + 256, TOK),
        ]
    )
    row_first = jnp.zeros_like(row_token)
    for k in range(4):
        row_first = jnp.where(row_segs == k, firsts[k], row_first)
    key_rows = jnp.asarray(KEY_TOKENS) + core * 256
    cosine, sine = angles(lax.dynamic_slice_in_dim(positions, own_start, TOK))

    def query_piece(pre_rot, scaling):
        return rotary(rms_scale(pre_rot, scaling), cosine[:, None, :], sine[:, None, :])

    def key_piece(pre_rot, scaling):
        return rotary(rms_scale(pre_rot, scaling), cosine, sine)

    wq_other = fetch_weight(w_query, 1)
    wq_both = jnp.concatenate([w_query, wq_other], axis=1)
    input_f = layer_input.astype(F32)
    h_attn = rms_scale(input_f, norm_attn).astype(BF)
    q_pre = jnp.dot(h_attn, wq_both, preferred_element_type=F32).reshape(TOK, HEADS, HD)
    q_rot = query_piece(q_pre, norm_query).astype(BF)
    q_scaled = (q_rot * BF(HD**-0.5)).transpose(1, 0, 2)
    k_pre = jnp.dot(h_attn, w_key, preferred_element_type=F32)
    k_rot = key_piece(k_pre, norm_key).astype(BF)
    v_own = jnp.dot(h_attn, w_value, preferred_element_type=F32).astype(BF)
    kv_own = jnp.concatenate([k_rot, v_own], axis=1)
    kv_all, q_all, wo_other, o_heads, inverse = attention_forward(
        kv_own, q_scaled, w_out, key_rows, row_token[:, None], row_first[:, None], 2
    )
    wo_both = jnp.concatenate([w_out, wo_other], axis=0)
    o_cat = o_heads.transpose(1, 0, 2).astype(BF).reshape(TOK, HEADS * HD)
    attn_out = jnp.dot(o_cat, wo_both, preferred_element_type=F32)
    mid = input_f + rms_scale(attn_out, norm_post)
    h_ffn = rms_scale(mid, norm_ffn).astype(BF)

    def units(weight, dim):
        part = lax.dynamic_slice_in_dim(weight, x_hi * HID, HID, axis=dim)
        pads = [(0, 0), (0, 0)]
        pads[dim] = (0, HID_PAD - HID)
        return jnp.pad(part, pads)

    gate_w, up_w, down_w = units(w_gate, 1), units(w_up, 1), units(w_down, 0)
    h_line = x_gather(h_ffn, 3).reshape(4 * TOK, D)
    gate = jnp.dot(h_line, gate_w, preferred_element_type=F32)
    upper = jnp.dot(h_line, up_w, preferred_element_type=F32)
    act = glu_piece(gate, upper).astype(BF)
    ffn_term = jnp.dot(act, down_w, preferred_element_type=F32).astype(BF)
    ffn_out = x_scatter(ffn_term.reshape(4, TOK, D), 4)
    layer_output = (mid + rms_scale(ffn_out, norm_out)).astype(BF)
    grad_out = cotangent.astype(F32)
    _, pull_out = jax.vjp(rms_scale, ffn_out, norm_out)
    d_ffn_out, d_norm_out = pull_out(grad_out)
    d_ffn_line = x_gather(d_ffn_out.astype(BF), 5).reshape(4 * TOK, D)
    d_act = contract(d_ffn_line, down_w, 1, 1)
    _, pull_glu = jax.vjp(glu_piece, gate, upper)
    d_gate, d_upper = pull_glu(d_act)
    d_gate = d_gate.astype(BF)
    d_upper = d_upper.astype(BF)
    d_h_term = (contract(d_gate, gate_w, 1, 1) + contract(d_upper, up_w, 1, 1)).astype(BF)
    d_h_ffn = x_scatter(d_h_term.reshape(4, TOK, D), 6)
    d_w_gate = contract(h_line, d_gate, 0, 0).astype(BF)
    d_w_up = contract(h_line, d_upper, 0, 0).astype(BF)
    d_w_down = contract(d_ffn_line, act, 0, 0).astype(BF)
    wide = jnp.concatenate(
        [
            d_w_gate.reshape(D, 2, 896),
            d_w_up.reshape(D, 2, 896),
            d_w_down.reshape(D, 2, 896),
            jnp.zeros((D, 2, 128), BF),
        ],
        axis=2,
    )
    terms = wide.reshape(4, 2, 144, 2, 2, HALF).transpose(3, 0, 1, 4, 2, 5)
    ffn_done = ffn_grads(terms, 7)
    ffn_done = (
        ffn_done.reshape(2, 2, 2, 32, HALF)[:, :, :, :18]
        .transpose(3, 0, 1, 2, 4)
        .reshape(18, 2, 2, 2 * HALF)
        .astype(F32)
    )

    def home(which):
        part = ffn_done[..., 896 * which : 896 * (which + 1)].reshape(18, 2, HID_PAD)
        return part[:, :, :HID].reshape(18, 2 * HID)

    _, pull_ffn = jax.vjp(rms_scale, mid, norm_ffn)
    d_mid_norm, d_norm_ffn = pull_ffn(d_h_ffn)
    d_mid = grad_out + d_mid_norm
    _, pull_post = jax.vjp(rms_scale, attn_out, norm_post)
    d_attn_out, d_norm_post = pull_post(d_mid)
    d_attn = d_attn_out.astype(BF)
    d_o = contract(d_attn, wo_both, 1, 1).astype(BF).reshape(TOK, HEADS, HD).transpose(1, 0, 2)
    inv_rows = inverse[..., :1]
    d_o_f = d_o.astype(F32)
    delta = jnp.sum(d_o_f * o_heads, axis=2) * inverse[..., 0]
    delta = jnp.concatenate([delta, jnp.zeros((4, TOK), F32)], axis=0)
    dq_turned, d_kv = attention_backward(
        kv_all,
        q_all,
        (d_o_f * inv_rows).astype(BF),
        delta,
        key_rows.reshape(4, 8, CHUNK, 1),
        row_token[None, :],
        row_first[None, :],
        8,
    )
    d_q_rot = (dq_turned.transpose(2, 0, 1) * HD**-0.5).astype(BF).astype(F32)
    d_kv = d_kv.astype(BF)
    _, pull_key = jax.vjp(key_piece, k_pre, norm_key)
    d_k_pre, d_norm_key = pull_key(d_kv[:, :HD].astype(F32))
    d_k_pre = d_k_pre.astype(BF)
    d_value = d_kv[:, HD:]
    _, pull_query = jax.vjp(query_piece, q_pre, norm_query)
    d_q_pre, d_norm_query = pull_query(d_q_rot)
    d_q_pre = d_q_pre.reshape(TOK, HEADS * HD).astype(BF)
    d_h_attn = (
        contract(d_q_pre, wq_both, 1, 1)
        + contract(d_k_pre, w_key, 1, 1)
        + contract(d_value, w_value, 1, 1)
    )
    _, pull_attn = jax.vjp(rms_scale, input_f, norm_attn)
    d_input_norm, d_norm_attn = pull_attn(d_h_attn)
    d_input = (d_mid + d_input_norm).astype(BF)

    def in_order(both):
        return jnp.where(tp == 0, both, jnp.roll(both, 2 * HD, axis=1))

    small = jnp.concatenate(
        [
            contract(in_order(d_q_pre), h_attn, 0, 0),
            contract(d_k_pre, h_attn, 0, 0),
            contract(in_order(o_cat), d_attn, 0, 0),
            contract(d_value, h_attn, 0, 0),
        ],
        axis=0,
    ).astype(BF)
    gains = jnp.stack(
        [
            d_norm_attn,
            d_norm_post,
            d_norm_ffn,
            d_norm_out,
            jnp.concatenate([d_norm_query, d_norm_key, jnp.zeros((D - 2 * HD,), F32)]),
            *([jnp.zeros((D,), F32)] * 3),
        ]
    )
    small, gains = small_grads(small.reshape(2, 1280, D), gains, 9)

    def cut(matrix):
        return lax.dynamic_slice(matrix, (tp * 512, sp * 18), (512, 18)).astype(F32)

    return (
        layer_output,
        d_input,
        cut(small[0, :1024]).T,
        small[0, 1024:].astype(F32).T,
        small[1, 1024:].astype(F32).T,
        cut(small[1, :1024]),
        home(0),
        home(1),
        home(2).T,
        gains[0],
        gains[4, :HD],
        gains[4, HD : 2 * HD],
        gains[1],
        gains[2],
        gains[3],
    )


def solution(mesh):
    rows = P(("sp", "tp"), None)
    in_specs = (
        rows,
        P(),
        P(),
        P(None, "tp"),
        P(),
        P(),
        P("tp", None),
        P(None, "tp"),
        P(None, "tp"),
        P("tp", None),
        P(),
        P(),
        P(),
        P(),
        P(),
        P(),
        rows,
    )
    out_specs = (
        rows,
        rows,
        P("sp", "tp"),
        P(),
        P(),
        P("tp", "sp"),
        P("sp", "tp"),
        P("sp", "tp"),
        P("tp", "sp"),
        P(),
        P(),
        P(),
        P(),
        P(),
        P(),
    )
    return jax.shard_map(shards, mesh=mesh, in_specs=in_specs, out_specs=out_specs, check_vma=False)
```

```python
import jax
import jax.numpy as jnp
import numpy as np
from jax import lax
from jax.experimental import pallas as pl
from jax.experimental.pallas import tpu as pltpu
from jax.sharding import PartitionSpec as P

EPS = 1e-06
THETA = 1000000.0
BF = jnp.bfloat16
F32 = jnp.float32
MESH = pl.DeviceIdType.MESH
IN_VMEM = pl.BlockSpec(memory_space=pltpu.VMEM)
VMEM_BYTES = 58 * 1024 * 1024

TOK = 128
D = 1152
HD = 256
HEADS = 4
ROWS = 2 * TOK
HID = 1728
HID_PAD = 1792
HALF = 1408
CUT = 768
CHUNK = 256


class Place:
    def __init__(self):
        sp = lax.axis_index("sp")
        self.core = lax.rem(sp, 2)
        self.z = lax.rem(lax.div(sp, 2), 4)
        self.y = lax.div(sp, 16)
        self.x = lax.rem(lax.div(sp, 8), 2) * 2 + lax.axis_index("tp")

    def device(self, **moved):
        x, y, z, core = (moved.get(name, getattr(self, name)) for name in ("x", "y", "z", "core"))
        return (((y * 2 + lax.div(x, 2)) * 4 + z) * 2 + core, lax.rem(x, 2))

    def step(self, axis, by):
        return lax.rem(getattr(self, axis) + by, 4)

    def toward(self, axis, by):
        return self.device(**{axis: self.step(axis, by)})

    def partner(self):
        return self.device(core=1 - self.core)


class Net:
    def __init__(self, send, recv):
        self.send, self.recv, self.used, self.started = send, recv, 0, []

    def copy(self, source, target, device):
        at = self.used
        self.used += 1
        return pltpu.make_async_remote_copy(
            src_ref=source,
            dst_ref=target,
            send_sem=self.send.at[at],
            recv_sem=self.recv.at[at],
            device_id=device,
            device_id_type=MESH,
        )

    def go(self, copy):
        copy.start()
        self.started.append(copy)

    def drain(self):
        for copy in self.started:
            copy.wait_send()
        self.started = []


def greet(devices):
    barrier = pltpu.get_barrier_semaphore()
    for device in devices:
        pl.semaphore_signal(barrier, inc=1, device_id=device, device_id_type=MESH)
    pl.semaphore_wait(barrier, len(devices))


def ring(place, axis):
    return [place.toward(axis, 1), place.toward(axis, 3)]


class RingGather:
    def __init__(self, net, place, axis, view, lo, hi):
        self.net = net
        me, nxt, prev = getattr(place, axis), place.step(axis, 1), place.step(axis, 3)
        right, left = ring(place, axis)
        self.to_right = net.copy(view(me), view(me), right)
        self.to_left = net.copy(view(me), view(me), left)
        self.on_right = net.copy(lo(prev), lo(prev), right)
        self.on_left = net.copy(hi(nxt), hi(nxt), left)

    def start(self):
        self.net.go(self.to_right)
        self.net.go(self.to_left)

    def forward(self):
        self.to_right.wait_recv()
        self.net.go(self.on_right)
        self.to_left.wait_recv()
        self.net.go(self.on_left)

    def finish(self):
        self.on_right.wait_recv()
        self.on_left.wait_recv()


def by_rows(ref, act):
    *lead, rows, _ = ref.shape
    block = next(size for size in (64, 48, 32, 16) if rows % size == 0)
    for spot in np.ndindex(*lead):

        def one(i, carry, spot=spot):
            act(spot, pl.ds(pl.multiple_of(i * block, block), block))
            return carry

        lax.fori_loop(0, rows // block, one, 0)


def add_to(target, other):
    def act(spot, rows):
        at = (*spot, rows, slice(None))
        target[at] = (target[at].astype(F32) + other[at].astype(F32)).astype(target.dtype)

    by_rows(target, act)


def sum_to(target, others):
    def act(spot, rows):
        at = (*spot, rows, slice(None))
        total = others[0][at].astype(F32)
        for other in others[1:]:
            total = total + other[at].astype(F32)
        target[at] = total.astype(target.dtype)

    by_rows(target, act)


class RingScatter:
    def __init__(self, net, place, axis, lo, hi, room):
        self.net, self.lo, self.hi = net, lo, hi
        self.me, self.nxt, self.opp, self.prev = (place.step(axis, by) for by in range(4))
        right, left = ring(place, axis)
        self.lo1, self.lo_l, self.lo_r, self.hi1, self.hi_l, self.hi_r = room
        self.a = net.copy(lo(self.opp), self.lo1, right)
        self.b = net.copy(hi(self.opp), self.hi1, left)
        self.c_hi = net.copy(hi(self.nxt), self.hi_l, right)
        self.d_lo = net.copy(lo(self.prev), self.lo_r, left)
        self.c_lo = net.copy(self.lo1, self.lo_l, right)
        self.d_hi = net.copy(self.hi1, self.hi_r, left)

    def start_far(self):
        self.net.go(self.a)
        self.net.go(self.b)

    def start_near(self):
        self.net.go(self.c_hi)
        self.net.go(self.d_lo)

    def middle(self):
        self.a.wait_recv()
        add_to(self.lo1, self.lo(self.nxt))
        self.net.go(self.c_lo)
        self.b.wait_recv()
        add_to(self.hi1, self.hi(self.prev))
        self.net.go(self.d_hi)

    def finish(self, lo_out, hi_out):
        self.c_hi.wait_recv()
        self.d_hi.wait_recv()
        sum_to(hi_out, [self.hi(self.me), self.hi_l, self.hi_r])
        self.d_lo.wait_recv()
        self.c_lo.wait_recv()
        sum_to(lo_out, [self.lo(self.me), self.lo_l, self.lo_r])

    @staticmethod
    def room_shapes(lo_shape, hi_shape):
        return [pltpu.VMEM(lo_shape, BF)] * 3 + [pltpu.VMEM(hi_shape, BF)] * 3


def params(call_id):
    return pltpu.CompilerParams(
        collective_id=call_id, has_side_effects=True, vmem_limit_bytes=VMEM_BYTES
    )


def sems(count):
    return [pltpu.SemaphoreType.DMA((count,)), pltpu.SemaphoreType.DMA((count,))]


def weight_kernel(w_ref, other_ref, send, recv):
    place, net = Place(), Net(send, recv)
    right, left = ring(place, "x")
    quarter = w_ref.shape[0] // 4
    greet([right, left, place.partner()])
    finish = swap_weight(place, net, w_ref, other_ref, quarter)
    finish()
    net.drain()


def swap_weight(place, net, w_ref, other_ref, quarter):
    right, left = ring(place, "x")
    core = place.core

    def rows(side):
        return pl.ds(pl.multiple_of((2 * side + core) * quarter, 16), quarter)

    def cores_rows(side):
        return other_ref.at[rows(side)]

    one = net.copy(w_ref.at[rows(0)], cores_rows(0), left)
    two = net.copy(w_ref.at[rows(1)], cores_rows(1), right)
    trades = [net.copy(cores_rows(side), cores_rows(side), place.partner()) for side in (0, 1)]
    net.go(one)
    net.go(two)

    def finish():
        for first, trade in zip((one, two), trades):
            first.wait_recv()
            net.go(trade)
        for trade in trades:
            trade.wait_recv()

    return finish


def fetch_weight(w, call_id):
    return pl.pallas_call(
        weight_kernel,
        out_shape=jax.ShapeDtypeStruct(w.shape, w.dtype),
        in_specs=[IN_VMEM],
        out_specs=IN_VMEM,
        scratch_shapes=sems(4),
        compiler_params=params(call_id),
    )(w)


PARTS = (
    (0, 48, 0, ("x", "y", "z")),
    (48, 48, 768, ("z", "x", "y")),
    (96, 32, 1536, ("y", "z", "x")),
)


def part_views(place, buf, part):
    _, rows, base, (first, second, third) = part
    at1, at2, at3 = (getattr(place, axis) for axis in (first, second, third))

    def block(lead, start, size):
        return buf.at[lead, pl.ds(pl.multiple_of(base + start, 16), size)]

    return (
        (first, lambda j: block(at3, (at2 * 4 + j) * rows, rows)),
        (second, lambda j: block(at3, j * 4 * rows, 4 * rows)),
        (third, lambda j: block(j, 0, 16 * rows)),
    )


def halves(view):
    return (lambda j: view(j).at[:, pl.ds(0, HD)]), (lambda j: view(j).at[:, pl.ds(HD, HD)])


def chunk_rows(n):
    return [256 * n + 64 * i if n < 6 else 1536 + 128 * i + 64 * (n - 6) for i in range(4)]


def key_tokens():
    out = np.zeros((4, 2048), np.int32)
    for skip, rows, base, axes in PARTS:
        for j in range(4):
            for r in range(16 * rows):
                spot = {axes[2]: j, axes[1]: r // (4 * rows), axes[0]: (r // rows) % 4}
                x, y, z = spot["x"], spot["y"], spot["z"]
                token = ((y * 2 + x // 2) * 4 + z) * 512 + (x % 2) * 128 + skip + r % rows
                out[j, base + r] = token
    order = np.zeros((8, CHUNK), np.int64)
    for c in range(8):
        for i in range(4):
            start = chunk_rows(c)[i]
            order[c, 64 * i : 64 * i + 64] = np.arange(start, start + 64)
    return out[:, order]


KEY_TOKENS = key_tokens()


def read_sets(place, buf, key_ref, chunks, by):
    keys, values, tokens = [], [], []
    for n in chunks:
        lead = place.step("zyx"[n // 3], by)
        rows = chunk_rows(n)
        keys += [buf[lead, start : start + 64, :HD] for start in rows]
        values += [buf[lead, start : start + 64, HD:] for start in rows]
        tokens.append(key_ref[lead, n : n + 1])
    return (
        jnp.concatenate(keys, axis=0),
        jnp.concatenate(values, axis=0),
        jnp.concatenate(tokens, axis=1),
    )


def contract(left, right, left_dim, right_dim):
    return lax.dot_general(
        left, right, (((left_dim,), (right_dim,)), ((), ())), preferred_element_type=F32
    )


def forward_kernel(
    kv_ref,
    q_ref,
    w_ref,
    key_ref,
    last_ref,
    first_ref,
    buf,
    q_all,
    w_other,
    o_out,
    inv_out,
    o_sum,
    l_sum,
    o_got,
    l_got,
    send,
    recv,
):
    place, net = Place(), Net(send, recv)
    core = place.core
    partner = place.partner()
    greet(ring(place, "x") + ring(place, "y") + ring(place, "z") + [partner])
    mine = pl.ds(pl.multiple_of(core * TOK, TOK), TOK)
    theirs = pl.ds(pl.multiple_of((1 - core) * TOK, TOK), TOK)
    q_all[:, mine] = q_ref[...]
    stages = []
    for part in PARTS:
        skip, rows, _, _ = part
        views = part_views(place, buf, part)
        axis, view = views[0]
        own = view(getattr(place, axis))
        own[...] = kv_ref[pl.ds(skip, rows)]
        stages.append([RingGather(net, place, axis, view, *halves(view)) for axis, view in views])
    for rings in stages:
        rings[0].start()
    swap_q = net.copy(q_all.at[:, mine], q_all.at[:, mine], partner)
    net.go(swap_q)
    for h in range(HEADS):
        o_sum[h] = jnp.zeros((ROWS, HD), F32)
        l_sum[h] = jnp.zeros((ROWS, 128), F32)
    for level in (0, 1):
        for rings in stages:
            rings[level].forward()
        for rings in stages:
            rings[level].finish()
            rings[level + 1].start()
    finish_w = swap_weight(place, net, w_ref, w_other, w_ref.shape[0] // 4)
    swap_q.wait_recv()

    def attend(by):
        keys, values, token = read_sets(place, buf, key_ref, range(8), by)
        allowed = (token <= last_ref[...]) & (token >= first_ref[...])
        for h in range(HEADS):
            weights = jnp.exp(contract(q_all[h], keys, 1, 1))
            weights = jnp.where(allowed, weights, 0.0)
            l_sum[h] += sum(weights[:, 128 * i : 128 * i + 128] for i in range(16))
            o_sum[h] += jnp.dot(weights.astype(BF), values, preferred_element_type=F32)

    attend(0)
    for rings in stages:
        rings[2].forward()
    finish_w()
    lax.fori_loop(0, 2, lambda i, c: (attend(1 + 2 * i), c)[1], 0)
    for rings in stages:
        rings[2].finish()
    attend(2)
    swap_o = net.copy(o_sum.at[:, theirs], o_got, partner)
    swap_l = net.copy(l_sum.at[:, theirs], l_got, partner)
    net.go(swap_l)
    net.go(swap_o)
    swap_l.wait_recv()
    swap_o.wait_recv()
    for h in range(HEADS):
        total = jnp.sum(l_sum[h, mine] + l_got[h], axis=1, keepdims=True)
        inverse = 1.0 / total
        o_out[h] = (o_sum[h, mine] + o_got[h]) * inverse
        inv_out[h] = jnp.broadcast_to(inverse, (TOK, 128))
    net.drain()


def attention_forward(kv, q, w_out, key_rows, last, first, call_id):
    shape = jax.ShapeDtypeStruct
    return pl.pallas_call(
        forward_kernel,
        out_shape=(
            shape((4, 2048, 2 * HD), BF),
            shape((HEADS, ROWS, HD), BF),
            shape(w_out.shape, BF),
            shape((HEADS, TOK, HD), F32),
            shape((HEADS, TOK, 128), F32),
        ),
        in_specs=[IN_VMEM] * 6,
        out_specs=[IN_VMEM] * 5,
        scratch_shapes=[
            pltpu.VMEM((HEADS, ROWS, HD), F32),
            pltpu.VMEM((HEADS, ROWS, 128), F32),
            pltpu.VMEM((HEADS, TOK, HD), F32),
            pltpu.VMEM((HEADS, TOK, 128), F32),
            *sems(48),
        ],
        compiler_params=params(call_id),
    )(kv, q, w_out, key_rows, last, first)


def backward_kernel(
    buf,
    q_all,
    do_ref,
    delta_ref,
    key_ref,
    last_ref,
    first_ref,
    sums_ref,
    dq_out,
    dkv_out,
    home_out,
    do_all,
    delta_all,
    grads,
    dq_sum,
    dq_got,
    *rest,
):
    rooms, rest = rest[:54], rest[54:]
    *weight_refs, send, recv, send2, recv2, here = rest
    place, net = Place(), Net(send, recv)
    core, partner = place.core, place.partner()
    weights = WeightSums(place, net, sums_ref, home_out, weight_refs, (send2, recv2, here))
    greet(weights.friends + ring(place, "x") + ring(place, "y"))
    mine = pl.ds(pl.multiple_of(core * TOK, TOK), TOK)
    theirs = pl.ds(pl.multiple_of((1 - core) * TOK, TOK), TOK)
    do_all[:, mine] = do_ref[...]
    delta_all[core] = delta_ref[...]
    swap_do = net.copy(do_all.at[:, mine], do_all.at[:, mine], partner)
    swap_delta = net.copy(delta_all.at[core], delta_all.at[core], partner)
    net.go(swap_do)
    net.go(swap_delta)
    for h in range(HEADS):
        dq_sum[h] = jnp.zeros((HD, ROWS), F32)
    stages = []
    for i, part in enumerate(PARTS):
        views = part_views(place, grads, part)
        rings = []
        for level, (axis, view) in enumerate(views):
            at = 6 * (3 * i + level)
            rings.append(RingScatter(net, place, axis, *halves(view), rooms[at : at + 6]))
        stages.append((rings, views))
    swap_do.wait_recv()
    swap_delta.wait_recv()

    def differ(first, by):
        chunks = range(first, first + 4)
        keys, values, token = read_sets(place, buf, key_ref, chunks, by)
        token = jnp.concatenate(
            [
                jnp.transpose(jnp.broadcast_to(token[:, 128 * i : 128 * i + 128], (128, 128)))
                for i in range(8)
            ],
            axis=0,
        )
        token = jnp.concatenate([token, token], axis=1)
        allowed = (token <= last_ref[...]) & (token >= first_ref[...])
        d_keys = d_values = None
        for h in range(HEADS):
            probs = jnp.exp(contract(keys, q_all[h], 1, 1))
            probs = jnp.where(allowed, probs, 0.0)
            delta = jnp.concatenate([delta_all[0, h : h + 1], delta_all[1, h : h + 1]], axis=1)
            d_scores = (probs * (contract(values, do_all[h], 1, 1) - delta)).astype(BF)
            value_term = jnp.dot(probs.astype(BF), do_all[h], preferred_element_type=F32)
            key_term = jnp.dot(d_scores, q_all[h], preferred_element_type=F32)
            d_values = value_term if h == 0 else d_values + value_term
            d_keys = key_term if h == 0 else d_keys + key_term
            dq_sum[h] += contract(keys, d_scores, 0, 0)
        d_keys, d_values = d_keys.astype(BF), d_values.astype(BF)
        for m, n in enumerate(chunks):
            lead = place.step("zyx"[n // 3], by)
            for i, start in enumerate(chunk_rows(n)):
                at = 256 * m + 64 * i
                grads[lead, start : start + 64, :HD] = d_keys[at : at + 64]
                grads[lead, start : start + 64, HD:] = d_values[at : at + 64]

    def visit(by):
        differ(0, by)
        differ(4, by)

    weights.begin()
    visit(2)
    for rings, _ in stages:
        rings[2].start_far()
    weights.turn()
    lax.fori_loop(0, 2, lambda i, c: (visit(1 + 2 * i), c)[1], 0)
    for rings, _ in stages:
        rings[2].start_near()
    for rings, _ in stages:
        rings[2].middle()
    weights.next()
    visit(0)
    swap_dq = net.copy(dq_sum.at[:, :, theirs], dq_got, partner)
    net.go(swap_dq)
    weights.turn_again()
    for level in (2, 1, 0):
        for (rings, views), part in zip(stages, PARTS):
            axis, view = views[level]
            lo, hi = halves(view)
            me = getattr(place, axis)
            skip, rows, _, _ = part
            if level:
                rings[level].finish(lo(me), hi(me))
                rings[level - 1].start_far()
                rings[level - 1].start_near()
            else:
                out = dkv_out.at[pl.ds(skip, rows)]
                rings[level].finish(out.at[:, pl.ds(0, HD)], out.at[:, pl.ds(HD, HD)])
        if level == 2:
            weights.send_home()
        if level:
            for rings, _ in stages:
                rings[level - 1].middle()
    weights.arrive()
    swap_dq.wait_recv()
    for h in range(HEADS):
        dq_out[h] = dq_sum[h, :, mine] + dq_got[h]
    net.drain()


def attention_backward(kv_all, q_all, d_heads, delta, key_rows, last, first, sums, call_id):
    shape = jax.ShapeDtypeStruct
    rooms = []
    for _, rows, _, _ in PARTS:
        for blocks in (1, 4, 16):
            rooms += RingScatter.room_shapes((blocks * rows, HD), (blocks * rows, HD))
    return pl.pallas_call(
        backward_kernel,
        out_shape=(
            shape((HEADS, HD, TOK), F32),
            shape((TOK, 2 * HD), F32),
            shape((8, 32, HALF), BF),
        ),
        in_specs=[IN_VMEM] * 8,
        out_specs=[IN_VMEM] * 3,
        scratch_shapes=[
            pltpu.VMEM((HEADS, ROWS, HD), BF),
            pltpu.VMEM((2, 8, TOK), F32),
            pltpu.VMEM((4, 2048, 2 * HD), BF),
            pltpu.VMEM((HEADS, HD, ROWS), F32),
            pltpu.VMEM((HEADS, HD, TOK), F32),
            *rooms,
            *WeightSums.scratch(),
            *sems(96),
            *sems(8),
            pltpu.SemaphoreType.DMA((1,)),
        ],
        compiler_params=params(call_id),
    )(kv_all, q_all, d_heads, delta, key_rows, last, first, sums)


def x_gather_kernel(rows_ref, out_ref, send, recv):
    place, net = Place(), Net(send, recv)
    greet(ring(place, "x"))
    out_ref[place.x] = rows_ref[...]
    line = RingGather(
        net,
        place,
        "x",
        lambda j: out_ref.at[j],
        lambda j: out_ref.at[j, pl.ds(0, TOK // 2)],
        lambda j: out_ref.at[j, pl.ds(TOK // 2, TOK // 2)],
    )
    line.start()
    line.forward()
    line.finish()
    net.drain()


def x_gather(rows, call_id):
    return pl.pallas_call(
        x_gather_kernel,
        out_shape=jax.ShapeDtypeStruct((4, TOK, D), BF),
        in_specs=[IN_VMEM],
        out_specs=IN_VMEM,
        scratch_shapes=sems(4),
        compiler_params=params(call_id),
    )(rows)


def x_scatter_kernel(terms_ref, out_ref, *rest):
    *room, send, recv = rest
    place, net = Place(), Net(send, recv)
    greet(ring(place, "x"))
    half = TOK // 2
    line = RingScatter(
        net,
        place,
        "x",
        lambda j: terms_ref.at[j, pl.ds(0, half)],
        lambda j: terms_ref.at[j, pl.ds(half, half)],
        room,
    )
    line.start_far()
    line.start_near()
    line.middle()
    line.finish(out_ref.at[pl.ds(0, half)], out_ref.at[pl.ds(half, half)])
    net.drain()


def x_scatter(terms, call_id):
    half = (TOK // 2, D)
    return pl.pallas_call(
        x_scatter_kernel,
        out_shape=jax.ShapeDtypeStruct((TOK, D), F32),
        in_specs=[IN_VMEM],
        out_specs=IN_VMEM,
        scratch_shapes=[*RingScatter.room_shapes(half, half), *sems(6)],
        compiler_params=params(call_id),
    )(terms)


def ffn_terms_kernel(
    terms_ref, h_ref, f_ref, gate_ref, up_ref, act_ref, dh_out, sums_out, snd, got, *rest
):
    *room, send, recv = rest
    place, net = Place(), Net(send, recv)
    core, partner = place.core, place.partner()
    greet(ring(place, "x") + [partner])
    half = TOK // 2
    line = RingScatter(
        net,
        place,
        "x",
        lambda j: terms_ref.at[j, pl.ds(0, half)],
        lambda j: terms_ref.at[j, pl.ds(half, half)],
        room,
    )
    line.start_far()
    line.start_near()

    def fill(target, which):
        columns = pl.ds(pl.multiple_of(which * 896, 128), 896)

        def some_rows(i, carry):
            rows = pl.ds(pl.multiple_of(i * 576, 64), 576)
            pairs = ((h_ref, gate_ref), (h_ref, up_ref), (f_ref, act_ref))
            for m, (left, right) in enumerate(pairs):
                term = jnp.dot(left[rows], right[:, columns], preferred_element_type=F32).astype(BF)
                for k in range(4):
                    piece = term[144 * k : 144 * k + 144]
                    for c in range(2):
                        low = max(896 * m, HALF * c)
                        high = min(896 * m + 896, HALF * c + HALF)
                        if low < high:
                            target[2 * i + k // 2, k % 2, c, :, low - HALF * c : high - HALF * c] = (
                                piece[:, low - 896 * m : high - 896 * m]
                            )
            return carry

        lax.fori_loop(0, 2, some_rows, 0)
        for y in range(4):
            target[y, :, 1, :, 1280:] = jnp.zeros((2, 144, 128), BF)

    fill(snd, 1 - core)
    swaps = [net.copy(snd.at[y], got.at[y], partner) for y in range(4)]
    for swap in swaps:
        net.go(swap)
    line.middle()
    fill(sums_out, core)
    line.finish(dh_out.at[pl.ds(0, half)], dh_out.at[pl.ds(half, half)])
    for y, swap in enumerate(swaps):
        swap.wait_recv()
        add_to(sums_out.at[y], got.at[y])
    net.drain()


def ffn_terms(terms, h_turned, f_turned, d_gate, d_up, act, call_id):
    half = (TOK // 2, D)
    shape = jax.ShapeDtypeStruct
    every = (4, 2, 2, 144, HALF)
    return pl.pallas_call(
        ffn_terms_kernel,
        out_shape=(shape((TOK, D), F32), shape(every, BF)),
        in_specs=[IN_VMEM] * 6,
        out_specs=[IN_VMEM] * 2,
        scratch_shapes=[
            pltpu.VMEM(every, BF),
            pltpu.VMEM(every, BF),
            *RingScatter.room_shapes(half, half),
            *sems(10),
        ],
        compiler_params=params(call_id),
    )(terms, h_turned, f_turned, d_gate, d_up, act)


class WeightSums:
    def __init__(self, place, net, sums, home, refs, marks):
        y1, z1, z2, y2, snd, rcv, *rooms = refs
        self.place, self.home, self.snd, self.rcv, self.marks = place, home, snd, rcv, marks
        self.y1, self.z1, self.y2, self.z2 = y1, z1, y2, z2
        self.x_hi, self.x_lo = lax.div(place.x, 2), lax.rem(place.x, 2)
        self.friends = []
        for k in range(1, 16):
            spot = lax.rem(self.x_hi * 8 + place.z * 2 + place.core + k, 16)
            x, z = lax.div(spot, 8) * 2 + self.x_lo, lax.rem(lax.div(spot, 2), 4)
            self.friends.append(place.device(x=x, z=z, core=lax.rem(spot, 2)))

        left, right = pl.ds(0, CUT), pl.ds(CUT, HALF - CUT)

        def z_spot(j):
            return sums.at[:, lax.div(j, 2), lax.rem(j, 2), :, right]

        def then_z(j):
            return y1.at[lax.div(j, 2), lax.rem(j, 2)]

        self.y_first = RingScatter(
            net,
            place,
            "y",
            lambda j: sums.at[j, 0, :, :, left],
            lambda j: sums.at[j, 1, :, :, left],
            rooms[0:6],
        )
        self.z_first = RingScatter(
            net,
            place,
            "z",
            lambda j: z_spot(j).at[pl.ds(0, 2)],
            lambda j: z_spot(j).at[pl.ds(2, 2)],
            rooms[6:12],
        )
        self.z_second = RingScatter(
            net,
            place,
            "z",
            lambda j: then_z(j).at[:, pl.ds(0, 384)],
            lambda j: then_z(j).at[:, pl.ds(384, 384)],
            rooms[12:18],
        )
        self.y_second = RingScatter(
            net,
            place,
            "y",
            lambda j: z1.at[j, :, pl.ds(0, 384)],
            lambda j: z1.at[j, :, pl.ds(384, 256)],
            rooms[18:24],
        )

    @staticmethod
    def scratch():
        rest = HALF - CUT
        return [
            pltpu.VMEM((2, 2, 144, CUT), BF),
            pltpu.VMEM((4, 144, rest), BF),
            pltpu.VMEM((144, CUT), F32),
            pltpu.VMEM((144, rest), F32),
            pltpu.VMEM((8, 32, HALF), BF),
            pltpu.VMEM((8, 32, HALF), BF),
            *RingScatter.room_shapes((2, 144, CUT), (2, 144, CUT)),
            *RingScatter.room_shapes((2, 144, rest), (2, 144, rest)),
            *RingScatter.room_shapes((144, 384), (144, 384)),
            *RingScatter.room_shapes((144, 384), (144, 256)),
        ]

    def begin(self):
        for line in (self.y_first, self.z_first):
            line.start_far()
            line.start_near()

    def turn(self):
        self.y_first.middle()
        self.z_first.middle()

    def next(self):
        self.y_first.finish(self.y1.at[0], self.y1.at[1])
        self.z_second.start_far()
        self.z_second.start_near()
        self.z_first.finish(self.z1.at[pl.ds(0, 2)], self.z1.at[pl.ds(2, 2)])
        self.y_second.start_far()
        self.y_second.start_near()

    def turn_again(self):
        self.z_second.middle()
        self.y_second.middle()

    def send_home(self):
        z2, y2, snd = self.z2, self.y2, self.snd
        self.z_second.finish(z2.at[:, pl.ds(0, 384)], z2.at[:, pl.ds(384, 384)])
        self.y_second.finish(y2.at[:, pl.ds(0, 384)], y2.at[:, pl.ds(384, 256)])
        total = jnp.concatenate([z2[...], y2[...]], axis=1)
        blank = jnp.zeros((14, HALF), F32)
        for k in range(8):
            snd[k] = jnp.concatenate([total[18 * k : 18 * k + 18], blank], axis=0).astype(BF)
        place = self.place
        send, recv, here = self.marks
        row_half = lax.div(place.z, 2)
        self.slot = self.x_hi * 4 + place.core * 2 + lax.rem(place.z, 2)
        self.own = place.z * 2 + place.core
        self.stays = row_half == self.x_hi
        for k in range(8):
            copy = pltpu.make_async_remote_copy(
                src_ref=snd.at[k],
                dst_ref=self.rcv.at[self.slot],
                send_sem=send.at[k],
                recv_sem=recv.at[self.slot],
                device_id=place.device(x=row_half * 2 + self.x_lo, z=k // 2, core=k % 2),
                device_id_type=MESH,
            )
            is_here = self.stays & (self.own == k)

            @pl.when(jnp.logical_not(is_here))
            def _(copy=copy):
                copy.start()

            @pl.when(is_here)
            def _(k=k):
                keep = pltpu.make_async_copy(snd.at[k], self.rcv.at[self.slot], here.at[0])
                keep.start()
                keep.wait()

    def arrive(self):
        send, recv, _ = self.marks
        for m in range(8):
            arrival = pltpu.make_async_remote_copy(
                src_ref=self.snd.at[m],
                dst_ref=self.rcv.at[m],
                send_sem=send.at[m],
                recv_sem=recv.at[m],
                device_id=self.place.partner(),
                device_id_type=MESH,
            )

            @pl.when(jnp.logical_not(self.stays & (self.slot == m)))
            def _(arrival=arrival):
                arrival.wait_recv()

            @pl.when(jnp.logical_not(self.stays & (self.own == m)))
            def _(arrival=arrival):
                arrival.wait_send()

        self.home[...] = self.rcv[...]


LANES = 384
ORDERS = (("x", "y", "z"), ("y", "z", "x"), ("z", "x", "y"))


def small_grads_kernel(terms_ref, gains_ref, out_ref, gains_out, got, sums, gain_got, *rest):
    *rooms, send, recv = rest
    place, net = Place(), Net(send, recv)
    core, partner = place.core, place.partner()
    greet(ring(place, "x") + ring(place, "y") + ring(place, "z") + [partner])
    swap = net.copy(terms_ref.at[1 - core], got, partner)
    gain_got[0, core] = gains_ref[...]
    gain_swap = net.copy(gain_got.at[0, core], gain_got.at[0, core], partner)
    net.go(gain_swap)
    net.go(swap)

    def gain_ring(level, axis):
        return RingGather(
            net,
            place,
            axis,
            lambda j: gain_got.at[level, j],
            lambda j: gain_got.at[level, j, :, pl.ds(0, 512)],
            lambda j: gain_got.at[level, j, :, pl.ds(512, 640)],
        )

    gain_lines = [gain_ring(1, "x"), gain_ring(2, "y"), gain_ring(3, "z")]
    gain_swap.wait_recv()
    gain_got[1, place.x] = gain_got[0, 0] + gain_got[0, 1]
    gain_lines[0].start()

    rows = out_ref.at[core]
    scatters, gathers = [], []
    for p, (first, second, third) in enumerate(ORDERS):
        lanes = pl.ds(LANES * p, LANES)
        at1, at2, at3 = (getattr(place, axis) for axis in (first, second, third))

        def views(ref, lanes=lanes, at1=at1):
            def piece(start, size):
                return ref.at[pl.ds(pl.multiple_of(start, 16), size), lanes]

            return (
                lambda j: piece(320 * j, 320),
                lambda j: piece(320 * j, 160),
                lambda j: piece(320 * j + 160, 160),
                lambda j: piece(320 * at1 + 80 * j, 80),
                lambda j: piece(320 * at1 + 80 * j, 48),
                lambda j: piece(320 * at1 + 80 * j + 48, 32),
            )

        _, lo1, hi1, term2, lo2, hi2 = views(got)
        room = rooms[12 * p : 12 * p + 12]
        scatters.append(
            (
                (RingScatter(net, place, first, lo1, hi1, room[:6]), lo1, hi1, at1),
                (RingScatter(net, place, second, lo2, hi2, room[6:]), lo2, hi2, at2),
            )
        )
        spot = sums.at[p]
        last = RingGather(
            net,
            place,
            third,
            lambda j, spot=spot: spot.at[j],
            lambda j, spot=spot: spot.at[j, pl.ds(0, 48)],
            lambda j, spot=spot: spot.at[j, pl.ds(48, 32)],
        )
        whole1, whole_lo1, whole_hi1, whole2, whole_lo2, whole_hi2 = views(rows)
        gathers.append(
            (
                last,
                RingGather(net, place, second, whole2, whole_lo2, whole_hi2),
                RingGather(net, place, first, whole1, whole_lo1, whole_hi1),
                term2(at2),
                whole2(at2),
                at3,
            )
        )
    swap.wait_recv()
    add_to(got, terms_ref.at[core])
    for level in (0, 1):
        for pair in scatters:
            pair[level][0].start_far()
            pair[level][0].start_near()
        for pair in scatters:
            pair[level][0].middle()
        gain_lines[level].forward()
        for pair in scatters:
            line, lo, hi, at = pair[level]
            line.finish(lo(at), hi(at))
        gain_lines[level].finish()
        nxt = place.y if level == 0 else place.z
        gain_got[level + 2, nxt] = (gain_got[level + 1, 0] + gain_got[level + 1, 1]) + (
            gain_got[level + 1, 2] + gain_got[level + 1, 3]
        )
        gain_lines[level + 1].start()
    for p, (last, _, _, term, _, at3) in enumerate(gathers):
        sums[p, at3] = term[...]
        last.start()
    for last, *_ in gathers:
        last.forward()
    gain_lines[2].forward()
    for p, (last, second, _, _, own, _) in enumerate(gathers):
        last.finish()
        sum_to(own, [sums.at[p, j] for j in range(4)])
        second.start()
    for _, second, *_ in gathers:
        second.forward()
    for _, second, first, *_ in gathers:
        second.finish()
        first.start()
    for _, _, first, *_ in gathers:
        first.forward()
    gain_lines[2].finish()
    gains_out[...] = (gain_got[3, 0] + gain_got[3, 1]) + (gain_got[3, 2] + gain_got[3, 3])
    for _, _, first, *_ in gathers:
        first.finish()
    final = net.copy(rows, rows, partner)
    net.go(final)
    final.wait_recv()
    net.drain()


def small_grads(terms, gains, call_id):
    shape = jax.ShapeDtypeStruct
    rooms = []
    for _ in ORDERS:
        rooms += RingScatter.room_shapes((160, LANES), (160, LANES))
        rooms += RingScatter.room_shapes((48, LANES), (32, LANES))
    return pl.pallas_call(
        small_grads_kernel,
        out_shape=(shape(terms.shape, BF), shape(gains.shape, F32)),
        in_specs=[IN_VMEM] * 2,
        out_specs=[IN_VMEM] * 2,
        scratch_shapes=[
            pltpu.VMEM((1280, D), BF),
            pltpu.VMEM((3, 4, 80, LANES), BF),
            pltpu.VMEM((4, 4, 8, D), F32),
            *rooms,
            *sems(96),
        ],
        compiler_params=params(call_id),
    )(terms, gains)


def rms_scale(tensor, scaling):
    return tensor * lax.rsqrt(jnp.mean(tensor * tensor, axis=-1, keepdims=True) + EPS) * scaling


def angles(token_pos):
    middle = HD // 2
    frequency = THETA ** (-2.0 * jnp.arange(middle, dtype=F32) / HD)
    turned = token_pos.astype(F32)[:, None] * frequency[None, :]
    return (jnp.cos(turned), jnp.sin(turned))


def rotary(tensor, cosine, sine):
    middle = tensor.shape[-1] // 2
    lower_half = tensor[..., :middle]
    upper_half = tensor[..., middle:]
    return jnp.concatenate(
        [lower_half * cosine - upper_half * sine, upper_half * cosine + lower_half * sine], axis=-1
    )


def glu_piece(gate_in, up_in):
    return jax.nn.gelu(gate_in, approximate=True) * up_in


def shards(
    layer_input,
    segment_ids,
    positions,
    w_query,
    w_key,
    w_value,
    w_out,
    w_gate,
    w_up,
    w_down,
    norm_attn,
    norm_query,
    norm_key,
    norm_post,
    norm_ffn,
    norm_out,
    cotangent,
):
    sp, tp = lax.axis_index("sp"), lax.axis_index("tp")
    core, x_hi = lax.rem(sp, 2), lax.rem(lax.div(sp, 8), 2)
    own_start = (sp * 2 + tp) * TOK
    chip_start = lax.div(sp, 2) * 512 + tp * TOK

    firsts = jnp.sum(
        (segment_ids[None, :] < jnp.arange(4, dtype=jnp.int32)[:, None]).astype(jnp.int32), axis=1
    )
    row_token = chip_start + jnp.concatenate([jnp.arange(TOK), 256 + jnp.arange(TOK)]).astype(
        jnp.int32
    )
    row_segs = jnp.concatenate(
        [
            lax.dynamic_slice_in_dim(segment_ids, chip_start, TOK),
            lax.dynamic_slice_in_dim(segment_ids, chip_start + 256, TOK),
        ]
    )
    row_first = jnp.zeros_like(row_token)
    for k in range(4):
        row_first = jnp.where(row_segs == k, firsts[k], row_first)
    key_rows = jnp.asarray(KEY_TOKENS) + core * 256
    cosine, sine = angles(lax.dynamic_slice_in_dim(positions, own_start, TOK))

    def query_piece(pre_rot, scaling):
        return rotary(rms_scale(pre_rot, scaling), cosine[:, None, :], sine[:, None, :])

    def key_piece(pre_rot, scaling):
        return rotary(rms_scale(pre_rot, scaling), cosine, sine)

    wq_other = fetch_weight(w_query, 1)
    wq_both = jnp.concatenate([w_query, wq_other], axis=1)
    input_f = layer_input.astype(F32)
    h_attn = rms_scale(input_f, norm_attn).astype(BF)
    q_pre = jnp.dot(h_attn, wq_both, preferred_element_type=F32).reshape(TOK, HEADS, HD)
    q_rot = query_piece(q_pre, norm_query).astype(BF)
    q_scaled = (q_rot * BF(HD**-0.5)).transpose(1, 0, 2)
    k_pre = jnp.dot(h_attn, w_key, preferred_element_type=F32)
    k_rot = key_piece(k_pre, norm_key).astype(BF)
    v_own = jnp.dot(h_attn, w_value, preferred_element_type=F32).astype(BF)
    kv_own = jnp.concatenate([k_rot, v_own], axis=1)
    kv_all, q_all, wo_other, o_heads, inverse = attention_forward(
        kv_own, q_scaled, w_out, key_rows, row_token[:, None], row_first[:, None], 2
    )
    wo_both = jnp.concatenate([w_out, wo_other], axis=0)
    o_cat = o_heads.transpose(1, 0, 2).astype(BF).reshape(TOK, HEADS * HD)
    attn_out = jnp.dot(o_cat, wo_both, preferred_element_type=F32)
    mid = input_f + rms_scale(attn_out, norm_post)
    h_ffn = rms_scale(mid, norm_ffn).astype(BF)

    def units(weight, dim):
        part = lax.dynamic_slice_in_dim(weight, x_hi * HID, HID, axis=dim)
        pads = [(0, 0), (0, 0)]
        pads[dim] = (0, HID_PAD - HID)
        return jnp.pad(part, pads)

    gate_w, up_w, down_w = units(w_gate, 1), units(w_up, 1), units(w_down, 0)
    h_line = x_gather(h_ffn, 3).reshape(4 * TOK, D)
    gate = jnp.dot(h_line, gate_w, preferred_element_type=F32)
    upper = jnp.dot(h_line, up_w, preferred_element_type=F32)
    act = glu_piece(gate, upper).astype(BF)
    ffn_term = jnp.dot(act, down_w, preferred_element_type=F32).astype(BF)
    ffn_out = x_scatter(ffn_term.reshape(4, TOK, D), 4)
    layer_output = (mid + rms_scale(ffn_out, norm_out)).astype(BF)
    grad_out = cotangent.astype(F32)
    _, pull_out = jax.vjp(rms_scale, ffn_out, norm_out)
    d_ffn_out, d_norm_out = pull_out(grad_out)
    d_ffn_line = x_gather(d_ffn_out.astype(BF), 5).reshape(4 * TOK, D)
    d_act = contract(d_ffn_line, down_w, 1, 1)
    _, pull_glu = jax.vjp(glu_piece, gate, upper)
    d_gate, d_upper = pull_glu(d_act)
    d_gate = d_gate.astype(BF)
    d_upper = d_upper.astype(BF)
    d_h_term = (contract(d_gate, gate_w, 1, 1) + contract(d_upper, up_w, 1, 1)).astype(BF)
    d_h_ffn, sums = ffn_terms(
        d_h_term.reshape(4, TOK, D), h_line.T, d_ffn_line.T, d_gate, d_upper, act, 6
    )

    _, pull_ffn = jax.vjp(rms_scale, mid, norm_ffn)
    d_mid_norm, d_norm_ffn = pull_ffn(d_h_ffn)
    d_mid = grad_out + d_mid_norm
    _, pull_post = jax.vjp(rms_scale, attn_out, norm_post)
    d_attn_out, d_norm_post = pull_post(d_mid)
    d_attn = d_attn_out.astype(BF)
    d_o = contract(d_attn, wo_both, 1, 1).astype(BF).reshape(TOK, HEADS, HD).transpose(1, 0, 2)
    inv_rows = inverse[..., :1]
    d_o_f = d_o.astype(F32)
    delta = jnp.sum(d_o_f * o_heads, axis=2) * inverse[..., 0]
    delta = jnp.concatenate([delta, jnp.zeros((4, TOK), F32)], axis=0)
    dq_turned, d_kv, ffn_done = attention_backward(
        kv_all,
        q_all,
        (d_o_f * inv_rows).astype(BF),
        delta,
        key_rows,
        row_token[None, :],
        row_first[None, :],
        sums,
        8,
    )
    ffn_done = (
        ffn_done.reshape(2, 2, 2, 32, HALF)[:, :, :, :18]
        .transpose(3, 0, 1, 2, 4)
        .reshape(18, 2, 2, 2 * HALF)
        .astype(F32)
    )

    def home(which):
        part = ffn_done[..., 896 * which : 896 * (which + 1)].reshape(18, 2, HID_PAD)
        return part[:, :, :HID].reshape(18, 2 * HID)

    d_q_rot = (dq_turned.transpose(2, 0, 1) * HD**-0.5).astype(BF).astype(F32)
    d_kv = d_kv.astype(BF)
    _, pull_key = jax.vjp(key_piece, k_pre, norm_key)
    d_k_pre, d_norm_key = pull_key(d_kv[:, :HD].astype(F32))
    d_k_pre = d_k_pre.astype(BF)
    d_value = d_kv[:, HD:]
    _, pull_query = jax.vjp(query_piece, q_pre, norm_query)
    d_q_pre, d_norm_query = pull_query(d_q_rot)
    d_q_pre = d_q_pre.reshape(TOK, HEADS * HD).astype(BF)
    d_h_attn = (
        contract(d_q_pre, wq_both, 1, 1)
        + contract(d_k_pre, w_key, 1, 1)
        + contract(d_value, w_value, 1, 1)
    )
    _, pull_attn = jax.vjp(rms_scale, input_f, norm_attn)
    d_input_norm, d_norm_attn = pull_attn(d_h_attn)
    d_input = (d_mid + d_input_norm).astype(BF)

    def in_order(both):
        return jnp.where(tp == 0, both, jnp.roll(both, 2 * HD, axis=1))

    small = jnp.concatenate(
        [
            contract(in_order(d_q_pre), h_attn, 0, 0),
            contract(d_k_pre, h_attn, 0, 0),
            contract(in_order(o_cat), d_attn, 0, 0),
            contract(d_value, h_attn, 0, 0),
        ],
        axis=0,
    ).astype(BF)
    gains = jnp.stack(
        [
            d_norm_attn,
            d_norm_post,
            d_norm_ffn,
            d_norm_out,
            jnp.concatenate([d_norm_query, d_norm_key, jnp.zeros((D - 2 * HD,), F32)]),
            *([jnp.zeros((D,), F32)] * 3),
        ]
    )
    small, gains = small_grads(small.reshape(2, 1280, D), gains, 9)

    def cut(matrix):
        return lax.dynamic_slice(matrix, (tp * 512, sp * 18), (512, 18)).astype(F32)

    return (
        layer_output,
        d_input,
        cut(small[0, :1024]).T,
        small[0, 1024:].astype(F32).T,
        small[1, 1024:].astype(F32).T,
        cut(small[1, :1024]),
        home(0),
        home(1),
        home(2).T,
        gains[0],
        gains[4, :HD],
        gains[4, HD : 2 * HD],
        gains[1],
        gains[2],
        gains[3],
    )


def solution(mesh):
    rows = P(("sp", "tp"), None)
    in_specs = (
        rows,
        P(),
        P(),
        P(None, "tp"),
        P(),
        P(),
        P("tp", None),
        P(None, "tp"),
        P(None, "tp"),
        P("tp", None),
        P(),
        P(),
        P(),
        P(),
        P(),
        P(),
        rows,
    )
    out_specs = (
        rows,
        rows,
        P("sp", "tp"),
        P(),
        P(),
        P("tp", "sp"),
        P("sp", "tp"),
        P("sp", "tp"),
        P("tp", "sp"),
        P(),
        P(),
        P(),
        P(),
        P(),
        P(),
    )
    return jax.shard_map(shards, mesh=mesh, in_specs=in_specs, out_specs=out_specs, check_vma=False)
```

```python
import jax
import jax.numpy as jnp
import numpy as np
from jax import lax
from jax.experimental import pallas as pl
from jax.experimental.pallas import tpu as pltpu
from jax.sharding import PartitionSpec as P

EPS = 1e-06
THETA = 1000000.0
BF = jnp.bfloat16
F32 = jnp.float32
MESH = pl.DeviceIdType.MESH
IN_VMEM = pl.BlockSpec(memory_space=pltpu.VMEM)
VMEM_BYTES = 58 * 1024 * 1024

TOK = 128
D = 1152
HD = 256
HEADS = 4
ROWS = 2 * TOK
HID = 1728
HID_PAD = 1792
HALF = 1408
CUT = 768
CHUNK = 256


class Place:
    def __init__(self):
        sp = lax.axis_index("sp")
        self.core = lax.rem(sp, 2)
        self.z = lax.rem(lax.div(sp, 2), 4)
        self.y = lax.div(sp, 16)
        self.x = lax.rem(lax.div(sp, 8), 2) * 2 + lax.axis_index("tp")

    def device(self, **moved):
        x, y, z, core = (moved.get(name, getattr(self, name)) for name in ("x", "y", "z", "core"))
        return (((y * 2 + lax.div(x, 2)) * 4 + z) * 2 + core, lax.rem(x, 2))

    def step(self, axis, by):
        return lax.rem(getattr(self, axis) + by, 4)

    def toward(self, axis, by):
        return self.device(**{axis: self.step(axis, by)})

    def partner(self):
        return self.device(core=1 - self.core)


class Net:
    def __init__(self, send, recv):
        self.send, self.recv, self.used, self.started = send, recv, 0, []

    def copy(self, source, target, device):
        at = self.used
        self.used += 1
        return pltpu.make_async_remote_copy(
            src_ref=source,
            dst_ref=target,
            send_sem=self.send.at[at],
            recv_sem=self.recv.at[at],
            device_id=device,
            device_id_type=MESH,
        )

    def go(self, copy):
        copy.start()
        self.started.append(copy)

    def drain(self):
        for copy in self.started:
            copy.wait_send()
        self.started = []


def greet(devices):
    barrier = pltpu.get_barrier_semaphore()
    for device in devices:
        pl.semaphore_signal(barrier, inc=1, device_id=device, device_id_type=MESH)
    pl.semaphore_wait(barrier, len(devices))


def ring(place, axis):
    return [place.toward(axis, 1), place.toward(axis, 3)]


class RingGather:
    def __init__(self, net, place, axis, view, lo, hi):
        self.net = net
        me, nxt, prev = getattr(place, axis), place.step(axis, 1), place.step(axis, 3)
        right, left = ring(place, axis)
        self.to_right = net.copy(view(me), view(me), right)
        self.to_left = net.copy(view(me), view(me), left)
        self.on_right = net.copy(lo(prev), lo(prev), right)
        self.on_left = net.copy(hi(nxt), hi(nxt), left)

    def start(self):
        self.net.go(self.to_right)
        self.net.go(self.to_left)

    def forward(self):
        self.to_right.wait_recv()
        self.net.go(self.on_right)
        self.to_left.wait_recv()
        self.net.go(self.on_left)

    def finish(self):
        self.on_right.wait_recv()
        self.on_left.wait_recv()


def by_rows(ref, act):
    *lead, rows, _ = ref.shape
    block = next(size for size in (64, 48, 32, 16) if rows % size == 0)
    for spot in np.ndindex(*lead):

        def one(i, carry, spot=spot):
            act(spot, pl.ds(pl.multiple_of(i * block, block), block))
            return carry

        lax.fori_loop(0, rows // block, one, 0)


def add_to(target, other):
    def act(spot, rows):
        at = (*spot, rows, slice(None))
        target[at] = (target[at].astype(F32) + other[at].astype(F32)).astype(target.dtype)

    by_rows(target, act)


def sum_to(target, others):
    def act(spot, rows):
        at = (*spot, rows, slice(None))
        total = others[0][at].astype(F32)
        for other in others[1:]:
            total = total + other[at].astype(F32)
        target[at] = total.astype(target.dtype)

    by_rows(target, act)


class RingScatter:
    def __init__(self, net, place, axis, lo, hi, room):
        self.net, self.lo, self.hi = net, lo, hi
        self.me, self.nxt, self.opp, self.prev = (place.step(axis, by) for by in range(4))
        right, left = ring(place, axis)
        self.lo1, self.lo_l, self.lo_r, self.hi1, self.hi_l, self.hi_r = room
        self.a = net.copy(lo(self.opp), self.lo1, right)
        self.b = net.copy(hi(self.opp), self.hi1, left)
        self.c_hi = net.copy(hi(self.nxt), self.hi_l, right)
        self.d_lo = net.copy(lo(self.prev), self.lo_r, left)
        self.c_lo = net.copy(self.lo1, self.lo_l, right)
        self.d_hi = net.copy(self.hi1, self.hi_r, left)

    def start_far(self):
        self.net.go(self.a)
        self.net.go(self.b)

    def start_near(self):
        self.net.go(self.c_hi)
        self.net.go(self.d_lo)

    def middle(self):
        self.a.wait_recv()
        add_to(self.lo1, self.lo(self.nxt))
        self.net.go(self.c_lo)
        self.b.wait_recv()
        add_to(self.hi1, self.hi(self.prev))
        self.net.go(self.d_hi)

    def finish(self, lo_out, hi_out):
        self.c_hi.wait_recv()
        self.d_hi.wait_recv()
        sum_to(hi_out, [self.hi(self.me), self.hi_l, self.hi_r])
        self.d_lo.wait_recv()
        self.c_lo.wait_recv()
        sum_to(lo_out, [self.lo(self.me), self.lo_l, self.lo_r])

    @staticmethod
    def room_shapes(lo_shape, hi_shape):
        return [pltpu.VMEM(lo_shape, BF)] * 3 + [pltpu.VMEM(hi_shape, BF)] * 3


def params(call_id):
    return pltpu.CompilerParams(
        collective_id=call_id, has_side_effects=True, vmem_limit_bytes=VMEM_BYTES
    )


def sems(count):
    return [pltpu.SemaphoreType.DMA((count,)), pltpu.SemaphoreType.DMA((count,))]


def weight_kernel(w_ref, other_ref, send, recv):
    place, net = Place(), Net(send, recv)
    right, left = ring(place, "x")
    quarter = w_ref.shape[0] // 4
    greet([right, left, place.partner()])
    finish = swap_weight(place, net, w_ref, other_ref, quarter)
    finish()
    net.drain()


def swap_weight(place, net, w_ref, other_ref, quarter):
    right, left = ring(place, "x")
    core = place.core

    def rows(side):
        return pl.ds(pl.multiple_of((2 * side + core) * quarter, 16), quarter)

    def cores_rows(side):
        return other_ref.at[rows(side)]

    one = net.copy(w_ref.at[rows(0)], cores_rows(0), left)
    two = net.copy(w_ref.at[rows(1)], cores_rows(1), right)
    trades = [net.copy(cores_rows(side), cores_rows(side), place.partner()) for side in (0, 1)]
    net.go(one)
    net.go(two)

    def finish():
        for first, trade in zip((one, two), trades):
            first.wait_recv()
            net.go(trade)
        for trade in trades:
            trade.wait_recv()

    return finish


def fetch_weight(w, call_id):
    return pl.pallas_call(
        weight_kernel,
        out_shape=jax.ShapeDtypeStruct(w.shape, w.dtype),
        in_specs=[IN_VMEM],
        out_specs=IN_VMEM,
        scratch_shapes=sems(4),
        compiler_params=params(call_id),
    )(w)


PARTS = (
    (0, 48, 0, ("x", "y", "z")),
    (48, 48, 768, ("z", "x", "y")),
    (96, 32, 1536, ("y", "z", "x")),
)


def part_views(place, buf, part):
    _, rows, base, (first, second, third) = part
    at1, at2, at3 = (getattr(place, axis) for axis in (first, second, third))

    def block(lead, start, size):
        return buf.at[lead, pl.ds(pl.multiple_of(base + start, 16), size)]

    return (
        (first, lambda j: block(at3, (at2 * 4 + j) * rows, rows)),
        (second, lambda j: block(at3, j * 4 * rows, 4 * rows)),
        (third, lambda j: block(j, 0, 16 * rows)),
    )


def halves(view):
    return (lambda j: view(j).at[:, pl.ds(0, HD)]), (lambda j: view(j).at[:, pl.ds(HD, HD)])


def chunk_rows(n):
    return [256 * n + 64 * i if n < 6 else 1536 + 128 * i + 64 * (n - 6) for i in range(4)]


def key_tokens():
    out = np.zeros((4, 2048), np.int32)
    for skip, rows, base, axes in PARTS:
        for j in range(4):
            for r in range(16 * rows):
                spot = {axes[2]: j, axes[1]: r // (4 * rows), axes[0]: (r // rows) % 4}
                x, y, z = spot["x"], spot["y"], spot["z"]
                token = ((y * 2 + x // 2) * 4 + z) * 512 + (x % 2) * 128 + skip + r % rows
                out[j, base + r] = token
    order = np.zeros((8, CHUNK), np.int64)
    for c in range(8):
        for i in range(4):
            start = chunk_rows(c)[i]
            order[c, 64 * i : 64 * i + 64] = np.arange(start, start + 64)
    return out[:, order]


KEY_TOKENS = key_tokens()


def read_sets(place, buf, key_ref, chunks, by):
    keys, values, tokens = [], [], []
    for n in chunks:
        lead = place.step("zyx"[n // 3], by)
        rows = chunk_rows(n)
        keys += [buf[lead, start : start + 64, :HD] for start in rows]
        values += [buf[lead, start : start + 64, HD:] for start in rows]
        tokens.append(key_ref[lead, n : n + 1])
    return (
        jnp.concatenate(keys, axis=0),
        jnp.concatenate(values, axis=0),
        jnp.concatenate(tokens, axis=1),
    )


def contract(left, right, left_dim, right_dim):
    return lax.dot_general(
        left, right, (((left_dim,), (right_dim,)), ((), ())), preferred_element_type=F32
    )


def forward_kernel(
    kv_ref,
    q_ref,
    w_ref,
    key_ref,
    last_ref,
    first_ref,
    buf,
    q_all,
    w_other,
    o_out,
    inv_out,
    o_sum,
    l_sum,
    o_got,
    l_got,
    send,
    recv,
):
    place, net = Place(), Net(send, recv)
    core = place.core
    partner = place.partner()
    greet(ring(place, "x") + ring(place, "y") + ring(place, "z") + [partner])
    mine = pl.ds(pl.multiple_of(core * TOK, TOK), TOK)
    theirs = pl.ds(pl.multiple_of((1 - core) * TOK, TOK), TOK)
    q_all[:, mine] = q_ref[...]
    stages = []
    for part in PARTS:
        skip, rows, _, _ = part
        views = part_views(place, buf, part)
        axis, view = views[0]
        own = view(getattr(place, axis))
        own[...] = kv_ref[pl.ds(skip, rows)]
        stages.append([RingGather(net, place, axis, view, *halves(view)) for axis, view in views])
    for rings in stages:
        rings[0].start()
    swap_q = net.copy(q_all.at[:, mine], q_all.at[:, mine], partner)
    net.go(swap_q)
    for h in range(HEADS):
        o_sum[h] = jnp.zeros((ROWS, HD), F32)
        l_sum[h] = jnp.zeros((ROWS, 128), F32)
    for level in (0, 1):
        for rings in stages:
            rings[level].forward()
        for rings in stages:
            rings[level].finish()
            rings[level + 1].start()
    finish_w = swap_weight(place, net, w_ref, w_other, w_ref.shape[0] // 4)
    swap_q.wait_recv()

    def attend(by):
        keys, values, token = read_sets(place, buf, key_ref, range(8), by)
        allowed = (token <= last_ref[...]) & (token >= first_ref[...])
        for h in range(HEADS):
            weights = jnp.exp(contract(q_all[h], keys, 1, 1))
            weights = jnp.where(allowed, weights, 0.0)
            l_sum[h] += sum(weights[:, 128 * i : 128 * i + 128] for i in range(16))
            o_sum[h] += jnp.dot(weights.astype(BF), values, preferred_element_type=F32)

    attend(0)
    for rings in stages:
        rings[2].forward()
    finish_w()
    lax.fori_loop(0, 2, lambda i, c: (attend(1 + 2 * i), c)[1], 0)
    for rings in stages:
        rings[2].finish()
    attend(2)
    swap_o = net.copy(o_sum.at[:, theirs], o_got, partner)
    swap_l = net.copy(l_sum.at[:, theirs], l_got, partner)
    net.go(swap_l)
    net.go(swap_o)
    swap_l.wait_recv()
    swap_o.wait_recv()
    for h in range(HEADS):
        total = jnp.sum(l_sum[h, mine] + l_got[h], axis=1, keepdims=True)
        inverse = 1.0 / total
        o_out[h] = (o_sum[h, mine] + o_got[h]) * inverse
        inv_out[h] = jnp.broadcast_to(inverse, (TOK, 128))
    net.drain()


def attention_forward(kv, q, w_out, key_rows, last, first, call_id):
    shape = jax.ShapeDtypeStruct
    return pl.pallas_call(
        forward_kernel,
        out_shape=(
            shape((4, 2048, 2 * HD), BF),
            shape((HEADS, ROWS, HD), BF),
            shape(w_out.shape, BF),
            shape((HEADS, TOK, HD), F32),
            shape((HEADS, TOK, 128), F32),
        ),
        in_specs=[IN_VMEM] * 6,
        out_specs=[IN_VMEM] * 5,
        scratch_shapes=[
            pltpu.VMEM((HEADS, ROWS, HD), F32),
            pltpu.VMEM((HEADS, ROWS, 128), F32),
            pltpu.VMEM((HEADS, TOK, HD), F32),
            pltpu.VMEM((HEADS, TOK, 128), F32),
            *sems(48),
        ],
        compiler_params=params(call_id),
    )(kv, q, w_out, key_rows, last, first)


def backward_kernel(
    buf,
    q_all,
    do_ref,
    delta_ref,
    key_ref,
    last_ref,
    first_ref,
    sums_ref,
    dq_out,
    dkv_out,
    home_out,
    do_all,
    delta_all,
    grads,
    dq_sum,
    dq_got,
    *rest,
):
    rooms, rest = rest[:54], rest[54:]
    *weight_refs, send, recv, send2, recv2, here = rest
    place, net = Place(), Net(send, recv)
    core, partner = place.core, place.partner()
    weights = WeightSums(place, net, sums_ref, home_out, weight_refs, (send2, recv2, here))
    greet(weights.friends + ring(place, "x") + ring(place, "y"))
    mine = pl.ds(pl.multiple_of(core * TOK, TOK), TOK)
    theirs = pl.ds(pl.multiple_of((1 - core) * TOK, TOK), TOK)
    do_all[:, mine] = do_ref[...]
    delta_all[core] = delta_ref[...]
    swap_do = net.copy(do_all.at[:, mine], do_all.at[:, mine], partner)
    swap_delta = net.copy(delta_all.at[core], delta_all.at[core], partner)
    net.go(swap_do)
    net.go(swap_delta)
    for h in range(HEADS):
        dq_sum[h] = jnp.zeros((HD, ROWS), F32)
    stages = []
    for i, part in enumerate(PARTS):
        views = part_views(place, grads, part)
        rings = []
        for level, (axis, view) in enumerate(views):
            at = 6 * (3 * i + level)
            rings.append(RingScatter(net, place, axis, *halves(view), rooms[at : at + 6]))
        stages.append((rings, views))
    swap_do.wait_recv()
    swap_delta.wait_recv()

    def differ(first, by):
        chunks = range(first, first + 4)
        keys, values, token = read_sets(place, buf, key_ref, chunks, by)
        token = jnp.concatenate(
            [
                jnp.transpose(jnp.broadcast_to(token[:, 128 * i : 128 * i + 128], (128, 128)))
                for i in range(8)
            ],
            axis=0,
        )
        token = jnp.concatenate([token, token], axis=1)
        allowed = (token <= last_ref[...]) & (token >= first_ref[...])
        d_keys = d_values = None
        for h in range(HEADS):
            probs = jnp.exp(contract(keys, q_all[h], 1, 1))
            probs = jnp.where(allowed, probs, 0.0)
            delta = jnp.concatenate([delta_all[0, h : h + 1], delta_all[1, h : h + 1]], axis=1)
            d_scores = (probs * (contract(values, do_all[h], 1, 1) - delta)).astype(BF)
            value_term = jnp.dot(probs.astype(BF), do_all[h], preferred_element_type=F32)
            key_term = jnp.dot(d_scores, q_all[h], preferred_element_type=F32)
            d_values = value_term if h == 0 else d_values + value_term
            d_keys = key_term if h == 0 else d_keys + key_term
            dq_sum[h] += contract(keys, d_scores, 0, 0)
        d_keys, d_values = d_keys.astype(BF), d_values.astype(BF)
        for m, n in enumerate(chunks):
            lead = place.step("zyx"[n // 3], by)
            for i, start in enumerate(chunk_rows(n)):
                at = 256 * m + 64 * i
                grads[lead, start : start + 64, :HD] = d_keys[at : at + 64]
                grads[lead, start : start + 64, HD:] = d_values[at : at + 64]

    def visit(by):
        differ(0, by)
        differ(4, by)

    weights.begin()
    visit(2)
    for rings, _ in stages:
        rings[2].start_far()
    weights.turn()
    lax.fori_loop(0, 2, lambda i, c: (visit(1 + 2 * i), c)[1], 0)
    for rings, _ in stages:
        rings[2].start_near()
    for rings, _ in stages:
        rings[2].middle()
    weights.next()
    visit(0)
    swap_dq = net.copy(dq_sum.at[:, :, theirs], dq_got, partner)
    net.go(swap_dq)
    weights.turn_again()
    for level in (2, 1, 0):
        for (rings, views), part in zip(stages, PARTS):
            axis, view = views[level]
            lo, hi = halves(view)
            me = getattr(place, axis)
            skip, rows, _, _ = part
            if level:
                rings[level].finish(lo(me), hi(me))
                rings[level - 1].start_far()
                rings[level - 1].start_near()
            else:
                out = dkv_out.at[pl.ds(skip, rows)]
                rings[level].finish(out.at[:, pl.ds(0, HD)], out.at[:, pl.ds(HD, HD)])
        if level == 2:
            weights.send_home()
        if level:
            for rings, _ in stages:
                rings[level - 1].middle()
    weights.arrive()
    swap_dq.wait_recv()
    for h in range(HEADS):
        dq_out[h] = dq_sum[h, :, mine] + dq_got[h]
    net.drain()


def attention_backward(kv_all, q_all, d_heads, delta, key_rows, last, first, sums, call_id):
    shape = jax.ShapeDtypeStruct
    rooms = []
    for _, rows, _, _ in PARTS:
        for blocks in (1, 4, 16):
            rooms += RingScatter.room_shapes((blocks * rows, HD), (blocks * rows, HD))
    return pl.pallas_call(
        backward_kernel,
        out_shape=(
            shape((HEADS, HD, TOK), F32),
            shape((TOK, 2 * HD), F32),
            shape((8, 32, HALF), BF),
        ),
        in_specs=[IN_VMEM] * 8,
        out_specs=[IN_VMEM] * 3,
        scratch_shapes=[
            pltpu.VMEM((HEADS, ROWS, HD), BF),
            pltpu.VMEM((2, 8, TOK), F32),
            pltpu.VMEM((4, 2048, 2 * HD), BF),
            pltpu.VMEM((HEADS, HD, ROWS), F32),
            pltpu.VMEM((HEADS, HD, TOK), F32),
            *rooms,
            *WeightSums.scratch(),
            *sems(96),
            *sems(8),
            pltpu.SemaphoreType.DMA((1,)),
        ],
        compiler_params=params(call_id),
    )(kv_all, q_all, d_heads, delta, key_rows, last, first, sums)


def norm_scale(v):
    return lax.rsqrt(jnp.mean(v * v, axis=-1, keepdims=True) + EPS)


def norm_back(v, r, gain, e):
    eg = e * gain
    dv = r * eg - v * (r * r * r) * jnp.mean(eg * v, axis=-1, keepdims=True)
    return dv, jnp.sum(e * v * r, axis=0, keepdims=True)


def feed_kernel(
    x_ref,
    o_ref,
    inv_ref,
    wo_ref,
    wo2_ref,
    gains_ref,
    cot_ref,
    wg_hbm,
    wu_hbm,
    wd_hbm,
    out_ref,
    dmid_out,
    dattn_out,
    do_out,
    delta_out,
    dgains_out,
    sums_hbm,
    wg,
    wu,
    wd,
    h_line,
    f_line,
    h_turned,
    f_turned,
    gelu_kept,
    slope_kept,
    act,
    d_gate,
    d_up,
    f_terms,
    h_terms,
    snd,
    got,
    attn,
    mid,
    ffn,
    *rest,
):
    *room, send, recv, local = rest
    place, net = Place(), Net(send, recv)
    core, partner = place.core, place.partner()
    x_hi = lax.div(place.x, 2)
    first_unit = pl.multiple_of(x_hi * (2 * HID - HID_PAD), 128)
    window = pl.ds(first_unit, HID_PAD)
    loads = [
        pltpu.make_async_copy(source, target, local.at[i])
        for i, (source, target) in enumerate(
            ((wg_hbm.at[:, window], wg), (wu_hbm.at[:, window], wu), (wd_hbm.at[window], wd))
        )
    ]
    for load in loads:
        load.start()
    greet(ring(place, "x") + [partner])
    half = TOK // 2
    top, bottom = pl.ds(0, half), pl.ds(half, half)
    g_post, g_ffn, g_out = (gains_ref[i : i + 1] for i in range(3))

    def gather(lines):
        line = RingGather(
            net,
            place,
            "x",
            lambda j: lines.at[j],
            lambda j: lines.at[j, top],
            lambda j: lines.at[j, bottom],
        )
        line.start()
        line.forward()
        line.finish()

    def scatter(terms, room):
        line = RingScatter(
            net, place, "x", lambda j: terms.at[j, top], lambda j: terms.at[j, bottom], room
        )
        line.start_far()
        line.start_near()
        return line

    o_cat = [o_ref[h].astype(BF) for h in range(HEADS)]
    a = jnp.dot(jnp.concatenate(o_cat[:2], axis=1), wo_ref[...], preferred_element_type=F32)
    a += jnp.dot(jnp.concatenate(o_cat[2:], axis=1), wo2_ref[...], preferred_element_type=F32)
    attn[...] = a
    mid[...] = x_ref[...].astype(F32) + a * norm_scale(a) * g_post
    m = mid[...]
    h_line[place.x] = (m * norm_scale(m) * g_ffn).astype(BF)
    gather(h_line)

    for load in loads:
        load.wait()
    lines = 4 * TOK
    low_unit, high_unit = jnp.where(x_hi == 0, 0, 64), jnp.where(x_hi == 0, HID, HID_PAD)

    def units(n):
        return pl.ds(pl.multiple_of(n * 256, 256), 256)

    def forward(n, carry):
        h = h_line[...].reshape(lines, D)
        gate = jnp.dot(h, wg[:, units(n)], preferred_element_type=F32)
        up = jnp.dot(h, wu[:, units(n)], preferred_element_type=F32)
        unit = n * 256 + lax.broadcasted_iota(jnp.int32, (1, 256), 1)
        own = jnp.where((unit >= low_unit) & (unit < high_unit), 1.0, 0.0)
        scale, cube = 0.7978845608028654, 0.044715
        square = gate * gate
        bent = jnp.tanh(scale * gate * (1.0 + cube * square))
        lifted = 0.5 * (1.0 + bent)
        gelu = gate * lifted * own
        slope = lifted + 0.5 * gate * (1.0 - bent * bent) * scale * (1.0 + 3.0 * cube * square)
        act[:, units(n)] = (gelu * up).astype(BF)
        gelu_kept[:, units(n)] = gelu.astype(BF)
        slope_kept[:, units(n)] = (slope * up * own).astype(BF)
        return carry

    lax.fori_loop(0, HID_PAD // 256, forward, 0)

    def columns(n):
        return pl.ds(pl.multiple_of(n * 384, 128), 384)

    def project(n, carry):
        term = jnp.dot(act[...], wd[:, columns(n)], preferred_element_type=F32)
        f_terms[:, :, columns(n)] = term.astype(BF).reshape(4, TOK, 384)
        return carry

    lax.fori_loop(0, 3, project, 0)
    line = scatter(f_terms, room[:6])
    h_turned[...] = jnp.transpose(h_line[...].reshape(lines, D))
    line.middle()
    line.finish(ffn.at[top], ffn.at[bottom])
    f = ffn[...]
    r_out = norm_scale(f)
    out_ref[...] = (mid[...] + f * r_out * g_out).astype(BF)
    df, d_out = norm_back(f, r_out, g_out, cot_ref[...].astype(F32))
    f_line[place.x] = df.astype(BF)
    gather(f_line)

    def backward(n, carry):
        d_act = contract(f_line[...].reshape(lines, D), wd[units(n)], 1, 1)
        d_gate[:, units(n)] = (d_act * slope_kept[:, units(n)].astype(F32)).astype(BF)
        d_up[:, units(n)] = (d_act * gelu_kept[:, units(n)].astype(F32)).astype(BF)
        return carry

    lax.fori_loop(0, HID_PAD // 256, backward, 0)

    def back_project(n, carry):
        term = contract(d_gate[...], wg[columns(n)], 1, 1) + contract(d_up[...], wu[columns(n)], 1, 1)
        h_terms[:, :, columns(n)] = term.astype(BF).reshape(4, TOK, 384)
        return carry

    lax.fori_loop(0, 3, back_project, 0)
    line = scatter(h_terms, room[6:])
    f_turned[...] = jnp.transpose(f_line[...].reshape(lines, D))

    def fill(i, which, put):
        some = pl.ds(pl.multiple_of(which * 896, 128), 896)
        rows = pl.ds(576 * i, 576)
        pairs = ((h_turned, d_gate), (h_turned, d_up), (f_turned, act))
        for m, (left, right) in enumerate(pairs):
            term = jnp.dot(left[rows], right[:, some], preferred_element_type=F32)
            for k in range(4):
                piece = term[144 * k : 144 * k + 144]
                for c in range(2):
                    low = max(896 * m, HALF * c)
                    high = min(896 * m + 896, HALF * c + HALF)
                    if low < high:
                        at = (2 * i + k // 2, k % 2, c, slice(None), slice(low - HALF * c, high - HALF * c))
                        put(at, piece[:, low - 896 * m : high - 896 * m])

    def put_snd(at, value):
        snd[at] = value.astype(BF)

    def put_got(at, value):
        got[at] = (got[at].astype(F32) + value).astype(BF)

    swaps = [net.copy(snd.at[y], got.at[y], partner) for y in range(4)]
    for y in range(4):
        snd[y, :, 1, :, 1280:] = jnp.zeros((2, 144, 128), BF)
    for i in range(2):
        fill(i, 1 - core, put_snd)
        net.go(swaps[2 * i])
        net.go(swaps[2 * i + 1])
    line.middle()
    stores = [pltpu.make_async_copy(got.at[y], sums_hbm.at[y], local.at[3 + y]) for y in range(4)]
    for i in range(2):
        swaps[2 * i].wait_recv()
        swaps[2 * i + 1].wait_recv()
        fill(i, core, put_got)
        stores[2 * i].start()
        stores[2 * i + 1].start()
    line.finish(ffn.at[top], ffn.at[bottom])

    m, a = mid[...], attn[...]
    dm, d_ffn = norm_back(m, norm_scale(m), g_ffn, ffn[...])
    d_mid = cot_ref[...].astype(F32) + dm
    dmid_out[...] = d_mid
    da, d_post = norm_back(a, norm_scale(a), g_post, d_mid)
    da = da.astype(BF)
    dattn_out[...] = da
    dgains_out[...] = jnp.concatenate([d_post, d_ffn, d_out, jnp.zeros((5, D), F32)], axis=0)
    delta_out[...] = jnp.zeros((8, TOK), F32)
    for h in range(HEADS):
        weight = (wo_ref, wo2_ref)[h // 2]
        d_o = contract(da, weight[256 * (h % 2) : 256 * (h % 2) + 256], 1, 1).astype(BF).astype(F32)
        inverse = inv_ref[h]
        do_out[h] = (d_o * jnp.concatenate([inverse, inverse], axis=1)).astype(BF)
        delta = jnp.sum(d_o * o_ref[h], axis=1, keepdims=True) * inverse
        delta_out[h : h + 1] = jnp.transpose(delta)[:1]
    for store in stores:
        store.wait()
    net.drain()


def feed_forward(x, o_heads, inverse, wo, wo2, gains, cotangent, w_gate, w_up, w_down, call_id):
    half = (TOK // 2, D)
    shape = jax.ShapeDtypeStruct
    every = (4, 2, 2, 144, HALF)
    lines = 4 * TOK
    anywhere = pl.BlockSpec(memory_space=pl.ANY)
    unit_rows = [pltpu.VMEM((lines, HID_PAD), BF)] * 5
    return pl.pallas_call(
        feed_kernel,
        out_shape=(
            shape((TOK, D), BF),
            shape((TOK, D), F32),
            shape((TOK, D), BF),
            shape((HEADS, TOK, HD), BF),
            shape((8, TOK), F32),
            shape((8, D), F32),
            shape(every, BF),
        ),
        in_specs=[IN_VMEM] * 7 + [anywhere] * 3,
        out_specs=[IN_VMEM] * 6 + [anywhere],
        scratch_shapes=[
            pltpu.VMEM((D, HID_PAD), BF),
            pltpu.VMEM((D, HID_PAD), BF),
            pltpu.VMEM((HID_PAD, D), BF),
            pltpu.VMEM((4, TOK, D), BF),
            pltpu.VMEM((4, TOK, D), BF),
            pltpu.VMEM((D, lines), BF),
            pltpu.VMEM((D, lines), BF),
            *unit_rows,
            pltpu.VMEM((4, TOK, D), BF),
            pltpu.VMEM((4, TOK, D), BF),
            pltpu.VMEM(every, BF),
            pltpu.VMEM(every, BF),
            pltpu.VMEM((TOK, D), F32),
            pltpu.VMEM((TOK, D), F32),
            pltpu.VMEM((TOK, D), F32),
            *RingScatter.room_shapes(half, half),
            *RingScatter.room_shapes(half, half),
            *sems(32),
            pltpu.SemaphoreType.DMA((7,)),
        ],
        compiler_params=params(call_id),
    )(x, o_heads, inverse, wo, wo2, gains, cotangent, w_gate, w_up, w_down)


class WeightSums:
    def __init__(self, place, net, sums, home, refs, marks):
        y1, z1, z2, y2, snd, rcv, *rooms = refs
        self.place, self.home, self.snd, self.rcv, self.marks = place, home, snd, rcv, marks
        self.y1, self.z1, self.y2, self.z2 = y1, z1, y2, z2
        self.x_hi, self.x_lo = lax.div(place.x, 2), lax.rem(place.x, 2)
        self.friends = []
        for k in range(1, 16):
            spot = lax.rem(self.x_hi * 8 + place.z * 2 + place.core + k, 16)
            x, z = lax.div(spot, 8) * 2 + self.x_lo, lax.rem(lax.div(spot, 2), 4)
            self.friends.append(place.device(x=x, z=z, core=lax.rem(spot, 2)))

        left, right = pl.ds(0, CUT), pl.ds(CUT, HALF - CUT)

        def z_spot(j):
            return sums.at[:, lax.div(j, 2), lax.rem(j, 2), :, right]

        def then_z(j):
            return y1.at[lax.div(j, 2), lax.rem(j, 2)]

        self.y_first = RingScatter(
            net,
            place,
            "y",
            lambda j: sums.at[j, 0, :, :, left],
            lambda j: sums.at[j, 1, :, :, left],
            rooms[0:6],
        )
        self.z_first = RingScatter(
            net,
            place,
            "z",
            lambda j: z_spot(j).at[pl.ds(0, 2)],
            lambda j: z_spot(j).at[pl.ds(2, 2)],
            rooms[6:12],
        )
        self.z_second = RingScatter(
            net,
            place,
            "z",
            lambda j: then_z(j).at[:, pl.ds(0, 384)],
            lambda j: then_z(j).at[:, pl.ds(384, 384)],
            rooms[12:18],
        )
        self.y_second = RingScatter(
            net,
            place,
            "y",
            lambda j: z1.at[j, :, pl.ds(0, 384)],
            lambda j: z1.at[j, :, pl.ds(384, 256)],
            rooms[18:24],
        )

    @staticmethod
    def scratch():
        rest = HALF - CUT
        return [
            pltpu.VMEM((2, 2, 144, CUT), BF),
            pltpu.VMEM((4, 144, rest), BF),
            pltpu.VMEM((144, CUT), F32),
            pltpu.VMEM((144, rest), F32),
            pltpu.VMEM((8, 32, HALF), BF),
            pltpu.VMEM((8, 32, HALF), BF),
            *RingScatter.room_shapes((2, 144, CUT), (2, 144, CUT)),
            *RingScatter.room_shapes((2, 144, rest), (2, 144, rest)),
            *RingScatter.room_shapes((144, 384), (144, 384)),
            *RingScatter.room_shapes((144, 384), (144, 256)),
        ]

    def begin(self):
        for line in (self.y_first, self.z_first):
            line.start_far()
            line.start_near()

    def turn(self):
        self.y_first.middle()
        self.z_first.middle()

    def next(self):
        self.y_first.finish(self.y1.at[0], self.y1.at[1])
        self.z_second.start_far()
        self.z_second.start_near()
        self.z_first.finish(self.z1.at[pl.ds(0, 2)], self.z1.at[pl.ds(2, 2)])
        self.y_second.start_far()
        self.y_second.start_near()

    def turn_again(self):
        self.z_second.middle()
        self.y_second.middle()

    def send_home(self):
        z2, y2, snd = self.z2, self.y2, self.snd
        self.z_second.finish(z2.at[:, pl.ds(0, 384)], z2.at[:, pl.ds(384, 384)])
        self.y_second.finish(y2.at[:, pl.ds(0, 384)], y2.at[:, pl.ds(384, 256)])
        total = jnp.concatenate([z2[...], y2[...]], axis=1)
        blank = jnp.zeros((14, HALF), F32)
        for k in range(8):
            snd[k] = jnp.concatenate([total[18 * k : 18 * k + 18], blank], axis=0).astype(BF)
        place = self.place
        send, recv, here = self.marks
        row_half = lax.div(place.z, 2)
        self.slot = self.x_hi * 4 + place.core * 2 + lax.rem(place.z, 2)
        self.own = place.z * 2 + place.core
        self.stays = row_half == self.x_hi
        for k in range(8):
            copy = pltpu.make_async_remote_copy(
                src_ref=snd.at[k],
                dst_ref=self.rcv.at[self.slot],
                send_sem=send.at[k],
                recv_sem=recv.at[self.slot],
                device_id=place.device(x=row_half * 2 + self.x_lo, z=k // 2, core=k % 2),
                device_id_type=MESH,
            )
            is_here = self.stays & (self.own == k)

            @pl.when(jnp.logical_not(is_here))
            def _(copy=copy):
                copy.start()

            @pl.when(is_here)
            def _(k=k):
                keep = pltpu.make_async_copy(snd.at[k], self.rcv.at[self.slot], here.at[0])
                keep.start()
                keep.wait()

    def arrive(self):
        send, recv, _ = self.marks
        for m in range(8):
            arrival = pltpu.make_async_remote_copy(
                src_ref=self.snd.at[m],
                dst_ref=self.rcv.at[m],
                send_sem=send.at[m],
                recv_sem=recv.at[m],
                device_id=self.place.partner(),
                device_id_type=MESH,
            )

            @pl.when(jnp.logical_not(self.stays & (self.slot == m)))
            def _(arrival=arrival):
                arrival.wait_recv()

            @pl.when(jnp.logical_not(self.stays & (self.own == m)))
            def _(arrival=arrival):
                arrival.wait_send()

        self.home[...] = self.rcv[...]


LANES = 384
ORDERS = (("x", "y", "z"), ("y", "z", "x"), ("z", "x", "y"))


def small_grads_kernel(terms_ref, gains_ref, out_ref, gains_out, got, sums, gain_got, *rest):
    *rooms, send, recv = rest
    place, net = Place(), Net(send, recv)
    core, partner = place.core, place.partner()
    greet(ring(place, "x") + ring(place, "y") + ring(place, "z") + [partner])
    swap = net.copy(terms_ref.at[1 - core], got, partner)
    gain_got[0, core] = gains_ref[...]
    gain_swap = net.copy(gain_got.at[0, core], gain_got.at[0, core], partner)
    net.go(gain_swap)
    net.go(swap)

    def gain_ring(level, axis):
        return RingGather(
            net,
            place,
            axis,
            lambda j: gain_got.at[level, j],
            lambda j: gain_got.at[level, j, :, pl.ds(0, 512)],
            lambda j: gain_got.at[level, j, :, pl.ds(512, 640)],
        )

    gain_lines = [gain_ring(1, "x"), gain_ring(2, "y"), gain_ring(3, "z")]
    gain_swap.wait_recv()
    gain_got[1, place.x] = gain_got[0, 0] + gain_got[0, 1]
    gain_lines[0].start()

    rows = out_ref.at[core]
    scatters, gathers = [], []
    for p, (first, second, third) in enumerate(ORDERS):
        lanes = pl.ds(LANES * p, LANES)
        at1, at2, at3 = (getattr(place, axis) for axis in (first, second, third))

        def views(ref, lanes=lanes, at1=at1):
            def piece(start, size):
                return ref.at[pl.ds(pl.multiple_of(start, 16), size), lanes]

            return (
                lambda j: piece(320 * j, 320),
                lambda j: piece(320 * j, 160),
                lambda j: piece(320 * j + 160, 160),
                lambda j: piece(320 * at1 + 80 * j, 80),
                lambda j: piece(320 * at1 + 80 * j, 48),
                lambda j: piece(320 * at1 + 80 * j + 48, 32),
            )

        _, lo1, hi1, term2, lo2, hi2 = views(got)
        room = rooms[12 * p : 12 * p + 12]
        scatters.append(
            (
                (RingScatter(net, place, first, lo1, hi1, room[:6]), lo1, hi1, at1),
                (RingScatter(net, place, second, lo2, hi2, room[6:]), lo2, hi2, at2),
            )
        )
        spot = sums.at[p]
        last = RingGather(
            net,
            place,
            third,
            lambda j, spot=spot: spot.at[j],
            lambda j, spot=spot: spot.at[j, pl.ds(0, 48)],
            lambda j, spot=spot: spot.at[j, pl.ds(48, 32)],
        )
        whole1, whole_lo1, whole_hi1, whole2, whole_lo2, whole_hi2 = views(rows)
        gathers.append(
            (
                last,
                RingGather(net, place, second, whole2, whole_lo2, whole_hi2),
                RingGather(net, place, first, whole1, whole_lo1, whole_hi1),
                term2(at2),
                whole2(at2),
                at3,
            )
        )
    swap.wait_recv()
    add_to(got, terms_ref.at[core])
    for level in (0, 1):
        for pair in scatters:
            pair[level][0].start_far()
            pair[level][0].start_near()
        for pair in scatters:
            pair[level][0].middle()
        gain_lines[level].forward()
        for pair in scatters:
            line, lo, hi, at = pair[level]
            line.finish(lo(at), hi(at))
        gain_lines[level].finish()
        nxt = place.y if level == 0 else place.z
        gain_got[level + 2, nxt] = (gain_got[level + 1, 0] + gain_got[level + 1, 1]) + (
            gain_got[level + 1, 2] + gain_got[level + 1, 3]
        )
        gain_lines[level + 1].start()
    for p, (last, _, _, term, _, at3) in enumerate(gathers):
        sums[p, at3] = term[...]
        last.start()
    for last, *_ in gathers:
        last.forward()
    gain_lines[2].forward()
    for p, (last, second, _, _, own, _) in enumerate(gathers):
        last.finish()
        sum_to(own, [sums.at[p, j] for j in range(4)])
        second.start()
    for _, second, *_ in gathers:
        second.forward()
    for _, second, first, *_ in gathers:
        second.finish()
        first.start()
    for _, _, first, *_ in gathers:
        first.forward()
    gain_lines[2].finish()
    gains_out[...] = (gain_got[3, 0] + gain_got[3, 1]) + (gain_got[3, 2] + gain_got[3, 3])
    for _, _, first, *_ in gathers:
        first.finish()
    final = net.copy(rows, rows, partner)
    net.go(final)
    final.wait_recv()
    net.drain()


def small_grads(terms, gains, call_id):
    shape = jax.ShapeDtypeStruct
    rooms = []
    for _ in ORDERS:
        rooms += RingScatter.room_shapes((160, LANES), (160, LANES))
        rooms += RingScatter.room_shapes((48, LANES), (32, LANES))
    return pl.pallas_call(
        small_grads_kernel,
        out_shape=(shape(terms.shape, BF), shape(gains.shape, F32)),
        in_specs=[IN_VMEM] * 2,
        out_specs=[IN_VMEM] * 2,
        scratch_shapes=[
            pltpu.VMEM((1280, D), BF),
            pltpu.VMEM((3, 4, 80, LANES), BF),
            pltpu.VMEM((4, 4, 8, D), F32),
            *rooms,
            *sems(96),
        ],
        compiler_params=params(call_id),
    )(terms, gains)


def rms_scale(tensor, scaling):
    return tensor * lax.rsqrt(jnp.mean(tensor * tensor, axis=-1, keepdims=True) + EPS) * scaling


def angles(token_pos):
    middle = HD // 2
    frequency = THETA ** (-2.0 * jnp.arange(middle, dtype=F32) / HD)
    turned = token_pos.astype(F32)[:, None] * frequency[None, :]
    return (jnp.cos(turned), jnp.sin(turned))


def rotary(tensor, cosine, sine):
    middle = tensor.shape[-1] // 2
    lower_half = tensor[..., :middle]
    upper_half = tensor[..., middle:]
    return jnp.concatenate(
        [lower_half * cosine - upper_half * sine, upper_half * cosine + lower_half * sine], axis=-1
    )


def shards(
    layer_input,
    segment_ids,
    positions,
    w_query,
    w_key,
    w_value,
    w_out,
    w_gate,
    w_up,
    w_down,
    norm_attn,
    norm_query,
    norm_key,
    norm_post,
    norm_ffn,
    norm_out,
    cotangent,
):
    sp, tp = lax.axis_index("sp"), lax.axis_index("tp")
    core = lax.rem(sp, 2)
    own_start = (sp * 2 + tp) * TOK
    chip_start = lax.div(sp, 2) * 512 + tp * TOK

    firsts = jnp.sum(
        (segment_ids[None, :] < jnp.arange(4, dtype=jnp.int32)[:, None]).astype(jnp.int32), axis=1
    )
    row_token = chip_start + jnp.concatenate([jnp.arange(TOK), 256 + jnp.arange(TOK)]).astype(
        jnp.int32
    )
    row_segs = jnp.concatenate(
        [
            lax.dynamic_slice_in_dim(segment_ids, chip_start, TOK),
            lax.dynamic_slice_in_dim(segment_ids, chip_start + 256, TOK),
        ]
    )
    row_first = jnp.zeros_like(row_token)
    for k in range(4):
        row_first = jnp.where(row_segs == k, firsts[k], row_first)
    key_rows = jnp.asarray(KEY_TOKENS) + core * 256
    cosine, sine = angles(lax.dynamic_slice_in_dim(positions, own_start, TOK))

    def query_piece(pre_rot, scaling):
        return rotary(rms_scale(pre_rot, scaling), cosine[:, None, :], sine[:, None, :])

    def key_piece(pre_rot, scaling):
        return rotary(rms_scale(pre_rot, scaling), cosine, sine)

    wq_other = fetch_weight(w_query, 1)
    wq_both = jnp.concatenate([w_query, wq_other], axis=1)
    input_f = layer_input.astype(F32)
    h_attn = rms_scale(input_f, norm_attn).astype(BF)
    q_pre = jnp.dot(h_attn, wq_both, preferred_element_type=F32).reshape(TOK, HEADS, HD)
    q_rot = query_piece(q_pre, norm_query).astype(BF)
    q_scaled = (q_rot * BF(HD**-0.5)).transpose(1, 0, 2)
    k_pre = jnp.dot(h_attn, w_key, preferred_element_type=F32)
    k_rot = key_piece(k_pre, norm_key).astype(BF)
    v_own = jnp.dot(h_attn, w_value, preferred_element_type=F32).astype(BF)
    kv_own = jnp.concatenate([k_rot, v_own], axis=1)
    kv_all, q_all, wo_other, o_heads, inverse = attention_forward(
        kv_own, q_scaled, w_out, key_rows, row_token[:, None], row_first[:, None], 2
    )
    o_cat = o_heads.transpose(1, 0, 2).astype(BF).reshape(TOK, HEADS * HD)
    layer_output, d_mid, d_attn, d_heads, delta, d_gains, sums = feed_forward(
        layer_input,
        o_heads,
        inverse,
        w_out,
        wo_other,
        jnp.stack([norm_post, norm_ffn, norm_out]),
        cotangent,
        w_gate,
        w_up,
        w_down,
        6,
    )
    dq_turned, d_kv, ffn_done = attention_backward(
        kv_all,
        q_all,
        d_heads,
        delta,
        key_rows,
        row_token[None, :],
        row_first[None, :],
        sums,
        8,
    )
    ffn_done = (
        ffn_done.reshape(2, 2, 2, 32, HALF)[:, :, :, :18]
        .transpose(3, 0, 1, 2, 4)
        .reshape(18, 2, 2, 2 * HALF)
        .astype(F32)
    )

    def home(which):
        part = ffn_done[..., 896 * which : 896 * (which + 1)].reshape(18, 2, HID_PAD)
        return jnp.concatenate([part[:, 0, :HID], part[:, 1, HID_PAD - HID :]], axis=1)

    d_q_rot = (dq_turned.transpose(2, 0, 1) * HD**-0.5).astype(BF).astype(F32)
    d_kv = d_kv.astype(BF)
    _, pull_key = jax.vjp(key_piece, k_pre, norm_key)
    d_k_pre, d_norm_key = pull_key(d_kv[:, :HD].astype(F32))
    d_k_pre = d_k_pre.astype(BF)
    d_value = d_kv[:, HD:]
    _, pull_query = jax.vjp(query_piece, q_pre, norm_query)
    d_q_pre, d_norm_query = pull_query(d_q_rot)
    d_q_pre = d_q_pre.reshape(TOK, HEADS * HD).astype(BF)
    d_h_attn = (
        contract(d_q_pre, wq_both, 1, 1)
        + contract(d_k_pre, w_key, 1, 1)
        + contract(d_value, w_value, 1, 1)
    )
    _, pull_attn = jax.vjp(rms_scale, input_f, norm_attn)
    d_input_norm, d_norm_attn = pull_attn(d_h_attn)
    d_input = (d_mid + d_input_norm).astype(BF)

    def in_order(both):
        return jnp.where(tp == 0, both, jnp.roll(both, 2 * HD, axis=1))

    small = jnp.concatenate(
        [
            contract(in_order(d_q_pre), h_attn, 0, 0),
            contract(d_k_pre, h_attn, 0, 0),
            contract(in_order(o_cat), d_attn, 0, 0),
            contract(d_value, h_attn, 0, 0),
        ],
        axis=0,
    ).astype(BF)
    gains = jnp.stack(
        [
            d_norm_attn,
            d_gains[0],
            d_gains[1],
            d_gains[2],
            jnp.concatenate([d_norm_query, d_norm_key, jnp.zeros((D - 2 * HD,), F32)]),
            *([jnp.zeros((D,), F32)] * 3),
        ]
    )
    small, gains = small_grads(small.reshape(2, 1280, D), gains, 9)

    def cut(matrix):
        return lax.dynamic_slice(matrix, (tp * 512, sp * 18), (512, 18)).astype(F32)

    return (
        layer_output,
        d_input,
        cut(small[0, :1024]).T,
        small[0, 1024:].astype(F32).T,
        small[1, 1024:].astype(F32).T,
        cut(small[1, :1024]),
        home(0),
        home(1),
        home(2).T,
        gains[0],
        gains[4, :HD],
        gains[4, HD : 2 * HD],
        gains[1],
        gains[2],
        gains[3],
    )


def solution(mesh):
    rows = P(("sp", "tp"), None)
    in_specs = (
        rows,
        P(),
        P(),
        P(None, "tp"),
        P(),
        P(),
        P("tp", None),
        P(None, "tp"),
        P(None, "tp"),
        P("tp", None),
        P(),
        P(),
        P(),
        P(),
        P(),
        P(),
        rows,
    )
    out_specs = (
        rows,
        rows,
        P("sp", "tp"),
        P(),
        P(),
        P("tp", "sp"),
        P("sp", "tp"),
        P("sp", "tp"),
        P("tp", "sp"),
        P(),
        P(),
        P(),
        P(),
        P(),
        P(),
    )
    return jax.shard_map(shards, mesh=mesh, in_specs=in_specs, out_specs=out_specs, check_vma=False)
```

```python
import jax
import jax.numpy as jnp
import numpy as np
from jax import lax
from jax.experimental import pallas as pl
from jax.experimental.pallas import tpu as pltpu
from jax.sharding import PartitionSpec as P

EPS = 1e-06
THETA = 1000000.0
BF = jnp.bfloat16
F32 = jnp.float32
MESH = pl.DeviceIdType.MESH
IN_VMEM = pl.BlockSpec(memory_space=pltpu.VMEM)
VMEM_BYTES = 58 * 1024 * 1024

TOK = 128
D = 1152
HD = 256
HEADS = 4
ROWS = 2 * TOK
HID = 1728
HID_PAD = 1792
HALF = 1408
CUT = 768
CHUNK = 256


class Place:
    def __init__(self):
        sp = lax.axis_index("sp")
        self.core = lax.rem(sp, 2)
        self.z = lax.rem(lax.div(sp, 2), 4)
        self.y = lax.div(sp, 16)
        self.x = lax.rem(lax.div(sp, 8), 2) * 2 + lax.axis_index("tp")

    def device(self, **moved):
        x, y, z, core = (moved.get(name, getattr(self, name)) for name in ("x", "y", "z", "core"))
        return (((y * 2 + lax.div(x, 2)) * 4 + z) * 2 + core, lax.rem(x, 2))

    def step(self, axis, by):
        return lax.rem(getattr(self, axis) + by, 4)

    def toward(self, axis, by):
        return self.device(**{axis: self.step(axis, by)})

    def partner(self):
        return self.device(core=1 - self.core)


class Net:
    def __init__(self, send, recv):
        self.send, self.recv, self.used, self.started = send, recv, 0, []

    def copy(self, source, target, device):
        at = self.used
        self.used += 1
        return pltpu.make_async_remote_copy(
            src_ref=source,
            dst_ref=target,
            send_sem=self.send.at[at],
            recv_sem=self.recv.at[at],
            device_id=device,
            device_id_type=MESH,
        )

    def go(self, copy):
        copy.start()
        self.started.append(copy)

    def settle(self, copy):
        copy.wait_send()
        self.started = [other for other in self.started if other is not copy]

    def drain(self):
        for copy in self.started:
            copy.wait_send()
        self.started = []


def greet(devices):
    barrier = pltpu.get_barrier_semaphore()
    for device in devices:
        pl.semaphore_signal(barrier, inc=1, device_id=device, device_id_type=MESH)
    pl.semaphore_wait(barrier, len(devices))


def ring(place, axis):
    return [place.toward(axis, 1), place.toward(axis, 3)]


class RingGather:
    def __init__(self, net, place, axis, view, lo, hi):
        self.net = net
        me, nxt, prev = getattr(place, axis), place.step(axis, 1), place.step(axis, 3)
        right, left = ring(place, axis)
        self.to_right = net.copy(view(me), view(me), right)
        self.to_left = net.copy(view(me), view(me), left)
        self.on_right = net.copy(lo(prev), lo(prev), right)
        self.on_left = net.copy(hi(nxt), hi(nxt), left)

    def start(self):
        self.net.go(self.to_right)
        self.net.go(self.to_left)

    def forward(self):
        self.to_right.wait_recv()
        self.net.go(self.on_right)
        self.to_left.wait_recv()
        self.net.go(self.on_left)

    def finish(self):
        self.on_right.wait_recv()
        self.on_left.wait_recv()


class Direct:
    def __init__(self, net, place, axis, source, landing):
        self.net = net
        self.copies = [
            net.copy(
                source(place.step(axis, by)), landing(getattr(place, axis)), place.toward(axis, by)
            )
            for by in (2, 1, 3)
        ]

    def start(self):
        for copy in self.copies:
            self.net.go(copy)

    def wait(self):
        for copy in self.copies:
            copy.wait_recv()


def by_rows(ref, act):
    *lead, rows, _ = ref.shape
    block = next(size for size in (64, 48, 32, 16) if rows % size == 0)
    for spot in np.ndindex(*lead):

        def one(i, carry, spot=spot):
            act(spot, pl.ds(pl.multiple_of(i * block, block), block))
            return carry

        lax.fori_loop(0, rows // block, one, 0)


def add_to(target, other):
    def act(spot, rows):
        at = (*spot, rows, slice(None))
        target[at] = (target[at].astype(F32) + other[at].astype(F32)).astype(target.dtype)

    by_rows(target, act)


def sum_to(target, others):
    def act(spot, rows):
        at = (*spot, rows, slice(None))
        total = others[0][at].astype(F32)
        for other in others[1:]:
            total = total + other[at].astype(F32)
        target[at] = total.astype(target.dtype)

    by_rows(target, act)


def stepped(place, axis, view):
    return lambda by: view(place.step(axis, by))


class RingScatter:
    def __init__(self, net, place, axis, lo, hi, room, lo_here=None, hi_here=None):
        self.net, self.lo, self.hi = net, lo_here or lo, hi_here or hi
        right, left = ring(place, axis)
        self.lo1, self.lo_l, self.lo_r, self.hi1, self.hi_l, self.hi_r = room
        self.a = net.copy(lo(2), self.lo1, right)
        self.b = net.copy(hi(2), self.hi1, left)
        self.c_hi = net.copy(hi(1), self.hi_l, right)
        self.d_lo = net.copy(lo(3), self.lo_r, left)
        self.c_lo = net.copy(self.lo1, self.lo_l, right)
        self.d_hi = net.copy(self.hi1, self.hi_r, left)

    def start_far(self):
        self.net.go(self.a)
        self.net.go(self.b)

    def start_near(self):
        self.net.go(self.c_hi)
        self.net.go(self.d_lo)

    def middle(self):
        self.a.wait_recv()
        add_to(self.lo1, self.lo(1))
        self.net.go(self.c_lo)
        self.b.wait_recv()
        add_to(self.hi1, self.hi(3))
        self.net.go(self.d_hi)

    def finish(self, lo_out, hi_out):
        self.c_hi.wait_recv()
        self.d_hi.wait_recv()
        sum_to(hi_out, [self.hi(0), self.hi_l, self.hi_r])
        self.d_lo.wait_recv()
        self.c_lo.wait_recv()
        sum_to(lo_out, [self.lo(0), self.lo_l, self.lo_r])

    @staticmethod
    def room_shapes(lo_shape, hi_shape):
        return [pltpu.VMEM(lo_shape, BF)] * 3 + [pltpu.VMEM(hi_shape, BF)] * 3


def params(call_id):
    return pltpu.CompilerParams(
        collective_id=call_id, has_side_effects=True, vmem_limit_bytes=VMEM_BYTES
    )


def sems(count):
    return [pltpu.SemaphoreType.DMA((count,)), pltpu.SemaphoreType.DMA((count,))]


def weight_kernel(w_ref, other_ref, send, recv):
    place, net = Place(), Net(send, recv)
    right, left = ring(place, "x")
    quarter = w_ref.shape[0] // 4
    greet([right, left, place.partner()])
    finish = swap_weight(place, net, w_ref, other_ref, quarter)
    finish()
    net.drain()


def swap_weight(place, net, w_ref, other_ref, quarter):
    right, left = ring(place, "x")
    core = place.core

    def rows(side):
        return pl.ds(pl.multiple_of((2 * side + core) * quarter, 16), quarter)

    def cores_rows(side):
        return other_ref.at[rows(side)]

    one = net.copy(w_ref.at[rows(0)], cores_rows(0), left)
    two = net.copy(w_ref.at[rows(1)], cores_rows(1), right)
    trades = [net.copy(cores_rows(side), cores_rows(side), place.partner()) for side in (0, 1)]
    net.go(one)
    net.go(two)

    def finish():
        for first, trade in zip((one, two), trades):
            first.wait_recv()
            net.go(trade)
        for trade in trades:
            trade.wait_recv()

    return finish


def fetch_weight(w, call_id):
    return pl.pallas_call(
        weight_kernel,
        out_shape=jax.ShapeDtypeStruct(w.shape, w.dtype),
        in_specs=[IN_VMEM],
        out_specs=IN_VMEM,
        scratch_shapes=sems(4),
        compiler_params=params(call_id),
    )(w)


PARTS = (
    (0, 48, 0, ("x", "y", "z")),
    (48, 48, 768, ("z", "x", "y")),
    (96, 32, 1536, ("y", "z", "x")),
)


def part_views(place, buf, part):
    _, rows, base, (first, second, third) = part
    at1, at2, at3 = (getattr(place, axis) for axis in (first, second, third))

    def block(lead, start, size):
        return buf.at[lead, pl.ds(pl.multiple_of(base + start, 16), size)]

    return (
        (first, lambda j: block(at3, (at2 * 4 + j) * rows, rows)),
        (second, lambda j: block(at3, j * 4 * rows, 4 * rows)),
        (third, lambda j: block(j, 0, 16 * rows)),
    )


def halves(view):
    return (lambda j: view(j).at[:, pl.ds(0, HD)]), (lambda j: view(j).at[:, pl.ds(HD, HD)])


def chunk_rows(n):
    return [256 * n + 64 * i if n < 6 else 1536 + 128 * i + 64 * (n - 6) for i in range(4)]


def key_tokens():
    out = np.zeros((4, 2048), np.int32)
    for skip, rows, base, axes in PARTS:
        for j in range(4):
            for r in range(16 * rows):
                spot = {axes[2]: j, axes[1]: r // (4 * rows), axes[0]: (r // rows) % 4}
                x, y, z = spot["x"], spot["y"], spot["z"]
                token = ((y * 2 + x // 2) * 4 + z) * 512 + (x % 2) * 128 + skip + r % rows
                out[j, base + r] = token
    order = np.zeros((8, CHUNK), np.int64)
    for c in range(8):
        for i in range(4):
            start = chunk_rows(c)[i]
            order[c, 64 * i : 64 * i + 64] = np.arange(start, start + 64)
    return out[:, order]


KEY_TOKENS = key_tokens()


def set_lead(place, n, by):
    return place.step("zyx"[n // 3], by)


def read_sets(buf, key_ref, chunks, leads, key_leads):
    keys, values, tokens = [], [], []
    for n, lead, key_lead in zip(chunks, leads, key_leads):
        rows = chunk_rows(n)
        keys += [buf[lead, start : start + 64, :HD] for start in rows]
        values += [buf[lead, start : start + 64, HD:] for start in rows]
        tokens.append(key_ref[key_lead, n : n + 1])
    return (
        jnp.concatenate(keys, axis=0),
        jnp.concatenate(values, axis=0),
        jnp.concatenate(tokens, axis=1),
    )


def contract(left, right, left_dim, right_dim):
    return lax.dot_general(
        left, right, (((left_dim,), (right_dim,)), ((), ())), preferred_element_type=F32
    )


def norm_scale(v):
    return lax.rsqrt(jnp.mean(v * v, axis=-1, keepdims=True) + EPS)


def norm_back(v, r, gain, e):
    eg = e * gain
    dv = r * eg - v * (r * r * r) * jnp.mean(eg * v, axis=-1, keepdims=True)
    return dv, jnp.sum(e * v * r, axis=0, keepdims=True)


def forward_kernel(
    kv_ref,
    q_ref,
    w_ref,
    key_ref,
    last_ref,
    first_ref,
    buf,
    q_all,
    w_other,
    o_out,
    inv_out,
    o_sum,
    l_sum,
    o_got,
    l_got,
    send,
    recv,
):
    place, net = Place(), Net(send, recv)
    core = place.core
    partner = place.partner()
    greet(ring(place, "x") + ring(place, "y") + ring(place, "z") + [partner])
    mine = pl.ds(pl.multiple_of(core * TOK, TOK), TOK)
    theirs = pl.ds(pl.multiple_of((1 - core) * TOK, TOK), TOK)
    q_all[:, mine] = q_ref[...]
    stages = []
    for part in PARTS:
        skip, rows, _, _ = part
        views = part_views(place, buf, part)
        axis, view = views[0]
        own = view(getattr(place, axis))
        own[...] = kv_ref[pl.ds(skip, rows)]
        stages.append([RingGather(net, place, axis, view, *halves(view)) for axis, view in views])
    for rings in stages:
        rings[0].start()
    swap_q = net.copy(q_all.at[:, mine], q_all.at[:, mine], partner)
    net.go(swap_q)
    for h in range(HEADS):
        o_sum[h] = jnp.zeros((ROWS, HD), F32)
        l_sum[h] = jnp.zeros((ROWS, 128), F32)
    for level in (0, 1):
        for rings in stages:
            rings[level].forward()
        for rings in stages:
            rings[level].finish()
            rings[level + 1].start()
    finish_w = swap_weight(place, net, w_ref, w_other, w_ref.shape[0] // 4)
    swap_q.wait_recv()

    def attend(by):
        leads = [set_lead(place, n, by) for n in range(8)]
        keys, values, token = read_sets(buf, key_ref, range(8), leads, leads)
        allowed = (token <= last_ref[...]) & (token >= first_ref[...])
        for h in range(HEADS):
            weights = jnp.exp(contract(q_all[h], keys, 1, 1))
            weights = jnp.where(allowed, weights, 0.0)
            l_sum[h] += sum(weights[:, 128 * i : 128 * i + 128] for i in range(16))
            o_sum[h] += jnp.dot(weights.astype(BF), values, preferred_element_type=F32)

    attend(0)
    for rings in stages:
        rings[2].forward()
    finish_w()
    lax.fori_loop(0, 2, lambda i, c: (attend(1 + 2 * i), c)[1], 0)
    for rings in stages:
        rings[2].finish()
    attend(2)
    swap_o = net.copy(o_sum.at[:, theirs], o_got, partner)
    swap_l = net.copy(l_sum.at[:, theirs], l_got, partner)
    net.go(swap_l)
    net.go(swap_o)
    swap_l.wait_recv()
    swap_o.wait_recv()
    for h in range(HEADS):
        total = jnp.sum(l_sum[h, mine] + l_got[h], axis=1, keepdims=True)
        inverse = 1.0 / total
        o_out[h] = (o_sum[h, mine] + o_got[h]) * inverse
        inv_out[h] = jnp.broadcast_to(inverse, (TOK, 128))
    net.drain()


def attention_forward(kv, q, w_out, key_rows, last, first, call_id):
    shape = jax.ShapeDtypeStruct
    return pl.pallas_call(
        forward_kernel,
        out_shape=(
            shape((4, 2048, 2 * HD), BF),
            shape((HEADS, ROWS, HD), BF),
            shape(w_out.shape, BF),
            shape((HEADS, TOK, HD), F32),
            shape((HEADS, TOK, 128), F32),
        ),
        in_specs=[IN_VMEM] * 6,
        out_specs=[IN_VMEM] * 5,
        scratch_shapes=[
            pltpu.VMEM((HEADS, ROWS, HD), F32),
            pltpu.VMEM((HEADS, ROWS, 128), F32),
            pltpu.VMEM((HEADS, TOK, HD), F32),
            pltpu.VMEM((HEADS, TOK, 128), F32),
            *sems(48),
        ],
        compiler_params=params(call_id),
    )(kv, q, w_out, key_rows, last, first)


GRAD_SLOT = {2: 0, 0: 0, 1: 1, 3: 2}


def turn_back(e, cosine, sine):
    half = HD // 2
    low, high = e[:, :half], e[:, half:]
    return jnp.concatenate([low * cosine + high * sine, high * cosine - low * sine], axis=1)


def backward_kernel(
    kv_hbm,
    sums_hbm,
    wq_hbm,
    wq2_hbm,
    wk_hbm,
    wv_hbm,
    q_all,
    do_ref,
    delta_ref,
    key_ref,
    last_ref,
    first_ref,
    q_pre,
    k_pre,
    cos_ref,
    sin_ref,
    h_ref,
    da_ref,
    o_ref,
    x_ref,
    dmid_ref,
    g_attn,
    g_query,
    g_key,
    gains_ref,
    dx_out,
    dwq_out,
    dwk_out,
    dwv_out,
    dwo_out,
    dwg_out,
    dwu_out,
    dwd_out,
    gains_out,
    buf,
    wk,
    wv,
    do_all,
    delta_all,
    grads,
    dq_sum,
    dq_got,
    dkv,
    h_line,
    da_line,
    o_line,
    dq_line,
    dq_own,
    o_own,
    late_all,
    late_got,
    late_y,
    late_z,
    gain_got,
    kv_own,
    kv_line,
    w_all,
    w_got,
    w_y,
    w_z,
    w_line,
    w_both,
    dh,
    *rest,
):
    rooms, late_rooms, rest = rest[:54], rest[54:66], rest[66:]
    *weight_refs, send, recv, send2, recv2, here = rest
    place, net = Place(), Net(send, recv)
    core, partner = place.core, place.partner()
    w_loads = [
        pltpu.make_async_copy(source, target, here.at[1 + i])
        for i, (source, target) in enumerate(
            (
                (wq_hbm, buf.at[0, pl.ds(0, D)]),
                (wq2_hbm, buf.at[1, pl.ds(0, D)]),
                (wk_hbm, wk),
                (wv_hbm, wv),
            )
        )
    ]
    w_loads[2].start()
    w_loads[3].start()

    def set_loads(by, slot):
        copies = []
        for i, (_, rows, base, axes) in enumerate(PARTS):
            span = pl.ds(base, 16 * rows)
            source = kv_hbm.at[place.step(axes[2], by), span]
            copies.append(
                pltpu.make_async_copy(source, buf.at[slot, span], here.at[16 + 3 * slot + i])
            )
        return copies

    sets = [set_loads(by, slot) for by, slot in ((2, 0), (1, 1), (3, 0), (0, 1))]
    for copy in sets[0] + sets[1]:
        copy.start()
    weights = WeightSums(place, net, sums_hbm, late_z, weight_refs, (send2, recv2, here))
    greet(weights.friends + ring(place, "x") + ring(place, "y"))
    mine = pl.ds(pl.multiple_of(core * TOK, TOK), TOK)
    theirs = pl.ds(pl.multiple_of((1 - core) * TOK, TOK), TOK)
    do_all[:, mine] = do_ref[...]
    delta_all[core] = delta_ref[...]
    swap_do = net.copy(do_all.at[:, mine], do_all.at[:, mine], partner)
    swap_delta = net.copy(delta_all.at[core], delta_all.at[core], partner)
    net.go(swap_do)
    net.go(swap_delta)

    x_lo = lax.rem(place.x, 2)
    half = TOK // 2

    def line_of(rows):
        return RingGather(
            net,
            place,
            "x",
            lambda j: rows.at[j],
            lambda j: rows.at[j, pl.ds(0, half)],
            lambda j: rows.at[j, pl.ds(half, half)],
        )

    def head_of(j):
        return jnp.where(lax.rem(j, 2) == x_lo, 0, 2) + lax.div(j, 2)

    h_line[place.x] = h_ref[...]
    da_line[place.x] = da_ref[...]
    for h in range(HEADS):
        o_own[h] = o_ref[h].astype(BF)
    o_line[place.x] = o_own[head_of(place.x)]
    line_h, line_da = line_of(h_line), line_of(da_line)
    o_swap = Direct(net, place, "x", lambda j: o_own.at[head_of(j)], lambda j: o_line.at[j])
    dq_swap = Direct(net, place, "x", lambda j: dq_own.at[head_of(j)], lambda j: dq_line.at[j])
    o_swap.start()
    line_h.start()
    line_da.start()
    for h in range(HEADS):
        dq_sum[h] = jnp.zeros((HD, ROWS), F32)
    stages = []
    for i, part in enumerate(PARTS):
        _, rows, base, (first, second, third) = part
        at1, at2 = getattr(place, first), getattr(place, second)

        def block(slot, start, size, base=base):
            return grads.at[slot, pl.ds(pl.multiple_of(base + start, 16), size)]

        views = (
            lambda by, block=block, first=first, at2=at2, rows=rows: block(
                0, (at2 * 4 + place.step(first, by)) * rows, rows
            ),
            lambda by, block=block, second=second, rows=rows: block(
                0, place.step(second, by) * 4 * rows, 4 * rows
            ),
            lambda by, block=block, rows=rows: block(GRAD_SLOT[by], 0, 16 * rows),
        )
        rings = []
        for level, axis in enumerate((first, second, third)):
            spot = 6 * (3 * i + level)
            rings.append(
                RingScatter(net, place, axis, *halves(views[level]), rooms[spot : spot + 6])
            )
        stages.append((rings, views))
    late_first = RingScatter(
        net,
        place,
        "y",
        stepped(place, "y", lambda j: late_got.at[j, 0]),
        stepped(place, "y", lambda j: late_got.at[j, 1]),
        late_rooms[:6],
    )

    def late_spot(j):
        return late_y.at[lax.div(j, 2), lax.rem(j, 2)]

    late_second = RingScatter(
        net,
        place,
        "z",
        stepped(place, "z", lambda j: late_spot(j).at[pl.ds(0, 80)]),
        stepped(place, "z", lambda j: late_spot(j).at[pl.ds(80, 64)]),
        late_rooms[6:],
    )

    def late_term(c, rows, columns):
        term = contract(rows[...].reshape(4 * TOK, D), columns[...].reshape(4 * TOK, HD), 0, 0)
        term = term.astype(BF)
        for k in range(8):
            for which in range(2):
                late_all[which, k // 2, k % 2, c] = term[
                    144 * k : 144 * k + 144, 128 * which : 128 * which + 128
                ]

    weights.begin()
    swap_do.wait_recv()
    swap_delta.wait_recv()

    def differ(chunks, by, slot):
        key_leads = [set_lead(place, n, by) for n in chunks]
        keys, values, token = read_sets(buf, key_ref, chunks, [slot] * len(chunks), key_leads)
        token = jnp.concatenate(
            [
                jnp.transpose(jnp.broadcast_to(token[:, 128 * i : 128 * i + 128], (128, 128)))
                for i in range(2 * len(chunks))
            ],
            axis=0,
        )
        token = jnp.concatenate([token, token], axis=1)
        allowed = (token <= last_ref[...]) & (token >= first_ref[...])
        d_keys = d_values = None
        for h in range(HEADS):
            probs = jnp.exp(contract(keys, q_all[h], 1, 1))
            probs = jnp.where(allowed, probs, 0.0)
            delta = jnp.concatenate([delta_all[0, h : h + 1], delta_all[1, h : h + 1]], axis=1)
            d_scores = (probs * (contract(values, do_all[h], 1, 1) - delta)).astype(BF)
            value_term = jnp.dot(probs.astype(BF), do_all[h], preferred_element_type=F32)
            key_term = jnp.dot(d_scores, q_all[h], preferred_element_type=F32)
            d_values = value_term if h == 0 else d_values + value_term
            d_keys = key_term if h == 0 else d_keys + key_term
            dq_sum[h] += contract(keys, d_scores, 0, 0)
        d_keys, d_values = d_keys.astype(BF), d_values.astype(BF)
        for m, n in enumerate(chunks):
            for i, start in enumerate(chunk_rows(n)):
                spot = 256 * m + 64 * i
                grads[GRAD_SLOT[by], start : start + 64, :HD] = d_keys[spot : spot + 64]
                grads[GRAD_SLOT[by], start : start + 64, HD:] = d_values[spot : spot + 64]

    def visit(step, after):
        by, slot = ((2, 0), (1, 1), (3, 0), (0, 1))[step]
        for copy in sets[step]:
            copy.wait()
        for chunks in ((0, 1, 2), (3, 4, 5), (6, 7)):
            differ(chunks, by, slot)
        for copy in after:
            copy.start()

    visit(0, sets[2])
    for rings, _ in stages:
        rings[2].start_far()
    line_h.forward()
    line_da.forward()
    weights.turn()
    visit(1, sets[3])
    visit(2, w_loads[0:1])
    for rings, _ in stages:
        rings[2].start_near()
    for rings, _ in stages:
        rings[2].middle()
    weights.next()
    for rings, _ in stages:
        net.settle(rings[2].a)
        net.settle(rings[2].b)
    visit(3, w_loads[1:2])
    swap_dq = net.copy(dq_sum.at[:, :, theirs], dq_got, partner)
    net.go(swap_dq)
    line_h.finish()
    line_da.finish()
    o_swap.wait()
    late_term(0, da_line, o_line)
    weights.turn_again()
    for load in w_loads:
        load.wait()

    swap_dq.wait_recv()
    d_query = jnp.zeros((1, HD), F32)
    for h in range(HEADS):
        e = jnp.transpose(dq_sum[h, :, mine] + dq_got[h]) * HD**-0.5
        e = turn_back(e.astype(BF).astype(F32), cos_ref[...], sin_ref[...])
        u = q_pre[h]
        du, gain = norm_back(u, norm_scale(u), g_query[...], e)
        d_query = d_query + gain
        dq_own[h] = du.astype(BF)
    dq_line[place.x] = dq_own[head_of(place.x)]
    dq_swap.start()
    for level in (2, 1, 0):
        for (rings, views), part in zip(stages, PARTS):
            lo, hi = halves(views[level])
            skip, rows, _, _ = part
            if level:
                rings[level].finish(lo(0), hi(0))
                rings[level - 1].start_far()
                rings[level - 1].start_near()
            else:
                out = dkv.at[pl.ds(skip, rows)]
                rings[level].finish(out.at[:, pl.ds(0, HD)], out.at[:, pl.ds(HD, HD)])
        if level == 2:
            d_h = sum(
                contract(dq_own[h], buf[h // 2, :D, 256 * (h % 2) : 256 * (h % 2) + 256], 1, 1)
                for h in range(HEADS)
            )
            dh[...] = d_h
            dq_swap.wait()
            late_term(1, h_line, dq_line)
            late_swap = net.copy(late_all.at[1 - core], late_got, partner)
            net.go(late_swap)
        if level:
            for rings, _ in stages:
                rings[level - 1].middle()
        if level == 2:
            late_swap.wait_recv()
            for y in range(4):
                add_to(late_got.at[y], late_all.at[core, y])
            late_first.start_far()
            late_first.start_near()
            weights.last()
        if level == 1:
            late_first.middle()
    late_first.finish(late_y.at[0], late_y.at[1])
    late_second.start_far()
    late_second.start_near()

    e = turn_back(dkv[:, :HD].astype(BF).astype(F32), cos_ref[...], sin_ref[...])
    u = k_pre[...]
    dk, d_key = norm_back(u, norm_scale(u), g_key[...], e)
    dk, dv = dk.astype(BF), dkv[:, HD:].astype(BF)
    for i in range(2):
        kv_own[i] = dk[:, 128 * i : 128 * i + 128]
        kv_own[2 + i] = dv[:, 128 * i : 128 * i + 128]
    kv_line[place.x] = kv_own[place.x]
    kv_swap = Direct(net, place, "x", lambda j: kv_own.at[j], lambda j: kv_line.at[j])
    kv_swap.start()
    d_h = dh[...] + contract(dk, wk[...], 1, 1) + contract(dv, wv[...], 1, 1)
    xf = x_ref[...].astype(F32)
    dx, d_attn = norm_back(xf, norm_scale(xf), g_attn[...], d_h)
    dx_out[...] = (dmid_ref[...] + dx).astype(BF)
    late_second.middle()

    def gain_swap(level, axis):
        return Direct(
            net, place, axis, lambda j: gain_got.at[level, at(axis)], lambda j: gain_got.at[level, j]
        )

    def at(axis):
        return getattr(place, axis)

    def gain_sum(level):
        return (gain_got[level, 0] + gain_got[level, 1]) + (gain_got[level, 2] + gain_got[level, 3])

    swaps = [gain_swap(0, "x"), gain_swap(1, "y"), gain_swap(2, "z")]
    norms = jnp.concatenate([d_query, d_key, jnp.zeros((1, D - 2 * HD), F32)], axis=1)
    gain_got[0, place.x] = jnp.concatenate(
        [d_attn, gains_ref[0:3], norms, jnp.zeros((3, D), F32)], axis=0
    )
    swaps[0].start()
    kv_swap.wait()
    term = contract(h_line[...].reshape(4 * TOK, D), kv_line[...].reshape(4 * TOK, 128), 0, 0)
    term = term.astype(BF)
    for k in range(8):
        w_all[k // 4, k % 4] = term[144 * k : 144 * k + 144]
    w_swap = net.copy(w_all.at[1 - core], w_got, partner)
    net.go(w_swap)
    late_second.finish(late_z.at[pl.ds(0, 80)], late_z.at[pl.ds(80, 64)])
    weights.send_home()
    swaps[0].wait()
    gain_got[1, place.y] = gain_sum(0)
    swaps[1].start()
    w_swap.wait_recv()
    add_to(w_got, w_all.at[core])
    w_scatter = Direct(net, place, "y", lambda j: w_got.at[j], lambda j: w_y.at[j])
    w_scatter.start()
    w_y[place.y] = w_got[place.y]
    swaps[1].wait()
    gain_got[2, place.z] = gain_sum(1)
    swaps[2].start()
    w_scatter.wait()
    sum_to(w_z.at[place.z], [w_y.at[j] for j in range(4)])
    w_sums = Direct(net, place, "z", lambda j: w_z.at[place.z], lambda j: w_z.at[j])
    w_sums.start()
    swaps[2].wait()
    gain_got[3, core] = gain_sum(2)
    gain_last = net.copy(gain_got.at[3, core], gain_got.at[3, core], partner)
    net.go(gain_last)
    w_sums.wait()
    sum_to(w_line.at[place.x, place.y], [w_z.at[j] for j in range(4)])
    y_back = Direct(
        net, place, "y", lambda j: w_line.at[place.x, place.y], lambda j: w_line.at[place.x, j]
    )
    y_back.start()
    weights.arrive(dwq_out, dwo_out, dwg_out, dwu_out, dwd_out)
    y_back.wait()
    x_back = Direct(net, place, "x", lambda j: w_line.at[place.x], lambda j: w_line.at[j])
    x_back.start()
    gain_last.wait_recv()
    gains_out[...] = gain_got[3, 0] + gain_got[3, 1]
    x_back.wait()
    w_both[core] = w_line[...]
    w_last = net.copy(w_line, w_both.at[core], partner)
    net.go(w_last)
    w_last.wait_recv()
    for which in range(2):
        for j in range(4):
            out = (dwk_out, dwv_out)[j // 2]
            for y in range(4):
                rows = pl.ds(576 * which + 144 * y, 144)
                out[rows, 128 * (j % 2) : 128 * (j % 2) + 128] = w_both[which, j, y].astype(F32)
    net.drain()


def attention_backward(hbm, small, call_id):
    shape = jax.ShapeDtypeStruct
    rooms = []
    for _, rows, _, _ in PARTS:
        for blocks in (1, 4, 16):
            rooms += RingScatter.room_shapes((blocks * rows, HD), (blocks * rows, HD))
    late_rooms = [
        *RingScatter.room_shapes((2, 144, 128), (2, 144, 128)),
        *RingScatter.room_shapes((80, 128), (64, 128)),
    ]
    return pl.pallas_call(
        backward_kernel,
        out_shape=(
            shape((TOK, D), BF),
            shape((18, 2 * HD), F32),
            shape((D, HD), F32),
            shape((D, HD), F32),
            shape((2 * HD, 18), F32),
            shape((18, 2 * HID), F32),
            shape((18, 2 * HID), F32),
            shape((2 * HID, 18), F32),
            shape((8, D), F32),
        ),
        in_specs=[pl.BlockSpec(memory_space=pl.ANY)] * 6 + [IN_VMEM] * len(small),
        out_specs=[IN_VMEM] * 9,
        scratch_shapes=[
            pltpu.VMEM((2, 2048, 2 * HD), BF),
            pltpu.VMEM((D, HD), BF),
            pltpu.VMEM((D, HD), BF),
            pltpu.VMEM((HEADS, ROWS, HD), BF),
            pltpu.VMEM((2, 8, TOK), F32),
            pltpu.VMEM((3, 2048, 2 * HD), BF),
            pltpu.VMEM((HEADS, HD, ROWS), F32),
            pltpu.VMEM((HEADS, HD, TOK), F32),
            pltpu.VMEM((TOK, 2 * HD), F32),
            pltpu.VMEM((4, TOK, D), BF),
            pltpu.VMEM((4, TOK, D), BF),
            pltpu.VMEM((4, TOK, HD), BF),
            pltpu.VMEM((4, TOK, HD), BF),
            pltpu.VMEM((4, TOK, HD), BF),
            pltpu.VMEM((4, TOK, HD), BF),
            pltpu.VMEM((2, 4, 2, 2, 144, 128), BF),
            pltpu.VMEM((4, 2, 2, 144, 128), BF),
            pltpu.VMEM((2, 2, 144, 128), BF),
            pltpu.VMEM((144, 128), F32),
            pltpu.VMEM((4, 4, 8, D), F32),
            pltpu.VMEM((4, TOK, 128), BF),
            pltpu.VMEM((4, TOK, 128), BF),
            pltpu.VMEM((2, 4, 144, 128), BF),
            pltpu.VMEM((4, 144, 128), BF),
            pltpu.VMEM((4, 144, 128), BF),
            pltpu.VMEM((4, 144, 128), BF),
            pltpu.VMEM((4, 4, 144, 128), BF),
            pltpu.VMEM((2, 4, 4, 144, 128), BF),
            pltpu.VMEM((TOK, D), F32),
            *rooms,
            *late_rooms,
            *WeightSums.scratch(),
            *sems(160),
            *sems(8),
            pltpu.SemaphoreType.DMA((24,)),
        ],
        compiler_params=params(call_id),
    )(*hbm, *small)


def feed_kernel(
    x_ref,
    o_ref,
    inv_ref,
    wo_ref,
    wo2_ref,
    gains_ref,
    cot_ref,
    wg_hbm,
    wu_hbm,
    wd_hbm,
    out_ref,
    dmid_out,
    dattn_out,
    do_out,
    delta_out,
    dgains_out,
    sums_hbm,
    wg,
    wu,
    wd,
    h_line,
    f_line,
    h_turned,
    f_turned,
    gelu_kept,
    slope_kept,
    act,
    d_gate,
    d_up,
    f_terms,
    h_terms,
    snd,
    got,
    attn,
    mid,
    ffn,
    *rest,
):
    *room, send, recv, local = rest
    place, net = Place(), Net(send, recv)
    core, partner = place.core, place.partner()
    x_hi = lax.div(place.x, 2)
    first_unit = pl.multiple_of(x_hi * (2 * HID - HID_PAD), 128)
    window = pl.ds(first_unit, HID_PAD)
    loads = [
        pltpu.make_async_copy(source, target, local.at[i])
        for i, (source, target) in enumerate(
            ((wg_hbm.at[:, window], wg), (wu_hbm.at[:, window], wu), (wd_hbm.at[window], wd))
        )
    ]
    for load in loads:
        load.start()
    greet(ring(place, "x") + [partner])
    half = TOK // 2
    top, bottom = pl.ds(0, half), pl.ds(half, half)
    g_post, g_ffn, g_out = (gains_ref[i : i + 1] for i in range(3))

    def gather(lines):
        line = RingGather(
            net,
            place,
            "x",
            lambda j: lines.at[j],
            lambda j: lines.at[j, top],
            lambda j: lines.at[j, bottom],
        )
        line.start()
        line.forward()
        line.finish()

    def scatter(terms, room):
        line = RingScatter(
            net,
            place,
            "x",
            stepped(place, "x", lambda j: terms.at[j, top]),
            stepped(place, "x", lambda j: terms.at[j, bottom]),
            room,
        )
        line.start_far()
        line.start_near()
        return line

    o_cat = [o_ref[h].astype(BF) for h in range(HEADS)]
    a = jnp.dot(jnp.concatenate(o_cat[:2], axis=1), wo_ref[...], preferred_element_type=F32)
    a += jnp.dot(jnp.concatenate(o_cat[2:], axis=1), wo2_ref[...], preferred_element_type=F32)
    attn[...] = a
    mid[...] = x_ref[...].astype(F32) + a * norm_scale(a) * g_post
    m = mid[...]
    h_line[place.x] = (m * norm_scale(m) * g_ffn).astype(BF)
    gather(h_line)

    for load in loads:
        load.wait()
    lines = 4 * TOK
    low_unit, high_unit = jnp.where(x_hi == 0, 0, 64), jnp.where(x_hi == 0, HID, HID_PAD)

    def units(n):
        return pl.ds(pl.multiple_of(n * 256, 256), 256)

    def forward(n, carry):
        h = h_line[...].reshape(lines, D)
        gate = jnp.dot(h, wg[:, units(n)], preferred_element_type=F32)
        up = jnp.dot(h, wu[:, units(n)], preferred_element_type=F32)
        unit = n * 256 + lax.broadcasted_iota(jnp.int32, (1, 256), 1)
        own = jnp.where((unit >= low_unit) & (unit < high_unit), 1.0, 0.0)
        scale, cube = 0.7978845608028654, 0.044715
        square = gate * gate
        bent = jnp.tanh(scale * gate * (1.0 + cube * square))
        lifted = 0.5 * (1.0 + bent)
        gelu = gate * lifted * own
        slope = lifted + 0.5 * gate * (1.0 - bent * bent) * scale * (1.0 + 3.0 * cube * square)
        act[:, units(n)] = (gelu * up).astype(BF)
        gelu_kept[:, units(n)] = gelu.astype(BF)
        slope_kept[:, units(n)] = (slope * up * own).astype(BF)
        return carry

    lax.fori_loop(0, HID_PAD // 256, forward, 0)

    def columns(n):
        return pl.ds(pl.multiple_of(n * 384, 128), 384)

    def project(n, carry):
        term = jnp.dot(act[...], wd[:, columns(n)], preferred_element_type=F32)
        f_terms[:, :, columns(n)] = term.astype(BF).reshape(4, TOK, 384)
        return carry

    lax.fori_loop(0, 3, project, 0)
    line = scatter(f_terms, room[:6])
    h_turned[...] = jnp.transpose(h_line[...].reshape(lines, D))
    line.middle()
    line.finish(ffn.at[top], ffn.at[bottom])
    f = ffn[...]
    r_out = norm_scale(f)
    out_ref[...] = (mid[...] + f * r_out * g_out).astype(BF)
    df, d_out = norm_back(f, r_out, g_out, cot_ref[...].astype(F32))
    f_line[place.x] = df.astype(BF)
    gather(f_line)

    def backward(n, carry):
        d_act = contract(f_line[...].reshape(lines, D), wd[units(n)], 1, 1)
        d_gate[:, units(n)] = (d_act * slope_kept[:, units(n)].astype(F32)).astype(BF)
        d_up[:, units(n)] = (d_act * gelu_kept[:, units(n)].astype(F32)).astype(BF)
        return carry

    lax.fori_loop(0, HID_PAD // 256, backward, 0)

    def back_project(n, carry):
        term = contract(d_gate[...], wg[columns(n)], 1, 1) + contract(d_up[...], wu[columns(n)], 1, 1)
        h_terms[:, :, columns(n)] = term.astype(BF).reshape(4, TOK, 384)
        return carry

    lax.fori_loop(0, 3, back_project, 0)
    line = scatter(h_terms, room[6:])
    f_turned[...] = jnp.transpose(f_line[...].reshape(lines, D))

    def fill(i, which, put):
        some = pl.ds(pl.multiple_of(which * 896, 128), 896)
        rows = pl.ds(576 * i, 576)
        pairs = ((h_turned, d_gate), (h_turned, d_up), (f_turned, act))
        for m, (left, right) in enumerate(pairs):
            term = jnp.dot(left[rows], right[:, some], preferred_element_type=F32)
            for k in range(4):
                piece = term[144 * k : 144 * k + 144]
                for c in range(2):
                    low = max(896 * m, HALF * c)
                    high = min(896 * m + 896, HALF * c + HALF)
                    if low < high:
                        at = (2 * i + k // 2, k % 2, c, slice(None), slice(low - HALF * c, high - HALF * c))
                        put(at, piece[:, low - 896 * m : high - 896 * m])

    def put_snd(at, value):
        snd[at] = value.astype(BF)

    def put_got(at, value):
        got[at] = (got[at].astype(F32) + value).astype(BF)

    swaps = [net.copy(snd.at[y], got.at[y], partner) for y in range(4)]
    for y in range(4):
        snd[y, :, 1, :, 1280:] = jnp.zeros((2, 144, 128), BF)
    for i in range(2):
        fill(i, 1 - core, put_snd)
        net.go(swaps[2 * i])
        net.go(swaps[2 * i + 1])
    line.middle()
    stores = [pltpu.make_async_copy(got.at[y], sums_hbm.at[y], local.at[3 + y]) for y in range(4)]
    for i in range(2):
        swaps[2 * i].wait_recv()
        swaps[2 * i + 1].wait_recv()
        fill(i, core, put_got)
        stores[2 * i].start()
        stores[2 * i + 1].start()
    line.finish(ffn.at[top], ffn.at[bottom])

    m, a = mid[...], attn[...]
    dm, d_ffn = norm_back(m, norm_scale(m), g_ffn, ffn[...])
    d_mid = cot_ref[...].astype(F32) + dm
    dmid_out[...] = d_mid
    da, d_post = norm_back(a, norm_scale(a), g_post, d_mid)
    da = da.astype(BF)
    dattn_out[...] = da
    dgains_out[...] = jnp.concatenate([d_post, d_ffn, d_out, jnp.zeros((5, D), F32)], axis=0)
    delta_out[...] = jnp.zeros((8, TOK), F32)
    for h in range(HEADS):
        weight = (wo_ref, wo2_ref)[h // 2]
        d_o = contract(da, weight[256 * (h % 2) : 256 * (h % 2) + 256], 1, 1).astype(BF).astype(F32)
        inverse = inv_ref[h]
        do_out[h] = (d_o * jnp.concatenate([inverse, inverse], axis=1)).astype(BF)
        delta = jnp.sum(d_o * o_ref[h], axis=1, keepdims=True) * inverse
        delta_out[h : h + 1] = jnp.transpose(delta)[:1]
    for store in stores:
        store.wait()
    net.drain()


def feed_forward(x, o_heads, inverse, wo, wo2, gains, cotangent, w_gate, w_up, w_down, call_id):
    half = (TOK // 2, D)
    shape = jax.ShapeDtypeStruct
    every = (4, 2, 2, 144, HALF)
    lines = 4 * TOK
    anywhere = pl.BlockSpec(memory_space=pl.ANY)
    unit_rows = [pltpu.VMEM((lines, HID_PAD), BF)] * 5
    return pl.pallas_call(
        feed_kernel,
        out_shape=(
            shape((TOK, D), BF),
            shape((TOK, D), F32),
            shape((TOK, D), BF),
            shape((HEADS, TOK, HD), BF),
            shape((8, TOK), F32),
            shape((8, D), F32),
            shape(every, BF),
        ),
        in_specs=[IN_VMEM] * 7 + [anywhere] * 3,
        out_specs=[IN_VMEM] * 6 + [anywhere],
        scratch_shapes=[
            pltpu.VMEM((D, HID_PAD), BF),
            pltpu.VMEM((D, HID_PAD), BF),
            pltpu.VMEM((HID_PAD, D), BF),
            pltpu.VMEM((4, TOK, D), BF),
            pltpu.VMEM((4, TOK, D), BF),
            pltpu.VMEM((D, lines), BF),
            pltpu.VMEM((D, lines), BF),
            *unit_rows,
            pltpu.VMEM((4, TOK, D), BF),
            pltpu.VMEM((4, TOK, D), BF),
            pltpu.VMEM(every, BF),
            pltpu.VMEM(every, BF),
            pltpu.VMEM((TOK, D), F32),
            pltpu.VMEM((TOK, D), F32),
            pltpu.VMEM((TOK, D), F32),
            *RingScatter.room_shapes(half, half),
            *RingScatter.room_shapes(half, half),
            *sems(32),
            pltpu.SemaphoreType.DMA((7,)),
        ],
        compiler_params=params(call_id),
    )(x, o_heads, inverse, wo, wo2, gains, cotangent, w_gate, w_up, w_down)


class WeightSums:
    def __init__(self, place, net, sums, late, refs, marks):
        y_here, z_here, y1, z1, z2, y2, snd, rcv, *rooms = refs
        self.place, self.late, self.snd, self.rcv, self.marks = place, late, snd, rcv, marks
        self.y1, self.z1, self.y2, self.z2 = y1, z1, y2, z2
        self.x_hi, self.x_lo = lax.div(place.x, 2), lax.rem(place.x, 2)
        self.friends = []
        for k in range(1, 16):
            spot = lax.rem(self.x_hi * 8 + place.z * 2 + place.core + k, 16)
            x, z = lax.div(spot, 8) * 2 + self.x_lo, lax.rem(lax.div(spot, 2), 4)
            self.friends.append(place.device(x=x, z=z, core=lax.rem(spot, 2)))

        left, right = pl.ds(0, CUT), pl.ds(CUT, HALF - CUT)

        def y_spot(half):
            return stepped(place, "y", lambda j: sums.at[j, half, :, :, left])

        def z_spot(half):
            return stepped(
                place,
                "z",
                lambda j: sums.at[pl.ds(2 * half, 2), lax.div(j, 2), lax.rem(j, 2), :, right],
            )

        self.loads = []
        here = []
        for i, spot in enumerate((y_spot, z_spot)):
            for k, (half, by) in enumerate(((0, 1), (1, 3), (0, 0), (1, 0))):
                target = (y_here, z_here)[i].at[k]
                here.append(target)
                self.loads.append(
                    pltpu.make_async_copy(spot(half)(by), target, marks[2].at[8 + 4 * i + k])
                )
        self.y_first = RingScatter(
            net,
            place,
            "y",
            y_spot(0),
            y_spot(1),
            rooms[0:6],
            {1: here[0], 0: here[2]}.get,
            {3: here[1], 0: here[3]}.get,
        )
        self.z_first = RingScatter(
            net,
            place,
            "z",
            z_spot(0),
            z_spot(1),
            rooms[6:12],
            {1: here[4], 0: here[6]}.get,
            {3: here[5], 0: here[7]}.get,
        )

        def then_z(j):
            return y1.at[lax.div(j, 2), lax.rem(j, 2)]

        self.z_second = RingScatter(
            net,
            place,
            "z",
            stepped(place, "z", lambda j: then_z(j).at[:, pl.ds(0, 384)]),
            stepped(place, "z", lambda j: then_z(j).at[:, pl.ds(384, 384)]),
            rooms[12:18],
        )
        self.y_second = RingScatter(
            net,
            place,
            "y",
            stepped(place, "y", lambda j: z1.at[j, :, pl.ds(0, 384)]),
            stepped(place, "y", lambda j: z1.at[j, :, pl.ds(384, 256)]),
            rooms[18:24],
        )

    @staticmethod
    def scratch():
        rest = HALF - CUT
        return [
            pltpu.VMEM((4, 2, 144, CUT), BF),
            pltpu.VMEM((4, 2, 144, rest), BF),
            pltpu.VMEM((2, 2, 144, CUT), BF),
            pltpu.VMEM((4, 144, rest), BF),
            pltpu.VMEM((144, CUT), F32),
            pltpu.VMEM((144, rest), F32),
            pltpu.VMEM((8, 32, HALF + 128), BF),
            pltpu.VMEM((8, 32, HALF + 128), BF),
            *RingScatter.room_shapes((2, 144, CUT), (2, 144, CUT)),
            *RingScatter.room_shapes((2, 144, rest), (2, 144, rest)),
            *RingScatter.room_shapes((144, 384), (144, 384)),
            *RingScatter.room_shapes((144, 384), (144, 256)),
        ]

    def begin(self):
        for load in self.loads:
            load.start()
        for line in (self.y_first, self.z_first):
            line.start_far()
            line.start_near()

    def turn(self):
        for load in self.loads:
            load.wait()
        self.y_first.middle()
        self.z_first.middle()

    def next(self):
        self.y_first.finish(self.y1.at[0], self.y1.at[1])
        self.z_second.start_far()
        self.z_second.start_near()
        self.z_first.finish(self.z1.at[pl.ds(0, 2)], self.z1.at[pl.ds(2, 2)])
        self.y_second.start_far()
        self.y_second.start_near()

    def turn_again(self):
        self.z_second.middle()
        self.y_second.middle()

    def last(self):
        z2, y2 = self.z2, self.y2
        self.z_second.finish(z2.at[:, pl.ds(0, 384)], z2.at[:, pl.ds(384, 384)])
        self.y_second.finish(y2.at[:, pl.ds(0, 384)], y2.at[:, pl.ds(384, 256)])

    def send_home(self):
        snd = self.snd
        total = jnp.concatenate([self.z2[...], self.y2[...], self.late[...]], axis=1)
        blank = jnp.zeros((14, HALF + 128), F32)
        for k in range(8):
            snd[k] = jnp.concatenate([total[18 * k : 18 * k + 18], blank], axis=0).astype(BF)
        place = self.place
        send, recv, here = self.marks
        row_half = lax.div(place.z, 2)
        self.slot = self.x_hi * 4 + place.core * 2 + lax.rem(place.z, 2)
        self.own = place.z * 2 + place.core
        self.stays = row_half == self.x_hi
        for k in range(8):
            copy = pltpu.make_async_remote_copy(
                src_ref=snd.at[k],
                dst_ref=self.rcv.at[self.slot],
                send_sem=send.at[k],
                recv_sem=recv.at[self.slot],
                device_id=place.device(x=row_half * 2 + self.x_lo, z=k // 2, core=k % 2),
                device_id_type=MESH,
            )
            is_here = self.stays & (self.own == k)

            @pl.when(jnp.logical_not(is_here))
            def _(copy=copy):
                copy.start()

            @pl.when(is_here)
            def _(k=k):
                keep = pltpu.make_async_copy(snd.at[k], self.rcv.at[self.slot], here.at[0])
                keep.start()
                keep.wait()

    def arrive(self, dwq, dwo, dwg, dwu, dwd):
        send, recv, _ = self.marks
        for m in range(8):
            arrival = pltpu.make_async_remote_copy(
                src_ref=self.snd.at[m],
                dst_ref=self.rcv.at[m],
                send_sem=send.at[m],
                recv_sem=recv.at[m],
                device_id=self.place.partner(),
                device_id_type=MESH,
            )

            @pl.when(jnp.logical_not(self.stays & (self.slot == m)))
            def _(arrival=arrival):
                arrival.wait_recv()

            @pl.when(jnp.logical_not(self.stays & (self.own == m)))
            def _(arrival=arrival):
                arrival.wait_send()

        def tile(x_hi, n):
            core, n = (n % 14) // 7, (n // 14) * 7 + n % 7
            c, n = n // 11, n % 11
            return self.rcv[x_hi * 4 + core * 2 + c, :, 128 * n : 128 * n + 128].astype(F32)[:24]

        def turned(value):
            value = jnp.concatenate([value, jnp.zeros((104, 128), F32)], axis=0)
            return jnp.transpose(value)[:, :18]

        for which, out in enumerate((dwg, dwu, dwd)):
            for n in range(27):
                value = None
                for x_hi in range(2):
                    if 0 <= n - 13 * x_hi < 14:
                        term = tile(x_hi, 14 * which + n - 13 * x_hi)
                        value = term if value is None else value + term
                span = slice(128 * n, 128 * n + 128)
                if which < 2:
                    out[:, span] = value[:18]
                else:
                    out[span] = turned(value)
        for x_hi in range(2):
            for core in range(2):
                at = x_hi * 4 + core * 2
                span = slice(128 * (at // 2), 128 * (at // 2) + 128)
                dwo[span] = turned(self.rcv[at, :, HALF:].astype(F32)[:24])
                dwq[:, span] = self.rcv[at + 1, :, HALF:].astype(F32)[:18]


def rms_scale(tensor, scaling):
    return tensor * lax.rsqrt(jnp.mean(tensor * tensor, axis=-1, keepdims=True) + EPS) * scaling


def angles(token_pos):
    middle = HD // 2
    frequency = THETA ** (-2.0 * jnp.arange(middle, dtype=F32) / HD)
    turned = token_pos.astype(F32)[:, None] * frequency[None, :]
    return (jnp.cos(turned), jnp.sin(turned))


def rotary(tensor, cosine, sine):
    middle = tensor.shape[-1] // 2
    lower_half = tensor[..., :middle]
    upper_half = tensor[..., middle:]
    return jnp.concatenate(
        [lower_half * cosine - upper_half * sine, upper_half * cosine + lower_half * sine], axis=-1
    )


def shards(
    layer_input,
    segment_ids,
    positions,
    w_query,
    w_key,
    w_value,
    w_out,
    w_gate,
    w_up,
    w_down,
    norm_attn,
    norm_query,
    norm_key,
    norm_post,
    norm_ffn,
    norm_out,
    cotangent,
):
    sp, tp = lax.axis_index("sp"), lax.axis_index("tp")
    core = lax.rem(sp, 2)
    own_start = (sp * 2 + tp) * TOK
    chip_start = lax.div(sp, 2) * 512 + tp * TOK

    firsts = jnp.sum(
        (segment_ids[None, :] < jnp.arange(4, dtype=jnp.int32)[:, None]).astype(jnp.int32), axis=1
    )
    row_token = chip_start + jnp.concatenate([jnp.arange(TOK), 256 + jnp.arange(TOK)]).astype(
        jnp.int32
    )
    row_segs = jnp.concatenate(
        [
            lax.dynamic_slice_in_dim(segment_ids, chip_start, TOK),
            lax.dynamic_slice_in_dim(segment_ids, chip_start + 256, TOK),
        ]
    )
    row_first = jnp.zeros_like(row_token)
    for k in range(4):
        row_first = jnp.where(row_segs == k, firsts[k], row_first)
    key_rows = jnp.asarray(KEY_TOKENS) + core * 256
    cosine, sine = angles(lax.dynamic_slice_in_dim(positions, own_start, TOK))

    def query_piece(pre_rot, scaling):
        return rotary(rms_scale(pre_rot, scaling), cosine[:, None, :], sine[:, None, :])

    def key_piece(pre_rot, scaling):
        return rotary(rms_scale(pre_rot, scaling), cosine, sine)

    wq_other = fetch_weight(w_query, 1)
    wq_both = jnp.concatenate([w_query, wq_other], axis=1)
    input_f = layer_input.astype(F32)
    h_attn = rms_scale(input_f, norm_attn).astype(BF)
    q_pre = jnp.dot(h_attn, wq_both, preferred_element_type=F32).reshape(TOK, HEADS, HD)
    q_rot = query_piece(q_pre, norm_query).astype(BF)
    q_scaled = (q_rot * BF(HD**-0.5)).transpose(1, 0, 2)
    k_pre = jnp.dot(h_attn, w_key, preferred_element_type=F32)
    k_rot = key_piece(k_pre, norm_key).astype(BF)
    v_own = jnp.dot(h_attn, w_value, preferred_element_type=F32).astype(BF)
    kv_own = jnp.concatenate([k_rot, v_own], axis=1)
    kv_all, q_all, wo_other, o_heads, inverse = attention_forward(
        kv_own, q_scaled, w_out, key_rows, row_token[:, None], row_first[:, None], 2
    )
    layer_output, d_mid, d_attn, d_heads, delta, d_gains, sums = feed_forward(
        layer_input,
        o_heads,
        inverse,
        w_out,
        wo_other,
        jnp.stack([norm_post, norm_ffn, norm_out]),
        cotangent,
        w_gate,
        w_up,
        w_down,
        6,
    )
    d_input, d_wq, d_wk, d_wv, d_wo, d_wg, d_wu, d_wd, gains = attention_backward(
        (kv_all, sums, w_query, wq_other, w_key, w_value),
        (
            q_all,
            d_heads,
            delta,
            key_rows,
            row_token[None, :],
            row_first[None, :],
            q_pre.transpose(1, 0, 2),
            k_pre,
            cosine,
            sine,
            h_attn,
            d_attn,
            o_heads,
            layer_input,
            d_mid,
            norm_attn[None, :],
            norm_query[None, :],
            norm_key[None, :],
            d_gains,
        ),
        8,
    )
    return (
        layer_output,
        d_input,
        d_wq,
        d_wk,
        d_wv,
        d_wo,
        d_wg,
        d_wu,
        d_wd,
        gains[0],
        gains[4, :HD],
        gains[4, HD : 2 * HD],
        gains[1],
        gains[2],
        gains[3],
    )


def solution(mesh):
    rows = P(("sp", "tp"), None)
    in_specs = (
        rows,
        P(),
        P(),
        P(None, "tp"),
        P(),
        P(),
        P("tp", None),
        P(None, "tp"),
        P(None, "tp"),
        P("tp", None),
        P(),
        P(),
        P(),
        P(),
        P(),
        P(),
        rows,
    )
    out_specs = (
        rows,
        rows,
        P("sp", "tp"),
        P(),
        P(),
        P("tp", "sp"),
        P("sp", "tp"),
        P("sp", "tp"),
        P("tp", "sp"),
        P(),
        P(),
        P(),
        P(),
        P(),
        P(),
    )
    return jax.shard_map(shards, mesh=mesh, in_specs=in_specs, out_specs=out_specs, check_vma=False)
```

```python
import jax
import jax.numpy as jnp
import numpy as np
from jax import lax
from jax.experimental import pallas as pl
from jax.experimental.pallas import tpu as pltpu
from jax.sharding import PartitionSpec as P

EPS = 1e-06
THETA = 1000000.0
BF = jnp.bfloat16
F32 = jnp.float32
MESH = pl.DeviceIdType.MESH
IN_VMEM = pl.BlockSpec(memory_space=pltpu.VMEM)
VMEM_BYTES = 58 * 1024 * 1024

TOK = 128
D = 1152
HD = 256
HEADS = 4
ROWS = 2 * TOK
HID = 1728
HID_PAD = 1792
HALF = 1408
CUT = 768
CHUNK = 256


class Place:
    def __init__(self):
        sp = lax.axis_index("sp")
        self.core = lax.rem(sp, 2)
        self.z = lax.rem(lax.div(sp, 2), 4)
        self.y = lax.div(sp, 16)
        self.x = lax.rem(lax.div(sp, 8), 2) * 2 + lax.axis_index("tp")

    def device(self, **moved):
        x, y, z, core = (moved.get(name, getattr(self, name)) for name in ("x", "y", "z", "core"))
        return (((y * 2 + lax.div(x, 2)) * 4 + z) * 2 + core, lax.rem(x, 2))

    def step(self, axis, by):
        return lax.rem(getattr(self, axis) + by, 4)

    def toward(self, axis, by):
        return self.device(**{axis: self.step(axis, by)})

    def partner(self):
        return self.device(core=1 - self.core)


class Net:
    def __init__(self, send, recv):
        self.send, self.recv, self.used, self.started = send, recv, 0, []

    def copy(self, source, target, device):
        at = self.used
        self.used += 1
        return pltpu.make_async_remote_copy(
            src_ref=source,
            dst_ref=target,
            send_sem=self.send.at[at],
            recv_sem=self.recv.at[at],
            device_id=device,
            device_id_type=MESH,
        )

    def go(self, copy):
        copy.start()
        self.started.append(copy)

    def settle(self, copy):
        copy.wait_send()
        self.started = [other for other in self.started if other is not copy]

    def drain(self):
        for copy in self.started:
            copy.wait_send()
        self.started = []


def greet(devices, meanwhile=None):
    barrier = pltpu.get_barrier_semaphore()
    for device in devices:
        pl.semaphore_signal(barrier, inc=1, device_id=device, device_id_type=MESH)
    if meanwhile is not None:
        meanwhile()
    pl.semaphore_wait(barrier, len(devices))


def ring(place, axis):
    return [place.toward(axis, 1), place.toward(axis, 3)]


class RingGather:
    def __init__(self, net, place, axis, view, lo, hi):
        self.net = net
        me, nxt, prev = getattr(place, axis), place.step(axis, 1), place.step(axis, 3)
        right, left = ring(place, axis)
        self.to_right = net.copy(view(me), view(me), right)
        self.to_left = net.copy(view(me), view(me), left)
        self.on_right = net.copy(lo(prev), lo(prev), right)
        self.on_left = net.copy(hi(nxt), hi(nxt), left)

    def start(self):
        self.net.go(self.to_right)
        self.net.go(self.to_left)

    def forward(self):
        self.to_right.wait_recv()
        self.net.go(self.on_right)
        self.to_left.wait_recv()
        self.net.go(self.on_left)

    def finish(self):
        self.on_right.wait_recv()
        self.on_left.wait_recv()


class Direct:
    def __init__(self, net, place, axis, source, landing):
        self.net = net
        self.copies = [
            net.copy(
                source(place.step(axis, by)), landing(getattr(place, axis)), place.toward(axis, by)
            )
            for by in (2, 1, 3)
        ]

    def start(self):
        for copy in self.copies:
            self.net.go(copy)

    def wait(self):
        for copy in self.copies:
            copy.wait_recv()


def by_rows(ref, act):
    *lead, rows, _ = ref.shape
    block = next(size for size in (64, 48, 32, 16) if rows % size == 0)
    for spot in np.ndindex(*lead):

        def one(i, carry, spot=spot):
            act(spot, pl.ds(pl.multiple_of(i * block, block), block))
            return carry

        lax.fori_loop(0, rows // block, one, 0)


def add_to(target, other):
    def act(spot, rows):
        at = (*spot, rows, slice(None))
        target[at] = (target[at].astype(F32) + other[at].astype(F32)).astype(target.dtype)

    by_rows(target, act)


def sum_to(target, others):
    def act(spot, rows):
        at = (*spot, rows, slice(None))
        total = others[0][at].astype(F32)
        for other in others[1:]:
            total = total + other[at].astype(F32)
        target[at] = total.astype(target.dtype)

    by_rows(target, act)


def stepped(place, axis, view):
    return lambda by: view(place.step(axis, by))


class RingScatter:
    def __init__(self, net, place, axis, lo, hi, room, lo_here=None, hi_here=None):
        self.net, self.lo, self.hi = net, lo_here or lo, hi_here or hi
        right, left = ring(place, axis)
        self.lo1, self.lo_l, self.lo_r, self.hi1, self.hi_l, self.hi_r = room
        self.a = net.copy(lo(2), self.lo1, right)
        self.b = net.copy(hi(2), self.hi1, left)
        self.c_hi = net.copy(hi(1), self.hi_l, right)
        self.d_lo = net.copy(lo(3), self.lo_r, left)
        self.c_lo = net.copy(self.lo1, self.lo_l, right)
        self.d_hi = net.copy(self.hi1, self.hi_r, left)

    def start_far(self):
        self.net.go(self.a)
        self.net.go(self.b)

    def start_near(self):
        self.net.go(self.c_hi)
        self.net.go(self.d_lo)

    def middle(self):
        self.a.wait_recv()
        add_to(self.lo1, self.lo(1))
        self.net.go(self.c_lo)
        self.b.wait_recv()
        add_to(self.hi1, self.hi(3))
        self.net.go(self.d_hi)

    def finish(self, lo_out, hi_out):
        self.c_hi.wait_recv()
        self.d_hi.wait_recv()
        sum_to(hi_out, [self.hi(0), self.hi_l, self.hi_r])
        self.d_lo.wait_recv()
        self.c_lo.wait_recv()
        sum_to(lo_out, [self.lo(0), self.lo_l, self.lo_r])

    @staticmethod
    def room_shapes(lo_shape, hi_shape):
        return [pltpu.VMEM(lo_shape, BF)] * 3 + [pltpu.VMEM(hi_shape, BF)] * 3


def params(call_id):
    return pltpu.CompilerParams(
        collective_id=call_id, has_side_effects=True, vmem_limit_bytes=VMEM_BYTES
    )


def sems(count):
    return [pltpu.SemaphoreType.DMA((count,)), pltpu.SemaphoreType.DMA((count,))]


class WeightSwap:
    def __init__(self, net, place, w_ref, other_ref):
        self.net = net
        quarter = w_ref.shape[0] // 4
        right, left = ring(place, "x")

        def rows(ref, side):
            return ref.at[pl.ds(pl.multiple_of((2 * side + place.core) * quarter, 16), quarter)]

        self.first = [
            net.copy(rows(w_ref, side), rows(other_ref, side), (left, right)[side])
            for side in (0, 1)
        ]
        self.trades = [
            net.copy(rows(other_ref, side), rows(other_ref, side), place.partner())
            for side in (0, 1)
        ]

    def start(self):
        for copy in self.first:
            self.net.go(copy)

    def forward(self):
        for copy, trade in zip(self.first, self.trades):
            copy.wait_recv()
            self.net.go(trade)

    def finish(self):
        for trade in self.trades:
            trade.wait_recv()


PARTS = (
    (0, 48, 0, ("x", "y", "z")),
    (48, 48, 768, ("z", "x", "y")),
    (96, 32, 1536, ("y", "z", "x")),
)


def part_views(place, buf, part):
    _, rows, base, (first, second, third) = part
    at1, at2, at3 = (getattr(place, axis) for axis in (first, second, third))

    def block(lead, start, size):
        return buf.at[lead, pl.ds(pl.multiple_of(base + start, 16), size)]

    return (
        (first, lambda j: block(at3, (at2 * 4 + j) * rows, rows)),
        (second, lambda j: block(at3, j * 4 * rows, 4 * rows)),
        (third, lambda j: block(j, 0, 16 * rows)),
    )


def halves(view):
    return (lambda j: view(j).at[:, pl.ds(0, HD)]), (lambda j: view(j).at[:, pl.ds(HD, HD)])


def chunk_rows(n):
    return [256 * n + 64 * i if n < 6 else 1536 + 128 * i + 64 * (n - 6) for i in range(4)]


def key_tokens():
    out = np.zeros((4, 2048), np.int32)
    for skip, rows, base, axes in PARTS:
        for j in range(4):
            for r in range(16 * rows):
                spot = {axes[2]: j, axes[1]: r // (4 * rows), axes[0]: (r // rows) % 4}
                x, y, z = spot["x"], spot["y"], spot["z"]
                token = ((y * 2 + x // 2) * 4 + z) * 512 + (x % 2) * 128 + skip + r % rows
                out[j, base + r] = token
    order = np.zeros((8, CHUNK), np.int64)
    for c in range(8):
        for i in range(4):
            start = chunk_rows(c)[i]
            order[c, 64 * i : 64 * i + 64] = np.arange(start, start + 64)
    return out[:, order]


KEY_TOKENS = key_tokens()


def set_lead(place, n, by):
    return place.step("zyx"[n // 3], by)


def read_sets(buf, key_ref, chunks, leads, key_leads):
    keys, values, tokens = [], [], []
    for n, lead, key_lead in zip(chunks, leads, key_leads):
        rows = chunk_rows(n)
        keys += [buf[lead, start : start + 64, :HD] for start in rows]
        values += [buf[lead, start : start + 64, HD:] for start in rows]
        tokens.append(key_ref[key_lead, n : n + 1])
    return (
        jnp.concatenate(keys, axis=0),
        jnp.concatenate(values, axis=0),
        jnp.concatenate(tokens, axis=1),
    )


def contract(left, right, left_dim, right_dim):
    return lax.dot_general(
        left, right, (((left_dim,), (right_dim,)), ((), ())), preferred_element_type=F32
    )


def turn(u, cosine, sine):
    half = HD // 2
    low, high = u[:, :half], u[:, half:]
    return jnp.concatenate([low * cosine - high * sine, high * cosine + low * sine], axis=1)


def row_bounds(place, segments):
    at = (place.y * 2 + lax.div(place.x, 2)) * 16 + place.z * 4 + lax.rem(place.x, 2)
    rows = jnp.concatenate([segments[pl.ds(at, 1)], segments[pl.ds(at + 2, 1)]], axis=1)
    every = segments[...]
    first = jnp.zeros((1, ROWS), jnp.int32)
    for k in range(1, 4):
        below = jnp.sum((every < k).astype(F32), axis=0, keepdims=True)
        below = jnp.sum(below, axis=1, keepdims=True).astype(jnp.int32)
        first = jnp.where(rows == k, below, first)
    lane = lax.broadcasted_iota(jnp.int32, (1, ROWS), 1)
    last = at * TOK + lane + jnp.where(lane < TOK, 0, TOK)
    return first, last


def down(row):
    return jnp.concatenate(
        [
            jnp.transpose(jnp.broadcast_to(row[:, 128 * i : 128 * i + 128], (128, 128)))
            for i in range(row.shape[1] // 128)
        ],
        axis=0,
    )


def across(ref):
    return ref[...].reshape(1, ref.shape[0])


def norm_scale(v):
    return lax.rsqrt(jnp.mean(v * v, axis=-1, keepdims=True) + EPS)


def norm_back(v, r, gain, e):
    eg = e * gain
    dv = r * eg - v * (r * r * r) * jnp.mean(eg * v, axis=-1, keepdims=True)
    return dv, jnp.sum(e * v * r, axis=0, keepdims=True)


def forward_kernel(
    x_ref,
    g_attn,
    g_query,
    g_key,
    wq_ref,
    wk_ref,
    wv_ref,
    w_ref,
    cos_ref,
    sin_ref,
    segments,
    key_ref,
    buf,
    q_all,
    wq_other,
    w_other,
    o_out,
    inv_out,
    q_pre,
    k_pre,
    h_out,
    o_sum,
    l_sum,
    o_got,
    l_got,
    send,
    recv,
):
    place, net = Place(), Net(send, recv)
    core = place.core
    partner = place.partner()
    mine = pl.ds(pl.multiple_of(core * TOK, TOK), TOK)
    theirs = pl.ds(pl.multiple_of((1 - core) * TOK, TOK), TOK)
    all_views = [part_views(place, buf, part) for part in PARTS]

    def keys_and_values():
        xf = x_ref[...].astype(F32)
        h = (xf * norm_scale(xf) * across(g_attn)).astype(BF)
        h_out[...] = h
        k = jnp.dot(h, wk_ref[...], preferred_element_type=F32)
        k_pre[...] = k
        k = turn(k * norm_scale(k) * across(g_key), cos_ref[...], sin_ref[...]).astype(BF)
        v = jnp.dot(h, wv_ref[...], preferred_element_type=F32).astype(BF)
        for (skip, rows, _, _), views in zip(PARTS, all_views):
            axis, view = views[0]
            own = view(getattr(place, axis))
            own[:, :HD] = k[skip : skip + rows]
            own[:, HD:] = v[skip : skip + rows]

    greet(
        ring(place, "x") + ring(place, "y") + ring(place, "z") + [partner],
        keys_and_values,
    )
    swap_wq = WeightSwap(net, place, wq_ref, wq_other)
    swap_w = WeightSwap(net, place, w_ref, w_other)
    stages = [
        [RingGather(net, place, axis, view, *halves(view)) for axis, view in views]
        for views in all_views
    ]
    for rings in stages:
        rings[0].start()
    swap_wq.start()

    def queries(which, w):
        q = jnp.dot(h_out[...], w[...], preferred_element_type=F32)
        for i in range(2):
            u = q[:, HD * i : HD * i + HD]
            q_pre[2 * which + i] = u
            u = turn(u * norm_scale(u) * across(g_query), cos_ref[...], sin_ref[...])
            q_all[2 * which + i, mine] = (u.astype(BF).astype(F32) * HD**-0.5).astype(BF)

    queries(0, wq_ref)
    for h in range(HEADS):
        o_sum[h] = jnp.zeros((ROWS, HD), F32)
        l_sum[h] = jnp.zeros((ROWS, 128), F32)
    for rings in stages:
        rings[0].forward()
    for rings in stages:
        rings[0].finish()
        rings[1].start()
    swap_wq.forward()
    first, last = (down(row) for row in row_bounds(place, segments))
    swap_wq.finish()
    queries(1, wq_other)
    swap_q = net.copy(q_all.at[:, mine], q_all.at[:, mine], partner)
    net.go(swap_q)
    for rings in stages:
        rings[1].forward()
    for rings in stages:
        rings[1].finish()
        rings[2].start()
    swap_w.start()
    swap_q.wait_recv()

    def attend(by):
        leads = [set_lead(place, n, by) for n in range(8)]
        keys, values, token = read_sets(buf, key_ref, range(8), leads, leads)
        token = token + core * 256
        allowed = jnp.concatenate(
            [
                (token[:, 128 * i : 128 * i + 128] <= last)
                & (token[:, 128 * i : 128 * i + 128] >= first)
                for i in range(16)
            ],
            axis=1,
        )
        for h in range(HEADS):
            weights = jnp.exp(contract(q_all[h], keys, 1, 1))
            weights = jnp.where(allowed, weights, 0.0)
            l_sum[h] += sum(weights[:, 128 * i : 128 * i + 128] for i in range(16))
            o_sum[h] += jnp.dot(weights.astype(BF), values, preferred_element_type=F32)

    attend(0)
    for rings in stages:
        rings[2].forward()
    swap_w.forward()
    lax.fori_loop(0, 2, lambda i, c: (attend(1 + 2 * i), c)[1], 0)
    for rings in stages:
        rings[2].finish()
    attend(2)
    swap_w.finish()
    swap_o = net.copy(o_sum.at[:, theirs], o_got, partner)
    swap_l = net.copy(l_sum.at[:, theirs], l_got, partner)
    net.go(swap_l)
    net.go(swap_o)
    swap_l.wait_recv()
    swap_o.wait_recv()
    for h in range(HEADS):
        total = jnp.sum(l_sum[h, mine] + l_got[h], axis=1, keepdims=True)
        inverse = 1.0 / total
        o_out[h] = (o_sum[h, mine] + o_got[h]) * inverse
        inv_out[h] = jnp.broadcast_to(inverse, (TOK, 128))
    net.drain()


def attention_forward(args, call_id):
    shape = jax.ShapeDtypeStruct
    return pl.pallas_call(
        forward_kernel,
        out_shape=(
            shape((4, 2048, 2 * HD), BF),
            shape((HEADS, ROWS, HD), BF),
            shape((D, 2 * HD), BF),
            shape((2 * HD, D), BF),
            shape((HEADS, TOK, HD), F32),
            shape((HEADS, TOK, 128), F32),
            shape((HEADS, TOK, HD), F32),
            shape((TOK, HD), F32),
            shape((TOK, D), BF),
        ),
        in_specs=[IN_VMEM] * len(args),
        out_specs=[IN_VMEM] * 9,
        scratch_shapes=[
            pltpu.VMEM((HEADS, ROWS, HD), F32),
            pltpu.VMEM((HEADS, ROWS, 128), F32),
            pltpu.VMEM((HEADS, TOK, HD), F32),
            pltpu.VMEM((HEADS, TOK, 128), F32),
            *sems(52),
        ],
        compiler_params=params(call_id),
    )(*args)


GRAD_SLOT = {2: 0, 0: 0, 1: 1, 3: 2}


def turn_back(e, cosine, sine):
    half = HD // 2
    low, high = e[:, :half], e[:, half:]
    return jnp.concatenate([low * cosine + high * sine, high * cosine - low * sine], axis=1)


def backward_kernel(
    kv_hbm,
    sums_hbm,
    wq_hbm,
    wq2_hbm,
    wk_hbm,
    wv_hbm,
    q_all,
    do_ref,
    delta_ref,
    key_ref,
    segments,
    q_pre,
    k_pre,
    cos_ref,
    sin_ref,
    h_ref,
    da_ref,
    o_ref,
    x_ref,
    dmid_ref,
    g_attn,
    g_query,
    g_key,
    gains_ref,
    dx_out,
    home_out,
    w_both,
    gains_out,
    buf,
    wk,
    wv,
    do_all,
    delta_all,
    grads,
    dq_sum,
    dq_got,
    dkv,
    h_line,
    da_line,
    o_line,
    dq_line,
    dq_own,
    o_own,
    late_all,
    late_got,
    late_y,
    late_z,
    gain_got,
    kv_own,
    kv_line,
    w_all,
    w_got,
    w_y,
    w_z,
    w_line,
    dh,
    *rest,
):
    rooms, late_rooms, rest = rest[:54], rest[54:66], rest[66:]
    *weight_refs, send, recv, send2, recv2, here = rest
    place, net = Place(), Net(send, recv)
    core, partner = place.core, place.partner()
    w_loads = [
        pltpu.make_async_copy(source, target, here.at[1 + i])
        for i, (source, target) in enumerate(
            (
                (wq_hbm, buf.at[0, pl.ds(0, D)]),
                (wq2_hbm, buf.at[1, pl.ds(0, D)]),
                (wk_hbm, wk),
                (wv_hbm, wv),
            )
        )
    ]
    w_loads[2].start()
    w_loads[3].start()

    def set_loads(by, slot):
        copies = []
        for i, (_, rows, base, axes) in enumerate(PARTS):
            span = pl.ds(base, 16 * rows)
            source = kv_hbm.at[place.step(axes[2], by), span]
            copies.append(
                pltpu.make_async_copy(source, buf.at[slot, span], here.at[16 + 3 * slot + i])
            )
        return copies

    sets = [set_loads(by, slot) for by, slot in ((2, 0), (1, 1), (3, 0), (0, 1))]
    for copy in sets[0] + sets[1]:
        copy.start()
    weights = WeightSums(place, net, sums_hbm, late_z, weight_refs, (send2, recv2, here))
    greet(weights.friends + ring(place, "x") + ring(place, "y"))
    mine = pl.ds(pl.multiple_of(core * TOK, TOK), TOK)
    theirs = pl.ds(pl.multiple_of((1 - core) * TOK, TOK), TOK)
    do_all[:, mine] = do_ref[...]
    delta_all[core] = delta_ref[...]
    swap_do = net.copy(do_all.at[:, mine], do_all.at[:, mine], partner)
    swap_delta = net.copy(delta_all.at[core], delta_all.at[core], partner)
    net.go(swap_do)
    net.go(swap_delta)

    x_lo = lax.rem(place.x, 2)
    half = TOK // 2

    def line_of(rows):
        return RingGather(
            net,
            place,
            "x",
            lambda j: rows.at[j],
            lambda j: rows.at[j, pl.ds(0, half)],
            lambda j: rows.at[j, pl.ds(half, half)],
        )

    def head_of(j):
        return jnp.where(lax.rem(j, 2) == x_lo, 0, 2) + lax.div(j, 2)

    h_line[place.x] = h_ref[...]
    da_line[place.x] = da_ref[...]
    for h in range(HEADS):
        o_own[h] = o_ref[h].astype(BF)
    o_line[place.x] = o_own[head_of(place.x)]
    line_h, line_da = line_of(h_line), line_of(da_line)
    o_swap = Direct(net, place, "x", lambda j: o_own.at[head_of(j)], lambda j: o_line.at[j])
    dq_swap = Direct(net, place, "x", lambda j: dq_own.at[head_of(j)], lambda j: dq_line.at[j])
    o_swap.start()
    line_h.start()
    line_da.start()
    for h in range(HEADS):
        dq_sum[h] = jnp.zeros((HD, ROWS), F32)
    stages = []
    for i, part in enumerate(PARTS):
        _, rows, base, (first, second, third) = part
        at1, at2 = getattr(place, first), getattr(place, second)

        def block(slot, start, size, base=base):
            return grads.at[slot, pl.ds(pl.multiple_of(base + start, 16), size)]

        views = (
            lambda by, block=block, first=first, at2=at2, rows=rows: block(
                0, (at2 * 4 + place.step(first, by)) * rows, rows
            ),
            lambda by, block=block, second=second, rows=rows: block(
                0, place.step(second, by) * 4 * rows, 4 * rows
            ),
            lambda by, block=block, rows=rows: block(GRAD_SLOT[by], 0, 16 * rows),
        )
        rings = []
        for level, axis in enumerate((first, second, third)):
            spot = 6 * (3 * i + level)
            rings.append(
                RingScatter(net, place, axis, *halves(views[level]), rooms[spot : spot + 6])
            )
        stages.append((rings, views))
    late_first = RingScatter(
        net,
        place,
        "y",
        stepped(place, "y", lambda j: late_got.at[j, 0]),
        stepped(place, "y", lambda j: late_got.at[j, 1]),
        late_rooms[:6],
    )

    def late_spot(j):
        return late_y.at[lax.div(j, 2), lax.rem(j, 2)]

    late_second = RingScatter(
        net,
        place,
        "z",
        stepped(place, "z", lambda j: late_spot(j).at[pl.ds(0, 80)]),
        stepped(place, "z", lambda j: late_spot(j).at[pl.ds(80, 64)]),
        late_rooms[6:],
    )

    def late_term(c, rows, columns):
        term = contract(rows[...].reshape(4 * TOK, D), columns[...].reshape(4 * TOK, HD), 0, 0)
        term = term.astype(BF)
        for k in range(8):
            for which in range(2):
                late_all[which, k // 2, k % 2, c] = term[
                    144 * k : 144 * k + 144, 128 * which : 128 * which + 128
                ]

    weights.begin()
    swap_do.wait_recv()
    swap_delta.wait_recv()

    first, last = row_bounds(place, segments)

    def differ(chunks, by, slot):
        key_leads = [set_lead(place, n, by) for n in chunks]
        keys, values, token = read_sets(buf, key_ref, chunks, [slot] * len(chunks), key_leads)
        token = down(token + core * 256)
        token = jnp.concatenate([token, token], axis=1)
        allowed = (token <= last) & (token >= first)
        d_keys = d_values = None
        for h in range(HEADS):
            probs = jnp.exp(contract(keys, q_all[h], 1, 1))
            probs = jnp.where(allowed, probs, 0.0)
            delta = jnp.concatenate([delta_all[0, h : h + 1], delta_all[1, h : h + 1]], axis=1)
            d_scores = (probs * (contract(values, do_all[h], 1, 1) - delta)).astype(BF)
            value_term = jnp.dot(probs.astype(BF), do_all[h], preferred_element_type=F32)
            key_term = jnp.dot(d_scores, q_all[h], preferred_element_type=F32)
            d_values = value_term if h == 0 else d_values + value_term
            d_keys = key_term if h == 0 else d_keys + key_term
            dq_sum[h] += contract(keys, d_scores, 0, 0)
        d_keys, d_values = d_keys.astype(BF), d_values.astype(BF)
        for m, n in enumerate(chunks):
            for i, start in enumerate(chunk_rows(n)):
                spot = 256 * m + 64 * i
                grads[GRAD_SLOT[by], start : start + 64, :HD] = d_keys[spot : spot + 64]
                grads[GRAD_SLOT[by], start : start + 64, HD:] = d_values[spot : spot + 64]

    def visit(step, after):
        by, slot = ((2, 0), (1, 1), (3, 0), (0, 1))[step]
        for copy in sets[step]:
            copy.wait()
        for chunks in ((0, 1, 2), (3, 4, 5), (6, 7)):
            differ(chunks, by, slot)
        for copy in after:
            copy.start()

    visit(0, sets[2])
    for rings, _ in stages:
        rings[2].start_far()
    line_h.forward()
    line_da.forward()
    weights.turn()
    visit(1, sets[3])
    visit(2, w_loads[0:1])
    for rings, _ in stages:
        rings[2].start_near()
    for rings, _ in stages:
        rings[2].middle()
    weights.next()
    for rings, _ in stages:
        net.settle(rings[2].a)
        net.settle(rings[2].b)
    visit(3, w_loads[1:2])
    swap_dq = net.copy(dq_sum.at[:, :, theirs], dq_got, partner)
    net.go(swap_dq)
    line_h.finish()
    line_da.finish()
    o_swap.wait()
    late_term(0, da_line, o_line)
    weights.turn_again()
    for load in w_loads:
        load.wait()

    swap_dq.wait_recv()
    d_query = jnp.zeros((1, HD), F32)
    for h in range(HEADS):
        e = jnp.transpose(dq_sum[h, :, mine] + dq_got[h]) * HD**-0.5
        e = turn_back(e.astype(BF).astype(F32), cos_ref[...], sin_ref[...])
        u = q_pre[h]
        du, gain = norm_back(u, norm_scale(u), across(g_query), e)
        d_query = d_query + gain
        dq_own[h] = du.astype(BF)
    dq_line[place.x] = dq_own[head_of(place.x)]
    dq_swap.start()
    for level in (2, 1, 0):
        for (rings, views), part in zip(stages, PARTS):
            lo, hi = halves(views[level])
            skip, rows, _, _ = part
            if level:
                rings[level].finish(lo(0), hi(0))
                rings[level - 1].start_far()
                rings[level - 1].start_near()
            else:
                out = dkv.at[pl.ds(skip, rows)]
                rings[level].finish(out.at[:, pl.ds(0, HD)], out.at[:, pl.ds(HD, HD)])
        if level == 2:
            d_h = sum(
                contract(dq_own[h], buf[h // 2, :D, 256 * (h % 2) : 256 * (h % 2) + 256], 1, 1)
                for h in range(HEADS)
            )
            dh[...] = d_h
            dq_swap.wait()
            late_term(1, h_line, dq_line)
            late_swap = net.copy(late_all.at[1 - core], late_got, partner)
            net.go(late_swap)
        if level:
            for rings, _ in stages:
                rings[level - 1].middle()
        if level == 2:
            late_swap.wait_recv()
            for y in range(4):
                add_to(late_got.at[y], late_all.at[core, y])
            late_first.start_far()
            late_first.start_near()
            weights.last()
        if level == 1:
            late_first.middle()
    late_first.finish(late_y.at[0], late_y.at[1])
    late_second.start_far()
    late_second.start_near()

    e = turn_back(dkv[:, :HD].astype(BF).astype(F32), cos_ref[...], sin_ref[...])
    u = k_pre[...]
    dk, d_key = norm_back(u, norm_scale(u), across(g_key), e)
    dk, dv = dk.astype(BF), dkv[:, HD:].astype(BF)
    for i in range(2):
        kv_own[i] = dk[:, 128 * i : 128 * i + 128]
        kv_own[2 + i] = dv[:, 128 * i : 128 * i + 128]
    kv_line[place.x] = kv_own[place.x]
    kv_swap = Direct(net, place, "x", lambda j: kv_own.at[j], lambda j: kv_line.at[j])
    kv_swap.start()
    d_h = dh[...] + contract(dk, wk[...], 1, 1) + contract(dv, wv[...], 1, 1)
    xf = x_ref[...].astype(F32)
    dx, d_attn = norm_back(xf, norm_scale(xf), across(g_attn), d_h)
    dx_out[...] = (dmid_ref[...] + dx).astype(BF)
    late_second.middle()

    def gain_swap(level, axis):
        return Direct(
            net, place, axis, lambda j: gain_got.at[level, at(axis)], lambda j: gain_got.at[level, j]
        )

    def at(axis):
        return getattr(place, axis)

    def gain_sum(level):
        return (gain_got[level, 0] + gain_got[level, 1]) + (gain_got[level, 2] + gain_got[level, 3])

    swaps = [gain_swap(0, "x"), gain_swap(1, "y"), gain_swap(2, "z")]
    norms = jnp.concatenate([d_query, d_key, jnp.zeros((1, D - 2 * HD), F32)], axis=1)
    gain_got[0, place.x] = jnp.concatenate(
        [d_attn, gains_ref[0:3], norms, jnp.zeros((3, D), F32)], axis=0
    )
    swaps[0].start()
    kv_swap.wait()
    term = contract(h_line[...].reshape(4 * TOK, D), kv_line[...].reshape(4 * TOK, 128), 0, 0)
    term = term.astype(BF)
    for k in range(8):
        w_all[k // 4, k % 4] = term[144 * k : 144 * k + 144]
    w_swap = net.copy(w_all.at[1 - core], w_got, partner)
    net.go(w_swap)
    late_second.finish(late_z.at[pl.ds(0, 80)], late_z.at[pl.ds(80, 64)])
    weights.send_home()
    swaps[0].wait()
    gain_got[1, place.y] = gain_sum(0)
    swaps[1].start()
    w_swap.wait_recv()
    add_to(w_got, w_all.at[core])
    w_scatter = Direct(net, place, "y", lambda j: w_got.at[j], lambda j: w_y.at[j])
    w_scatter.start()
    w_y[place.y] = w_got[place.y]
    swaps[1].wait()
    gain_got[2, place.z] = gain_sum(1)
    swaps[2].start()
    w_scatter.wait()
    sum_to(w_z.at[place.z], [w_y.at[j] for j in range(4)])
    w_sums = Direct(net, place, "z", lambda j: w_z.at[place.z], lambda j: w_z.at[j])
    w_sums.start()
    swaps[2].wait()
    gain_got[3, core] = gain_sum(2)
    gain_last = net.copy(gain_got.at[3, core], gain_got.at[3, core], partner)
    net.go(gain_last)
    w_sums.wait()
    sum_to(w_line.at[place.x, place.y], [w_z.at[j] for j in range(4)])
    y_back = Direct(
        net, place, "y", lambda j: w_line.at[place.x, place.y], lambda j: w_line.at[place.x, j]
    )
    y_back.start()
    weights.arrive()
    home_out[...] = weights.rcv[...]
    y_back.wait()
    x_back = Direct(net, place, "x", lambda j: w_line.at[place.x], lambda j: w_line.at[j])
    x_back.start()
    gain_last.wait_recv()
    gains_out[...] = gain_got[3, 0] + gain_got[3, 1]
    x_back.wait()
    w_both[core] = w_line[...]
    w_last = net.copy(w_line, w_both.at[core], partner)
    net.go(w_last)
    w_last.wait_recv()
    net.drain()


def attention_backward(hbm, small, call_id):
    shape = jax.ShapeDtypeStruct
    rooms = []
    for _, rows, _, _ in PARTS:
        for blocks in (1, 4, 16):
            rooms += RingScatter.room_shapes((blocks * rows, HD), (blocks * rows, HD))
    late_rooms = [
        *RingScatter.room_shapes((2, 144, 128), (2, 144, 128)),
        *RingScatter.room_shapes((80, 128), (64, 128)),
    ]
    return pl.pallas_call(
        backward_kernel,
        out_shape=(
            shape((TOK, D), BF),
            shape((8, 32, HALF + 128), BF),
            shape((2, 4, 4, 144, 128), BF),
            shape((8, D), F32),
        ),
        in_specs=[pl.BlockSpec(memory_space=pl.ANY)] * 6 + [IN_VMEM] * len(small),
        out_specs=[IN_VMEM] * 4,
        scratch_shapes=[
            pltpu.VMEM((2, 2048, 2 * HD), BF),
            pltpu.VMEM((D, HD), BF),
            pltpu.VMEM((D, HD), BF),
            pltpu.VMEM((HEADS, ROWS, HD), BF),
            pltpu.VMEM((2, 8, TOK), F32),
            pltpu.VMEM((3, 2048, 2 * HD), BF),
            pltpu.VMEM((HEADS, HD, ROWS), F32),
            pltpu.VMEM((HEADS, HD, TOK), F32),
            pltpu.VMEM((TOK, 2 * HD), F32),
            pltpu.VMEM((4, TOK, D), BF),
            pltpu.VMEM((4, TOK, D), BF),
            pltpu.VMEM((4, TOK, HD), BF),
            pltpu.VMEM((4, TOK, HD), BF),
            pltpu.VMEM((4, TOK, HD), BF),
            pltpu.VMEM((4, TOK, HD), BF),
            pltpu.VMEM((2, 4, 2, 2, 144, 128), BF),
            pltpu.VMEM((4, 2, 2, 144, 128), BF),
            pltpu.VMEM((2, 2, 144, 128), BF),
            pltpu.VMEM((144, 128), F32),
            pltpu.VMEM((4, 4, 8, D), F32),
            pltpu.VMEM((4, TOK, 128), BF),
            pltpu.VMEM((4, TOK, 128), BF),
            pltpu.VMEM((2, 4, 144, 128), BF),
            pltpu.VMEM((4, 144, 128), BF),
            pltpu.VMEM((4, 144, 128), BF),
            pltpu.VMEM((4, 144, 128), BF),
            pltpu.VMEM((4, 4, 144, 128), BF),
            pltpu.VMEM((TOK, D), F32),
            *rooms,
            *late_rooms,
            *WeightSums.scratch(),
            *sems(160),
            *sems(8),
            pltpu.SemaphoreType.DMA((24,)),
        ],
        compiler_params=params(call_id),
    )(*hbm, *small)


def feed_kernel(
    x_ref,
    o_ref,
    inv_ref,
    wo_ref,
    wo2_ref,
    post_ref,
    ffn_ref,
    out_gain_ref,
    cot_ref,
    wg_hbm,
    wu_hbm,
    wd_hbm,
    out_ref,
    dmid_out,
    dattn_out,
    do_out,
    delta_out,
    dgains_out,
    sums_hbm,
    wg,
    wu,
    wd,
    h_line,
    f_line,
    h_turned,
    f_turned,
    gelu_kept,
    slope_kept,
    act,
    d_gate,
    d_up,
    f_terms,
    h_terms,
    snd,
    got,
    attn,
    mid,
    ffn,
    *rest,
):
    *room, send, recv, local = rest
    place, net = Place(), Net(send, recv)
    core, partner = place.core, place.partner()
    x_hi = lax.div(place.x, 2)
    first_unit = pl.multiple_of(x_hi * (2 * HID - HID_PAD), 128)
    window = pl.ds(first_unit, HID_PAD)
    loads = [
        pltpu.make_async_copy(source, target, local.at[i])
        for i, (source, target) in enumerate(
            ((wg_hbm.at[:, window], wg), (wu_hbm.at[:, window], wu), (wd_hbm.at[window], wd))
        )
    ]
    for load in loads:
        load.start()
    greet(ring(place, "x") + [partner])
    half = TOK // 2
    top, bottom = pl.ds(0, half), pl.ds(half, half)
    g_post, g_ffn, g_out = (across(ref) for ref in (post_ref, ffn_ref, out_gain_ref))

    def gather(lines):
        line = RingGather(
            net,
            place,
            "x",
            lambda j: lines.at[j],
            lambda j: lines.at[j, top],
            lambda j: lines.at[j, bottom],
        )
        line.start()
        line.forward()
        line.finish()

    def scatter(terms, room):
        line = RingScatter(
            net,
            place,
            "x",
            stepped(place, "x", lambda j: terms.at[j, top]),
            stepped(place, "x", lambda j: terms.at[j, bottom]),
            room,
        )
        line.start_far()
        line.start_near()
        return line

    o_cat = [o_ref[h].astype(BF) for h in range(HEADS)]
    a = jnp.dot(jnp.concatenate(o_cat[:2], axis=1), wo_ref[...], preferred_element_type=F32)
    a += jnp.dot(jnp.concatenate(o_cat[2:], axis=1), wo2_ref[...], preferred_element_type=F32)
    attn[...] = a
    mid[...] = x_ref[...].astype(F32) + a * norm_scale(a) * g_post
    m = mid[...]
    h_line[place.x] = (m * norm_scale(m) * g_ffn).astype(BF)
    gather(h_line)

    for load in loads:
        load.wait()
    lines = 4 * TOK
    low_unit, high_unit = jnp.where(x_hi == 0, 0, 64), jnp.where(x_hi == 0, HID, HID_PAD)

    def units(n):
        return pl.ds(pl.multiple_of(n * 256, 256), 256)

    def forward(n, carry):
        h = h_line[...].reshape(lines, D)
        gate = jnp.dot(h, wg[:, units(n)], preferred_element_type=F32)
        up = jnp.dot(h, wu[:, units(n)], preferred_element_type=F32)
        unit = n * 256 + lax.broadcasted_iota(jnp.int32, (1, 256), 1)
        own = jnp.where((unit >= low_unit) & (unit < high_unit), 1.0, 0.0)
        scale, cube = 0.7978845608028654, 0.044715
        square = gate * gate
        bent = jnp.tanh(scale * gate * (1.0 + cube * square))
        lifted = 0.5 * (1.0 + bent)
        gelu = gate * lifted * own
        slope = lifted + 0.5 * gate * (1.0 - bent * bent) * scale * (1.0 + 3.0 * cube * square)
        act[:, units(n)] = (gelu * up).astype(BF)
        gelu_kept[:, units(n)] = gelu.astype(BF)
        slope_kept[:, units(n)] = (slope * up * own).astype(BF)
        return carry

    lax.fori_loop(0, HID_PAD // 256, forward, 0)

    def columns(n):
        return pl.ds(pl.multiple_of(n * 384, 128), 384)

    def project(n, carry):
        term = jnp.dot(act[...], wd[:, columns(n)], preferred_element_type=F32)
        f_terms[:, :, columns(n)] = term.astype(BF).reshape(4, TOK, 384)
        return carry

    lax.fori_loop(0, 3, project, 0)
    line = scatter(f_terms, room[:6])
    h_turned[...] = jnp.transpose(h_line[...].reshape(lines, D))
    line.middle()
    line.finish(ffn.at[top], ffn.at[bottom])
    f = ffn[...]
    r_out = norm_scale(f)
    out_ref[...] = (mid[...] + f * r_out * g_out).astype(BF)
    df, d_out = norm_back(f, r_out, g_out, cot_ref[...].astype(F32))
    f_line[place.x] = df.astype(BF)
    gather(f_line)

    def backward(n, carry):
        d_act = contract(f_line[...].reshape(lines, D), wd[units(n)], 1, 1)
        d_gate[:, units(n)] = (d_act * slope_kept[:, units(n)].astype(F32)).astype(BF)
        d_up[:, units(n)] = (d_act * gelu_kept[:, units(n)].astype(F32)).astype(BF)
        return carry

    lax.fori_loop(0, HID_PAD // 256, backward, 0)

    def back_project(n, carry):
        term = contract(d_gate[...], wg[columns(n)], 1, 1) + contract(d_up[...], wu[columns(n)], 1, 1)
        h_terms[:, :, columns(n)] = term.astype(BF).reshape(4, TOK, 384)
        return carry

    lax.fori_loop(0, 3, back_project, 0)
    line = scatter(h_terms, room[6:])
    f_turned[...] = jnp.transpose(f_line[...].reshape(lines, D))

    def fill(i, which, put):
        some = pl.ds(pl.multiple_of(which * 896, 128), 896)
        rows = pl.ds(576 * i, 576)
        pairs = ((h_turned, d_gate), (h_turned, d_up), (f_turned, act))
        for m, (left, right) in enumerate(pairs):
            term = jnp.dot(left[rows], right[:, some], preferred_element_type=F32)
            for k in range(4):
                piece = term[144 * k : 144 * k + 144]
                for c in range(2):
                    low = max(896 * m, HALF * c)
                    high = min(896 * m + 896, HALF * c + HALF)
                    if low < high:
                        at = (2 * i + k // 2, k % 2, c, slice(None), slice(low - HALF * c, high - HALF * c))
                        put(at, piece[:, low - 896 * m : high - 896 * m])

    def put_snd(at, value):
        snd[at] = value.astype(BF)

    def put_got(at, value):
        got[at] = (got[at].astype(F32) + value).astype(BF)

    swaps = [net.copy(snd.at[y], got.at[y], partner) for y in range(4)]
    for y in range(4):
        snd[y, :, 1, :, 1280:] = jnp.zeros((2, 144, 128), BF)
    for i in range(2):
        fill(i, 1 - core, put_snd)
        net.go(swaps[2 * i])
        net.go(swaps[2 * i + 1])
    line.middle()
    stores = [pltpu.make_async_copy(got.at[y], sums_hbm.at[y], local.at[3 + y]) for y in range(4)]
    for i in range(2):
        swaps[2 * i].wait_recv()
        swaps[2 * i + 1].wait_recv()
        fill(i, core, put_got)
        stores[2 * i].start()
        stores[2 * i + 1].start()
    line.finish(ffn.at[top], ffn.at[bottom])

    m, a = mid[...], attn[...]
    dm, d_ffn = norm_back(m, norm_scale(m), g_ffn, ffn[...])
    d_mid = cot_ref[...].astype(F32) + dm
    dmid_out[...] = d_mid
    da, d_post = norm_back(a, norm_scale(a), g_post, d_mid)
    da = da.astype(BF)
    dattn_out[...] = da
    dgains_out[...] = jnp.concatenate([d_post, d_ffn, d_out, jnp.zeros((5, D), F32)], axis=0)
    delta_out[...] = jnp.zeros((8, TOK), F32)
    for h in range(HEADS):
        weight = (wo_ref, wo2_ref)[h // 2]
        d_o = contract(da, weight[256 * (h % 2) : 256 * (h % 2) + 256], 1, 1).astype(BF).astype(F32)
        inverse = inv_ref[h]
        do_out[h] = (d_o * jnp.concatenate([inverse, inverse], axis=1)).astype(BF)
        delta = jnp.sum(d_o * o_ref[h], axis=1, keepdims=True) * inverse
        delta_out[h : h + 1] = jnp.transpose(delta)[:1]
    for store in stores:
        store.wait()
    net.drain()


def feed_forward(args, call_id):
    half = (TOK // 2, D)
    shape = jax.ShapeDtypeStruct
    every = (4, 2, 2, 144, HALF)
    lines = 4 * TOK
    anywhere = pl.BlockSpec(memory_space=pl.ANY)
    unit_rows = [pltpu.VMEM((lines, HID_PAD), BF)] * 5
    return pl.pallas_call(
        feed_kernel,
        out_shape=(
            shape((TOK, D), BF),
            shape((TOK, D), F32),
            shape((TOK, D), BF),
            shape((HEADS, TOK, HD), BF),
            shape((8, TOK), F32),
            shape((8, D), F32),
            shape(every, BF),
        ),
        in_specs=[IN_VMEM] * 9 + [anywhere] * 3,
        out_specs=[IN_VMEM] * 6 + [anywhere],
        scratch_shapes=[
            pltpu.VMEM((D, HID_PAD), BF),
            pltpu.VMEM((D, HID_PAD), BF),
            pltpu.VMEM((HID_PAD, D), BF),
            pltpu.VMEM((4, TOK, D), BF),
            pltpu.VMEM((4, TOK, D), BF),
            pltpu.VMEM((D, lines), BF),
            pltpu.VMEM((D, lines), BF),
            *unit_rows,
            pltpu.VMEM((4, TOK, D), BF),
            pltpu.VMEM((4, TOK, D), BF),
            pltpu.VMEM(every, BF),
            pltpu.VMEM(every, BF),
            pltpu.VMEM((TOK, D), F32),
            pltpu.VMEM((TOK, D), F32),
            pltpu.VMEM((TOK, D), F32),
            *RingScatter.room_shapes(half, half),
            *RingScatter.room_shapes(half, half),
            *sems(32),
            pltpu.SemaphoreType.DMA((7,)),
        ],
        compiler_params=params(call_id),
    )(*args)


class WeightSums:
    def __init__(self, place, net, sums, late, refs, marks):
        y_here, z_here, y1, z1, z2, y2, snd, rcv, *rooms = refs
        self.place, self.late, self.snd, self.rcv, self.marks = place, late, snd, rcv, marks
        self.y1, self.z1, self.y2, self.z2 = y1, z1, y2, z2
        self.x_hi, self.x_lo = lax.div(place.x, 2), lax.rem(place.x, 2)
        self.friends = []
        for k in range(1, 16):
            spot = lax.rem(self.x_hi * 8 + place.z * 2 + place.core + k, 16)
            x, z = lax.div(spot, 8) * 2 + self.x_lo, lax.rem(lax.div(spot, 2), 4)
            self.friends.append(place.device(x=x, z=z, core=lax.rem(spot, 2)))

        left, right = pl.ds(0, CUT), pl.ds(CUT, HALF - CUT)

        def y_spot(half):
            return stepped(place, "y", lambda j: sums.at[j, half, :, :, left])

        def z_spot(half):
            return stepped(
                place,
                "z",
                lambda j: sums.at[pl.ds(2 * half, 2), lax.div(j, 2), lax.rem(j, 2), :, right],
            )

        self.loads = []
        here = []
        for i, spot in enumerate((y_spot, z_spot)):
            for k, (half, by) in enumerate(((0, 1), (1, 3), (0, 0), (1, 0))):
                target = (y_here, z_here)[i].at[k]
                here.append(target)
                self.loads.append(
                    pltpu.make_async_copy(spot(half)(by), target, marks[2].at[8 + 4 * i + k])
                )
        self.y_first = RingScatter(
            net,
            place,
            "y",
            y_spot(0),
            y_spot(1),
            rooms[0:6],
            {1: here[0], 0: here[2]}.get,
            {3: here[1], 0: here[3]}.get,
        )
        self.z_first = RingScatter(
            net,
            place,
            "z",
            z_spot(0),
            z_spot(1),
            rooms[6:12],
            {1: here[4], 0: here[6]}.get,
            {3: here[5], 0: here[7]}.get,
        )

        def then_z(j):
            return y1.at[lax.div(j, 2), lax.rem(j, 2)]

        self.z_second = RingScatter(
            net,
            place,
            "z",
            stepped(place, "z", lambda j: then_z(j).at[:, pl.ds(0, 384)]),
            stepped(place, "z", lambda j: then_z(j).at[:, pl.ds(384, 384)]),
            rooms[12:18],
        )
        self.y_second = RingScatter(
            net,
            place,
            "y",
            stepped(place, "y", lambda j: z1.at[j, :, pl.ds(0, 384)]),
            stepped(place, "y", lambda j: z1.at[j, :, pl.ds(384, 256)]),
            rooms[18:24],
        )

    @staticmethod
    def scratch():
        rest = HALF - CUT
        return [
            pltpu.VMEM((4, 2, 144, CUT), BF),
            pltpu.VMEM((4, 2, 144, rest), BF),
            pltpu.VMEM((2, 2, 144, CUT), BF),
            pltpu.VMEM((4, 144, rest), BF),
            pltpu.VMEM((144, CUT), F32),
            pltpu.VMEM((144, rest), F32),
            pltpu.VMEM((8, 32, HALF + 128), BF),
            pltpu.VMEM((8, 32, HALF + 128), BF),
            *RingScatter.room_shapes((2, 144, CUT), (2, 144, CUT)),
            *RingScatter.room_shapes((2, 144, rest), (2, 144, rest)),
            *RingScatter.room_shapes((144, 384), (144, 384)),
            *RingScatter.room_shapes((144, 384), (144, 256)),
        ]

    def begin(self):
        for load in self.loads:
            load.start()
        for line in (self.y_first, self.z_first):
            line.start_far()
            line.start_near()

    def turn(self):
        for load in self.loads:
            load.wait()
        self.y_first.middle()
        self.z_first.middle()

    def next(self):
        self.y_first.finish(self.y1.at[0], self.y1.at[1])
        self.z_second.start_far()
        self.z_second.start_near()
        self.z_first.finish(self.z1.at[pl.ds(0, 2)], self.z1.at[pl.ds(2, 2)])
        self.y_second.start_far()
        self.y_second.start_near()

    def turn_again(self):
        self.z_second.middle()
        self.y_second.middle()

    def last(self):
        z2, y2 = self.z2, self.y2
        self.z_second.finish(z2.at[:, pl.ds(0, 384)], z2.at[:, pl.ds(384, 384)])
        self.y_second.finish(y2.at[:, pl.ds(0, 384)], y2.at[:, pl.ds(384, 256)])

    def send_home(self):
        snd = self.snd
        total = jnp.concatenate([self.z2[...], self.y2[...], self.late[...]], axis=1)
        blank = jnp.zeros((14, HALF + 128), F32)
        for k in range(8):
            snd[k] = jnp.concatenate([total[18 * k : 18 * k + 18], blank], axis=0).astype(BF)
        place = self.place
        send, recv, here = self.marks
        row_half = lax.div(place.z, 2)
        self.slot = self.x_hi * 4 + place.core * 2 + lax.rem(place.z, 2)
        self.own = place.z * 2 + place.core
        self.stays = row_half == self.x_hi
        for k in range(8):
            copy = pltpu.make_async_remote_copy(
                src_ref=snd.at[k],
                dst_ref=self.rcv.at[self.slot],
                send_sem=send.at[k],
                recv_sem=recv.at[self.slot],
                device_id=place.device(x=row_half * 2 + self.x_lo, z=k // 2, core=k % 2),
                device_id_type=MESH,
            )
            is_here = self.stays & (self.own == k)

            @pl.when(jnp.logical_not(is_here))
            def _(copy=copy):
                copy.start()

            @pl.when(is_here)
            def _(k=k):
                keep = pltpu.make_async_copy(snd.at[k], self.rcv.at[self.slot], here.at[0])
                keep.start()
                keep.wait()

    def arrive(self):
        send, recv, _ = self.marks
        for m in range(8):
            arrival = pltpu.make_async_remote_copy(
                src_ref=self.snd.at[m],
                dst_ref=self.rcv.at[m],
                send_sem=send.at[m],
                recv_sem=recv.at[m],
                device_id=self.place.partner(),
                device_id_type=MESH,
            )

            @pl.when(jnp.logical_not(self.stays & (self.slot == m)))
            def _(arrival=arrival):
                arrival.wait_recv()

            @pl.when(jnp.logical_not(self.stays & (self.own == m)))
            def _(arrival=arrival):
                arrival.wait_send()


def last_kernel(
    home_ref,
    w_ref,
    gains_ref,
    y_ref,
    dx_ref,
    y_out,
    dx_out,
    dwq_out,
    dwk_out,
    dwv_out,
    dwo_out,
    dwg_out,
    dwu_out,
    dwd_out,
    *gain_outs,
):
    y_out[...] = y_ref[...]
    dx_out[...] = dx_ref[...]

    def tile(x_hi, n):
        core, n = (n % 14) // 7, (n // 14) * 7 + n % 7
        c, n = n // 11, n % 11
        return home_ref[x_hi * 4 + core * 2 + c, :, 128 * n : 128 * n + 128].astype(F32)[:24]

    for which, out in enumerate((dwg_out, dwu_out, dwd_out)):
        for n in range(27):
            value = None
            for x_hi in range(2):
                if 0 <= n - 13 * x_hi < 14:
                    term = tile(x_hi, 14 * which + n - 13 * x_hi)
                    value = term if value is None else value + term
            span = slice(128 * n, 128 * n + 128)
            out[:, span] = value[:18]
    for k in range(4):
        span = slice(128 * k, 128 * k + 128)
        dwo_out[:, span] = home_ref[2 * k, :, HALF:].astype(F32)[:18]
        dwq_out[:, span] = home_ref[2 * k + 1, :, HALF:].astype(F32)[:18]
    for which in range(2):
        for j in range(4):
            out = (dwk_out, dwv_out)[j // 2]
            for y in range(4):
                rows = slice(576 * which + 144 * y, 576 * which + 144 * y + 144)
                out[rows, 128 * (j % 2) : 128 * (j % 2) + 128] = w_ref[which, j, y].astype(F32)
    for out, row, start in zip(gain_outs, (0, 4, 4, 1, 2, 3), (0, 0, HD, 0, 0, 0)):
        size = out.shape[0]
        out[...] = gains_ref[row : row + 1, start : start + size].reshape(size)


def last_layout(*args):
    shape = jax.ShapeDtypeStruct
    return pl.pallas_call(
        last_kernel,
        out_shape=(
            shape((TOK, D), BF),
            shape((TOK, D), BF),
            shape((18, 2 * HD), F32),
            shape((D, HD), F32),
            shape((D, HD), F32),
            shape((18, 2 * HD), F32),
            shape((18, 2 * HID), F32),
            shape((18, 2 * HID), F32),
            shape((18, 2 * HID), F32),
            *(shape((size,), F32) for size in (D, HD, HD, D, D, D)),
        ),
        in_specs=[IN_VMEM] * 5,
        out_specs=[IN_VMEM] * 15,
        compiler_params=pltpu.CompilerParams(vmem_limit_bytes=VMEM_BYTES),
    )(*args)


def angles(token_pos):
    middle = HD // 2
    frequency = THETA ** (-2.0 * jnp.arange(middle, dtype=F32) / HD)
    turned = token_pos.astype(F32)[:, None] * frequency[None, :]
    return (jnp.cos(turned), jnp.sin(turned))


def shards(
    layer_input,
    segment_ids,
    positions,
    w_query,
    w_key,
    w_value,
    w_out,
    w_gate,
    w_up,
    w_down,
    norm_attn,
    norm_query,
    norm_key,
    norm_post,
    norm_ffn,
    norm_out,
    cotangent,
):
    sp, tp = lax.axis_index("sp"), lax.axis_index("tp")
    cosine, sine = angles(lax.dynamic_slice_in_dim(positions, (sp * 2 + tp) * TOK, TOK))
    segments = segment_ids.reshape(128, 128)
    key_rows = jnp.asarray(KEY_TOKENS)
    kv_all, q_all, wq_other, wo_other, o_heads, inverse, q_pre, k_pre, h_attn = attention_forward(
        (
            layer_input,
            norm_attn,
            norm_query,
            norm_key,
            w_query,
            w_key,
            w_value,
            w_out,
            cosine,
            sine,
            segments,
            key_rows,
        ),
        2,
    )
    layer_output, d_mid, d_attn, d_heads, delta, d_gains, sums = feed_forward(
        (
            layer_input,
            o_heads,
            inverse,
            w_out,
            wo_other,
            norm_post,
            norm_ffn,
            norm_out,
            cotangent,
            w_gate,
            w_up,
            w_down,
        ),
        6,
    )
    d_input, home, w_both, gains = attention_backward(
        (kv_all, sums, w_query, wq_other, w_key, w_value),
        (
            q_all,
            d_heads,
            delta,
            key_rows,
            segments,
            q_pre,
            k_pre,
            cosine,
            sine,
            h_attn,
            d_attn,
            o_heads,
            layer_input,
            d_mid,
            norm_attn,
            norm_query,
            norm_key,
            d_gains,
        ),
        8,
    )
    y, dx, d_wq, d_wk, d_wv, d_wo, d_wg, d_wu, d_wd, *d_norms = last_layout(
        home, w_both, gains, layer_output, d_input
    )
    return (y, dx, d_wq, d_wk, d_wv, d_wo.T, d_wg, d_wu, d_wd.T, *d_norms)


def solution(mesh):
    rows = P(("sp", "tp"), None)
    in_specs = (
        rows,
        P(),
        P(),
        P(None, "tp"),
        P(),
        P(),
        P("tp", None),
        P(None, "tp"),
        P(None, "tp"),
        P("tp", None),
        P(),
        P(),
        P(),
        P(),
        P(),
        P(),
        rows,
    )
    out_specs = (
        rows,
        rows,
        P("sp", "tp"),
        P(),
        P(),
        P("tp", "sp"),
        P("sp", "tp"),
        P("sp", "tp"),
        P("tp", "sp"),
        P(),
        P(),
        P(),
        P(),
        P(),
        P(),
    )
    return jax.shard_map(shards, mesh=mesh, in_specs=in_specs, out_specs=out_specs, check_vma=False)
```

```python
import functools

import jax
import jax.numpy as jnp
import numpy as np
from jax import lax
from jax.experimental import pallas as pl
from jax.experimental.pallas import tpu as pltpu
from jax.sharding import PartitionSpec as P

EPS = 1e-06
THETA = 1000000.0
BF = jnp.bfloat16
F32 = jnp.float32
MESH = pl.DeviceIdType.MESH
IN_VMEM = pl.BlockSpec(memory_space=pltpu.VMEM)
VMEM_BYTES = 58 * 1024 * 1024

TOK = 128
D = 1152
HD = 256
HEADS = 4
ROWS = 2 * TOK
HID = 1728
HID_PAD = 1792
AHEAD, AHEAD_CUT = 512, 256
LATER, LATER_CUT = 896, 512
CUT = AHEAD_CUT + LATER_CUT
HALF = AHEAD + LATER
CHUNK = 256


class Place:
    def __init__(self):
        sp = lax.axis_index("sp")
        self.core = lax.rem(sp, 2)
        self.z = lax.rem(lax.div(sp, 2), 4)
        self.y = lax.div(sp, 16)
        self.x = lax.rem(lax.div(sp, 8), 2) * 2 + lax.axis_index("tp")

    def device(self, **moved):
        x, y, z, core = (moved.get(name, getattr(self, name)) for name in ("x", "y", "z", "core"))
        return (((y * 2 + lax.div(x, 2)) * 4 + z) * 2 + core, lax.rem(x, 2))

    def step(self, axis, by):
        return lax.rem(getattr(self, axis) + by, 4)

    def toward(self, axis, by):
        return self.device(**{axis: self.step(axis, by)})

    def partner(self):
        return self.device(core=1 - self.core)


class Net:
    def __init__(self, send, recv):
        self.send, self.recv, self.used, self.started = send, recv, 0, []

    def copy(self, source, target, device):
        at = self.used
        self.used += 1
        return pltpu.make_async_remote_copy(
            src_ref=source,
            dst_ref=target,
            send_sem=self.send.at[at],
            recv_sem=self.recv.at[at],
            device_id=device,
            device_id_type=MESH,
        )

    def go(self, copy):
        copy.start()
        self.started.append(copy)

    def settle(self, copy):
        copy.wait_send()
        self.started = [other for other in self.started if other is not copy]

    def drain(self):
        for copy in self.started:
            copy.wait_send()
        self.started = []


def greet(devices, meanwhile=None):
    barrier = pltpu.get_barrier_semaphore()
    for device in devices:
        pl.semaphore_signal(barrier, inc=1, device_id=device, device_id_type=MESH)
    if meanwhile is not None:
        meanwhile()
    pl.semaphore_wait(barrier, len(devices))


def ring(place, axis):
    return [place.toward(axis, 1), place.toward(axis, 3)]


class RingGather:
    def __init__(self, net, place, axis, view, lo, hi):
        self.net = net
        me, nxt, prev = getattr(place, axis), place.step(axis, 1), place.step(axis, 3)
        right, left = ring(place, axis)
        self.to_right = net.copy(view(me), view(me), right)
        self.to_left = net.copy(view(me), view(me), left)
        self.on_right = net.copy(lo(prev), lo(prev), right)
        self.on_left = net.copy(hi(nxt), hi(nxt), left)

    def start(self):
        self.net.go(self.to_right)
        self.net.go(self.to_left)

    def forward(self):
        self.to_right.wait_recv()
        self.net.go(self.on_right)
        self.to_left.wait_recv()
        self.net.go(self.on_left)

    def finish(self):
        self.on_right.wait_recv()
        self.on_left.wait_recv()


class Direct:
    def __init__(self, net, place, axis, source, landing):
        self.net = net
        self.copies = [
            net.copy(
                source(place.step(axis, by)), landing(getattr(place, axis)), place.toward(axis, by)
            )
            for by in (2, 1, 3)
        ]

    def start(self):
        for copy in self.copies:
            self.net.go(copy)

    def wait(self):
        for copy in self.copies:
            copy.wait_recv()


def by_rows(ref, act):
    *lead, rows, _ = ref.shape
    block = next(size for size in (64, 48, 32, 16) if rows % size == 0)
    for spot in np.ndindex(*lead):

        def one(i, carry, spot=spot):
            act(spot, pl.ds(pl.multiple_of(i * block, block), block))
            return carry

        lax.fori_loop(0, rows // block, one, 0)


def add_to(target, other):
    def act(spot, rows):
        at = (*spot, rows, slice(None))
        target[at] = (target[at].astype(F32) + other[at].astype(F32)).astype(target.dtype)

    by_rows(target, act)


def sum_to(target, others):
    def act(spot, rows):
        at = (*spot, rows, slice(None))
        total = others[0][at].astype(F32)
        for other in others[1:]:
            total = total + other[at].astype(F32)
        target[at] = total.astype(target.dtype)

    by_rows(target, act)


def stepped(place, axis, view):
    return lambda by: view(place.step(axis, by))


class RingScatter:
    def __init__(self, net, place, axis, lo, hi, room, lo_here=None, hi_here=None):
        self.net, self.lo, self.hi = net, lo_here or lo, hi_here or hi
        right, left = ring(place, axis)
        self.lo1, self.lo_l, self.lo_r, self.hi1, self.hi_l, self.hi_r = room
        self.a = net.copy(lo(2), self.lo1, right)
        self.b = net.copy(hi(2), self.hi1, left)
        self.c_hi = net.copy(hi(1), self.hi_l, right)
        self.d_lo = net.copy(lo(3), self.lo_r, left)
        self.c_lo = net.copy(self.lo1, self.lo_l, right)
        self.d_hi = net.copy(self.hi1, self.hi_r, left)

    def start_far(self):
        self.net.go(self.a)
        self.net.go(self.b)

    def start_right(self):
        self.net.go(self.c_hi)

    def start_left(self):
        self.net.go(self.d_lo)

    def start(self):
        self.start_far()
        self.start_right()
        self.start_left()

    def middle_right(self):
        self.a.wait_recv()
        add_to(self.lo1, self.lo(1))
        self.net.go(self.c_lo)

    def middle_left(self):
        self.b.wait_recv()
        add_to(self.hi1, self.hi(3))
        self.net.go(self.d_hi)

    def middle(self):
        self.middle_right()
        self.middle_left()

    def finish(self, lo_out, hi_out):
        self.c_hi.wait_recv()
        self.d_hi.wait_recv()
        sum_to(hi_out, [self.hi(0), self.hi_l, self.hi_r])
        self.d_lo.wait_recv()
        self.c_lo.wait_recv()
        sum_to(lo_out, [self.lo(0), self.lo_l, self.lo_r])

    @staticmethod
    def room_shapes(lo_shape, hi_shape):
        return [pltpu.VMEM(lo_shape, BF)] * 3 + [pltpu.VMEM(hi_shape, BF)] * 3


def params(call_id):
    return pltpu.CompilerParams(
        collective_id=call_id, has_side_effects=True, vmem_limit_bytes=VMEM_BYTES
    )


def sems(count):
    return [pltpu.SemaphoreType.DMA((count,)), pltpu.SemaphoreType.DMA((count,))]


class WeightSwap:
    def __init__(self, net, place, w_ref, other_ref):
        self.net = net
        quarter = w_ref.shape[0] // 4
        right, left = ring(place, "x")

        def rows(ref, side):
            return ref.at[pl.ds(pl.multiple_of((2 * side + place.core) * quarter, 16), quarter)]

        self.first = [
            net.copy(rows(w_ref, side), rows(other_ref, side), (left, right)[side])
            for side in (0, 1)
        ]
        self.trades = [
            net.copy(rows(other_ref, side), rows(other_ref, side), place.partner())
            for side in (0, 1)
        ]

    def start(self):
        for copy in self.first:
            self.net.go(copy)

    def forward(self):
        for copy, trade in zip(self.first, self.trades):
            copy.wait_recv()
            self.net.go(trade)

    def finish(self):
        for trade in self.trades:
            trade.wait_recv()


PARTS = (
    (0, 48, 0, ("x", "y", "z")),
    (48, 48, 768, ("z", "x", "y")),
    (96, 32, 1536, ("y", "z", "x")),
)


def part_views(place, buf, part):
    _, rows, base, (first, second, third) = part
    at1, at2, at3 = (getattr(place, axis) for axis in (first, second, third))

    def block(lead, start, size):
        return buf.at[lead, pl.ds(pl.multiple_of(base + start, 16), size)]

    return (
        (first, lambda j: block(at3, (at2 * 4 + j) * rows, rows)),
        (second, lambda j: block(at3, j * 4 * rows, 4 * rows)),
        (third, lambda j: block(j, 0, 16 * rows)),
    )


def halves(view):
    return (lambda j: view(j).at[:, pl.ds(0, HD)]), (lambda j: view(j).at[:, pl.ds(HD, HD)])


def chunk_rows(n):
    return [256 * n + 64 * i if n < 6 else 1536 + 128 * i + 64 * (n - 6) for i in range(4)]


def key_tokens():
    out = np.zeros((4, 2048), np.int32)
    for skip, rows, base, axes in PARTS:
        for j in range(4):
            for r in range(16 * rows):
                spot = {axes[2]: j, axes[1]: r // (4 * rows), axes[0]: (r // rows) % 4}
                x, y, z = spot["x"], spot["y"], spot["z"]
                token = ((y * 2 + x // 2) * 4 + z) * 512 + (x % 2) * 128 + skip + r % rows
                out[j, base + r] = token
    order = np.zeros((8, CHUNK), np.int64)
    for c in range(8):
        for i in range(4):
            start = chunk_rows(c)[i]
            order[c, 64 * i : 64 * i + 64] = np.arange(start, start + 64)
    return out[:, order]


KEY_TOKENS = key_tokens()


def set_lead(place, n, by):
    return place.step("zyx"[n // 3], by)


def read_sets(buf, key_ref, chunks, leads, key_leads):
    keys, values, tokens = [], [], []
    for n, lead, key_lead in zip(chunks, leads, key_leads):
        rows = chunk_rows(n)
        keys += [buf[lead, start : start + 64, :HD] for start in rows]
        values += [buf[lead, start : start + 64, HD:] for start in rows]
        tokens.append(key_ref[key_lead, n : n + 1])
    return (
        jnp.concatenate(keys, axis=0),
        jnp.concatenate(values, axis=0),
        jnp.concatenate(tokens, axis=1),
    )


def contract(left, right, left_dim, right_dim):
    return lax.dot_general(
        left, right, (((left_dim,), (right_dim,)), ((), ())), preferred_element_type=F32
    )


def turn(u, cosine, sine):
    half = HD // 2
    low, high = u[:, :half], u[:, half:]
    return jnp.concatenate([low * cosine - high * sine, high * cosine + low * sine], axis=1)


def row_bounds(place, segments):
    at = (place.y * 2 + lax.div(place.x, 2)) * 16 + place.z * 4 + lax.rem(place.x, 2)
    rows = jnp.concatenate([segments[pl.ds(at, 1)], segments[pl.ds(at + 2, 1)]], axis=1)
    every = segments[...]
    first = jnp.zeros((1, ROWS), jnp.int32)
    for k in range(1, 4):
        below = jnp.sum((every < k).astype(F32), axis=0, keepdims=True)
        below = jnp.sum(below, axis=1, keepdims=True).astype(jnp.int32)
        first = jnp.where(rows == k, below, first)
    lane = lax.broadcasted_iota(jnp.int32, (1, ROWS), 1)
    last = at * TOK + lane + jnp.where(lane < TOK, 0, TOK)
    return first, last


def down(row):
    return jnp.concatenate(
        [
            jnp.transpose(jnp.broadcast_to(row[:, 128 * i : 128 * i + 128], (128, 128)))
            for i in range(row.shape[1] // 128)
        ],
        axis=0,
    )


def across(ref):
    return ref[...].reshape(1, ref.shape[0])


def norm_scale(v):
    return lax.rsqrt(jnp.mean(v * v, axis=-1, keepdims=True) + EPS)


def norm_back(v, r, gain, e):
    eg = e * gain
    dv = r * eg - v * (r * r * r) * jnp.mean(eg * v, axis=-1, keepdims=True)
    return dv, jnp.sum(e * v * r, axis=0, keepdims=True)


def forward_kernel(
    x_ref,
    g_attn,
    g_query,
    g_key,
    wq_ref,
    wk_ref,
    wv_ref,
    w_ref,
    cos_ref,
    sin_ref,
    segments,
    key_ref,
    buf,
    q_all,
    wq_other,
    w_other,
    o_out,
    inv_out,
    q_pre,
    k_pre,
    h_out,
    o_sum,
    l_sum,
    o_got,
    l_got,
    send,
    recv,
):
    place, net = Place(), Net(send, recv)
    core = place.core
    partner = place.partner()
    mine = pl.ds(pl.multiple_of(core * TOK, TOK), TOK)
    theirs = pl.ds(pl.multiple_of((1 - core) * TOK, TOK), TOK)
    all_views = [part_views(place, buf, part) for part in PARTS]

    def keys_and_values():
        xf = x_ref[...].astype(F32)
        h = (xf * norm_scale(xf) * across(g_attn)).astype(BF)
        h_out[...] = h
        k = jnp.dot(h, wk_ref[...], preferred_element_type=F32)
        k_pre[...] = k
        k = turn(k * norm_scale(k) * across(g_key), cos_ref[...], sin_ref[...]).astype(BF)
        v = jnp.dot(h, wv_ref[...], preferred_element_type=F32).astype(BF)
        for (skip, rows, _, _), views in zip(PARTS, all_views):
            axis, view = views[0]
            own = view(getattr(place, axis))
            own[:, :HD] = k[skip : skip + rows]
            own[:, HD:] = v[skip : skip + rows]

    greet(
        ring(place, "x") + ring(place, "y") + ring(place, "z") + [partner],
        keys_and_values,
    )
    swap_wq = WeightSwap(net, place, wq_ref, wq_other)
    swap_w = WeightSwap(net, place, w_ref, w_other)
    stages = [
        [RingGather(net, place, axis, view, *halves(view)) for axis, view in views]
        for views in all_views
    ]
    for rings in stages:
        rings[0].start()
    swap_wq.start()

    def queries(which, w):
        q = jnp.dot(h_out[...], w[...], preferred_element_type=F32)
        for i in range(2):
            u = q[:, HD * i : HD * i + HD]
            q_pre[2 * which + i] = u
            u = turn(u * norm_scale(u) * across(g_query), cos_ref[...], sin_ref[...])
            q_all[2 * which + i, mine] = (u.astype(BF).astype(F32) * HD**-0.5).astype(BF)

    queries(0, wq_ref)
    for h in range(HEADS):
        o_sum[h] = jnp.zeros((ROWS, HD), F32)
        l_sum[h] = jnp.zeros((ROWS, 128), F32)
    for rings in stages:
        rings[0].forward()
    for rings in stages:
        rings[0].finish()
        rings[1].start()
    swap_wq.forward()
    first, last = (down(row) for row in row_bounds(place, segments))
    swap_wq.finish()
    queries(1, wq_other)
    swap_q = net.copy(q_all.at[:, mine], q_all.at[:, mine], partner)
    net.go(swap_q)
    for rings in stages:
        rings[1].forward()
    for rings in stages:
        rings[1].finish()
        rings[2].start()
    swap_w.start()
    swap_q.wait_recv()

    def attend(by):
        leads = [set_lead(place, n, by) for n in range(8)]
        keys, values, token = read_sets(buf, key_ref, range(8), leads, leads)
        token = token + core * 256
        allowed = jnp.concatenate(
            [
                (token[:, 128 * i : 128 * i + 128] <= last)
                & (token[:, 128 * i : 128 * i + 128] >= first)
                for i in range(16)
            ],
            axis=1,
        )
        for h in range(HEADS):
            weights = jnp.exp(contract(q_all[h], keys, 1, 1))
            weights = jnp.where(allowed, weights, 0.0)
            l_sum[h] += sum(weights[:, 128 * i : 128 * i + 128] for i in range(16))
            o_sum[h] += jnp.dot(weights.astype(BF), values, preferred_element_type=F32)

    attend(0)
    for rings in stages:
        rings[2].forward()
    swap_w.forward()
    lax.fori_loop(0, 2, lambda i, c: (attend(1 + 2 * i), c)[1], 0)
    for rings in stages:
        rings[2].finish()
    attend(2)
    swap_w.finish()
    swap_o = net.copy(o_sum.at[:, theirs], o_got, partner)
    swap_l = net.copy(l_sum.at[:, theirs], l_got, partner)
    net.go(swap_l)
    net.go(swap_o)
    swap_l.wait_recv()
    swap_o.wait_recv()
    for h in range(HEADS):
        total = jnp.sum(l_sum[h, mine] + l_got[h], axis=1, keepdims=True)
        inverse = 1.0 / total
        o_out[h] = (o_sum[h, mine] + o_got[h]) * inverse
        inv_out[h] = jnp.broadcast_to(inverse, (TOK, 128))
    net.drain()


def attention_forward(args, call_id):
    shape = jax.ShapeDtypeStruct
    return pl.pallas_call(
        forward_kernel,
        out_shape=(
            shape((4, 2048, 2 * HD), BF),
            shape((HEADS, ROWS, HD), BF),
            shape((D, 2 * HD), BF),
            shape((2 * HD, D), BF),
            shape((HEADS, TOK, HD), F32),
            shape((HEADS, TOK, 128), F32),
            shape((HEADS, TOK, HD), F32),
            shape((TOK, HD), F32),
            shape((TOK, D), BF),
        ),
        in_specs=[IN_VMEM] * len(args),
        out_specs=[IN_VMEM] * 9,
        scratch_shapes=[
            pltpu.VMEM((HEADS, ROWS, HD), F32),
            pltpu.VMEM((HEADS, ROWS, 128), F32),
            pltpu.VMEM((HEADS, TOK, HD), F32),
            pltpu.VMEM((HEADS, TOK, 128), F32),
            *sems(52),
        ],
        compiler_params=params(call_id),
    )(*args)


GRAD_SLOT = {2: 0, 0: 0, 1: 1, 3: 2}


def kept_head(place, j):
    return jnp.where(lax.rem(j, 2) == lax.rem(place.x, 2), 0, 2) + lax.div(j, 2)


def turn_back(e, cosine, sine):
    half = HD // 2
    low, high = e[:, :half], e[:, half:]
    return jnp.concatenate([low * cosine + high * sine, high * cosine - low * sine], axis=1)


def backward_kernel(
    kv_hbm,
    sums_hbm,
    ahead_y,
    ahead_z,
    wq_hbm,
    wq2_hbm,
    wk_hbm,
    wv_hbm,
    q_all,
    do_ref,
    delta_ref,
    key_ref,
    segments,
    q_pre,
    k_pre,
    cos_ref,
    sin_ref,
    h_ref,
    da_ref,
    o_ref,
    x_ref,
    dmid_ref,
    g_attn,
    g_query,
    g_key,
    gains_ref,
    dx_out,
    home_out,
    w_both,
    gains_out,
    buf,
    wk,
    wv,
    do_all,
    delta_all,
    grads,
    dq_sum,
    dq_got,
    dkv,
    h_line,
    da_line,
    o_line,
    dq_line,
    dq_own,
    o_own,
    late_all,
    late_got,
    late_y,
    late_z,
    gain_got,
    kv_own,
    kv_line,
    w_all,
    w_got,
    w_y,
    w_z,
    w_line,
    dh,
    *rest,
):
    rooms, late_rooms, rest = rest[:54], rest[54:66], rest[66:]
    *weight_refs, send, recv, send2, recv2, here = rest
    place, net = Place(), Net(send, recv)
    core, partner = place.core, place.partner()
    w_loads = [
        pltpu.make_async_copy(source, target, here.at[1 + i])
        for i, (source, target) in enumerate(
            (
                (wq_hbm, buf.at[0, pl.ds(0, D)]),
                (wq2_hbm, buf.at[1, pl.ds(0, D)]),
                (wk_hbm, wk),
                (wv_hbm, wv),
            )
        )
    ]
    for load in w_loads[2:]:
        load.start()

    def set_loads(by, slot):
        copies = []
        for i, (_, rows, base, axes) in enumerate(PARTS):
            span = pl.ds(base, 16 * rows)
            source = kv_hbm.at[place.step(axes[2], by), span]
            copies.append(
                pltpu.make_async_copy(source, buf.at[slot, span], here.at[16 + 3 * slot + i])
            )
        return copies

    sets = [set_loads(by, slot) for by, slot in ((2, 0), (1, 1), (3, 0), (0, 1))]
    for copy in sets[0] + sets[1]:
        copy.start()
    weights = WeightSums(place, net, sums_hbm, late_z, weight_refs, (send2, recv2, here))
    y1, z1 = weights.y1, weights.z1
    ahead_loads = [
        pltpu.make_async_copy(ahead_y, y1.at[:, :, :, pl.ds(0, AHEAD_CUT)], here.at[6]),
        pltpu.make_async_copy(ahead_z, z1.at[:, :, pl.ds(0, AHEAD - AHEAD_CUT)], here.at[7]),
    ]
    for load in ahead_loads:
        load.start()
    greet(weights.friends + ring(place, "x") + ring(place, "y"))
    mine = pl.ds(pl.multiple_of(core * TOK, TOK), TOK)
    theirs = pl.ds(pl.multiple_of((1 - core) * TOK, TOK), TOK)
    do_all[:, mine] = do_ref[...]
    delta_all[core] = delta_ref[...]
    swap_do = net.copy(do_all.at[:, mine], do_all.at[:, mine], partner)
    swap_delta = net.copy(delta_all.at[core], delta_all.at[core], partner)
    net.go(swap_do)
    net.go(swap_delta)

    half = TOK // 2

    def line_of(rows):
        return RingGather(
            net,
            place,
            "x",
            lambda j: rows.at[j],
            lambda j: rows.at[j, pl.ds(0, half)],
            lambda j: rows.at[j, pl.ds(half, half)],
        )

    def head_of(j):
        return kept_head(place, j)

    h_line[place.x] = h_ref[...]
    da_line[place.x] = da_ref[...]
    for h in range(HEADS):
        o_own[h] = o_ref[h].astype(BF)
    o_line[place.x] = o_own[head_of(place.x)]
    line_h, line_da = line_of(h_line), line_of(da_line)
    o_swap = Direct(net, place, "x", lambda j: o_own.at[head_of(j)], lambda j: o_line.at[j])
    dq_swap = Direct(net, place, "x", lambda j: dq_own.at[head_of(j)], lambda j: dq_line.at[j])
    line_da.start()
    o_swap.start()
    for h in range(HEADS):
        dq_sum[h] = jnp.zeros((HD, ROWS), F32)
    stages = []
    for i, part in enumerate(PARTS):
        _, rows, base, (first, second, third) = part
        at1, at2 = getattr(place, first), getattr(place, second)

        def block(slot, start, size, base=base):
            return grads.at[slot, pl.ds(pl.multiple_of(base + start, 16), size)]

        views = (
            lambda by, block=block, first=first, at2=at2, rows=rows: block(
                0, (at2 * 4 + place.step(first, by)) * rows, rows
            ),
            lambda by, block=block, second=second, rows=rows: block(
                0, place.step(second, by) * 4 * rows, 4 * rows
            ),
            lambda by, block=block, rows=rows: block(GRAD_SLOT[by], 0, 16 * rows),
        )
        rings = []
        for level, axis in enumerate((first, second, third)):
            spot = 6 * (3 * i + level)
            rings.append(
                RingScatter(net, place, axis, *halves(views[level]), rooms[spot : spot + 6])
            )
        stages.append((rings, views))
    late_first = RingScatter(
        net,
        place,
        "y",
        stepped(place, "y", lambda j: late_got.at[j, 0]),
        stepped(place, "y", lambda j: late_got.at[j, 1]),
        late_rooms[:6],
    )

    def late_spot(j):
        return late_y.at[lax.div(j, 2), lax.rem(j, 2)]

    late_second = RingScatter(
        net,
        place,
        "z",
        stepped(place, "z", lambda j: late_spot(j).at[pl.ds(0, 80)]),
        stepped(place, "z", lambda j: late_spot(j).at[pl.ds(80, 64)]),
        late_rooms[6:],
    )

    def late_term(c, rows, columns):
        term = contract(rows[...].reshape(4 * TOK, D), columns[...].reshape(4 * TOK, HD), 0, 0)
        term = term.astype(BF)
        for k in range(8):
            for which in range(2):
                late_all[which, k // 2, k % 2, c] = term[
                    144 * k : 144 * k + 144, 128 * which : 128 * which + 128
                ]

    weights.first.begin()
    weights.first.go_on()
    swap_do.wait_recv()
    swap_delta.wait_recv()

    first, last = row_bounds(place, segments)

    def differ(chunks, by, slot):
        key_leads = [set_lead(place, n, by) for n in chunks]
        keys, values, token = read_sets(buf, key_ref, chunks, [slot] * len(chunks), key_leads)
        token = down(token + core * 256)
        token = jnp.concatenate([token, token], axis=1)
        allowed = (token <= last) & (token >= first)
        d_keys = d_values = None
        for h in range(HEADS):
            probs = jnp.exp(contract(keys, q_all[h], 1, 1))
            probs = jnp.where(allowed, probs, 0.0)
            delta = jnp.concatenate([delta_all[0, h : h + 1], delta_all[1, h : h + 1]], axis=1)
            d_scores = (probs * (contract(values, do_all[h], 1, 1) - delta)).astype(BF)
            value_term = jnp.dot(probs.astype(BF), do_all[h], preferred_element_type=F32)
            key_term = jnp.dot(d_scores, q_all[h], preferred_element_type=F32)
            d_values = value_term if h == 0 else d_values + value_term
            d_keys = key_term if h == 0 else d_keys + key_term
            dq_sum[h] += contract(keys, d_scores, 0, 0)
        d_keys, d_values = d_keys.astype(BF), d_values.astype(BF)
        for m, n in enumerate(chunks):
            for i, start in enumerate(chunk_rows(n)):
                spot = 256 * m + 64 * i
                grads[GRAD_SLOT[by], start : start + 64, :HD] = d_keys[spot : spot + 64]
                grads[GRAD_SLOT[by], start : start + 64, HD:] = d_values[spot : spot + 64]

    def visit(step, after):
        by, slot = ((2, 0), (1, 1), (3, 0), (0, 1))[step]
        for copy in sets[step]:
            copy.wait()
        for chunks in ((0, 1, 2), (3, 4, 5), (6, 7)):
            differ(chunks, by, slot)
        for copy in after:
            copy.start()

    visit(0, sets[2])
    for rings, _ in stages:
        rings[2].start_far()
    visit(1, sets[3])
    for rings, _ in stages:
        rings[2].start_right()
    for rings, _ in stages:
        rings[2].middle_right()
    weights.first.turn()
    line_da.forward()
    line_h.start()
    visit(2, w_loads[0:1])
    for rings, _ in stages:
        rings[2].start_left()
    for rings, _ in stages:
        rings[2].middle_left()
    for rings, _ in stages:
        net.settle(rings[2].a)
        net.settle(rings[2].b)
    visit(3, w_loads[1:2])
    swap_dq = net.copy(dq_sum.at[:, :, theirs], dq_got, partner)
    net.go(swap_dq)
    line_h.forward()
    line_da.finish()
    o_swap.wait()
    late_term(0, da_line, o_line)
    for load in w_loads:
        load.wait()

    swap_dq.wait_recv()
    d_query = jnp.zeros((1, HD), F32)
    for h in range(HEADS):
        e = jnp.transpose(dq_sum[h, :, mine] + dq_got[h]) * HD**-0.5
        e = turn_back(e.astype(BF).astype(F32), cos_ref[...], sin_ref[...])
        u = q_pre[h]
        du, gain = norm_back(u, norm_scale(u), across(g_query), e)
        d_query = d_query + gain
        dq_own[h] = du.astype(BF)
    dq_line[place.x] = dq_own[head_of(place.x)]
    dq_swap.start()
    for load in ahead_loads:
        load.wait()
    weights.next()

    def finish_keys(level):
        for (rings, views), (skip, rows, _, _) in zip(stages, PARTS):
            lo, hi = halves(views[level])
            if level:
                rings[level].finish(lo(0), hi(0))
                rings[level - 1].start()
            else:
                out = dkv.at[pl.ds(skip, rows)]
                rings[level].finish(out.at[:, pl.ds(0, HD)], out.at[:, pl.ds(HD, HD)])

    finish_keys(2)
    d_h = sum(
        contract(dq_own[h], buf[h // 2, :D, 256 * (h % 2) : 256 * (h % 2) + 256], 1, 1)
        for h in range(HEADS)
    )
    dh[...] = d_h
    line_h.finish()
    dq_swap.wait()
    late_term(1, h_line, dq_line)
    late_swap = net.copy(late_all.at[1 - core], late_got, partner)
    net.go(late_swap)
    for rings, _ in stages:
        rings[1].middle()
    late_swap.wait_recv()
    for y in range(4):
        add_to(late_got.at[y], late_all.at[core, y])
    late_first.start()
    finish_keys(1)
    weights.turn_again()
    for rings, _ in stages:
        rings[0].middle()
    late_first.middle()
    finish_keys(0)

    e = turn_back(dkv[:, :HD].astype(BF).astype(F32), cos_ref[...], sin_ref[...])
    u = k_pre[...]
    dk, d_key = norm_back(u, norm_scale(u), across(g_key), e)
    dk, dv = dk.astype(BF), dkv[:, HD:].astype(BF)
    for i in range(2):
        kv_own[i] = dk[:, 128 * i : 128 * i + 128]
        kv_own[2 + i] = dv[:, 128 * i : 128 * i + 128]
    kv_line[place.x] = kv_own[place.x]
    kv_swap = Direct(net, place, "x", lambda j: kv_own.at[j], lambda j: kv_line.at[j])
    kv_swap.start()
    d_h = dh[...] + contract(dk, wk[...], 1, 1) + contract(dv, wv[...], 1, 1)
    xf = x_ref[...].astype(F32)
    dx, d_attn = norm_back(xf, norm_scale(xf), across(g_attn), d_h)
    dx_out[...] = (dmid_ref[...] + dx).astype(BF)
    late_first.finish(late_y.at[0], late_y.at[1])
    late_second.start()

    def gain_swap(level, axis):
        return Direct(
            net, place, axis, lambda j: gain_got.at[level, at(axis)], lambda j: gain_got.at[level, j]
        )

    def at(axis):
        return getattr(place, axis)

    def gain_sum(level):
        return (gain_got[level, 0] + gain_got[level, 1]) + (gain_got[level, 2] + gain_got[level, 3])

    swaps = [gain_swap(0, "x"), gain_swap(1, "y"), gain_swap(2, "z")]
    norms = jnp.concatenate([d_query, d_key, jnp.zeros((1, D - 2 * HD), F32)], axis=1)
    gain_got[0, place.x] = jnp.concatenate(
        [d_attn, gains_ref[0:3], norms, jnp.zeros((3, D), F32)], axis=0
    )
    swaps[0].start()
    kv_swap.wait()
    term = contract(h_line[...].reshape(4 * TOK, D), kv_line[...].reshape(4 * TOK, 128), 0, 0)
    term = term.astype(BF)
    for k in range(8):
        w_all[k // 4, k % 4] = term[144 * k : 144 * k + 144]
    w_swap = net.copy(w_all.at[1 - core], w_got, partner)
    net.go(w_swap)
    late_second.middle()
    swaps[0].wait()
    gain_got[1, place.y] = gain_sum(0)
    swaps[1].start()
    w_swap.wait_recv()
    add_to(w_got, w_all.at[core])
    w_scatter = Direct(net, place, "y", lambda j: w_got.at[j], lambda j: w_y.at[j])
    w_scatter.start()
    w_y[place.y] = w_got[place.y]
    weights.last()
    late_second.finish(late_z.at[pl.ds(0, 80)], late_z.at[pl.ds(80, 64)])
    weights.send_home()
    swaps[1].wait()
    gain_got[2, place.z] = gain_sum(1)
    swaps[2].start()
    w_scatter.wait()
    sum_to(w_z.at[place.z], [w_y.at[j] for j in range(4)])
    w_sums = Direct(net, place, "z", lambda j: w_z.at[place.z], lambda j: w_z.at[j])
    w_sums.start()
    swaps[2].wait()
    gain_got[3, core] = gain_sum(2)
    gain_last = net.copy(gain_got.at[3, core], gain_got.at[3, core], partner)
    net.go(gain_last)
    w_sums.wait()
    sum_to(w_line.at[place.x, place.y], [w_z.at[j] for j in range(4)])
    y_back = Direct(
        net, place, "y", lambda j: w_line.at[place.x, place.y], lambda j: w_line.at[place.x, j]
    )
    y_back.start()
    weights.arrive()
    home_out[...] = weights.rcv[...]
    y_back.wait()
    x_back = Direct(net, place, "x", lambda j: w_line.at[place.x], lambda j: w_line.at[j])
    x_back.start()
    gain_last.wait_recv()
    gains_out[...] = gain_got[3, 0] + gain_got[3, 1]
    x_back.wait()
    w_both[core] = w_line[...]
    w_last = net.copy(w_line, w_both.at[core], partner)
    net.go(w_last)
    w_last.wait_recv()
    net.drain()


def attention_backward(hbm, small, call_id):
    shape = jax.ShapeDtypeStruct
    rooms = []
    for _, rows, _, _ in PARTS:
        for blocks in (1, 4, 16):
            rooms += RingScatter.room_shapes((blocks * rows, HD), (blocks * rows, HD))
    late_rooms = [
        *RingScatter.room_shapes((2, 144, 128), (2, 144, 128)),
        *RingScatter.room_shapes((80, 128), (64, 128)),
    ]
    return pl.pallas_call(
        backward_kernel,
        out_shape=(
            shape((TOK, D), BF),
            shape((8, 16, HALF + 384), BF),
            shape((2, 4, 4, 144, 128), BF),
            shape((8, D), F32),
        ),
        in_specs=[pl.BlockSpec(memory_space=pl.ANY)] * len(hbm) + [IN_VMEM] * len(small),
        out_specs=[IN_VMEM] * 4,
        scratch_shapes=[
            pltpu.VMEM((2, 2048, 2 * HD), BF),
            pltpu.VMEM((D, HD), BF),
            pltpu.VMEM((D, HD), BF),
            pltpu.VMEM((HEADS, ROWS, HD), BF),
            pltpu.VMEM((2, 8, TOK), F32),
            pltpu.VMEM((3, 2048, 2 * HD), BF),
            pltpu.VMEM((HEADS, HD, ROWS), F32),
            pltpu.VMEM((HEADS, HD, TOK), F32),
            pltpu.VMEM((TOK, 2 * HD), F32),
            pltpu.VMEM((4, TOK, D), BF),
            pltpu.VMEM((4, TOK, D), BF),
            pltpu.VMEM((4, TOK, HD), BF),
            pltpu.VMEM((4, TOK, HD), BF),
            pltpu.VMEM((4, TOK, HD), BF),
            pltpu.VMEM((4, TOK, HD), BF),
            pltpu.VMEM((2, 4, 2, 2, 144, 128), BF),
            pltpu.VMEM((4, 2, 2, 144, 128), BF),
            pltpu.VMEM((2, 2, 144, 128), BF),
            pltpu.VMEM((144, 128), F32),
            pltpu.VMEM((4, 4, 8, D), F32),
            pltpu.VMEM((4, TOK, 128), BF),
            pltpu.VMEM((4, TOK, 128), BF),
            pltpu.VMEM((2, 4, 144, 128), BF),
            pltpu.VMEM((4, 144, 128), BF),
            pltpu.VMEM((4, 144, 128), BF),
            pltpu.VMEM((4, 144, 128), BF),
            pltpu.VMEM((4, 4, 144, 128), BF),
            pltpu.VMEM((TOK, D), F32),
            *rooms,
            *late_rooms,
            *WeightSums.scratch(),
            *sems(160),
            *sems(8),
            pltpu.SemaphoreType.DMA((24,)),
        ],
        compiler_params=params(call_id),
    )(*hbm, *small)


def feed_kernel(
    x_ref,
    o_ref,
    inv_ref,
    wo_ref,
    wo2_ref,
    post_ref,
    ffn_ref,
    out_gain_ref,
    cot_ref,
    wg_hbm,
    wu_hbm,
    wd_hbm,
    out_ref,
    dmid_out,
    dattn_out,
    do_out,
    delta_out,
    dgains_out,
    ahead_y,
    ahead_z,
    sums_hbm,
    wg,
    wu,
    wd,
    h_line,
    f_line,
    h_turned,
    f_turned,
    gelu_kept,
    slope_kept,
    act,
    d_gate,
    d_up,
    f_terms,
    h_terms,
    ahead_snd,
    ahead_got,
    snd,
    got,
    attn,
    mid,
    ffn,
    *rest,
):
    *room, send, recv, local = rest
    place, net = Place(), Net(send, recv)
    core, partner = place.core, place.partner()
    x_hi = lax.div(place.x, 2)
    first_unit = pl.multiple_of(x_hi * (2 * HID - HID_PAD), 128)
    window = pl.ds(first_unit, HID_PAD)
    loads = [
        pltpu.make_async_copy(source, target, local.at[i])
        for i, (source, target) in enumerate(
            ((wg_hbm.at[:, window], wg), (wu_hbm.at[:, window], wu), (wd_hbm.at[window], wd))
        )
    ]
    for load in loads:
        load.start()
    greet(ring(place, "x") + ring(place, "y") + ring(place, "z") + [partner])
    half, quarter = TOK // 2, TOK // 4
    top, bottom = pl.ds(0, quarter), pl.ds(quarter, quarter)
    g_post, g_ffn, g_out = (across(ref) for ref in (post_ref, ffn_ref, out_gain_ref))

    def rows_of(part):
        return slice(half * part, half * part + half)

    def lines_of(part):
        return slice(4 * half * part, 4 * half * part + 4 * half)

    def gather(lines):
        return RingGather(
            net,
            place,
            "x",
            lambda j: lines.at[j],
            lambda j: lines.at[j, top],
            lambda j: lines.at[j, bottom],
        )

    def scatter(terms, room):
        return RingScatter(
            net,
            place,
            "x",
            stepped(place, "x", lambda j: terms.at[j, top]),
            stepped(place, "x", lambda j: terms.at[j, bottom]),
            room,
        )

    def summed(line, part):
        at = half * part
        line.finish(ffn.at[pl.ds(at, quarter)], ffn.at[pl.ds(at + quarter, quarter)])

    o_cat = [o_ref[h].astype(BF) for h in range(HEADS)]
    a = jnp.dot(jnp.concatenate(o_cat[:2], axis=1), wo_ref[...], preferred_element_type=F32)
    a += jnp.dot(jnp.concatenate(o_cat[2:], axis=1), wo2_ref[...], preferred_element_type=F32)
    attn[...] = a
    mid[...] = x_ref[...].astype(F32) + a * norm_scale(a) * g_post
    m = mid[...]
    h = (m * norm_scale(m) * g_ffn).astype(BF)
    for part in range(2):
        h_line[part, place.x] = h[rows_of(part)]
    h_gathers = [gather(h_line.at[part]) for part in range(2)]
    f_gathers = [gather(f_line.at[part]) for part in range(2)]
    f_sums = [scatter(f_terms.at[part], room[6 * part : 6 * part + 6]) for part in range(2)]
    h_sums = [
        scatter(h_terms.at[part], room[12 + 6 * part : 18 + 6 * part]) for part in range(2)
    ]
    h_gathers[0].start()

    for load in loads:
        load.wait()
    low_unit, high_unit = jnp.where(x_hi == 0, 0, 64), jnp.where(x_hi == 0, HID, HID_PAD)

    def units(n):
        return pl.ds(pl.multiple_of(n * 256, 256), 256)

    def forward(part, n, carry):
        h = h_line[part].reshape(4 * half, D)
        gate = jnp.dot(h, wg[:, units(n)], preferred_element_type=F32)
        up = jnp.dot(h, wu[:, units(n)], preferred_element_type=F32)
        unit = n * 256 + lax.broadcasted_iota(jnp.int32, (1, 256), 1)
        own = jnp.where((unit >= low_unit) & (unit < high_unit), 1.0, 0.0)
        scale, cube = 0.7978845608028654, 0.044715
        square = gate * gate
        bent = jnp.tanh(scale * gate * (1.0 + cube * square))
        lifted = 0.5 * (1.0 + bent)
        gelu = gate * lifted * own
        slope = lifted + 0.5 * gate * (1.0 - bent * bent) * scale * (1.0 + 3.0 * cube * square)
        act[lines_of(part), units(n)] = (gelu * up).astype(BF)
        gelu_kept[lines_of(part), units(n)] = gelu.astype(BF)
        slope_kept[lines_of(part), units(n)] = (slope * up * own).astype(BF)
        return carry

    def columns(n):
        return pl.ds(pl.multiple_of(n * 384, 128), 384)

    def project(part, n, carry):
        term = jnp.dot(act[lines_of(part)], wd[:, columns(n)], preferred_element_type=F32)
        f_terms[part, :, :, columns(n)] = term.astype(BF).reshape(4, half, 384)
        return carry

    def backward(part, n, carry):
        d_act = contract(f_line[part].reshape(4 * half, D), wd[units(n)], 1, 1)
        rows = lines_of(part)
        d_gate[rows, units(n)] = (d_act * slope_kept[rows, units(n)].astype(F32)).astype(BF)
        d_up[rows, units(n)] = (d_act * gelu_kept[rows, units(n)].astype(F32)).astype(BF)
        return carry

    def back_project(part, n, carry):
        rows = lines_of(part)
        term = contract(d_gate[rows], wg[columns(n)], 1, 1)
        term += contract(d_up[rows], wu[columns(n)], 1, 1)
        h_terms[part, :, :, columns(n)] = term.astype(BF).reshape(4, half, 384)
        return carry

    def each(times, step, part):
        lax.fori_loop(0, times, functools.partial(step, part), 0)

    blocks = HID_PAD // 256

    def turn_round(part):
        rows = rows_of(part)
        summed(f_sums[part], part)
        f = ffn[rows]
        r = norm_scale(f)
        out_ref[rows] = (mid[rows] + f * r * g_out).astype(BF)
        df, gain = norm_back(f, r, g_out, cot_ref[rows].astype(F32))
        f_line[part, place.x] = df.astype(BF)
        f_gathers[part].start()
        return gain

    h_gathers[0].forward()
    h_gathers[1].start()
    h_gathers[0].finish()
    each(blocks, forward, 0)
    h_gathers[1].forward()
    each(3, project, 0)
    f_sums[0].start()
    h_gathers[1].finish()
    each(blocks, forward, 1)
    f_sums[0].middle()
    each(3, project, 1)
    f_sums[1].start()
    d_out = turn_round(0)
    f_sums[1].middle()
    h_turned[...] = jnp.transpose(h_line[...].reshape(8 * half, D))
    f_gathers[0].forward()
    d_out = d_out + turn_round(1)
    f_gathers[0].finish()
    each(blocks, backward, 0)
    f_gathers[1].forward()
    each(3, back_project, 0)
    h_sums[0].start()
    f_gathers[1].finish()
    f_turned[...] = jnp.transpose(f_line[...].reshape(8 * half, D))

    def halves_of(which):
        return pl.ds(pl.multiple_of(which * 896, 128), 896)

    def fill(target, i, which, left, right, c, add):
        term = jnp.dot(
            left[576 * i : 576 * i + 576], right[:, halves_of(which)], preferred_element_type=F32
        )
        spans = ((c, 0, 896),) if c is not None else ((0, 0, AHEAD), (1, AHEAD, 896))
        for k in range(4):
            for half, low, high in spans:
                at = (2 * i + k // 2, k % 2, half, slice(None), slice(0, high - low))
                value = term[144 * k : 144 * k + 144, low:high]
                if add:
                    value = value + target[at].astype(F32)
                target[at] = value.astype(BF)

    def fill_later(target, i, which, add):
        fill(target, i, which, h_turned, d_gate, 0, add)
        fill(target, i, which, h_turned, d_up, 1, add)

    for y in range(4):
        ahead_snd[y, :, 1, :, 896 - AHEAD :] = jnp.zeros((2, 144, 2 * AHEAD - 896), BF)
    ahead_swap = net.copy(ahead_snd, ahead_got, partner)
    swaps = [net.copy(snd.at[y], got.at[y], partner) for y in range(4)]
    ahead = FirstSums(net, place, ahead_got, AHEAD_CUT, room[24:])
    for i in range(2):
        fill(ahead_snd, i, 1 - core, f_turned, act, None, False)
    net.go(ahead_swap)
    each(blocks, backward, 1)
    h_sums[0].middle()
    each(3, back_project, 1)
    h_sums[1].start()
    ahead_swap.wait_recv()
    for i in range(2):
        fill(ahead_got, i, core, f_turned, act, None, True)
    ahead.begin()
    ahead.go_on()
    for i in range(2):
        fill_later(snd, i, 1 - core, False)
        net.go(swaps[2 * i])
        net.go(swaps[2 * i + 1])
    summed(h_sums[0], 0)
    h_sums[1].middle()
    stores = [pltpu.make_async_copy(got.at[y], sums_hbm.at[y], local.at[3 + y]) for y in range(4)]
    for i in range(2):
        swaps[2 * i].wait_recv()
        swaps[2 * i + 1].wait_recv()
        fill_later(got, i, core, True)
        stores[2 * i].start()
        stores[2 * i + 1].start()
    ahead.turn()
    summed(h_sums[1], 1)

    m, a = mid[...], attn[...]
    dm, d_ffn = norm_back(m, norm_scale(m), g_ffn, ffn[...])
    d_mid = cot_ref[...].astype(F32) + dm
    dmid_out[...] = d_mid
    da, d_post = norm_back(a, norm_scale(a), g_post, d_mid)
    da = da.astype(BF)
    dattn_out[...] = da
    dgains_out[...] = jnp.concatenate([d_post, d_ffn, d_out, jnp.zeros((5, D), F32)], axis=0)
    delta_out[...] = jnp.zeros((8, TOK), F32)
    for h in range(HEADS):
        weight = (wo_ref, wo2_ref)[h // 2]
        d_o = contract(da, weight[256 * (h % 2) : 256 * (h % 2) + 256], 1, 1).astype(BF).astype(F32)
        inverse = inv_ref[h]
        do_out[h] = (d_o * jnp.concatenate([inverse, inverse], axis=1)).astype(BF)
        delta = jnp.sum(d_o * o_ref[h], axis=1, keepdims=True) * inverse
        delta_out[h : h + 1] = jnp.transpose(delta)[:1]
    y_line, z_line = ahead.lines
    y_line.finish(ahead_y.at[0], ahead_y.at[1])
    z_line.finish(ahead_z.at[pl.ds(0, 2)], ahead_z.at[pl.ds(2, 2)])
    for store in stores:
        store.wait()
    net.drain()


def feed_forward(args, call_id):
    quarter = (TOK // 4, D)
    shape = jax.ShapeDtypeStruct
    every = (4, 2, 2, 144, LATER)
    every_ahead = (4, 2, 2, 144, AHEAD)
    lines = 4 * TOK
    anywhere = pl.BlockSpec(memory_space=pl.ANY)
    unit_rows = [pltpu.VMEM((lines, HID_PAD), BF)] * 5
    return pl.pallas_call(
        feed_kernel,
        out_shape=(
            shape((TOK, D), BF),
            shape((TOK, D), F32),
            shape((TOK, D), BF),
            shape((HEADS, TOK, HD), BF),
            shape((8, TOK), F32),
            shape((8, D), F32),
            shape((2, 2, 144, AHEAD_CUT), BF),
            shape((4, 144, AHEAD - AHEAD_CUT), BF),
            shape(every, BF),
        ),
        in_specs=[IN_VMEM] * 9 + [anywhere] * 3,
        out_specs=[IN_VMEM] * 8 + [anywhere],
        scratch_shapes=[
            pltpu.VMEM((D, HID_PAD), BF),
            pltpu.VMEM((D, HID_PAD), BF),
            pltpu.VMEM((HID_PAD, D), BF),
            pltpu.VMEM((2, 4, TOK // 2, D), BF),
            pltpu.VMEM((2, 4, TOK // 2, D), BF),
            pltpu.VMEM((D, lines), BF),
            pltpu.VMEM((D, lines), BF),
            *unit_rows,
            pltpu.VMEM((2, 4, TOK // 2, D), BF),
            pltpu.VMEM((2, 4, TOK // 2, D), BF),
            pltpu.VMEM(every_ahead, BF),
            pltpu.VMEM(every_ahead, BF),
            pltpu.VMEM(every, BF),
            pltpu.VMEM(every, BF),
            pltpu.VMEM((TOK, D), F32),
            pltpu.VMEM((TOK, D), F32),
            pltpu.VMEM((TOK, D), F32),
            *(RingScatter.room_shapes(quarter, quarter) * 4),
            *FirstSums.room_shapes(AHEAD_CUT, AHEAD - AHEAD_CUT),
            *sems(72),
            pltpu.SemaphoreType.DMA((7,)),
        ],
        compiler_params=params(call_id),
    )(*args)


class FirstSums:
    def __init__(self, net, place, sums, cut, rooms, here=None, marks=None):
        left, right = pl.ds(0, cut), pl.ds(cut, sums.shape[-1] - cut)

        def y_spot(half):
            return stepped(place, "y", lambda j: sums.at[j, half, :, :, left])

        def z_spot(half):
            return stepped(
                place,
                "z",
                lambda j: sums.at[pl.ds(2 * half, 2), lax.div(j, 2), lax.rem(j, 2), :, right],
            )

        self.loads = []
        self.lines = []
        for i, (axis, spot) in enumerate((("y", y_spot), ("z", z_spot))):
            near = (None, None)
            if here is not None:
                near = ({}, {})
                for k, (half, by) in enumerate(((0, 1), (1, 3), (0, 0), (1, 0))):
                    target = here[i].at[k]
                    near[half][by] = target
                    self.loads.append(
                        pltpu.make_async_copy(spot(half)(by), target, marks.at[8 + 4 * i + k])
                    )
                near = (near[0].get, near[1].get)
            room = rooms[6 * i : 6 * i + 6]
            self.lines.append(RingScatter(net, place, axis, spot(0), spot(1), room, *near))

    @staticmethod
    def room_shapes(cut, rest):
        return [
            *RingScatter.room_shapes((2, 144, cut), (2, 144, cut)),
            *RingScatter.room_shapes((2, 144, rest), (2, 144, rest)),
        ]

    def begin(self):
        for load in self.loads:
            load.start()
        for line in self.lines:
            line.start_far()

    def go_on(self):
        for line in self.lines:
            line.start_right()
            line.start_left()

    def turn(self):
        for load in self.loads:
            load.wait()
        for line in self.lines:
            line.middle()


class WeightSums:
    def __init__(self, place, net, sums, late, refs, marks):
        y_here, z_here, y1, z1, z2, y2, snd, rcv, *rooms = refs
        self.place, self.late, self.snd, self.rcv, self.marks = place, late, snd, rcv, marks
        self.y1, self.z1, self.y2, self.z2 = y1, z1, y2, z2
        self.x_hi, self.x_lo = lax.div(place.x, 2), lax.rem(place.x, 2)
        self.friends = []
        for k in range(1, 16):
            spot = lax.rem(self.x_hi * 8 + place.z * 2 + place.core + k, 16)
            x, z = lax.div(spot, 8) * 2 + self.x_lo, lax.rem(lax.div(spot, 2), 4)
            self.friends.append(place.device(x=x, z=z, core=lax.rem(spot, 2)))

        self.first = FirstSums(net, place, sums, LATER_CUT, rooms[:12], (y_here, z_here), marks[2])

        def then_z(j):
            return y1.at[lax.div(j, 2), lax.rem(j, 2)]

        self.z_second = RingScatter(
            net,
            place,
            "z",
            stepped(place, "z", lambda j: then_z(j).at[:, pl.ds(0, 384)]),
            stepped(place, "z", lambda j: then_z(j).at[:, pl.ds(384, 384)]),
            rooms[12:18],
        )
        self.y_second = RingScatter(
            net,
            place,
            "y",
            stepped(place, "y", lambda j: z1.at[j, :, pl.ds(0, 384)]),
            stepped(place, "y", lambda j: z1.at[j, :, pl.ds(384, 256)]),
            rooms[18:24],
        )

    @staticmethod
    def scratch():
        rest = HALF - CUT
        return [
            pltpu.VMEM((4, 2, 144, LATER_CUT), BF),
            pltpu.VMEM((4, 2, 144, LATER - LATER_CUT), BF),
            pltpu.VMEM((2, 2, 144, CUT), BF),
            pltpu.VMEM((4, 144, rest), BF),
            pltpu.VMEM((144, CUT), F32),
            pltpu.VMEM((144, rest), F32),
            pltpu.VMEM((8, 16, HALF + 384), BF),
            pltpu.VMEM((8, 16, HALF + 384), BF),
            *FirstSums.room_shapes(LATER_CUT, LATER - LATER_CUT),
            *RingScatter.room_shapes((144, 384), (144, 384)),
            *RingScatter.room_shapes((144, 384), (144, 256)),
        ]

    def next(self):
        y_line, z_line = self.first.lines
        after = pl.ds(AHEAD_CUT, LATER_CUT)
        y_line.finish(self.y1.at[0, :, :, after], self.y1.at[1, :, :, after])
        self.z_second.start()
        after = pl.ds(AHEAD - AHEAD_CUT, LATER - LATER_CUT)
        z_line.finish(self.z1.at[pl.ds(0, 2), :, after], self.z1.at[pl.ds(2, 2), :, after])
        self.y_second.start()

    def turn_again(self):
        self.z_second.middle()
        self.y_second.middle()

    def last(self):
        z2, y2 = self.z2, self.y2
        self.z_second.finish(z2.at[:, pl.ds(0, 384)], z2.at[:, pl.ds(384, 384)])
        self.y_second.finish(y2.at[:, pl.ds(0, 384)], y2.at[:, pl.ds(384, 256)])

    def send_home(self):
        snd = self.snd
        total = jnp.concatenate([self.z2[...], self.y2[...], self.late[...]], axis=1)
        blank = jnp.zeros((8, 128), F32)
        for k in range(8):
            extra = total[18 * k + 16 : 18 * k + 18]
            pieces = [extra[:, 128 * n : 128 * n + 128] for n in range(12)]
            snd[k, :, : HALF + 128] = total[18 * k : 18 * k + 16].astype(BF)
            for n, group in enumerate((pieces[:8], pieces[8:] + [blank])):
                at = HALF + 128 + 128 * n
                snd[k, :, at : at + 128] = jnp.concatenate(group, axis=0).astype(BF)
        place = self.place
        send, recv, here = self.marks
        row_half = lax.div(place.z, 2)
        self.slot = self.x_hi * 4 + place.core * 2 + lax.rem(place.z, 2)
        self.own = place.z * 2 + place.core
        self.stays = row_half == self.x_hi
        for k in range(8):
            copy = pltpu.make_async_remote_copy(
                src_ref=snd.at[k],
                dst_ref=self.rcv.at[self.slot],
                send_sem=send.at[k],
                recv_sem=recv.at[self.slot],
                device_id=place.device(x=row_half * 2 + self.x_lo, z=k // 2, core=k % 2),
                device_id_type=MESH,
            )
            is_here = self.stays & (self.own == k)

            @pl.when(jnp.logical_not(is_here))
            def _(copy=copy):
                copy.start()

            @pl.when(is_here)
            def _(k=k):
                keep = pltpu.make_async_copy(snd.at[k], self.rcv.at[self.slot], here.at[0])
                keep.start()
                keep.wait()

    def arrive(self):
        send, recv, _ = self.marks
        for m in range(8):
            arrival = pltpu.make_async_remote_copy(
                src_ref=self.snd.at[m],
                dst_ref=self.rcv.at[m],
                send_sem=send.at[m],
                recv_sem=recv.at[m],
                device_id=self.place.partner(),
                device_id_type=MESH,
            )

            @pl.when(jnp.logical_not(self.stays & (self.slot == m)))
            def _(arrival=arrival):
                arrival.wait_recv()

            @pl.when(jnp.logical_not(self.stays & (self.own == m)))
            def _(arrival=arrival):
                arrival.wait_send()


def last_kernel(
    home_ref,
    w_ref,
    gains_ref,
    y_ref,
    dx_ref,
    y_out,
    dx_out,
    dwq_out,
    dwk_out,
    dwv_out,
    dwo_out,
    dwg_out,
    dwu_out,
    dwd_out,
    *gain_outs,
):
    y_out[...] = y_ref[...]
    dx_out[...] = dx_ref[...]

    def rows_at(slot, n):
        spare, at = HALF + 128 + 128 * (n // 8), 2 * (n % 8)
        more = home_ref[slot, :, spare : spare + 128].astype(F32)[at : at + 2]
        return jnp.concatenate(
            [home_ref[slot, :, 128 * n : 128 * n + 128].astype(F32), more], axis=0
        )

    def tile(x_hi, which, n):
        core, n = n // 7, n % 7
        if which < 2:
            c, at = which, AHEAD_CUT + 128 * n if n < 4 else AHEAD + 128 * n
        else:
            c, n = n // 4, n % 4
            at = 128 * n if n < 2 else CUT + 128 * (n - 2)
        return rows_at(x_hi * 4 + core * 2 + c, at // 128)

    for which, out in enumerate((dwg_out, dwu_out, dwd_out)):
        for n in range(27):
            value = None
            for x_hi in range(2):
                if 0 <= n - 13 * x_hi < 14:
                    term = tile(x_hi, which, n - 13 * x_hi)
                    value = term if value is None else value + term
            span = slice(128 * n, 128 * n + 128)
            out[:, span] = value
    for k in range(4):
        span = slice(128 * k, 128 * k + 128)
        dwo_out[:, span] = rows_at(2 * k, HALF // 128)
        dwq_out[:, span] = rows_at(2 * k + 1, HALF // 128)
    for which in range(2):
        for j in range(4):
            out = (dwk_out, dwv_out)[j // 2]
            for y in range(4):
                rows = slice(576 * which + 144 * y, 576 * which + 144 * y + 144)
                out[rows, 128 * (j % 2) : 128 * (j % 2) + 128] = w_ref[which, j, y].astype(F32)
    for out, row, start in zip(gain_outs, (0, 4, 4, 1, 2, 3), (0, 0, HD, 0, 0, 0)):
        size = out.shape[0]
        out[...] = gains_ref[row : row + 1, start : start + size].reshape(size)


def last_layout(*args):
    shape = jax.ShapeDtypeStruct
    return pl.pallas_call(
        last_kernel,
        out_shape=(
            shape((TOK, D), BF),
            shape((TOK, D), BF),
            shape((18, 2 * HD), F32),
            shape((D, HD), F32),
            shape((D, HD), F32),
            shape((18, 2 * HD), F32),
            shape((18, 2 * HID), F32),
            shape((18, 2 * HID), F32),
            shape((18, 2 * HID), F32),
            *(shape((size,), F32) for size in (D, HD, HD, D, D, D)),
        ),
        in_specs=[IN_VMEM] * 5,
        out_specs=[IN_VMEM] * 15,
        compiler_params=pltpu.CompilerParams(vmem_limit_bytes=VMEM_BYTES),
    )(*args)


def angles(token_pos):
    middle = HD // 2
    frequency = THETA ** (-2.0 * jnp.arange(middle, dtype=F32) / HD)
    turned = token_pos.astype(F32)[:, None] * frequency[None, :]
    return (jnp.cos(turned), jnp.sin(turned))


def shards(
    layer_input,
    segment_ids,
    positions,
    w_query,
    w_key,
    w_value,
    w_out,
    w_gate,
    w_up,
    w_down,
    norm_attn,
    norm_query,
    norm_key,
    norm_post,
    norm_ffn,
    norm_out,
    cotangent,
):
    sp, tp = lax.axis_index("sp"), lax.axis_index("tp")
    cosine, sine = angles(lax.dynamic_slice_in_dim(positions, (sp * 2 + tp) * TOK, TOK))
    segments = segment_ids.reshape(128, 128)
    key_rows = jnp.asarray(KEY_TOKENS)
    kv_all, q_all, wq_other, wo_other, o_heads, inverse, q_pre, k_pre, h_attn = attention_forward(
        (
            layer_input,
            norm_attn,
            norm_query,
            norm_key,
            w_query,
            w_key,
            w_value,
            w_out,
            cosine,
            sine,
            segments,
            key_rows,
        ),
        2,
    )
    (
        layer_output,
        d_mid,
        d_attn,
        d_heads,
        delta,
        d_gains,
        ahead_y,
        ahead_z,
        sums,
    ) = feed_forward(
        (
            layer_input,
            o_heads,
            inverse,
            w_out,
            wo_other,
            norm_post,
            norm_ffn,
            norm_out,
            cotangent,
            w_gate,
            w_up,
            w_down,
        ),
        6,
    )
    d_input, home, w_both, gains = attention_backward(
        (kv_all, sums, ahead_y, ahead_z, w_query, wq_other, w_key, w_value),
        (
            q_all,
            d_heads,
            delta,
            key_rows,
            segments,
            q_pre,
            k_pre,
            cosine,
            sine,
            h_attn,
            d_attn,
            o_heads,
            layer_input,
            d_mid,
            norm_attn,
            norm_query,
            norm_key,
            d_gains,
        ),
        8,
    )
    y, dx, d_wq, d_wk, d_wv, d_wo, d_wg, d_wu, d_wd, *d_norms = last_layout(
        home, w_both, gains, layer_output, d_input
    )
    return (y, dx, d_wq, d_wk, d_wv, d_wo.T, d_wg, d_wu, d_wd.T, *d_norms)


def solution(mesh):
    rows = P(("sp", "tp"), None)
    in_specs = (
        rows,
        P(),
        P(),
        P(None, "tp"),
        P(),
        P(),
        P("tp", None),
        P(None, "tp"),
        P(None, "tp"),
        P("tp", None),
        P(),
        P(),
        P(),
        P(),
        P(),
        P(),
        rows,
    )
    out_specs = (
        rows,
        rows,
        P("sp", "tp"),
        P(),
        P(),
        P("tp", "sp"),
        P("sp", "tp"),
        P("sp", "tp"),
        P("tp", "sp"),
        P(),
        P(),
        P(),
        P(),
        P(),
        P(),
    )
    return jax.shard_map(shards, mesh=mesh, in_specs=in_specs, out_specs=out_specs, check_vma=False)
```

```python
import functools

import jax
import jax.numpy as jnp
import numpy as np
from jax import lax
from jax.experimental import pallas as pl
from jax.experimental.pallas import tpu as pltpu
from jax.sharding import PartitionSpec as P

EPS = 1e-06
THETA = 1000000.0
BF = jnp.bfloat16
F32 = jnp.float32
MESH = pl.DeviceIdType.MESH
IN_VMEM = pl.BlockSpec(memory_space=pltpu.VMEM)
VMEM_BYTES = 58 * 1024 * 1024

TOK = 128
D = 1152
HD = 256
HEADS = 4
ROWS = 2 * TOK
HID = 1728
HID_PAD = 1792
AHEAD, AHEAD_CUT = 512, 256
LATER, LATER_CUT = 896, 512
CUT = AHEAD_CUT + LATER_CUT
HALF = AHEAD + LATER
STRIPE = TOK // 4
KEYS = 16 * STRIPE


class Place:
    def __init__(self):
        sp = lax.axis_index("sp")
        self.core = lax.rem(sp, 2)
        self.z = lax.rem(lax.div(sp, 2), 4)
        self.y = lax.div(sp, 16)
        self.x = lax.rem(lax.div(sp, 8), 2) * 2 + lax.axis_index("tp")

    def device(self, **moved):
        x, y, z, core = (moved.get(name, getattr(self, name)) for name in ("x", "y", "z", "core"))
        return (((y * 2 + lax.div(x, 2)) * 4 + z) * 2 + core, lax.rem(x, 2))

    def step(self, axis, by):
        return lax.rem(getattr(self, axis) + by, 4)

    def toward(self, axis, by):
        return self.device(**{axis: self.step(axis, by)})

    def partner(self):
        return self.device(core=1 - self.core)


class Net:
    def __init__(self, send, recv):
        self.send, self.recv, self.used, self.started = send, recv, 0, []

    def copy(self, source, target, device):
        at = self.used
        self.used += 1
        return pltpu.make_async_remote_copy(
            src_ref=source,
            dst_ref=target,
            send_sem=self.send.at[at],
            recv_sem=self.recv.at[at],
            device_id=device,
            device_id_type=MESH,
        )

    def go(self, copy):
        copy.start()
        self.started.append(copy)

    def settle(self, copy):
        copy.wait_send()
        self.started = [other for other in self.started if other is not copy]

    def drain(self):
        for copy in self.started:
            copy.wait_send()
        self.started = []


def greet(devices, meanwhile=None):
    barrier = pltpu.get_barrier_semaphore()
    for device in devices:
        pl.semaphore_signal(barrier, inc=1, device_id=device, device_id_type=MESH)
    if meanwhile is not None:
        meanwhile()
    pl.semaphore_wait(barrier, len(devices))


def ring(place, axis):
    return [place.toward(axis, 1), place.toward(axis, 3)]


class RingGather:
    def __init__(self, net, place, axis, view, lo, hi):
        self.net = net
        me, nxt, prev = getattr(place, axis), place.step(axis, 1), place.step(axis, 3)
        right, left = ring(place, axis)
        self.to_right = net.copy(view(me), view(me), right)
        self.to_left = net.copy(view(me), view(me), left)
        self.on_right = net.copy(lo(prev), lo(prev), right)
        self.on_left = net.copy(hi(nxt), hi(nxt), left)

    def start(self):
        self.net.go(self.to_right)
        self.net.go(self.to_left)

    def forward(self):
        self.to_right.wait_recv()
        self.net.go(self.on_right)
        self.to_left.wait_recv()
        self.net.go(self.on_left)

    def finish(self):
        self.on_right.wait_recv()
        self.on_left.wait_recv()


class Direct:
    def __init__(self, net, place, axis, source, landing):
        self.net = net
        self.copies = [
            net.copy(
                source(place.step(axis, by)), landing(getattr(place, axis)), place.toward(axis, by)
            )
            for by in (2, 1, 3)
        ]

    def start(self):
        for copy in self.copies:
            self.net.go(copy)

    def wait(self):
        for copy in self.copies:
            copy.wait_recv()


def by_rows(ref, act):
    *lead, rows, _ = ref.shape
    block = next(size for size in (64, 48, 32, 16) if rows % size == 0)
    for spot in np.ndindex(*lead):

        def one(i, carry, spot=spot):
            act(spot, pl.ds(pl.multiple_of(i * block, block), block))
            return carry

        lax.fori_loop(0, rows // block, one, 0)


def add_to(target, other):
    def act(spot, rows):
        at = (*spot, rows, slice(None))
        target[at] = (target[at].astype(F32) + other[at].astype(F32)).astype(target.dtype)

    by_rows(target, act)


def sum_to(target, others):
    def act(spot, rows):
        at = (*spot, rows, slice(None))
        total = others[0][at].astype(F32)
        for other in others[1:]:
            total = total + other[at].astype(F32)
        target[at] = total.astype(target.dtype)

    by_rows(target, act)


def stepped(place, axis, view):
    return lambda by: view(place.step(axis, by))


class RingScatter:
    def __init__(self, net, place, axis, lo, hi, room, lo_here=None, hi_here=None):
        self.net, self.lo, self.hi = net, lo_here or lo, hi_here or hi
        right, left = ring(place, axis)
        self.lo1, self.lo_l, self.lo_r, self.hi1, self.hi_l, self.hi_r = room
        self.a = net.copy(lo(2), self.lo1, right)
        self.b = net.copy(hi(2), self.hi1, left)
        self.c_hi = net.copy(hi(1), self.hi_l, right)
        self.d_lo = net.copy(lo(3), self.lo_r, left)
        self.c_lo = net.copy(self.lo1, self.lo_l, right)
        self.d_hi = net.copy(self.hi1, self.hi_r, left)

    def start_far(self):
        self.net.go(self.a)
        self.net.go(self.b)

    def start_right(self):
        self.net.go(self.c_hi)

    def start_left(self):
        self.net.go(self.d_lo)

    def start(self):
        self.start_far()
        self.start_right()
        self.start_left()

    def middle_right(self):
        self.a.wait_recv()
        add_to(self.lo1, self.lo(1))
        self.net.go(self.c_lo)

    def middle_left(self):
        self.b.wait_recv()
        add_to(self.hi1, self.hi(3))
        self.net.go(self.d_hi)

    def middle(self):
        self.middle_right()
        self.middle_left()

    def finish(self, lo_out, hi_out):
        self.c_hi.wait_recv()
        self.d_hi.wait_recv()
        sum_to(hi_out, [self.hi(0), self.hi_l, self.hi_r])
        self.d_lo.wait_recv()
        self.c_lo.wait_recv()
        sum_to(lo_out, [self.lo(0), self.lo_l, self.lo_r])

    @staticmethod
    def room_shapes(lo_shape, hi_shape):
        return [pltpu.VMEM(lo_shape, BF)] * 3 + [pltpu.VMEM(hi_shape, BF)] * 3


def params(call_id):
    return pltpu.CompilerParams(
        collective_id=call_id, has_side_effects=True, vmem_limit_bytes=VMEM_BYTES
    )


def sems(count):
    return [pltpu.SemaphoreType.DMA((count,)), pltpu.SemaphoreType.DMA((count,))]


class WeightSwap:
    def __init__(self, net, place, w_ref, other_ref):
        self.net = net
        quarter = w_ref.shape[0] // 4
        right, left = ring(place, "x")

        def rows(ref, side):
            return ref.at[pl.ds(pl.multiple_of((2 * side + place.core) * quarter, 16), quarter)]

        self.first = [
            net.copy(rows(w_ref, side), rows(other_ref, side), (left, right)[side])
            for side in (0, 1)
        ]
        self.trades = [
            net.copy(rows(other_ref, side), rows(other_ref, side), place.partner())
            for side in (0, 1)
        ]

    def start(self):
        for copy in self.first:
            self.net.go(copy)

    def forward(self):
        for copy, trade in zip(self.first, self.trades):
            copy.wait_recv()
            self.net.go(trade)

    def finish(self):
        for trade in self.trades:
            trade.wait_recv()


def key_lines(place, ref):
    def stage(axis, first, at):
        return (
            axis,
            lambda j: ref.at[(pl.ds(first, 2), *at(j))],
            lambda j: ref.at[(first, *at(j))],
            lambda j: ref.at[(first + 1, *at(j))],
        )

    every = slice(None)
    return (
        (stage("x", 0, lambda j: (place.z, j)), stage("z", 0, lambda j: (j,))),
        (stage("z", 2, lambda j: (j, place.x)), stage("x", 2, lambda j: (every, j))),
    )


def key_tokens():
    z, x, row = np.meshgrid(np.arange(4), np.arange(4), np.arange(STRIPE), indexing="ij")
    return ((x // 2) * 2048 + z * 512 + (x % 2) * 128 + row).reshape(1, KEYS).astype(np.int32)


KEY_TOKENS = key_tokens()


def first_key(place, y):
    return y * 4096 + place.core * 256 + STRIPE * place.y


def contract(left, right, left_dim, right_dim):
    return lax.dot_general(
        left, right, (((left_dim,), (right_dim,)), ((), ())), preferred_element_type=F32
    )


def turn(u, cosine, sine):
    half = HD // 2
    low, high = u[:, :half], u[:, half:]
    return jnp.concatenate([low * cosine - high * sine, high * cosine + low * sine], axis=1)


def row_bounds(place, segments, y):
    at = (y * 2 + lax.div(place.x, 2)) * 16 + place.z * 4 + lax.rem(place.x, 2)
    rows = jnp.concatenate([segments[pl.ds(at, 1)], segments[pl.ds(at + 2, 1)]], axis=1)
    every = segments[...]
    first = jnp.zeros((1, ROWS), jnp.int32)
    for k in range(1, 4):
        below = jnp.sum((every < k).astype(F32), axis=0, keepdims=True)
        below = jnp.sum(below, axis=1, keepdims=True).astype(jnp.int32)
        first = jnp.where(rows == k, below, first)
    lane = lax.broadcasted_iota(jnp.int32, (1, ROWS), 1)
    last = at * TOK + lane + jnp.where(lane < TOK, 0, TOK)
    return first, last


def down(row):
    return jnp.concatenate(
        [
            jnp.transpose(jnp.broadcast_to(row[:, 128 * i : 128 * i + 128], (128, 128)))
            for i in range(row.shape[1] // 128)
        ],
        axis=0,
    )


def across(ref):
    return ref[...].reshape(1, ref.shape[0])


def norm_scale(v):
    return lax.rsqrt(jnp.mean(v * v, axis=-1, keepdims=True) + EPS)


def norm_back(v, r, gain, e):
    eg = e * gain
    dv = r * eg - v * (r * r * r) * jnp.mean(eg * v, axis=-1, keepdims=True)
    return dv, jnp.sum(e * v * r, axis=0, keepdims=True)


def forward_kernel(
    x_ref,
    g_attn,
    g_query,
    g_key,
    wq_ref,
    wk_ref,
    wv_ref,
    w_hbm,
    cos_ref,
    sin_ref,
    segments,
    key_ref,
    kv_hbm,
    q_all,
    wq_other,
    w_other,
    o_out,
    inv_out,
    q_pre,
    k_pre,
    h_out,
    buf,
    kv_own,
    o_sum,
    l_sum,
    o_snd,
    o_part,
    o_got,
    o_done,
    l_mine,
    l_got,
    l_core,
    *rest,
):
    *room, send, recv, local = rest
    place, net = Place(), Net(send, recv)
    core = place.core
    partner = place.partner()
    mine = pl.ds(pl.multiple_of(core * TOK, TOK), TOK)
    theirs = pl.ds(pl.multiple_of((1 - core) * TOK, TOK), TOK)

    def keys_and_values():
        xf = x_ref[...].astype(F32)
        h = (xf * norm_scale(xf) * across(g_attn)).astype(BF)
        h_out[...] = h
        k = jnp.dot(h, wk_ref[...], preferred_element_type=F32)
        k_pre[...] = k
        k = turn(k * norm_scale(k) * across(g_key), cos_ref[...], sin_ref[...]).astype(BF)
        v = jnp.dot(h, wv_ref[...], preferred_element_type=F32).astype(BF)
        for j in range(4):
            kv_own[j, :, :HD] = k[STRIPE * j : STRIPE * j + STRIPE]
            kv_own[j, :, HD:] = v[STRIPE * j : STRIPE * j + STRIPE]
        buf[place.y, place.z, place.x] = kv_own[place.y]

    greet(
        ring(place, "x")
        + ring(place, "y")
        + ring(place, "z")
        + [partner, place.toward("y", 2)],
        keys_and_values,
    )
    swap_wq = WeightSwap(net, place, wq_ref, wq_other)
    swap_w = WeightSwap(net, place, w_hbm, w_other)
    stripes = Direct(
        net,
        place,
        "y",
        lambda j: kv_own.at[j],
        lambda j: buf.at[j, place.z, place.x],
    )
    stripes.start()
    swap_wq.start()
    (first_a, then_a), (first_b, then_b) = (
        [RingGather(net, place, *stage) for stage in part] for part in key_lines(place, buf)
    )
    q_ring = RingGather(
        net,
        place,
        "y",
        lambda j: q_all.at[j, :, mine],
        lambda j: q_all.at[j, pl.ds(0, 2), mine],
        lambda j: q_all.at[j, pl.ds(2, 2), mine],
    )

    def block_of(by):
        return q_all.at[place.step("y", by), :, mine]

    q_core = [net.copy(block_of(by), block_of(by), partner) for by in range(4)]

    def queries(which, w):
        q = jnp.dot(h_out[...], w[...], preferred_element_type=F32)
        for i in range(2):
            u = q[:, HD * i : HD * i + HD]
            q_pre[2 * which + i] = u
            u = turn(u * norm_scale(u) * across(g_query), cos_ref[...], sin_ref[...])
            q_all[place.y, 2 * which + i, mine] = (u.astype(BF).astype(F32) * HD**-0.5).astype(BF)

    queries(0, wq_ref)
    for by in range(4):
        for h in range(HEADS):
            o_sum[by, h] = jnp.zeros((ROWS, HD), F32)
            l_sum[by, h] = jnp.zeros((ROWS, 128), F32)
    stripes.wait()
    first_a.start()
    first_b.start()
    swap_wq.forward()
    first_a.forward()
    first_b.forward()
    swap_wq.finish()
    queries(1, wq_other)
    q_ring.start()
    net.go(q_core[0])
    first_a.finish()
    then_a.start()
    first_b.finish()
    then_b.start()
    q_ring.forward()
    net.go(q_core[1])
    net.go(q_core[3])
    then_a.forward()
    then_b.forward()
    q_ring.finish()
    net.go(q_core[2])
    then_a.finish()
    then_b.finish()
    swap_w.start()
    store = pltpu.make_async_copy(buf, kv_hbm, local.at[0])
    store.start()

    o_core = [net.copy(o_snd.at[by], o_got.at[by], partner) for by in range(4)]

    def attend(by):
        y = place.step("y", by)
        q_core[by].wait_recv()
        first, last = (down(row) for row in row_bounds(place, segments, y))

        def some_keys(key_y, carry):
            keys = buf[key_y, :, :, :, :HD].reshape(KEYS, HD)
            values = buf[key_y, :, :, :, HD:].reshape(KEYS, HD)
            token = key_ref[...] + first_key(place, key_y)
            allowed = jnp.concatenate(
                [
                    (token[:, 128 * i : 128 * i + 128] <= last)
                    & (token[:, 128 * i : 128 * i + 128] >= first)
                    for i in range(KEYS // 128)
                ],
                axis=1,
            )
            for h in range(HEADS):
                weights = jnp.exp(contract(q_all[y, h], keys, 1, 1))
                weights = jnp.where(allowed, weights, 0.0)
                l_sum[by, h] += sum(
                    weights[:, 128 * i : 128 * i + 128] for i in range(KEYS // 128)
                )
                o_sum[by, h] += jnp.dot(weights.astype(BF), values, preferred_element_type=F32)
            return carry

        lax.fori_loop(0, y + 1, some_keys, 0)
        for h in range(HEADS):
            o_snd[by, h] = o_sum[by, h, theirs].astype(BF)
            o_part[by, h] = o_sum[by, h, mine].astype(BF)
            total = jnp.sum(l_sum[by, h], axis=1, keepdims=True)
            l_mine[y, h : h + 1] = jnp.transpose(jnp.broadcast_to(total, (ROWS, 128)))[:1]
        net.go(o_core[by])

    def both_cores(by):
        o_core[by].wait_recv()
        add_to(o_part.at[by], o_got.at[by])

    o_ring = RingScatter(
        net,
        place,
        "y",
        lambda by: o_part.at[by, pl.ds(0, 2)],
        lambda by: o_part.at[by, pl.ds(2, 2)],
        room,
    )
    attend(0)
    attend(2)
    attend(1)
    both_cores(2)
    o_ring.start_far()
    swap_w.forward()
    attend(3)
    l_swap = Direct(net, place, "y", lambda j: l_mine.at[j], lambda j: l_got.at[j])
    l_swap.start()
    l_got[place.y] = l_mine[place.y]
    both_cores(1)
    o_ring.start_right()
    o_ring.middle_right()
    both_cores(3)
    o_ring.start_left()
    o_ring.middle_left()
    both_cores(0)
    swap_w.finish()
    l_swap.wait()
    l_core[core] = (l_got[0] + l_got[1]) + (l_got[2] + l_got[3])
    l_over = net.copy(l_core.at[core], l_core.at[core], partner)
    net.go(l_over)
    l_over.wait_recv()
    total = l_core[0] + l_core[1]
    inverse = 1.0 / jnp.where(core == 0, total[:, :TOK], total[:, TOK:])
    o_ring.finish(o_done.at[pl.ds(0, 2)], o_done.at[pl.ds(2, 2)])
    for h in range(HEADS):
        scale = down(inverse[h : h + 1])
        o_out[h] = o_done[h] * jnp.concatenate([scale, scale], axis=1)
        inv_out[h] = scale
    store.wait()
    net.drain()


def attention_forward(args, call_id):
    shape = jax.ShapeDtypeStruct
    anywhere = pl.BlockSpec(memory_space=pl.ANY)
    halves = (2, TOK, HD)
    return pl.pallas_call(
        forward_kernel,
        out_shape=(
            shape((4, 4, 4, STRIPE, 2 * HD), BF),
            shape((4, HEADS, ROWS, HD), BF),
            shape((D, 2 * HD), BF),
            shape((2 * HD, D), BF),
            shape((HEADS, TOK, HD), F32),
            shape((HEADS, TOK, 128), F32),
            shape((HEADS, TOK, HD), F32),
            shape((TOK, HD), F32),
            shape((TOK, D), BF),
        ),
        in_specs=[IN_VMEM] * 7 + [anywhere] + [IN_VMEM] * 4,
        out_specs=[anywhere] + [IN_VMEM] * 2 + [anywhere] + [IN_VMEM] * 5,
        scratch_shapes=[
            pltpu.VMEM((4, 4, 4, STRIPE, 2 * HD), BF),
            pltpu.VMEM((4, STRIPE, 2 * HD), BF),
            pltpu.VMEM((4, HEADS, ROWS, HD), F32),
            pltpu.VMEM((4, HEADS, ROWS, 128), F32),
            pltpu.VMEM((4, HEADS, TOK, HD), BF),
            pltpu.VMEM((4, HEADS, TOK, HD), BF),
            pltpu.VMEM((4, HEADS, TOK, HD), BF),
            pltpu.VMEM((HEADS, TOK, HD), F32),
            pltpu.VMEM((4, 8, ROWS), F32),
            pltpu.VMEM((4, 8, ROWS), F32),
            pltpu.VMEM((2, 8, ROWS), F32),
            *RingScatter.room_shapes(halves, halves),
            *sems(64),
            pltpu.SemaphoreType.DMA((1,)),
        ],
        compiler_params=params(call_id),
    )(*args)


def kept_head(place, j):
    return jnp.where(lax.rem(j, 2) == lax.rem(place.x, 2), 0, 2) + lax.div(j, 2)


def turn_back(e, cosine, sine):
    half = HD // 2
    low, high = e[:, :half], e[:, half:]
    return jnp.concatenate([low * cosine + high * sine, high * cosine - low * sine], axis=1)


def backward_kernel(
    kv_hbm,
    sums_hbm,
    ahead_y,
    ahead_z,
    wq_hbm,
    wq2_hbm,
    wk_hbm,
    wv_hbm,
    q_all,
    do_ref,
    delta_ref,
    key_ref,
    segments,
    q_pre,
    k_pre,
    cos_ref,
    sin_ref,
    h_ref,
    da_ref,
    o_ref,
    x_ref,
    dmid_ref,
    g_attn,
    g_query,
    g_key,
    gains_ref,
    dx_out,
    home_out,
    late_out,
    w_top,
    w_low,
    gains_out,
    buf,
    wq,
    wq2,
    wk,
    wv,
    do_all,
    delta_all,
    tokens,
    grads,
    fin,
    fin_got,
    dq_sum,
    dq_snd,
    dq_part,
    dq_got,
    dq_done,
    h_line,
    da_line,
    turned,
    o_line,
    dq_line,
    dq_own,
    o_own,
    late_all,
    late_got,
    late_y,
    late_z,
    gain_got,
    kv_own,
    kv_line,
    turned_other,
    w_got,
    w_y,
    w_z,
    *rest,
):
    rooms, dq_rooms, late_rooms, rest = rest[:24], rest[24:30], rest[30:42], rest[42:]
    *weight_refs, send, recv, send2, recv2, here = rest
    place, net = Place(), Net(send, recv)
    core, partner = place.core, place.partner()
    w_loads = [
        pltpu.make_async_copy(source, target, here.at[1 + i])
        for i, (source, target) in enumerate(
            (
                (kv_hbm, buf),
                (wq_hbm, wq),
                (wq2_hbm, wq2),
                (wk_hbm, wk),
                (wv_hbm, wv),
            )
        )
    ]
    for load in w_loads:
        load.start()
    weights = WeightSums(place, net, sums_hbm, late_z, weight_refs, (send2, recv2, here))
    y1, z1 = weights.y1, weights.z1
    ahead_loads = [
        pltpu.make_async_copy(ahead_y, y1.at[:, :, :, pl.ds(0, AHEAD_CUT)], here.at[16]),
        pltpu.make_async_copy(ahead_z, z1.at[:, :, pl.ds(0, AHEAD - AHEAD_CUT)], here.at[17]),
    ]
    for load in ahead_loads:
        load.start()
    across_x = [place.device(x=place.step("x", by), core=1 - core) for by in (1, 3)]
    greet(
        weights.friends
        + ring(place, "x")
        + ring(place, "y")
        + across_x
        + [place.toward("y", 2)]
    )
    mine = pl.ds(pl.multiple_of(core * TOK, TOK), TOK)
    theirs = pl.ds(pl.multiple_of((1 - core) * TOK, TOK), TOK)
    do_all[place.y, :, mine] = do_ref[...]
    delta_all[place.y, core] = delta_ref[...]
    do_ring = RingGather(
        net,
        place,
        "y",
        lambda j: do_all.at[j, :, mine],
        lambda j: do_all.at[j, pl.ds(0, 2), mine],
        lambda j: do_all.at[j, pl.ds(2, 2), mine],
    )

    def block_of(by):
        return do_all.at[place.step("y", by), :, mine]

    do_core = [net.copy(block_of(by), block_of(by), partner) for by in range(4)]
    delta_swap = Direct(
        net,
        place,
        "y",
        lambda j: delta_all.at[place.y, core],
        lambda j: delta_all.at[j, core],
    )
    delta_core = net.copy(delta_all.at[:, core], delta_all.at[:, core], partner)
    do_ring.start()
    delta_swap.start()
    net.go(do_core[0])

    half = TOK // 2

    def line_of(rows):
        return RingGather(
            net,
            place,
            "x",
            lambda j: rows.at[j],
            lambda j: rows.at[j, pl.ds(0, half)],
            lambda j: rows.at[j, pl.ds(half, half)],
        )

    def head_of(j):
        return kept_head(place, j)

    h_line[place.x] = h_ref[...]
    da_line[place.x] = da_ref[...]
    for h in range(HEADS):
        o_own[h] = o_ref[h].astype(BF)
    o_line[place.x] = o_own[head_of(place.x)]
    line_h, line_da = line_of(h_line), line_of(da_line)
    o_swap = Direct(net, place, "x", lambda j: o_own.at[head_of(j)], lambda j: o_line.at[j])
    dq_swap = Direct(net, place, "x", lambda j: dq_own.at[head_of(j)], lambda j: dq_line.at[j])
    line_da.start()
    o_swap.start()
    key_rings = []
    for i, (inner, outer) in enumerate(key_lines(place, grads)):
        for k, (axis, _, lo, hi) in enumerate((outer, inner)):
            spot = 12 * i + 6 * k
            key_rings.append(
                RingScatter(
                    net,
                    place,
                    axis,
                    stepped(place, axis, lo),
                    stepped(place, axis, hi),
                    rooms[spot : spot + 6],
                )
            )
    first_a, then_a, first_b, then_b = key_rings
    fin_swap = Direct(net, place, "y", lambda j: fin.at[j], lambda j: fin_got.at[j])
    dq_core = net.copy(dq_snd, dq_got, partner)
    dq_ring = RingScatter(
        net,
        place,
        "y",
        stepped(place, "y", lambda j: dq_part.at[j, pl.ds(0, 2)]),
        stepped(place, "y", lambda j: dq_part.at[j, pl.ds(2, 2)]),
        dq_rooms,
    )
    late_first = RingScatter(
        net,
        place,
        "y",
        stepped(place, "y", lambda j: late_got.at[j, 0]),
        stepped(place, "y", lambda j: late_got.at[j, 1]),
        late_rooms[:6],
    )

    def late_spot(j):
        return late_y.at[lax.div(j, 2), lax.rem(j, 2)]

    late_second = RingScatter(
        net,
        place,
        "z",
        stepped(place, "z", lambda j: late_spot(j).at[pl.ds(0, 80)]),
        stepped(place, "z", lambda j: late_spot(j).at[pl.ds(80, 64)]),
        late_rooms[6:],
    )

    def late_term(c, turned, columns):
        term = jnp.dot(
            turned[...], columns[...].reshape(4 * TOK, HD), preferred_element_type=F32
        ).astype(BF)
        for k in range(8):
            for which in range(2):
                late_all[which, k // 2, k % 2, c] = term[
                    144 * k : 144 * k + 144, 128 * which : 128 * which + 128
                ]

    do_ring.forward()
    net.go(do_core[1])
    net.go(do_core[3])
    weights.first.begin()
    weights.first.go_on()
    delta_swap.wait()
    net.go(delta_core)
    tokens[...] = down(key_ref[...])
    bounds = [row_bounds(place, segments, y) for y in range(4)]
    do_ring.finish()
    net.go(do_core[2])
    w_loads[0].wait()
    for copy in do_core:
        copy.wait_recv()
    delta_core.wait_recv()

    def differ(key_y):
        keys = buf[key_y, :, :, :, :HD].reshape(KEYS, HD)
        values = buf[key_y, :, :, :, HD:].reshape(KEYS, HD)
        token = tokens[...] + first_key(place, key_y)
        token = jnp.concatenate([token, token], axis=1)
        d_keys = d_values = None
        for y in range(key_y, 4):
            first, last = bounds[y]
            allowed = (token <= last) & (token >= first)
            for h in range(HEADS):
                probs = jnp.exp(contract(keys, q_all[y, h], 1, 1))
                probs = jnp.where(allowed, probs, 0.0)
                delta = jnp.concatenate(
                    [delta_all[y, 0, h : h + 1], delta_all[y, 1, h : h + 1]], axis=1
                )
                d_scores = (probs * (contract(values, do_all[y, h], 1, 1) - delta)).astype(BF)
                value_term = jnp.dot(probs.astype(BF), do_all[y, h], preferred_element_type=F32)
                key_term = jnp.dot(d_scores, q_all[y, h], preferred_element_type=F32)
                d_values = value_term if d_values is None else d_values + value_term
                d_keys = key_term if d_keys is None else d_keys + key_term
                query_term = contract(keys, d_scores, 0, 0)
                if y == key_y:
                    dq_sum[y, h] = query_term
                else:
                    dq_sum[y, h] += query_term
        grads[key_y, :, :, :, :HD] = d_keys.astype(BF).reshape(4, 4, STRIPE, HD)
        grads[key_y, :, :, :, HD:] = d_values.astype(BF).reshape(4, 4, STRIPE, HD)

    differ(3)
    differ(2)
    first_b.start()
    line_da.forward()
    line_h.start()
    differ(1)
    first_b.middle()
    differ(0)
    first_a.start()
    for y in range(4):
        for h in range(HEADS):
            dq_snd[y, h] = dq_sum[y, h, :, theirs].astype(BF)
            dq_part[y, h] = dq_sum[y, h, :, mine].astype(BF)
    net.go(dq_core)
    weights.first.turn()
    dq_core.wait_recv()
    for y in range(4):
        add_to(dq_part.at[y], dq_got.at[y])
    dq_ring.start()
    first_a.middle()
    first_b.finish(first_b.lo(0), first_b.hi(0))
    then_b.start()
    first_a.finish(first_a.lo(0), first_a.hi(0))
    then_a.start()
    for load in ahead_loads:
        load.wait()
    weights.next()
    line_h.forward()
    line_da.finish()
    o_swap.wait()
    turned[...] = jnp.transpose(da_line[...].reshape(4 * TOK, D))
    late_term(0, turned, o_line)
    dq_ring.middle()
    then_b.middle()
    then_a.middle()
    then_b.finish(fin.at[2], fin.at[3])
    then_a.finish(fin.at[0], fin.at[1])
    fin_got[place.y] = fin[place.y]
    fin_swap.start()
    for load in w_loads[1:]:
        load.wait()

    dq_ring.finish(dq_done.at[pl.ds(0, 2)], dq_done.at[pl.ds(2, 2)])
    d_query = jnp.zeros((1, HD), F32)
    for h in range(HEADS):
        e = jnp.transpose(dq_done[h]) * HD**-0.5
        e = turn_back(e.astype(BF).astype(F32), cos_ref[...], sin_ref[...])
        u = q_pre[h]
        du, gain = norm_back(u, norm_scale(u), across(g_query), e)
        d_query = d_query + gain
        dq_own[h] = du.astype(BF)
    dq_line[place.x] = dq_own[head_of(place.x)]
    dq_swap.start()
    line_h.finish()
    turned[...] = jnp.transpose(h_line[...].reshape(4 * TOK, D))
    turned_swap = net.copy(
        turned.at[pl.ds(pl.multiple_of((1 - core) * 576, 16), 576)], turned_other, partner
    )
    net.go(turned_swap)
    fin_swap.wait()

    dkv = jnp.concatenate([fin_got[j] for j in range(4)], axis=0)
    e = turn_back(dkv[:, :HD].astype(BF).astype(F32), cos_ref[...], sin_ref[...])
    u = k_pre[...]
    dk, d_key = norm_back(u, norm_scale(u), across(g_key), e)
    dk, dv = dk.astype(BF), dkv[:, HD:].astype(BF)
    for i in range(2):
        kv_own[i] = dk[:, 128 * i : 128 * i + 128]
        kv_own[2 + i] = dv[:, 128 * i : 128 * i + 128]
    kv_line[core, place.x] = kv_own[place.x]
    kv_swap = Direct(net, place, "x", lambda j: kv_own.at[j], lambda j: kv_line.at[core, j])
    kv_swap.start()
    kv_across = []
    for by in range(4):
        j = place.step("x", by)
        device = place.device(x=j, core=1 - core)
        kv_across.append(net.copy(kv_own.at[j], kv_line.at[core, place.x], device))
        net.go(kv_across[by])
    weights.turn_again()
    dq_swap.wait()
    late_term(1, turned, dq_line)
    late_swap = net.copy(late_all.at[1 - core], late_got, partner)
    net.go(late_swap)
    d_h = contract(dk, wk[...], 1, 1) + contract(dv, wv[...], 1, 1)
    for h in range(HEADS):
        w = (wq, wq2)[h // 2]
        d_h = d_h + contract(dq_own[h], w[:, 256 * (h % 2) : 256 * (h % 2) + 256], 1, 1)
    xf = x_ref[...].astype(F32)
    dx, d_attn = norm_back(xf, norm_scale(xf), across(g_attn), d_h)
    dx_out[...] = (dmid_ref[...] + dx).astype(BF)
    def gain_swap(level, axis):
        return Direct(
            net, place, axis, lambda j: gain_got.at[level, at(axis)], lambda j: gain_got.at[level, j]
        )

    def at(axis):
        return getattr(place, axis)

    def gain_sum(level):
        return (gain_got[level, 0] + gain_got[level, 1]) + (gain_got[level, 2] + gain_got[level, 3])

    swaps = [gain_swap(0, "x"), gain_swap(1, "y"), gain_swap(2, "z")]
    norms = jnp.concatenate([d_query, d_key, jnp.zeros((1, D - 2 * HD), F32)], axis=1)
    gain_got[0, place.x] = jnp.concatenate(
        [d_attn, gains_ref[0:3], norms, jnp.zeros((3, D), F32)], axis=0
    )
    swaps[0].start()
    turned_swap.wait_recv()
    kv_swap.wait()
    for copy in kv_across:
        copy.wait_recv()
    term = jnp.dot(
        turned[pl.ds(pl.multiple_of(core * 576, 16), 576)],
        kv_line[core].reshape(4 * TOK, 128),
        preferred_element_type=F32,
    )
    term += jnp.dot(
        turned_other[...], kv_line[1 - core].reshape(4 * TOK, 128), preferred_element_type=F32
    )
    term = term.astype(BF)
    for k in range(4):
        w_got[k] = term[144 * k : 144 * k + 144]
    w_scatter = Direct(net, place, "y", lambda j: w_got.at[j], lambda j: w_y.at[j])
    w_scatter.start()
    w_y[place.y] = w_got[place.y]
    late_swap.wait_recv()
    for y in range(4):
        add_to(late_got.at[y], late_all.at[core, y])
    late_first.start()
    swaps[0].wait()
    gain_got[1, place.y] = gain_sum(0)
    swaps[1].start()
    weights.last()
    swaps[1].wait()
    gain_got[2, place.z] = gain_sum(1)
    swaps[2].start()
    w_scatter.wait()
    sum_to(w_z.at[place.z], [w_y.at[j] for j in range(4)])
    w_sums = Direct(net, place, "z", lambda j: w_z.at[place.z], lambda j: w_z.at[j])
    w_sums.start()
    late_first.middle()
    swaps[2].wait()
    gain_got[3, core] = gain_sum(2)
    gain_last = net.copy(gain_got.at[3, core], gain_got.at[3, core], partner)
    net.go(gain_last)
    w_sums.wait()
    upper, lower = w_top.at[core], w_low.at[core]
    sum_to(upper.at[place.x, place.y], [w_z.at[j, pl.ds(0, 80)] for j in range(4)])
    sum_to(lower.at[place.x, place.y], [w_z.at[j, pl.ds(80, 64)] for j in range(4)])

    def spread(axis, view):
        return Direct(net, place, axis, lambda j: view(at(axis)), view)

    first_way = [
        spread("y", lambda j: upper.at[place.x, j]),
        spread("x", lambda j: lower.at[j, place.y]),
    ]
    second_way = [spread("x", lambda j: upper.at[j]), spread("y", lambda j: lower.at[:, j])]
    for line in first_way:
        line.start()
    late_first.finish(late_y.at[0], late_y.at[1])
    late_second.start()
    for line, then in zip(first_way, second_way):
        line.wait()
        then.start()
    late_second.middle()
    gain_last.wait_recv()
    gains_out[...] = gain_got[3, 0] + gain_got[3, 1]
    over = [net.copy(upper, upper, partner), net.copy(lower, lower, partner)]
    for line, copy in zip(second_way, over):
        line.wait()
        net.go(copy)
    late_second.finish(late_z.at[pl.ds(0, 80)], late_z.at[pl.ds(80, 64)])
    weights.send_late()
    for copy in over:
        copy.wait_recv()
    weights.arrive()
    home_out[...] = weights.rcv[...]
    late_out[...] = weights.late_rcv[...]
    net.drain()


def attention_backward(hbm, small, call_id):
    shape = jax.ShapeDtypeStruct
    rooms = []
    for _ in range(2):
        rooms += RingScatter.room_shapes((4, STRIPE, 2 * HD), (4, STRIPE, 2 * HD))
        rooms += RingScatter.room_shapes((STRIPE, 2 * HD), (STRIPE, 2 * HD))
    rooms += RingScatter.room_shapes((2, HD, TOK), (2, HD, TOK))
    late_rooms = [
        *RingScatter.room_shapes((2, 144, 128), (2, 144, 128)),
        *RingScatter.room_shapes((80, 128), (64, 128)),
    ]
    return pl.pallas_call(
        backward_kernel,
        out_shape=(
            shape((TOK, D), BF),
            shape((8, 16, HALF + 256), BF),
            shape((8, 16, 256), BF),
            shape((2, 4, 4, 80, 128), BF),
            shape((2, 4, 4, 64, 128), BF),
            shape((8, D), F32),
        ),
        in_specs=[pl.BlockSpec(memory_space=pl.ANY)] * len(hbm) + [IN_VMEM] * len(small),
        out_specs=[IN_VMEM] * 6,
        scratch_shapes=[
            pltpu.VMEM((4, 4, 4, STRIPE, 2 * HD), BF),
            pltpu.VMEM((D, 2 * HD), BF),
            pltpu.VMEM((D, 2 * HD), BF),
            pltpu.VMEM((D, HD), BF),
            pltpu.VMEM((D, HD), BF),
            pltpu.VMEM((4, HEADS, ROWS, HD), BF),
            pltpu.VMEM((4, 2, 8, TOK), F32),
            pltpu.VMEM((KEYS, 128), jnp.int32),
            pltpu.VMEM((4, 4, 4, STRIPE, 2 * HD), BF),
            pltpu.VMEM((4, STRIPE, 2 * HD), F32),
            pltpu.VMEM((4, STRIPE, 2 * HD), F32),
            pltpu.VMEM((4, HEADS, HD, ROWS), F32),
            pltpu.VMEM((4, HEADS, HD, TOK), BF),
            pltpu.VMEM((4, HEADS, HD, TOK), BF),
            pltpu.VMEM((4, HEADS, HD, TOK), BF),
            pltpu.VMEM((HEADS, HD, TOK), F32),
            pltpu.VMEM((4, TOK, D), BF),
            pltpu.VMEM((4, TOK, D), BF),
            pltpu.VMEM((D, 4 * TOK), BF),
            pltpu.VMEM((4, TOK, HD), BF),
            pltpu.VMEM((4, TOK, HD), BF),
            pltpu.VMEM((4, TOK, HD), BF),
            pltpu.VMEM((4, TOK, HD), BF),
            pltpu.VMEM((2, 4, 2, 2, 144, 128), BF),
            pltpu.VMEM((4, 2, 2, 144, 128), BF),
            pltpu.VMEM((2, 2, 144, 128), BF),
            pltpu.VMEM((144, 128), F32),
            pltpu.VMEM((4, 4, 8, D), F32),
            pltpu.VMEM((4, TOK, 128), BF),
            pltpu.VMEM((2, 4, TOK, 128), BF),
            pltpu.VMEM((576, 4 * TOK), BF),
            pltpu.VMEM((4, 144, 128), BF),
            pltpu.VMEM((4, 144, 128), BF),
            pltpu.VMEM((4, 144, 128), BF),
            *rooms,
            *late_rooms,
            *WeightSums.scratch(),
            *sems(160),
            *sems(16),
            pltpu.SemaphoreType.DMA((24,)),
        ],
        compiler_params=params(call_id),
    )(*hbm, *small)


def feed_kernel(
    x_ref,
    o_ref,
    inv_ref,
    wo_ref,
    wo2_ref,
    post_ref,
    ffn_ref,
    out_gain_ref,
    cot_ref,
    wg_hbm,
    wu_hbm,
    wd_hbm,
    out_ref,
    dmid_out,
    dattn_out,
    do_out,
    delta_out,
    dgains_out,
    ahead_y,
    ahead_z,
    sums_hbm,
    wg,
    wu,
    wd,
    h_line,
    f_line,
    h_turned,
    f_turned,
    gelu_kept,
    slope_kept,
    act,
    d_gate,
    d_up,
    f_terms,
    h_terms,
    ahead_snd,
    ahead_got,
    snd,
    got,
    attn,
    mid,
    ffn,
    *rest,
):
    *room, send, recv, local = rest
    place, net = Place(), Net(send, recv)
    core, partner = place.core, place.partner()
    x_hi = lax.div(place.x, 2)
    first_unit = pl.multiple_of(x_hi * (2 * HID - HID_PAD), 128)
    window = pl.ds(first_unit, HID_PAD)
    loads = [
        pltpu.make_async_copy(source, target, local.at[i])
        for i, (source, target) in enumerate(
            ((wg_hbm.at[:, window], wg), (wu_hbm.at[:, window], wu), (wd_hbm.at[window], wd))
        )
    ]
    for load in loads:
        load.start()
    greet(ring(place, "x") + ring(place, "y") + ring(place, "z") + [partner])
    half, quarter = TOK // 2, TOK // 4
    top, bottom = pl.ds(0, quarter), pl.ds(quarter, quarter)
    g_post, g_ffn, g_out = (across(ref) for ref in (post_ref, ffn_ref, out_gain_ref))

    def rows_of(part):
        return slice(half * part, half * part + half)

    def lines_of(part):
        return slice(4 * half * part, 4 * half * part + 4 * half)

    def gather(lines):
        return RingGather(
            net,
            place,
            "x",
            lambda j: lines.at[j],
            lambda j: lines.at[j, top],
            lambda j: lines.at[j, bottom],
        )

    def scatter(terms, room):
        return RingScatter(
            net,
            place,
            "x",
            stepped(place, "x", lambda j: terms.at[j, top]),
            stepped(place, "x", lambda j: terms.at[j, bottom]),
            room,
        )

    def summed(line, part):
        at = half * part
        line.finish(ffn.at[pl.ds(at, quarter)], ffn.at[pl.ds(at + quarter, quarter)])

    o_cat = [o_ref[h].astype(BF) for h in range(HEADS)]
    a = jnp.dot(jnp.concatenate(o_cat[:2], axis=1), wo_ref[...], preferred_element_type=F32)
    a += jnp.dot(jnp.concatenate(o_cat[2:], axis=1), wo2_ref[...], preferred_element_type=F32)
    attn[...] = a
    mid[...] = x_ref[...].astype(F32) + a * norm_scale(a) * g_post
    m = mid[...]
    h = (m * norm_scale(m) * g_ffn).astype(BF)
    for part in range(2):
        h_line[part, place.x] = h[rows_of(part)]
    h_gathers = [gather(h_line.at[part]) for part in range(2)]
    f_gathers = [gather(f_line.at[part]) for part in range(2)]
    f_sums = [scatter(f_terms.at[part], room[6 * part : 6 * part + 6]) for part in range(2)]
    h_sums = [
        scatter(h_terms.at[part], room[12 + 6 * part : 18 + 6 * part]) for part in range(2)
    ]
    h_gathers[0].start()

    for load in loads:
        load.wait()
    low_unit, high_unit = jnp.where(x_hi == 0, 0, 64), jnp.where(x_hi == 0, HID, HID_PAD)

    def units(n):
        return pl.ds(pl.multiple_of(n * 256, 256), 256)

    def forward(part, n, carry):
        h = h_line[part].reshape(4 * half, D)
        gate = jnp.dot(h, wg[:, units(n)], preferred_element_type=F32)
        up = jnp.dot(h, wu[:, units(n)], preferred_element_type=F32)
        unit = n * 256 + lax.broadcasted_iota(jnp.int32, (1, 256), 1)
        own = jnp.where((unit >= low_unit) & (unit < high_unit), 1.0, 0.0)
        scale, cube = 0.7978845608028654, 0.044715
        square = gate * gate
        bent = jnp.tanh(scale * gate * (1.0 + cube * square))
        lifted = 0.5 * (1.0 + bent)
        gelu = gate * lifted * own
        slope = lifted + 0.5 * gate * (1.0 - bent * bent) * scale * (1.0 + 3.0 * cube * square)
        act[lines_of(part), units(n)] = (gelu * up).astype(BF)
        gelu_kept[lines_of(part), units(n)] = gelu.astype(BF)
        slope_kept[lines_of(part), units(n)] = (slope * up * own).astype(BF)
        return carry

    def columns(n):
        return pl.ds(pl.multiple_of(n * 384, 128), 384)

    def project(part, n, carry):
        term = jnp.dot(act[lines_of(part)], wd[:, columns(n)], preferred_element_type=F32)
        f_terms[part, :, :, columns(n)] = term.astype(BF).reshape(4, half, 384)
        return carry

    def backward(part, n, carry):
        d_act = contract(f_line[part].reshape(4 * half, D), wd[units(n)], 1, 1)
        rows = lines_of(part)
        d_gate[rows, units(n)] = (d_act * slope_kept[rows, units(n)].astype(F32)).astype(BF)
        d_up[rows, units(n)] = (d_act * gelu_kept[rows, units(n)].astype(F32)).astype(BF)
        return carry

    def back_project(part, n, carry):
        rows = lines_of(part)
        term = contract(d_gate[rows], wg[columns(n)], 1, 1)
        term += contract(d_up[rows], wu[columns(n)], 1, 1)
        h_terms[part, :, :, columns(n)] = term.astype(BF).reshape(4, half, 384)
        return carry

    def each(times, step, part):
        lax.fori_loop(0, times, functools.partial(step, part), 0)

    blocks = HID_PAD // 256

    def turn_round(part):
        rows = rows_of(part)
        summed(f_sums[part], part)
        f = ffn[rows]
        r = norm_scale(f)
        out_ref[rows] = (mid[rows] + f * r * g_out).astype(BF)
        df, gain = norm_back(f, r, g_out, cot_ref[rows].astype(F32))
        f_line[part, place.x] = df.astype(BF)
        f_gathers[part].start()
        return gain

    h_gathers[0].forward()
    h_gathers[1].start()
    h_gathers[0].finish()
    each(blocks, forward, 0)
    h_gathers[1].forward()
    each(3, project, 0)
    f_sums[0].start()
    h_gathers[1].finish()
    each(blocks, forward, 1)
    f_sums[0].middle()
    each(3, project, 1)
    f_sums[1].start()
    d_out = turn_round(0)
    f_sums[1].middle()
    h_turned[...] = jnp.transpose(h_line[...].reshape(8 * half, D))
    f_gathers[0].forward()
    d_out = d_out + turn_round(1)
    f_gathers[0].finish()
    each(blocks, backward, 0)
    f_gathers[1].forward()
    each(3, back_project, 0)
    h_sums[0].start()
    f_gathers[1].finish()
    f_turned[...] = jnp.transpose(f_line[...].reshape(8 * half, D))

    def halves_of(which):
        return pl.ds(pl.multiple_of(which * 896, 128), 896)

    def fill(target, i, which, left, right, c, add):
        term = jnp.dot(
            left[576 * i : 576 * i + 576], right[:, halves_of(which)], preferred_element_type=F32
        )
        spans = ((c, 0, 896),) if c is not None else ((0, 0, AHEAD), (1, AHEAD, 896))
        for k in range(4):
            for half, low, high in spans:
                at = (2 * i + k // 2, k % 2, half, slice(None), slice(0, high - low))
                value = term[144 * k : 144 * k + 144, low:high]
                if add:
                    value = value + target[at].astype(F32)
                target[at] = value.astype(BF)

    def fill_later(target, i, which, add):
        fill(target, i, which, h_turned, d_gate, 0, add)
        fill(target, i, which, h_turned, d_up, 1, add)

    for y in range(4):
        ahead_snd[y, :, 1, :, 896 - AHEAD :] = jnp.zeros((2, 144, 2 * AHEAD - 896), BF)
    ahead_swap = net.copy(ahead_snd, ahead_got, partner)
    swaps = [net.copy(snd.at[y], got.at[y], partner) for y in range(4)]
    ahead = FirstSums(net, place, ahead_got, AHEAD_CUT, room[24:])
    for i in range(2):
        fill(ahead_snd, i, 1 - core, f_turned, act, None, False)
    net.go(ahead_swap)
    each(blocks, backward, 1)
    h_sums[0].middle()
    ahead_swap.wait_recv()
    for i in range(2):
        fill(ahead_got, i, core, f_turned, act, None, True)
    ahead.begin()
    ahead.go_on()
    each(3, back_project, 1)
    h_sums[1].start()
    for i in range(2):
        fill_later(snd, i, 1 - core, False)
        net.go(swaps[2 * i])
        net.go(swaps[2 * i + 1])
    summed(h_sums[0], 0)
    h_sums[1].middle()
    stores = [pltpu.make_async_copy(got.at[y], sums_hbm.at[y], local.at[3 + y]) for y in range(4)]
    for i in range(2):
        swaps[2 * i].wait_recv()
        swaps[2 * i + 1].wait_recv()
        fill_later(got, i, core, True)
        stores[2 * i].start()
        stores[2 * i + 1].start()
    ahead.turn()
    summed(h_sums[1], 1)

    m, a = mid[...], attn[...]
    dm, d_ffn = norm_back(m, norm_scale(m), g_ffn, ffn[...])
    d_mid = cot_ref[...].astype(F32) + dm
    dmid_out[...] = d_mid
    da, d_post = norm_back(a, norm_scale(a), g_post, d_mid)
    da = da.astype(BF)
    dattn_out[...] = da
    dgains_out[...] = jnp.concatenate([d_post, d_ffn, d_out, jnp.zeros((5, D), F32)], axis=0)
    delta_out[...] = jnp.zeros((8, TOK), F32)
    for h in range(HEADS):
        weight = (wo_ref, wo2_ref)[h // 2]
        d_o = contract(da, weight[256 * (h % 2) : 256 * (h % 2) + 256], 1, 1).astype(BF).astype(F32)
        inverse = inv_ref[h]
        do_out[h] = (d_o * jnp.concatenate([inverse, inverse], axis=1)).astype(BF)
        delta = jnp.sum(d_o * o_ref[h], axis=1, keepdims=True) * inverse
        delta_out[h : h + 1] = jnp.transpose(delta)[:1]
    y_line, z_line = ahead.lines
    y_line.finish(ahead_y.at[0], ahead_y.at[1])
    z_line.finish(ahead_z.at[pl.ds(0, 2)], ahead_z.at[pl.ds(2, 2)])
    for store in stores:
        store.wait()
    net.drain()


def feed_forward(args, call_id):
    quarter = (TOK // 4, D)
    shape = jax.ShapeDtypeStruct
    every = (4, 2, 2, 144, LATER)
    every_ahead = (4, 2, 2, 144, AHEAD)
    lines = 4 * TOK
    anywhere = pl.BlockSpec(memory_space=pl.ANY)
    unit_rows = [pltpu.VMEM((lines, HID_PAD), BF)] * 5
    return pl.pallas_call(
        feed_kernel,
        out_shape=(
            shape((TOK, D), BF),
            shape((TOK, D), F32),
            shape((TOK, D), BF),
            shape((HEADS, TOK, HD), BF),
            shape((8, TOK), F32),
            shape((8, D), F32),
            shape((2, 2, 144, AHEAD_CUT), BF),
            shape((4, 144, AHEAD - AHEAD_CUT), BF),
            shape(every, BF),
        ),
        in_specs=[IN_VMEM] * 9 + [anywhere] * 3,
        out_specs=[IN_VMEM] * 8 + [anywhere],
        scratch_shapes=[
            pltpu.VMEM((D, HID_PAD), BF),
            pltpu.VMEM((D, HID_PAD), BF),
            pltpu.VMEM((HID_PAD, D), BF),
            pltpu.VMEM((2, 4, TOK // 2, D), BF),
            pltpu.VMEM((2, 4, TOK // 2, D), BF),
            pltpu.VMEM((D, lines), BF),
            pltpu.VMEM((D, lines), BF),
            *unit_rows,
            pltpu.VMEM((2, 4, TOK // 2, D), BF),
            pltpu.VMEM((2, 4, TOK // 2, D), BF),
            pltpu.VMEM(every_ahead, BF),
            pltpu.VMEM(every_ahead, BF),
            pltpu.VMEM(every, BF),
            pltpu.VMEM(every, BF),
            pltpu.VMEM((TOK, D), F32),
            pltpu.VMEM((TOK, D), F32),
            pltpu.VMEM((TOK, D), F32),
            *(RingScatter.room_shapes(quarter, quarter) * 4),
            *FirstSums.room_shapes(AHEAD_CUT, AHEAD - AHEAD_CUT),
            *sems(72),
            pltpu.SemaphoreType.DMA((7,)),
        ],
        compiler_params=params(call_id),
    )(*args)


class FirstSums:
    def __init__(self, net, place, sums, cut, rooms, here=None, marks=None):
        left, right = pl.ds(0, cut), pl.ds(cut, sums.shape[-1] - cut)

        def y_spot(half):
            return stepped(place, "y", lambda j: sums.at[j, half, :, :, left])

        def z_spot(half):
            return stepped(
                place,
                "z",
                lambda j: sums.at[pl.ds(2 * half, 2), lax.div(j, 2), lax.rem(j, 2), :, right],
            )

        self.loads = []
        self.lines = []
        for i, (axis, spot) in enumerate((("y", y_spot), ("z", z_spot))):
            near = (None, None)
            if here is not None:
                near = ({}, {})
                for k, (half, by) in enumerate(((0, 1), (1, 3), (0, 0), (1, 0))):
                    target = here[i].at[k]
                    near[half][by] = target
                    self.loads.append(
                        pltpu.make_async_copy(spot(half)(by), target, marks.at[8 + 4 * i + k])
                    )
                near = (near[0].get, near[1].get)
            room = rooms[6 * i : 6 * i + 6]
            self.lines.append(RingScatter(net, place, axis, spot(0), spot(1), room, *near))

    @staticmethod
    def room_shapes(cut, rest):
        return [
            *RingScatter.room_shapes((2, 144, cut), (2, 144, cut)),
            *RingScatter.room_shapes((2, 144, rest), (2, 144, rest)),
        ]

    def begin(self):
        for load in self.loads:
            load.start()
        for line in self.lines:
            line.start_far()

    def go_on(self):
        for line in self.lines:
            line.start_right()
            line.start_left()

    def turn(self):
        for load in self.loads:
            load.wait()
        for line in self.lines:
            line.middle()


class WeightSums:
    def __init__(self, place, net, sums, late, refs, marks):
        y_here, z_here, y1, z1, z2, y2, snd, late_snd, rcv, late_rcv, *rooms = refs
        self.late_snd, self.late_rcv = late_snd, late_rcv
        self.place, self.late, self.snd, self.rcv, self.marks = place, late, snd, rcv, marks
        self.y1, self.z1, self.y2, self.z2 = y1, z1, y2, z2
        self.x_hi, self.x_lo = lax.div(place.x, 2), lax.rem(place.x, 2)
        self.friends = []
        for k in range(1, 16):
            spot = lax.rem(self.x_hi * 8 + place.z * 2 + place.core + k, 16)
            x, z = lax.div(spot, 8) * 2 + self.x_lo, lax.rem(lax.div(spot, 2), 4)
            self.friends.append(place.device(x=x, z=z, core=lax.rem(spot, 2)))

        self.first = FirstSums(net, place, sums, LATER_CUT, rooms[:12], (y_here, z_here), marks[2])

        def then_z(j):
            return y1.at[lax.div(j, 2), lax.rem(j, 2)]

        self.z_second = RingScatter(
            net,
            place,
            "z",
            stepped(place, "z", lambda j: then_z(j).at[:, pl.ds(0, 384)]),
            stepped(place, "z", lambda j: then_z(j).at[:, pl.ds(384, 384)]),
            rooms[12:18],
        )
        self.y_second = RingScatter(
            net,
            place,
            "y",
            stepped(place, "y", lambda j: z1.at[j, :, pl.ds(0, 384)]),
            stepped(place, "y", lambda j: z1.at[j, :, pl.ds(384, 256)]),
            rooms[18:24],
        )

    @staticmethod
    def scratch():
        rest = HALF - CUT
        return [
            pltpu.VMEM((4, 2, 144, LATER_CUT), BF),
            pltpu.VMEM((4, 2, 144, LATER - LATER_CUT), BF),
            pltpu.VMEM((2, 2, 144, CUT), BF),
            pltpu.VMEM((4, 144, rest), BF),
            pltpu.VMEM((144, CUT), F32),
            pltpu.VMEM((144, rest), F32),
            pltpu.VMEM((8, 16, HALF + 256), BF),
            pltpu.VMEM((8, 16, 256), BF),
            pltpu.VMEM((8, 16, HALF + 256), BF),
            pltpu.VMEM((8, 16, 256), BF),
            *FirstSums.room_shapes(LATER_CUT, LATER - LATER_CUT),
            *RingScatter.room_shapes((144, 384), (144, 384)),
            *RingScatter.room_shapes((144, 384), (144, 256)),
        ]

    def next(self):
        y_line, z_line = self.first.lines
        after = pl.ds(AHEAD_CUT, LATER_CUT)
        y_line.finish(self.y1.at[0, :, :, after], self.y1.at[1, :, :, after])
        self.z_second.start()
        after = pl.ds(AHEAD - AHEAD_CUT, LATER - LATER_CUT)
        z_line.finish(self.z1.at[pl.ds(0, 2), :, after], self.z1.at[pl.ds(2, 2), :, after])
        self.y_second.start()

    def turn_again(self):
        self.z_second.middle()
        self.y_second.middle()

    def last(self):
        z2, y2 = self.z2, self.y2
        self.z_second.finish(z2.at[:, pl.ds(0, 384)], z2.at[:, pl.ds(384, 384)])
        self.y_second.finish(y2.at[:, pl.ds(0, 384)], y2.at[:, pl.ds(384, 256)])
        total = jnp.concatenate([z2[...], y2[...]], axis=1)
        self.pack(total, self.snd)
        self.exchange(self.snd, self.rcv, 0)

    def send_late(self):
        self.pack(self.late[...], self.late_snd)
        self.exchange(self.late_snd, self.late_rcv, 8)

    @staticmethod
    def pack(total, snd):
        width = total.shape[1]
        count = width // 128
        for k in range(8):
            extra = total[18 * k + 16 : 18 * k + 18]
            pieces = [extra[:, 128 * n : 128 * n + 128] for n in range(count)]
            snd[k, :, :width] = total[18 * k : 18 * k + 16].astype(BF)
            for n in range(0, count, 8):
                group = pieces[n : n + 8]
                if len(group) < 8:
                    group.append(jnp.zeros((16 - 2 * len(group), 128), F32))
                at = width + 16 * n
                snd[k, :, at : at + 128] = jnp.concatenate(group, axis=0).astype(BF)

    def exchange(self, snd, rcv, mark):
        place = self.place
        send, recv, here = self.marks
        row_half = lax.div(place.z, 2)
        self.slot = self.x_hi * 4 + place.core * 2 + lax.rem(place.z, 2)
        self.own = place.z * 2 + place.core
        self.stays = row_half == self.x_hi
        for k in range(8):
            copy = pltpu.make_async_remote_copy(
                src_ref=snd.at[k],
                dst_ref=rcv.at[self.slot],
                send_sem=send.at[mark + k],
                recv_sem=recv.at[mark + self.slot],
                device_id=place.device(x=row_half * 2 + self.x_lo, z=k // 2, core=k % 2),
                device_id_type=MESH,
            )
            is_here = self.stays & (self.own == k)

            @pl.when(jnp.logical_not(is_here))
            def _(copy=copy):
                copy.start()

            @pl.when(is_here)
            def _(k=k):
                keep = pltpu.make_async_copy(snd.at[k], rcv.at[self.slot], here.at[0])
                keep.start()
                keep.wait()

    def arrive(self):
        send, recv, _ = self.marks
        for mark, snd, rcv in ((0, self.snd, self.rcv), (8, self.late_snd, self.late_rcv)):
            for m in range(8):
                arrival = pltpu.make_async_remote_copy(
                    src_ref=snd.at[m],
                    dst_ref=rcv.at[m],
                    send_sem=send.at[mark + m],
                    recv_sem=recv.at[mark + m],
                    device_id=self.place.partner(),
                    device_id_type=MESH,
                )

                @pl.when(jnp.logical_not(self.stays & (self.slot == m)))
                def _(arrival=arrival):
                    arrival.wait_recv()

                @pl.when(jnp.logical_not(self.stays & (self.own == m)))
                def _(arrival=arrival):
                    arrival.wait_send()


def last_kernel(
    home_ref,
    late_ref,
    top_ref,
    low_ref,
    gains_ref,
    y_ref,
    dx_ref,
    y_out,
    dx_out,
    dwq_out,
    dwk_out,
    dwv_out,
    dwo_out,
    dwg_out,
    dwu_out,
    dwd_out,
    *gain_outs,
):
    y_out[...] = y_ref[...]
    dx_out[...] = dx_ref[...]

    def rows_at(ref, slot, n):
        spare = (HALF if ref is home_ref else 128) + 128 * (n // 8)
        more = ref[slot, :, spare : spare + 128].astype(F32)[2 * (n % 8) : 2 * (n % 8) + 2]
        return jnp.concatenate(
            [ref[slot, :, 128 * n : 128 * n + 128].astype(F32), more], axis=0
        )

    def tile(x_hi, which, n):
        core, n = n // 7, n % 7
        if which < 2:
            c, at = which, AHEAD_CUT + 128 * n if n < 4 else AHEAD + 128 * n
        else:
            c, n = n // 4, n % 4
            at = 128 * n if n < 2 else CUT + 128 * (n - 2)
        return rows_at(home_ref, x_hi * 4 + core * 2 + c, at // 128)

    for which, out in enumerate((dwg_out, dwu_out, dwd_out)):
        for n in range(27):
            value = None
            for x_hi in range(2):
                if 0 <= n - 13 * x_hi < 14:
                    term = tile(x_hi, which, n - 13 * x_hi)
                    value = term if value is None else value + term
            span = slice(128 * n, 128 * n + 128)
            out[:, span] = value
    for k in range(4):
        span = slice(128 * k, 128 * k + 128)
        dwo_out[:, span] = rows_at(late_ref, 2 * k, 0)
        dwq_out[:, span] = rows_at(late_ref, 2 * k + 1, 0)
    for which in range(2):
        for j in range(4):
            out = (dwk_out, dwv_out)[j // 2]
            for y in range(4):
                span = slice(128 * (j % 2), 128 * (j % 2) + 128)
                at = 576 * which + 144 * y
                out[at : at + 80, span] = top_ref[which, j, y].astype(F32)
                out[at + 80 : at + 144, span] = low_ref[which, j, y].astype(F32)
    for out, row, start in zip(gain_outs, (0, 4, 4, 1, 2, 3), (0, 0, HD, 0, 0, 0)):
        size = out.shape[0]
        out[...] = gains_ref[row : row + 1, start : start + size].reshape(size)


def last_layout(*args):
    shape = jax.ShapeDtypeStruct
    return pl.pallas_call(
        last_kernel,
        out_shape=(
            shape((TOK, D), BF),
            shape((TOK, D), BF),
            shape((18, 2 * HD), F32),
            shape((D, HD), F32),
            shape((D, HD), F32),
            shape((18, 2 * HD), F32),
            shape((18, 2 * HID), F32),
            shape((18, 2 * HID), F32),
            shape((18, 2 * HID), F32),
            *(shape((size,), F32) for size in (D, HD, HD, D, D, D)),
        ),
        in_specs=[IN_VMEM] * len(args),
        out_specs=[IN_VMEM] * 15,
        compiler_params=pltpu.CompilerParams(vmem_limit_bytes=VMEM_BYTES),
    )(*args)


def angles(token_pos):
    middle = HD // 2
    frequency = THETA ** (-2.0 * jnp.arange(middle, dtype=F32) / HD)
    turned = token_pos.astype(F32)[:, None] * frequency[None, :]
    return (jnp.cos(turned), jnp.sin(turned))


def shards(
    layer_input,
    segment_ids,
    positions,
    w_query,
    w_key,
    w_value,
    w_out,
    w_gate,
    w_up,
    w_down,
    norm_attn,
    norm_query,
    norm_key,
    norm_post,
    norm_ffn,
    norm_out,
    cotangent,
):
    sp, tp = lax.axis_index("sp"), lax.axis_index("tp")
    cosine, sine = angles(lax.dynamic_slice_in_dim(positions, (sp * 2 + tp) * TOK, TOK))
    segments = segment_ids.reshape(128, 128)
    key_rows = jnp.asarray(KEY_TOKENS)
    kv_all, q_all, wq_other, wo_other, o_heads, inverse, q_pre, k_pre, h_attn = attention_forward(
        (
            layer_input,
            norm_attn,
            norm_query,
            norm_key,
            w_query,
            w_key,
            w_value,
            w_out,
            cosine,
            sine,
            segments,
            key_rows,
        ),
        2,
    )
    (
        layer_output,
        d_mid,
        d_attn,
        d_heads,
        delta,
        d_gains,
        ahead_y,
        ahead_z,
        sums,
    ) = feed_forward(
        (
            layer_input,
            o_heads,
            inverse,
            w_out,
            wo_other,
            norm_post,
            norm_ffn,
            norm_out,
            cotangent,
            w_gate,
            w_up,
            w_down,
        ),
        6,
    )
    d_input, home, late, w_top, w_low, gains = attention_backward(
        (kv_all, sums, ahead_y, ahead_z, w_query, wq_other, w_key, w_value),
        (
            q_all,
            d_heads,
            delta,
            key_rows,
            segments,
            q_pre,
            k_pre,
            cosine,
            sine,
            h_attn,
            d_attn,
            o_heads,
            layer_input,
            d_mid,
            norm_attn,
            norm_query,
            norm_key,
            d_gains,
        ),
        8,
    )
    y, dx, d_wq, d_wk, d_wv, d_wo, d_wg, d_wu, d_wd, *d_norms = last_layout(
        home, late, w_top, w_low, gains, layer_output, d_input
    )
    return (y, dx, d_wq, d_wk, d_wv, d_wo.T, d_wg, d_wu, d_wd.T, *d_norms)


def solution(mesh):
    rows = P(("sp", "tp"), None)
    in_specs = (
        rows,
        P(),
        P(),
        P(None, "tp"),
        P(),
        P(),
        P("tp", None),
        P(None, "tp"),
        P(None, "tp"),
        P("tp", None),
        P(),
        P(),
        P(),
        P(),
        P(),
        P(),
        rows,
    )
    out_specs = (
        rows,
        rows,
        P("sp", "tp"),
        P(),
        P(),
        P("tp", "sp"),
        P("sp", "tp"),
        P("sp", "tp"),
        P("tp", "sp"),
        P(),
        P(),
        P(),
        P(),
        P(),
        P(),
    )
    return jax.shard_map(shards, mesh=mesh, in_specs=in_specs, out_specs=out_specs, check_vma=False)
```

```python
import functools

import jax
import jax.numpy as jnp
import numpy as np
from jax import lax
from jax.experimental import pallas as pl
from jax.experimental.pallas import tpu as pltpu
from jax.sharding import PartitionSpec as P

EPS = 1e-06
THETA = 1000000.0
BF = jnp.bfloat16
F32 = jnp.float32
MESH = pl.DeviceIdType.MESH
IN_VMEM = pl.BlockSpec(memory_space=pltpu.VMEM)
VMEM_BYTES = 58 * 1024 * 1024

TOK = 128
D = 1152
HD = 256
HEADS = 4
ROWS = 2 * TOK
HID = 1728
HID_PAD = 1792
CUT = 768
HALF = 1408
STRIPE = TOK // 4
KEYS = 16 * STRIPE


class Place:
    def __init__(self):
        sp = lax.axis_index("sp")
        self.core = lax.rem(sp, 2)
        self.z = lax.rem(lax.div(sp, 2), 4)
        self.y = lax.div(sp, 16)
        self.x = lax.rem(lax.div(sp, 8), 2) * 2 + lax.axis_index("tp")

    def device(self, **moved):
        x, y, z, core = (moved.get(name, getattr(self, name)) for name in ("x", "y", "z", "core"))
        return (((y * 2 + lax.div(x, 2)) * 4 + z) * 2 + core, lax.rem(x, 2))

    def step(self, axis, by):
        return lax.rem(getattr(self, axis) + by, 4)

    def toward(self, axis, by):
        return self.device(**{axis: self.step(axis, by)})

    def partner(self):
        return self.device(core=1 - self.core)


class Net:
    def __init__(self, send, recv):
        self.send, self.recv, self.used, self.started = send, recv, 0, []

    def copy(self, source, target, device):
        at = self.used
        self.used += 1
        return pltpu.make_async_remote_copy(
            src_ref=source,
            dst_ref=target,
            send_sem=self.send.at[at],
            recv_sem=self.recv.at[at],
            device_id=device,
            device_id_type=MESH,
        )

    def go(self, copy):
        copy.start()
        self.started.append(copy)

    def settle(self, copy):
        copy.wait_send()
        self.started = [other for other in self.started if other is not copy]

    def drain(self):
        for copy in self.started:
            copy.wait_send()
        self.started = []


def greet(devices, meanwhile=None):
    barrier = pltpu.get_barrier_semaphore()
    for device in devices:
        pl.semaphore_signal(barrier, inc=1, device_id=device, device_id_type=MESH)
    if meanwhile is not None:
        meanwhile()
    pl.semaphore_wait(barrier, len(devices))


def ring(place, axis):
    return [place.toward(axis, 1), place.toward(axis, 3)]


class RingGather:
    def __init__(self, net, place, axis, view, lo, hi):
        self.net = net
        me, nxt, prev = getattr(place, axis), place.step(axis, 1), place.step(axis, 3)
        right, left = ring(place, axis)
        self.to_right = net.copy(view(me), view(me), right)
        self.to_left = net.copy(view(me), view(me), left)
        self.on_right = net.copy(lo(prev), lo(prev), right)
        self.on_left = net.copy(hi(nxt), hi(nxt), left)

    def start(self):
        self.net.go(self.to_right)
        self.net.go(self.to_left)

    def forward(self):
        self.to_right.wait_recv()
        self.net.go(self.on_right)
        self.to_left.wait_recv()
        self.net.go(self.on_left)

    def finish(self):
        self.on_right.wait_recv()
        self.on_left.wait_recv()


class Direct:
    def __init__(self, net, place, axis, source, landing):
        self.net = net
        self.copies = [
            net.copy(
                source(place.step(axis, by)), landing(getattr(place, axis)), place.toward(axis, by)
            )
            for by in (2, 1, 3)
        ]

    def start(self):
        for copy in self.copies:
            self.net.go(copy)

    def wait(self):
        for copy in self.copies:
            copy.wait_recv()


def by_rows(ref, act):
    *lead, rows, _ = ref.shape
    block = next(size for size in (64, 48, 32, 16) if rows % size == 0)
    for spot in np.ndindex(*lead):

        def one(i, carry, spot=spot):
            act(spot, pl.ds(pl.multiple_of(i * block, block), block))
            return carry

        lax.fori_loop(0, rows // block, one, 0)


def add_to(target, other):
    def act(spot, rows):
        at = (*spot, rows, slice(None))
        target[at] = (target[at].astype(F32) + other[at].astype(F32)).astype(target.dtype)

    by_rows(target, act)


def sum_to(target, others):
    def act(spot, rows):
        at = (*spot, rows, slice(None))
        total = others[0][at].astype(F32)
        for other in others[1:]:
            total = total + other[at].astype(F32)
        target[at] = total.astype(target.dtype)

    by_rows(target, act)


def stepped(place, axis, view):
    return lambda by: view(place.step(axis, by))


class RingScatter:
    def __init__(self, net, place, axis, lo, hi, room, lo_here=None, hi_here=None):
        self.net, self.lo, self.hi = net, lo_here or lo, hi_here or hi
        right, left = ring(place, axis)
        self.lo1, self.lo_l, self.lo_r, self.hi1, self.hi_l, self.hi_r = room
        self.a = net.copy(lo(2), self.lo1, right)
        self.b = net.copy(hi(2), self.hi1, left)
        self.c_hi = net.copy(hi(1), self.hi_l, right)
        self.d_lo = net.copy(lo(3), self.lo_r, left)
        self.c_lo = net.copy(self.lo1, self.lo_l, right)
        self.d_hi = net.copy(self.hi1, self.hi_r, left)

    def start_far(self):
        self.net.go(self.a)
        self.net.go(self.b)

    def start_right(self):
        self.net.go(self.c_hi)

    def start_left(self):
        self.net.go(self.d_lo)

    def start(self):
        self.start_far()
        self.start_right()
        self.start_left()

    def middle_right(self):
        self.a.wait_recv()
        add_to(self.lo1, self.lo(1))
        self.net.go(self.c_lo)

    def middle_left(self):
        self.b.wait_recv()
        add_to(self.hi1, self.hi(3))
        self.net.go(self.d_hi)

    def middle(self):
        self.middle_right()
        self.middle_left()

    def finish(self, lo_out, hi_out):
        self.c_hi.wait_recv()
        self.d_hi.wait_recv()
        sum_to(hi_out, [self.hi(0), self.hi_l, self.hi_r])
        self.d_lo.wait_recv()
        self.c_lo.wait_recv()
        sum_to(lo_out, [self.lo(0), self.lo_l, self.lo_r])

    @staticmethod
    def room_shapes(lo_shape, hi_shape):
        return [pltpu.VMEM(lo_shape, BF)] * 3 + [pltpu.VMEM(hi_shape, BF)] * 3


def params(call_id):
    return pltpu.CompilerParams(
        collective_id=call_id, has_side_effects=True, vmem_limit_bytes=VMEM_BYTES
    )


def sems(count):
    return [pltpu.SemaphoreType.DMA((count,)), pltpu.SemaphoreType.DMA((count,))]


class WeightSwap:
    def __init__(self, net, place, w_ref, other_ref):
        self.net = net
        quarter = w_ref.shape[0] // 4
        right, left = ring(place, "x")

        def rows(ref, side):
            return ref.at[pl.ds(pl.multiple_of((2 * side + place.core) * quarter, 16), quarter)]

        self.first = [
            net.copy(rows(w_ref, side), rows(other_ref, side), (left, right)[side])
            for side in (0, 1)
        ]
        self.trades = [
            net.copy(rows(other_ref, side), rows(other_ref, side), place.partner())
            for side in (0, 1)
        ]

    def start(self):
        for copy in self.first:
            self.net.go(copy)

    def forward(self):
        for copy, trade in zip(self.first, self.trades):
            copy.wait_recv()
            self.net.go(trade)

    def finish(self):
        for trade in self.trades:
            trade.wait_recv()


def key_lines(place, ref):
    def stage(axis, first, at):
        return (
            axis,
            lambda j: ref.at[(pl.ds(first, 2), *at(j))],
            lambda j: ref.at[(first, *at(j))],
            lambda j: ref.at[(first + 1, *at(j))],
        )

    every = slice(None)
    return (
        (stage("x", 0, lambda j: (place.z, j)), stage("z", 0, lambda j: (j,))),
        (stage("z", 2, lambda j: (j, place.x)), stage("x", 2, lambda j: (every, j))),
    )


def key_tokens():
    z, x, row = np.meshgrid(np.arange(4), np.arange(4), np.arange(STRIPE), indexing="ij")
    return ((x // 2) * 2048 + z * 512 + (x % 2) * 128 + row).reshape(1, KEYS).astype(np.int32)


KEY_TOKENS = key_tokens()


def first_key(place, y):
    return y * 4096 + place.core * 256 + STRIPE * place.y


def contract(left, right, left_dim, right_dim):
    return lax.dot_general(
        left, right, (((left_dim,), (right_dim,)), ((), ())), preferred_element_type=F32
    )


def turn(u, cosine, sine):
    half = HD // 2
    low, high = u[:, :half], u[:, half:]
    return jnp.concatenate([low * cosine - high * sine, high * cosine + low * sine], axis=1)


def row_bounds(place, segments, y):
    at = (y * 2 + lax.div(place.x, 2)) * 16 + place.z * 4 + lax.rem(place.x, 2)
    rows = jnp.concatenate([segments[pl.ds(at, 1)], segments[pl.ds(at + 2, 1)]], axis=1)
    every = segments[...]
    first = jnp.zeros((1, ROWS), jnp.int32)
    for k in range(1, 4):
        below = jnp.sum((every < k).astype(F32), axis=0, keepdims=True)
        below = jnp.sum(below, axis=1, keepdims=True).astype(jnp.int32)
        first = jnp.where(rows == k, below, first)
    lane = lax.broadcasted_iota(jnp.int32, (1, ROWS), 1)
    last = at * TOK + lane + jnp.where(lane < TOK, 0, TOK)
    return first, last


def down(row):
    return jnp.concatenate(
        [
            jnp.transpose(jnp.broadcast_to(row[:, 128 * i : 128 * i + 128], (128, 128)))
            for i in range(row.shape[1] // 128)
        ],
        axis=0,
    )


def across(ref):
    return ref[...].reshape(1, ref.shape[0])


def norm_scale(v):
    return lax.rsqrt(jnp.mean(v * v, axis=-1, keepdims=True) + EPS)


def norm_back(v, r, gain, e):
    eg = e * gain
    dv = r * eg - v * (r * r * r) * jnp.mean(eg * v, axis=-1, keepdims=True)
    return dv, jnp.sum(e * v * r, axis=0, keepdims=True)


def forward_kernel(
    x_ref,
    g_attn,
    g_query,
    g_key,
    wq_ref,
    wk_ref,
    wv_ref,
    w_hbm,
    cos_ref,
    sin_ref,
    segments,
    key_ref,
    kv_hbm,
    q_all,
    wq_other,
    w_other,
    o_out,
    inv_out,
    q_pre,
    k_pre,
    h_out,
    buf,
    kv_own,
    o_sum,
    l_sum,
    o_snd,
    o_part,
    o_got,
    o_done,
    l_mine,
    l_got,
    l_core,
    *rest,
):
    *room, send, recv, local = rest
    place, net = Place(), Net(send, recv)
    core = place.core
    partner = place.partner()
    mine = pl.ds(pl.multiple_of(core * TOK, TOK), TOK)
    theirs = pl.ds(pl.multiple_of((1 - core) * TOK, TOK), TOK)

    def keys_and_values():
        xf = x_ref[...].astype(F32)
        h = (xf * norm_scale(xf) * across(g_attn)).astype(BF)
        h_out[...] = h
        k = jnp.dot(h, wk_ref[...], preferred_element_type=F32)
        k_pre[...] = k
        k = turn(k * norm_scale(k) * across(g_key), cos_ref[...], sin_ref[...]).astype(BF)
        v = jnp.dot(h, wv_ref[...], preferred_element_type=F32).astype(BF)
        for j in range(4):
            kv_own[j, :, :HD] = k[STRIPE * j : STRIPE * j + STRIPE]
            kv_own[j, :, HD:] = v[STRIPE * j : STRIPE * j + STRIPE]
        buf[place.y, place.z, place.x] = kv_own[place.y]

    greet(
        ring(place, "x")
        + ring(place, "y")
        + ring(place, "z")
        + [partner, place.toward("y", 2)],
        keys_and_values,
    )
    swap_wq = WeightSwap(net, place, wq_ref, wq_other)
    swap_w = WeightSwap(net, place, w_hbm, w_other)
    stripes = Direct(
        net,
        place,
        "y",
        lambda j: kv_own.at[j],
        lambda j: buf.at[j, place.z, place.x],
    )
    stripes.start()
    swap_wq.start()
    (first_a, then_a), (first_b, then_b) = (
        [RingGather(net, place, *stage) for stage in part] for part in key_lines(place, buf)
    )
    q_ring = RingGather(
        net,
        place,
        "y",
        lambda j: q_all.at[j, :, mine],
        lambda j: q_all.at[j, pl.ds(0, 2), mine],
        lambda j: q_all.at[j, pl.ds(2, 2), mine],
    )

    def block_of(by):
        return q_all.at[place.step("y", by), :, mine]

    q_core = [net.copy(block_of(by), block_of(by), partner) for by in range(4)]

    def queries(which, w):
        q = jnp.dot(h_out[...], w[...], preferred_element_type=F32)
        for i in range(2):
            u = q[:, HD * i : HD * i + HD]
            q_pre[2 * which + i] = u
            u = turn(u * norm_scale(u) * across(g_query), cos_ref[...], sin_ref[...])
            q_all[place.y, 2 * which + i, mine] = (u.astype(BF).astype(F32) * HD**-0.5).astype(BF)

    queries(0, wq_ref)
    stripes.wait()
    first_a.start()
    first_b.start()
    swap_wq.forward()
    first_a.forward()
    first_b.forward()
    swap_wq.finish()
    queries(1, wq_other)
    q_ring.start()
    net.go(q_core[0])
    first_a.finish()
    then_a.start()
    first_b.finish()
    then_b.start()
    q_ring.forward()
    net.go(q_core[1])
    net.go(q_core[3])
    then_a.forward()
    then_b.forward()
    q_ring.finish()
    net.go(q_core[2])
    then_a.finish()
    then_b.finish()
    swap_w.start()
    store = pltpu.make_async_copy(buf, kv_hbm, local.at[0])
    store.start()

    o_core = [net.copy(o_snd.at[by], o_got.at[by], partner) for by in range(4)]

    def attend(by):
        y = place.step("y", by)
        q_core[by].wait_recv()
        first, last = (down(row) for row in row_bounds(place, segments, y))

        keys = buf[:, :, :, :, :HD].reshape(4 * KEYS, HD)
        values = buf[:, :, :, :, HD:].reshape(4 * KEYS, HD)
        token = jnp.concatenate([key_ref[...] + first_key(place, j) for j in range(4)], axis=1)
        allowed = jnp.concatenate(
            [
                (token[:, 128 * i : 128 * i + 128] <= last)
                & (token[:, 128 * i : 128 * i + 128] >= first)
                for i in range(4 * KEYS // 128)
            ],
            axis=1,
        )
        for h in range(HEADS):
            weights = jnp.exp(contract(q_all[y, h], keys, 1, 1))
            weights = jnp.where(allowed, weights, 0.0)
            l_sum[by, h] = sum(
                weights[:, 128 * i : 128 * i + 128] for i in range(4 * KEYS // 128)
            )
            o_sum[by, h] = jnp.dot(weights.astype(BF), values, preferred_element_type=F32)
        for h in range(HEADS):
            o_snd[by, h] = o_sum[by, h, theirs].astype(BF)
            o_part[by, h] = o_sum[by, h, mine].astype(BF)
            total = jnp.sum(l_sum[by, h], axis=1, keepdims=True)
            l_mine[y, h : h + 1] = jnp.transpose(jnp.broadcast_to(total, (ROWS, 128)))[:1]
        net.go(o_core[by])

    def both_cores(by):
        o_core[by].wait_recv()
        add_to(o_part.at[by], o_got.at[by])

    o_ring = RingScatter(
        net,
        place,
        "y",
        lambda by: o_part.at[by, pl.ds(0, 2)],
        lambda by: o_part.at[by, pl.ds(2, 2)],
        room,
    )
    attend(0)
    attend(2)
    attend(1)
    both_cores(2)
    o_ring.start_far()
    swap_w.forward()
    attend(3)
    l_swap = Direct(net, place, "y", lambda j: l_mine.at[j], lambda j: l_got.at[j])
    l_swap.start()
    l_got[place.y] = l_mine[place.y]
    both_cores(1)
    o_ring.start_right()
    o_ring.middle_right()
    both_cores(3)
    o_ring.start_left()
    o_ring.middle_left()
    both_cores(0)
    swap_w.finish()
    l_swap.wait()
    l_core[core] = (l_got[0] + l_got[1]) + (l_got[2] + l_got[3])
    l_over = net.copy(l_core.at[core], l_core.at[core], partner)
    net.go(l_over)
    l_over.wait_recv()
    total = l_core[0] + l_core[1]
    inverse = 1.0 / jnp.where(core == 0, total[:, :TOK], total[:, TOK:])
    o_ring.finish(o_done.at[pl.ds(0, 2)], o_done.at[pl.ds(2, 2)])
    for h in range(HEADS):
        scale = down(inverse[h : h + 1])
        o_out[h] = o_done[h] * jnp.concatenate([scale, scale], axis=1)
        inv_out[h] = scale
    store.wait()
    net.drain()


def attention_forward(args, call_id):
    shape = jax.ShapeDtypeStruct
    anywhere = pl.BlockSpec(memory_space=pl.ANY)
    halves = (2, TOK, HD)
    return pl.pallas_call(
        forward_kernel,
        out_shape=(
            shape((4, 4, 4, STRIPE, 2 * HD), BF),
            shape((4, HEADS, ROWS, HD), BF),
            shape((D, 2 * HD), BF),
            shape((2 * HD, D), BF),
            shape((HEADS, TOK, HD), F32),
            shape((HEADS, TOK, 128), F32),
            shape((HEADS, TOK, HD), F32),
            shape((TOK, HD), F32),
            shape((TOK, D), BF),
        ),
        in_specs=[IN_VMEM] * 7 + [anywhere] + [IN_VMEM] * 4,
        out_specs=[anywhere] + [IN_VMEM] * 2 + [anywhere] + [IN_VMEM] * 5,
        scratch_shapes=[
            pltpu.VMEM((4, 4, 4, STRIPE, 2 * HD), BF),
            pltpu.VMEM((4, STRIPE, 2 * HD), BF),
            pltpu.VMEM((4, HEADS, ROWS, HD), F32),
            pltpu.VMEM((4, HEADS, ROWS, 128), F32),
            pltpu.VMEM((4, HEADS, TOK, HD), BF),
            pltpu.VMEM((4, HEADS, TOK, HD), BF),
            pltpu.VMEM((4, HEADS, TOK, HD), BF),
            pltpu.VMEM((HEADS, TOK, HD), F32),
            pltpu.VMEM((4, 8, ROWS), F32),
            pltpu.VMEM((4, 8, ROWS), F32),
            pltpu.VMEM((2, 8, ROWS), F32),
            *RingScatter.room_shapes(halves, halves),
            *sems(64),
            pltpu.SemaphoreType.DMA((1,)),
        ],
        compiler_params=params(call_id),
    )(*args)


def kept_head(place, j):
    return jnp.where(lax.rem(j, 2) == lax.rem(place.x, 2), 0, 2) + lax.div(j, 2)


def turn_back(e, cosine, sine):
    half = HD // 2
    low, high = e[:, :half], e[:, half:]
    return jnp.concatenate([low * cosine + high * sine, high * cosine - low * sine], axis=1)


def backward_kernel(
    kv_hbm,
    sums_hbm,
    wq_hbm,
    wq2_hbm,
    wk_hbm,
    wv_hbm,
    q_all,
    do_all,
    delta_all,
    key_ref,
    segments,
    q_pre,
    k_pre,
    cos_ref,
    sin_ref,
    h_ref,
    da_ref,
    o_ref,
    x_ref,
    dmid_ref,
    g_attn,
    g_query,
    g_key,
    gains_ref,
    dx_out,
    home_out,
    late_out,
    w_top,
    w_low,
    gains_out,
    buf,
    wq,
    wq2,
    wk,
    wv,
    tokens,
    grads,
    fin,
    fin_got,
    dq_sum,
    dq_snd,
    dq_part,
    dq_got,
    dq_done,
    h_line,
    da_line,
    turned,
    o_line,
    dq_line,
    dq_own,
    o_own,
    late_all,
    late_got,
    late_y,
    late_z,
    gain_got,
    kv_own,
    kv_line,
    turned_other,
    w_got,
    w_y,
    w_z,
    *rest,
):
    rooms, dq_rooms, late_rooms, rest = rest[:24], rest[24:30], rest[30:42], rest[42:]
    *weight_refs, send, recv, send2, recv2, here = rest
    place, net = Place(), Net(send, recv)
    core, partner = place.core, place.partner()
    w_loads = [
        pltpu.make_async_copy(source, target, here.at[1 + i])
        for i, (source, target) in enumerate(
            (
                (kv_hbm, buf),
                (wq_hbm, wq),
                (wq2_hbm, wq2),
                (wk_hbm, wk),
                (wv_hbm, wv),
            )
        )
    ]
    for load in w_loads:
        load.start()
    weights = WeightSums(place, net, sums_hbm, late_z, weight_refs, (send2, recv2, here))
    across_x = [place.device(x=place.step("x", by), core=1 - core) for by in (1, 3)]
    greet(
        weights.friends
        + ring(place, "x")
        + ring(place, "y")
        + across_x
        + [place.toward("y", 2)]
    )
    mine = pl.ds(pl.multiple_of(core * TOK, TOK), TOK)
    theirs = pl.ds(pl.multiple_of((1 - core) * TOK, TOK), TOK)
    half = TOK // 2

    def line_of(rows):
        return RingGather(
            net,
            place,
            "x",
            lambda j: rows.at[j],
            lambda j: rows.at[j, pl.ds(0, half)],
            lambda j: rows.at[j, pl.ds(half, half)],
        )

    def head_of(j):
        return kept_head(place, j)

    h_line[place.x] = h_ref[...]
    da_line[place.x] = da_ref[...]
    for h in range(HEADS):
        o_own[h] = o_ref[h].astype(BF)
    o_line[place.x] = o_own[head_of(place.x)]
    line_h, line_da = line_of(h_line), line_of(da_line)
    o_swap = Direct(net, place, "x", lambda j: o_own.at[head_of(j)], lambda j: o_line.at[j])
    dq_swap = Direct(net, place, "x", lambda j: dq_own.at[head_of(j)], lambda j: dq_line.at[j])
    line_da.start()
    o_swap.start()
    key_rings = []
    for i, (inner, outer) in enumerate(key_lines(place, grads)):
        for k, (axis, _, lo, hi) in enumerate((outer, inner)):
            spot = 12 * i + 6 * k
            key_rings.append(
                RingScatter(
                    net,
                    place,
                    axis,
                    stepped(place, axis, lo),
                    stepped(place, axis, hi),
                    rooms[spot : spot + 6],
                )
            )
    first_a, then_a, first_b, then_b = key_rings
    fin_swap = Direct(net, place, "y", lambda j: fin.at[j], lambda j: fin_got.at[j])
    dq_core = net.copy(dq_snd, dq_got, partner)
    dq_ring = RingScatter(
        net,
        place,
        "y",
        stepped(place, "y", lambda j: dq_part.at[j, pl.ds(0, 2)]),
        stepped(place, "y", lambda j: dq_part.at[j, pl.ds(2, 2)]),
        dq_rooms,
    )
    late_first = RingScatter(
        net,
        place,
        "y",
        stepped(place, "y", lambda j: late_got.at[j, 0]),
        stepped(place, "y", lambda j: late_got.at[j, 1]),
        late_rooms[:6],
    )

    def late_spot(j):
        return late_y.at[lax.div(j, 2), lax.rem(j, 2)]

    late_second = RingScatter(
        net,
        place,
        "z",
        stepped(place, "z", lambda j: late_spot(j).at[pl.ds(0, 80)]),
        stepped(place, "z", lambda j: late_spot(j).at[pl.ds(80, 64)]),
        late_rooms[6:],
    )

    def late_term(c, turned, columns):
        term = jnp.dot(
            turned[...], columns[...].reshape(4 * TOK, HD), preferred_element_type=F32
        ).astype(BF)
        for k in range(8):
            for which in range(2):
                late_all[which, k // 2, k % 2, c] = term[
                    144 * k : 144 * k + 144, 128 * which : 128 * which + 128
                ]

    weights.first.begin()
    weights.first.go_on()
    tokens[...] = down(key_ref[...])
    bounds = [row_bounds(place, segments, y) for y in range(4)]
    w_loads[0].wait()

    def differ(key_y):
        keys = buf[key_y, :, :, :, :HD].reshape(KEYS, HD)
        values = buf[key_y, :, :, :, HD:].reshape(KEYS, HD)
        token = tokens[...] + first_key(place, key_y)
        token = jnp.concatenate([token, token], axis=1)
        d_keys = d_values = None
        for y in range(key_y, 4):
            first, last = bounds[y]
            allowed = (token <= last) & (token >= first)
            for h in range(HEADS):
                probs = jnp.exp(contract(keys, q_all[y, h], 1, 1))
                probs = jnp.where(allowed, probs, 0.0)
                delta = jnp.concatenate(
                    [delta_all[y, 0, h : h + 1], delta_all[y, 1, h : h + 1]], axis=1
                )
                d_scores = (probs * (contract(values, do_all[y, h], 1, 1) - delta)).astype(BF)
                value_term = jnp.dot(probs.astype(BF), do_all[y, h], preferred_element_type=F32)
                key_term = jnp.dot(d_scores, q_all[y, h], preferred_element_type=F32)
                d_values = value_term if d_values is None else d_values + value_term
                d_keys = key_term if d_keys is None else d_keys + key_term
                query_term = contract(keys, d_scores, 0, 0)
                if y == key_y:
                    dq_sum[y, h] = query_term
                else:
                    dq_sum[y, h] += query_term
        grads[key_y, :, :, :, :HD] = d_keys.astype(BF).reshape(4, 4, STRIPE, HD)
        grads[key_y, :, :, :, HD:] = d_values.astype(BF).reshape(4, 4, STRIPE, HD)

    differ(3)
    differ(2)
    first_b.start()
    line_da.forward()
    line_h.start()
    differ(1)
    first_b.middle()
    differ(0)
    first_a.start()
    for y in range(4):
        for h in range(HEADS):
            dq_snd[y, h] = dq_sum[y, h, :, theirs].astype(BF)
            dq_part[y, h] = dq_sum[y, h, :, mine].astype(BF)
    net.go(dq_core)
    weights.first.turn()
    dq_core.wait_recv()
    for y in range(4):
        add_to(dq_part.at[y], dq_got.at[y])
    dq_ring.start()
    first_a.middle()
    first_b.finish(first_b.lo(0), first_b.hi(0))
    then_b.start()
    first_a.finish(first_a.lo(0), first_a.hi(0))
    then_a.start()
    weights.next()
    line_h.forward()
    line_da.finish()
    o_swap.wait()
    turned[...] = jnp.transpose(da_line[...].reshape(4 * TOK, D))
    late_term(0, turned, o_line)
    dq_ring.middle()
    then_b.middle()
    then_a.middle()
    then_b.finish(fin.at[2], fin.at[3])
    then_a.finish(fin.at[0], fin.at[1])
    fin_got[place.y] = fin[place.y]
    fin_swap.start()
    for load in w_loads[1:]:
        load.wait()

    dq_ring.finish(dq_done.at[pl.ds(0, 2)], dq_done.at[pl.ds(2, 2)])
    d_query = jnp.zeros((1, HD), F32)
    for h in range(HEADS):
        e = jnp.transpose(dq_done[h]) * HD**-0.5
        e = turn_back(e.astype(BF).astype(F32), cos_ref[...], sin_ref[...])
        u = q_pre[h]
        du, gain = norm_back(u, norm_scale(u), across(g_query), e)
        d_query = d_query + gain
        dq_own[h] = du.astype(BF)
    dq_line[place.x] = dq_own[head_of(place.x)]
    dq_swap.start()
    line_h.finish()
    turned[...] = jnp.transpose(h_line[...].reshape(4 * TOK, D))
    turned_swap = net.copy(
        turned.at[pl.ds(pl.multiple_of((1 - core) * 576, 16), 576)], turned_other, partner
    )
    net.go(turned_swap)
    fin_swap.wait()

    dkv = jnp.concatenate([fin_got[j] for j in range(4)], axis=0)
    e = turn_back(dkv[:, :HD].astype(BF).astype(F32), cos_ref[...], sin_ref[...])
    u = k_pre[...]
    dk, d_key = norm_back(u, norm_scale(u), across(g_key), e)
    dk, dv = dk.astype(BF), dkv[:, HD:].astype(BF)
    for i in range(2):
        kv_own[i] = dk[:, 128 * i : 128 * i + 128]
        kv_own[2 + i] = dv[:, 128 * i : 128 * i + 128]
    kv_line[core, place.x] = kv_own[place.x]
    kv_swap = Direct(net, place, "x", lambda j: kv_own.at[j], lambda j: kv_line.at[core, j])
    kv_swap.start()
    kv_across = []
    for by in range(4):
        j = place.step("x", by)
        device = place.device(x=j, core=1 - core)
        kv_across.append(net.copy(kv_own.at[j], kv_line.at[core, place.x], device))
        net.go(kv_across[by])
    weights.turn_again()
    dq_swap.wait()
    late_term(1, turned, dq_line)
    late_swap = net.copy(late_all.at[1 - core], late_got, partner)
    net.go(late_swap)
    d_h = contract(dk, wk[...], 1, 1) + contract(dv, wv[...], 1, 1)
    for h in range(HEADS):
        w = (wq, wq2)[h // 2]
        d_h = d_h + contract(dq_own[h], w[:, 256 * (h % 2) : 256 * (h % 2) + 256], 1, 1)
    xf = x_ref[...].astype(F32)
    dx, d_attn = norm_back(xf, norm_scale(xf), across(g_attn), d_h)
    dx_out[...] = (dmid_ref[...] + dx).astype(BF)
    def gain_swap(level, axis):
        return Direct(
            net, place, axis, lambda j: gain_got.at[level, at(axis)], lambda j: gain_got.at[level, j]
        )

    def at(axis):
        return getattr(place, axis)

    def gain_sum(level):
        return (gain_got[level, 0] + gain_got[level, 1]) + (gain_got[level, 2] + gain_got[level, 3])

    swaps = [gain_swap(0, "x"), gain_swap(1, "y"), gain_swap(2, "z")]
    norms = jnp.concatenate([d_query, d_key, jnp.zeros((1, D - 2 * HD), F32)], axis=1)
    gain_got[0, place.x] = jnp.concatenate(
        [d_attn, gains_ref[0:3], norms, jnp.zeros((3, D), F32)], axis=0
    )
    swaps[0].start()
    turned_swap.wait_recv()
    kv_swap.wait()
    for copy in kv_across:
        copy.wait_recv()
    term = jnp.dot(
        turned[pl.ds(pl.multiple_of(core * 576, 16), 576)],
        kv_line[core].reshape(4 * TOK, 128),
        preferred_element_type=F32,
    )
    term += jnp.dot(
        turned_other[...], kv_line[1 - core].reshape(4 * TOK, 128), preferred_element_type=F32
    )
    term = term.astype(BF)
    for k in range(4):
        w_got[k] = term[144 * k : 144 * k + 144]
    w_scatter = Direct(net, place, "y", lambda j: w_got.at[j], lambda j: w_y.at[j])
    w_scatter.start()
    w_y[place.y] = w_got[place.y]
    late_swap.wait_recv()
    for y in range(4):
        add_to(late_got.at[y], late_all.at[core, y])
    late_first.start()
    swaps[0].wait()
    gain_got[1, place.y] = gain_sum(0)
    swaps[1].start()
    weights.last()
    swaps[1].wait()
    gain_got[2, place.z] = gain_sum(1)
    swaps[2].start()
    w_scatter.wait()
    sum_to(w_z.at[place.z], [w_y.at[j] for j in range(4)])
    w_sums = Direct(net, place, "z", lambda j: w_z.at[place.z], lambda j: w_z.at[j])
    w_sums.start()
    late_first.middle()
    swaps[2].wait()
    gain_got[3, core] = gain_sum(2)
    gain_last = net.copy(gain_got.at[3, core], gain_got.at[3, core], partner)
    net.go(gain_last)
    w_sums.wait()
    upper, lower = w_top.at[core], w_low.at[core]
    sum_to(upper.at[place.x, place.y], [w_z.at[j, pl.ds(0, 80)] for j in range(4)])
    sum_to(lower.at[place.x, place.y], [w_z.at[j, pl.ds(80, 64)] for j in range(4)])

    def spread(axis, view):
        return Direct(net, place, axis, lambda j: view(at(axis)), view)

    first_way = [
        spread("y", lambda j: upper.at[place.x, j]),
        spread("x", lambda j: lower.at[j, place.y]),
    ]
    second_way = [spread("x", lambda j: upper.at[j]), spread("y", lambda j: lower.at[:, j])]
    for line in first_way:
        line.start()
    late_first.finish(late_y.at[0], late_y.at[1])
    late_second.start()
    for line, then in zip(first_way, second_way):
        line.wait()
        then.start()
    late_second.middle()
    gain_last.wait_recv()
    gains_out[...] = gain_got[3, 0] + gain_got[3, 1]
    over = [net.copy(upper, upper, partner), net.copy(lower, lower, partner)]
    for line, copy in zip(second_way, over):
        line.wait()
        net.go(copy)
    late_second.finish(late_z.at[pl.ds(0, 80)], late_z.at[pl.ds(80, 64)])
    weights.send_late()
    for copy in over:
        copy.wait_recv()
    weights.arrive()
    home_out[...] = weights.rcv[...]
    late_out[...] = weights.late_rcv[...]
    net.drain()


def attention_backward(hbm, small, call_id):
    shape = jax.ShapeDtypeStruct
    rooms = []
    for _ in range(2):
        rooms += RingScatter.room_shapes((4, STRIPE, 2 * HD), (4, STRIPE, 2 * HD))
        rooms += RingScatter.room_shapes((STRIPE, 2 * HD), (STRIPE, 2 * HD))
    rooms += RingScatter.room_shapes((2, HD, TOK), (2, HD, TOK))
    late_rooms = [
        *RingScatter.room_shapes((2, 144, 128), (2, 144, 128)),
        *RingScatter.room_shapes((80, 128), (64, 128)),
    ]
    return pl.pallas_call(
        backward_kernel,
        out_shape=(
            shape((TOK, D), BF),
            shape((8, 16, HALF + 256), BF),
            shape((8, 16, 256), BF),
            shape((2, 4, 4, 80, 128), BF),
            shape((2, 4, 4, 64, 128), BF),
            shape((8, D), F32),
        ),
        in_specs=[pl.BlockSpec(memory_space=pl.ANY)] * len(hbm) + [IN_VMEM] * len(small),
        out_specs=[IN_VMEM] * 6,
        scratch_shapes=[
            pltpu.VMEM((4, 4, 4, STRIPE, 2 * HD), BF),
            pltpu.VMEM((D, 2 * HD), BF),
            pltpu.VMEM((D, 2 * HD), BF),
            pltpu.VMEM((D, HD), BF),
            pltpu.VMEM((D, HD), BF),
            pltpu.VMEM((KEYS, 128), jnp.int32),
            pltpu.VMEM((4, 4, 4, STRIPE, 2 * HD), BF),
            pltpu.VMEM((4, STRIPE, 2 * HD), F32),
            pltpu.VMEM((4, STRIPE, 2 * HD), F32),
            pltpu.VMEM((4, HEADS, HD, ROWS), F32),
            pltpu.VMEM((4, HEADS, HD, TOK), BF),
            pltpu.VMEM((4, HEADS, HD, TOK), BF),
            pltpu.VMEM((4, HEADS, HD, TOK), BF),
            pltpu.VMEM((HEADS, HD, TOK), F32),
            pltpu.VMEM((4, TOK, D), BF),
            pltpu.VMEM((4, TOK, D), BF),
            pltpu.VMEM((D, 4 * TOK), BF),
            pltpu.VMEM((4, TOK, HD), BF),
            pltpu.VMEM((4, TOK, HD), BF),
            pltpu.VMEM((4, TOK, HD), BF),
            pltpu.VMEM((4, TOK, HD), BF),
            pltpu.VMEM((2, 4, 2, 2, 144, 128), BF),
            pltpu.VMEM((4, 2, 2, 144, 128), BF),
            pltpu.VMEM((2, 2, 144, 128), BF),
            pltpu.VMEM((144, 128), F32),
            pltpu.VMEM((4, 4, 8, D), F32),
            pltpu.VMEM((4, TOK, 128), BF),
            pltpu.VMEM((2, 4, TOK, 128), BF),
            pltpu.VMEM((576, 4 * TOK), BF),
            pltpu.VMEM((4, 144, 128), BF),
            pltpu.VMEM((4, 144, 128), BF),
            pltpu.VMEM((4, 144, 128), BF),
            *rooms,
            *late_rooms,
            *WeightSums.scratch(),
            *sems(160),
            *sems(16),
            pltpu.SemaphoreType.DMA((24,)),
        ],
        compiler_params=params(call_id),
    )(*hbm, *small)


def feed_kernel(
    x_ref,
    o_ref,
    inv_ref,
    wo_ref,
    wo2_ref,
    post_ref,
    ffn_ref,
    out_gain_ref,
    cot_ref,
    wg_hbm,
    wu_hbm,
    wd_hbm,
    out_ref,
    dmid_out,
    dattn_out,
    do_all,
    delta_all,
    dgains_out,
    sums_hbm,
    wg,
    wu,
    wd,
    h_line,
    f_line,
    h_turned,
    f_turned,
    gelu_kept,
    slope_kept,
    act,
    d_gate,
    d_up,
    f_terms,
    h_terms,
    snd,
    got,
    attn,
    mid,
    ffn,
    delta_rows,
    *rest,
):
    *room, send, recv, local = rest
    place, net = Place(), Net(send, recv)
    core, partner = place.core, place.partner()
    x_hi = lax.div(place.x, 2)
    first_unit = pl.multiple_of(x_hi * (2 * HID - HID_PAD), 128)
    window = pl.ds(first_unit, HID_PAD)
    loads = [
        pltpu.make_async_copy(source, target, local.at[i])
        for i, (source, target) in enumerate(
            ((wg_hbm.at[:, window], wg), (wu_hbm.at[:, window], wu), (wd_hbm.at[window], wd))
        )
    ]
    for load in loads:
        load.start()
    greet(
        ring(place, "x")
        + ring(place, "y")
        + ring(place, "z")
        + [partner, place.toward("y", 2)]
    )
    half, quarter = TOK // 2, TOK // 4
    top, bottom = pl.ds(0, quarter), pl.ds(quarter, quarter)
    g_post, g_ffn, g_out = (across(ref) for ref in (post_ref, ffn_ref, out_gain_ref))

    def rows_of(part):
        return slice(half * part, half * part + half)

    def lines_of(part):
        return slice(4 * half * part, 4 * half * part + 4 * half)

    def gather(lines):
        return RingGather(
            net,
            place,
            "x",
            lambda j: lines.at[j],
            lambda j: lines.at[j, top],
            lambda j: lines.at[j, bottom],
        )

    def scatter(terms, room):
        return RingScatter(
            net,
            place,
            "x",
            stepped(place, "x", lambda j: terms.at[j, top]),
            stepped(place, "x", lambda j: terms.at[j, bottom]),
            room,
        )

    def summed(line, part):
        at = half * part
        line.finish(ffn.at[pl.ds(at, quarter)], ffn.at[pl.ds(at + quarter, quarter)])

    o_cat = [o_ref[h].astype(BF) for h in range(HEADS)]
    a = jnp.dot(jnp.concatenate(o_cat[:2], axis=1), wo_ref[...], preferred_element_type=F32)
    a += jnp.dot(jnp.concatenate(o_cat[2:], axis=1), wo2_ref[...], preferred_element_type=F32)
    attn[...] = a
    mid[...] = x_ref[...].astype(F32) + a * norm_scale(a) * g_post
    m = mid[...]
    h = (m * norm_scale(m) * g_ffn).astype(BF)
    for part in range(2):
        h_line[part, place.x] = h[rows_of(part)]
    h_gathers = [gather(h_line.at[part]) for part in range(2)]
    f_gathers = [gather(f_line.at[part]) for part in range(2)]
    f_sums = [scatter(f_terms.at[part], room[6 * part : 6 * part + 6]) for part in range(2)]
    h_sums = [
        scatter(h_terms.at[part], room[12 + 6 * part : 18 + 6 * part]) for part in range(2)
    ]
    h_gathers[0].start()

    for load in loads:
        load.wait()
    low_unit, high_unit = jnp.where(x_hi == 0, 0, 64), jnp.where(x_hi == 0, HID, HID_PAD)

    def units(n):
        return pl.ds(pl.multiple_of(n * 256, 256), 256)

    def forward(part, n, carry):
        h = h_line[part].reshape(4 * half, D)
        gate = jnp.dot(h, wg[:, units(n)], preferred_element_type=F32)
        up = jnp.dot(h, wu[:, units(n)], preferred_element_type=F32)
        unit = n * 256 + lax.broadcasted_iota(jnp.int32, (1, 256), 1)
        own = jnp.where((unit >= low_unit) & (unit < high_unit), 1.0, 0.0)
        scale, cube = 0.7978845608028654, 0.044715
        square = gate * gate
        bent = jnp.tanh(scale * gate * (1.0 + cube * square))
        lifted = 0.5 * (1.0 + bent)
        gelu = gate * lifted * own
        slope = lifted + 0.5 * gate * (1.0 - bent * bent) * scale * (1.0 + 3.0 * cube * square)
        act[lines_of(part), units(n)] = (gelu * up).astype(BF)
        gelu_kept[lines_of(part), units(n)] = gelu.astype(BF)
        slope_kept[lines_of(part), units(n)] = (slope * up * own).astype(BF)
        return carry

    def columns(n):
        return pl.ds(pl.multiple_of(n * 384, 128), 384)

    def project(part, n, carry):
        term = jnp.dot(act[lines_of(part)], wd[:, columns(n)], preferred_element_type=F32)
        f_terms[part, :, :, columns(n)] = term.astype(BF).reshape(4, half, 384)
        return carry

    def backward(part, n, carry):
        d_act = contract(f_line[part].reshape(4 * half, D), wd[units(n)], 1, 1)
        rows = lines_of(part)
        d_gate[rows, units(n)] = (d_act * slope_kept[rows, units(n)].astype(F32)).astype(BF)
        d_up[rows, units(n)] = (d_act * gelu_kept[rows, units(n)].astype(F32)).astype(BF)
        return carry

    def back_project(part, n, carry):
        rows = lines_of(part)
        term = contract(d_gate[rows], wg[columns(n)], 1, 1)
        term += contract(d_up[rows], wu[columns(n)], 1, 1)
        h_terms[part, :, :, columns(n)] = term.astype(BF).reshape(4, half, 384)
        return carry

    def each(times, step, part):
        lax.fori_loop(0, times, functools.partial(step, part), 0)

    blocks = HID_PAD // 256

    def turn_round(part):
        rows = rows_of(part)
        summed(f_sums[part], part)
        f = ffn[rows]
        r = norm_scale(f)
        out_ref[rows] = (mid[rows] + f * r * g_out).astype(BF)
        df, gain = norm_back(f, r, g_out, cot_ref[rows].astype(F32))
        f_line[part, place.x] = df.astype(BF)
        f_gathers[part].start()
        return gain

    h_gathers[0].forward()
    h_gathers[1].start()
    h_gathers[0].finish()
    each(blocks, forward, 0)
    h_gathers[1].forward()
    each(3, project, 0)
    f_sums[0].start()
    h_gathers[1].finish()
    each(blocks, forward, 1)
    f_sums[0].middle()
    each(3, project, 1)
    f_sums[1].start()
    d_out = turn_round(0)
    f_sums[1].middle()
    h_turned[...] = jnp.transpose(h_line[...].reshape(8 * half, D))
    f_gathers[0].forward()
    d_out = d_out + turn_round(1)
    f_gathers[0].finish()
    each(blocks, backward, 0)
    f_gathers[1].forward()
    each(3, back_project, 0)
    h_sums[0].start()
    f_gathers[1].finish()
    f_turned[...] = jnp.transpose(f_line[...].reshape(8 * half, D))

    def halves_of(which):
        return pl.ds(pl.multiple_of(which * 896, 128), 896)

    def fill(target, i, which, left, right, spans, add):
        term = jnp.dot(
            left[576 * i : 576 * i + 576], right[:, halves_of(which)], preferred_element_type=F32
        )
        for k in range(4):
            for half, low, high, start in spans:
                at = (2 * i + k // 2, k % 2, half, slice(None), slice(start, start + high - low))
                value = term[144 * k : 144 * k + 144, low:high]
                if add:
                    value = value + target[at].astype(F32)
                target[at] = value.astype(BF)

    down_spans = ((0, 0, 256, 0), (0, 256, 512, CUT), (1, 512, 768, 0), (1, 768, 896, CUT))

    def fill_down(target, i, which, add):
        fill(target, i, which, f_turned, act, down_spans, add)

    def fill_others(target, i, which, add):
        for c, right in enumerate((d_gate, d_up)):
            spans = ((c, 0, 512, 256), (c, 512, 896, CUT + 256))
            fill(target, i, which, h_turned, right, spans, add)

    for y in range(4):
        snd[y, :, 1, :, CUT + 128 : CUT + 256] = jnp.zeros((2, 144, 128), BF)
    swaps = [net.copy(snd.at[y], got.at[y], partner) for y in range(4)]
    for i in range(2):
        fill_down(snd, i, 1 - core, False)
    each(blocks, backward, 1)
    h_sums[0].middle()
    each(3, back_project, 1)
    h_sums[1].start()
    def mine_of(part):
        return pl.ds(pl.multiple_of(core * TOK + half * part, half), half)

    def do_ring_of(part):
        mine = mine_of(part)
        return RingGather(
            net,
            place,
            "y",
            lambda j: do_all.at[j, :, mine],
            lambda j: do_all.at[j, pl.ds(0, 2), mine],
            lambda j: do_all.at[j, pl.ds(2, 2), mine],
        )

    def block_of(part, by):
        return do_all.at[place.step("y", by), :, mine_of(part)]

    do_rings = [do_ring_of(part) for part in range(2)]
    do_core = [
        [net.copy(block_of(part, by), block_of(part, by), partner) for by in range(4)]
        for part in range(2)
    ]
    delta_swap = Direct(
        net,
        place,
        "y",
        lambda j: delta_all.at[place.y, core],
        lambda j: delta_all.at[j, core],
    )
    delta_core = net.copy(delta_all.at[:, core], delta_all.at[:, core], partner)

    def heads_back(part):
        rows = rows_of(part)
        m, a = mid[rows], attn[rows]
        dm, d_ffn = norm_back(m, norm_scale(m), g_ffn, ffn[rows])
        d_mid = cot_ref[rows].astype(F32) + dm
        dmid_out[rows] = d_mid
        da, d_post = norm_back(a, norm_scale(a), g_post, d_mid)
        da = da.astype(BF)
        dattn_out[rows] = da
        for h in range(HEADS):
            w = (wo_ref, wo2_ref)[h // 2][256 * (h % 2) : 256 * (h % 2) + 256]
            d_o = contract(da, w, 1, 1).astype(BF).astype(F32)
            inverse = inv_ref[h, rows]
            scaled = d_o * jnp.concatenate([inverse, inverse], axis=1)
            do_all[place.y, h, mine_of(part)] = scaled.astype(BF)
            delta_rows[h, rows] = jnp.sum(d_o * o_ref[h, rows], axis=1, keepdims=True) * inverse
        do_rings[part].start()
        net.go(do_core[part][0])
        return d_post, d_ffn

    for i in range(2):
        fill_others(snd, i, 1 - core, False)
        net.go(swaps[2 * i])
        net.go(swaps[2 * i + 1])
    h_sums[1].middle()
    summed(h_sums[0], 0)
    gains_top = heads_back(0)
    summed(h_sums[1], 1)
    gains_low = heads_back(1)
    d_post, d_ffn = (top + low for top, low in zip(gains_top, gains_low))
    dgains_out[...] = jnp.concatenate([d_post, d_ffn, d_out, jnp.zeros((5, D), F32)], axis=0)
    delta_all[place.y, core] = jnp.concatenate(
        [jnp.transpose(delta_rows[h])[:1] for h in range(HEADS)] + [jnp.zeros((4, TOK), F32)],
        axis=0,
    )
    delta_swap.start()
    stores = [pltpu.make_async_copy(got.at[y], sums_hbm.at[y], local.at[3 + y]) for y in range(4)]

    def do_near(part):
        do_rings[part].forward()
        net.go(do_core[part][1])
        net.go(do_core[part][3])

    def do_far(part):
        do_rings[part].finish()
        net.go(do_core[part][2])

    do_near(0)
    for i in range(2):
        swaps[2 * i].wait_recv()
        swaps[2 * i + 1].wait_recv()
        fill_others(got, i, core, True)
        fill_down(got, i, core, True)
        stores[2 * i].start()
        stores[2 * i + 1].start()
        if i == 0:
            do_far(0)
            do_near(1)
    do_far(1)
    delta_swap.wait()
    net.go(delta_core)
    for copies in do_core:
        for copy in copies:
            copy.wait_recv()
    delta_core.wait_recv()
    for store in stores:
        store.wait()
    net.drain()


def feed_forward(args, call_id):
    quarter = (TOK // 4, D)
    shape = jax.ShapeDtypeStruct
    every = (4, 2, 2, 144, HALF)
    lines = 4 * TOK
    anywhere = pl.BlockSpec(memory_space=pl.ANY)
    unit_rows = [pltpu.VMEM((lines, HID_PAD), BF)] * 5
    return pl.pallas_call(
        feed_kernel,
        out_shape=(
            shape((TOK, D), BF),
            shape((TOK, D), F32),
            shape((TOK, D), BF),
            shape((4, HEADS, ROWS, HD), BF),
            shape((4, 2, 8, TOK), F32),
            shape((8, D), F32),
            shape(every, BF),
        ),
        in_specs=[IN_VMEM] * 9 + [anywhere] * 3,
        out_specs=[IN_VMEM] * 6 + [anywhere],
        scratch_shapes=[
            pltpu.VMEM((D, HID_PAD), BF),
            pltpu.VMEM((D, HID_PAD), BF),
            pltpu.VMEM((HID_PAD, D), BF),
            pltpu.VMEM((2, 4, TOK // 2, D), BF),
            pltpu.VMEM((2, 4, TOK // 2, D), BF),
            pltpu.VMEM((D, lines), BF),
            pltpu.VMEM((D, lines), BF),
            *unit_rows,
            pltpu.VMEM((2, 4, TOK // 2, D), BF),
            pltpu.VMEM((2, 4, TOK // 2, D), BF),
            pltpu.VMEM(every, BF),
            pltpu.VMEM(every, BF),
            pltpu.VMEM((TOK, D), F32),
            pltpu.VMEM((TOK, D), F32),
            pltpu.VMEM((TOK, D), F32),
            pltpu.VMEM((HEADS, TOK, TOK), F32),
            *(RingScatter.room_shapes(quarter, quarter) * 4),
            *sems(88),
            pltpu.SemaphoreType.DMA((7,)),
        ],
        compiler_params=params(call_id),
    )(*args)


class FirstSums:
    def __init__(self, net, place, sums, cut, rooms, here=None, marks=None):
        left, right = pl.ds(0, cut), pl.ds(cut, sums.shape[-1] - cut)

        def y_spot(half):
            return stepped(place, "y", lambda j: sums.at[j, half, :, :, left])

        def z_spot(half):
            return stepped(
                place,
                "z",
                lambda j: sums.at[pl.ds(2 * half, 2), lax.div(j, 2), lax.rem(j, 2), :, right],
            )

        self.loads = []
        self.lines = []
        for i, (axis, spot) in enumerate((("y", y_spot), ("z", z_spot))):
            near = (None, None)
            if here is not None:
                near = ({}, {})
                for k, (half, by) in enumerate(((0, 1), (1, 3), (0, 0), (1, 0))):
                    target = here[i].at[k]
                    near[half][by] = target
                    self.loads.append(
                        pltpu.make_async_copy(spot(half)(by), target, marks.at[8 + 4 * i + k])
                    )
                near = (near[0].get, near[1].get)
            room = rooms[6 * i : 6 * i + 6]
            self.lines.append(RingScatter(net, place, axis, spot(0), spot(1), room, *near))

    @staticmethod
    def room_shapes(cut, rest):
        return [
            *RingScatter.room_shapes((2, 144, cut), (2, 144, cut)),
            *RingScatter.room_shapes((2, 144, rest), (2, 144, rest)),
        ]

    def begin(self):
        for load in self.loads:
            load.start()
        for line in self.lines:
            line.start_far()

    def go_on(self):
        for line in self.lines:
            line.start_right()
            line.start_left()

    def turn(self):
        for load in self.loads:
            load.wait()
        for line in self.lines:
            line.middle()


class WeightSums:
    def __init__(self, place, net, sums, late, refs, marks):
        y_here, z_here, y1, z1, z2, y2, snd, late_snd, rcv, late_rcv, *rooms = refs
        self.late_snd, self.late_rcv = late_snd, late_rcv
        self.place, self.late, self.snd, self.rcv, self.marks = place, late, snd, rcv, marks
        self.y1, self.z1, self.y2, self.z2 = y1, z1, y2, z2
        self.x_hi, self.x_lo = lax.div(place.x, 2), lax.rem(place.x, 2)
        self.friends = []
        for k in range(1, 16):
            spot = lax.rem(self.x_hi * 8 + place.z * 2 + place.core + k, 16)
            x, z = lax.div(spot, 8) * 2 + self.x_lo, lax.rem(lax.div(spot, 2), 4)
            self.friends.append(place.device(x=x, z=z, core=lax.rem(spot, 2)))

        self.first = FirstSums(net, place, sums, CUT, rooms[:12], (y_here, z_here), marks[2])

        def then_z(j):
            return y1.at[lax.div(j, 2), lax.rem(j, 2)]

        self.z_second = RingScatter(
            net,
            place,
            "z",
            stepped(place, "z", lambda j: then_z(j).at[:, pl.ds(0, 384)]),
            stepped(place, "z", lambda j: then_z(j).at[:, pl.ds(384, 384)]),
            rooms[12:18],
        )
        self.y_second = RingScatter(
            net,
            place,
            "y",
            stepped(place, "y", lambda j: z1.at[j, :, pl.ds(0, 384)]),
            stepped(place, "y", lambda j: z1.at[j, :, pl.ds(384, 256)]),
            rooms[18:24],
        )

    @staticmethod
    def scratch():
        rest = HALF - CUT
        return [
            pltpu.VMEM((4, 2, 144, CUT), BF),
            pltpu.VMEM((4, 2, 144, rest), BF),
            pltpu.VMEM((2, 2, 144, CUT), BF),
            pltpu.VMEM((4, 144, rest), BF),
            pltpu.VMEM((144, CUT), F32),
            pltpu.VMEM((144, rest), F32),
            pltpu.VMEM((8, 16, HALF + 256), BF),
            pltpu.VMEM((8, 16, 256), BF),
            pltpu.VMEM((8, 16, HALF + 256), BF),
            pltpu.VMEM((8, 16, 256), BF),
            *FirstSums.room_shapes(CUT, rest),
            *RingScatter.room_shapes((144, 384), (144, 384)),
            *RingScatter.room_shapes((144, 384), (144, 256)),
        ]

    def next(self):
        y_line, z_line = self.first.lines
        y_line.finish(self.y1.at[0], self.y1.at[1])
        self.z_second.start()
        z_line.finish(self.z1.at[pl.ds(0, 2)], self.z1.at[pl.ds(2, 2)])
        self.y_second.start()

    def turn_again(self):
        self.z_second.middle()
        self.y_second.middle()

    def last(self):
        z2, y2 = self.z2, self.y2
        self.z_second.finish(z2.at[:, pl.ds(0, 384)], z2.at[:, pl.ds(384, 384)])
        self.y_second.finish(y2.at[:, pl.ds(0, 384)], y2.at[:, pl.ds(384, 256)])
        total = jnp.concatenate([z2[...], y2[...]], axis=1)
        self.pack(total, self.snd)
        self.exchange(self.snd, self.rcv, 0)

    def send_late(self):
        self.pack(self.late[...], self.late_snd)
        self.exchange(self.late_snd, self.late_rcv, 8)

    @staticmethod
    def pack(total, snd):
        width = total.shape[1]
        count = width // 128
        for k in range(8):
            extra = total[18 * k + 16 : 18 * k + 18]
            pieces = [extra[:, 128 * n : 128 * n + 128] for n in range(count)]
            snd[k, :, :width] = total[18 * k : 18 * k + 16].astype(BF)
            for n in range(0, count, 8):
                group = pieces[n : n + 8]
                if len(group) < 8:
                    group.append(jnp.zeros((16 - 2 * len(group), 128), F32))
                at = width + 16 * n
                snd[k, :, at : at + 128] = jnp.concatenate(group, axis=0).astype(BF)

    def exchange(self, snd, rcv, mark):
        place = self.place
        send, recv, here = self.marks
        row_half = lax.div(place.z, 2)
        self.slot = self.x_hi * 4 + place.core * 2 + lax.rem(place.z, 2)
        self.own = place.z * 2 + place.core
        self.stays = row_half == self.x_hi
        for k in range(8):
            copy = pltpu.make_async_remote_copy(
                src_ref=snd.at[k],
                dst_ref=rcv.at[self.slot],
                send_sem=send.at[mark + k],
                recv_sem=recv.at[mark + self.slot],
                device_id=place.device(x=row_half * 2 + self.x_lo, z=k // 2, core=k % 2),
                device_id_type=MESH,
            )
            is_here = self.stays & (self.own == k)

            @pl.when(jnp.logical_not(is_here))
            def _(copy=copy):
                copy.start()

            @pl.when(is_here)
            def _(k=k):
                keep = pltpu.make_async_copy(snd.at[k], rcv.at[self.slot], here.at[0])
                keep.start()
                keep.wait()

    def arrive(self):
        send, recv, _ = self.marks
        for mark, snd, rcv in ((0, self.snd, self.rcv), (8, self.late_snd, self.late_rcv)):
            for m in range(8):
                arrival = pltpu.make_async_remote_copy(
                    src_ref=snd.at[m],
                    dst_ref=rcv.at[m],
                    send_sem=send.at[mark + m],
                    recv_sem=recv.at[mark + m],
                    device_id=self.place.partner(),
                    device_id_type=MESH,
                )

                @pl.when(jnp.logical_not(self.stays & (self.slot == m)))
                def _(arrival=arrival):
                    arrival.wait_recv()

                @pl.when(jnp.logical_not(self.stays & (self.own == m)))
                def _(arrival=arrival):
                    arrival.wait_send()


def last_kernel(
    home_ref,
    late_ref,
    top_ref,
    low_ref,
    gains_ref,
    y_ref,
    dx_ref,
    y_out,
    dx_out,
    dwq_out,
    dwk_out,
    dwv_out,
    dwo_out,
    dwg_out,
    dwu_out,
    dwd_out,
    *gain_outs,
):
    y_out[...] = y_ref[...]
    dx_out[...] = dx_ref[...]

    def rows_at(ref, slot, n):
        spare = (HALF if ref is home_ref else 128) + 128 * (n // 8)
        more = ref[slot, :, spare : spare + 128].astype(F32)[2 * (n % 8) : 2 * (n % 8) + 2]
        return jnp.concatenate(
            [ref[slot, :, 128 * n : 128 * n + 128].astype(F32), more], axis=0
        )

    def tile(x_hi, which, n):
        core, n = n // 7, n % 7
        if which < 2:
            c, at = which, 256 + 128 * n if n < 4 else 512 + 128 * n
        else:
            c, n = n // 4, n % 4
            at = 128 * n if n < 2 else CUT + 128 * (n - 2)
        return rows_at(home_ref, x_hi * 4 + core * 2 + c, at // 128)

    for which, out in enumerate((dwg_out, dwu_out, dwd_out)):
        for n in range(27):
            value = None
            for x_hi in range(2):
                if 0 <= n - 13 * x_hi < 14:
                    term = tile(x_hi, which, n - 13 * x_hi)
                    value = term if value is None else value + term
            span = slice(128 * n, 128 * n + 128)
            out[:, span] = value
    for k in range(4):
        span = slice(128 * k, 128 * k + 128)
        dwo_out[:, span] = rows_at(late_ref, 2 * k, 0)
        dwq_out[:, span] = rows_at(late_ref, 2 * k + 1, 0)
    for which in range(2):
        for j in range(4):
            out = (dwk_out, dwv_out)[j // 2]
            for y in range(4):
                span = slice(128 * (j % 2), 128 * (j % 2) + 128)
                at = 576 * which + 144 * y
                out[at : at + 80, span] = top_ref[which, j, y].astype(F32)
                out[at + 80 : at + 144, span] = low_ref[which, j, y].astype(F32)
    for out, row, start in zip(gain_outs, (0, 4, 4, 1, 2, 3), (0, 0, HD, 0, 0, 0)):
        size = out.shape[0]
        out[...] = gains_ref[row : row + 1, start : start + size].reshape(size)


def last_layout(*args):
    shape = jax.ShapeDtypeStruct
    return pl.pallas_call(
        last_kernel,
        out_shape=(
            shape((TOK, D), BF),
            shape((TOK, D), BF),
            shape((18, 2 * HD), F32),
            shape((D, HD), F32),
            shape((D, HD), F32),
            shape((18, 2 * HD), F32),
            shape((18, 2 * HID), F32),
            shape((18, 2 * HID), F32),
            shape((18, 2 * HID), F32),
            *(shape((size,), F32) for size in (D, HD, HD, D, D, D)),
        ),
        in_specs=[IN_VMEM] * len(args),
        out_specs=[IN_VMEM] * 15,
        compiler_params=pltpu.CompilerParams(vmem_limit_bytes=VMEM_BYTES),
    )(*args)


def angles(token_pos):
    middle = HD // 2
    frequency = THETA ** (-2.0 * jnp.arange(middle, dtype=F32) / HD)
    turned = token_pos.astype(F32)[:, None] * frequency[None, :]
    return (jnp.cos(turned), jnp.sin(turned))


def shards(
    layer_input,
    segment_ids,
    positions,
    w_query,
    w_key,
    w_value,
    w_out,
    w_gate,
    w_up,
    w_down,
    norm_attn,
    norm_query,
    norm_key,
    norm_post,
    norm_ffn,
    norm_out,
    cotangent,
):
    sp, tp = lax.axis_index("sp"), lax.axis_index("tp")
    cosine, sine = angles(lax.dynamic_slice_in_dim(positions, (sp * 2 + tp) * TOK, TOK))
    segments = segment_ids.reshape(128, 128)
    key_rows = jnp.asarray(KEY_TOKENS)
    kv_all, q_all, wq_other, wo_other, o_heads, inverse, q_pre, k_pre, h_attn = attention_forward(
        (
            layer_input,
            norm_attn,
            norm_query,
            norm_key,
            w_query,
            w_key,
            w_value,
            w_out,
            cosine,
            sine,
            segments,
            key_rows,
        ),
        2,
    )
    (
        layer_output,
        d_mid,
        d_attn,
        d_heads,
        delta,
        d_gains,
        sums,
    ) = feed_forward(
        (
            layer_input,
            o_heads,
            inverse,
            w_out,
            wo_other,
            norm_post,
            norm_ffn,
            norm_out,
            cotangent,
            w_gate,
            w_up,
            w_down,
        ),
        6,
    )
    d_input, home, late, w_top, w_low, gains = attention_backward(
        (kv_all, sums, w_query, wq_other, w_key, w_value),
        (
            q_all,
            d_heads,
            delta,
            key_rows,
            segments,
            q_pre,
            k_pre,
            cosine,
            sine,
            h_attn,
            d_attn,
            o_heads,
            layer_input,
            d_mid,
            norm_attn,
            norm_query,
            norm_key,
            d_gains,
        ),
        8,
    )
    y, dx, d_wq, d_wk, d_wv, d_wo, d_wg, d_wu, d_wd, *d_norms = last_layout(
        home, late, w_top, w_low, gains, layer_output, d_input
    )
    return (y, dx, d_wq, d_wk, d_wv, d_wo.T, d_wg, d_wu, d_wd.T, *d_norms)


def solution(mesh):
    rows = P(("sp", "tp"), None)
    in_specs = (
        rows,
        P(),
        P(),
        P(None, "tp"),
        P(),
        P(),
        P("tp", None),
        P(None, "tp"),
        P(None, "tp"),
        P("tp", None),
        P(),
        P(),
        P(),
        P(),
        P(),
        P(),
        rows,
    )
    out_specs = (
        rows,
        rows,
        P("sp", "tp"),
        P(),
        P(),
        P("tp", "sp"),
        P("sp", "tp"),
        P("sp", "tp"),
        P("tp", "sp"),
        P(),
        P(),
        P(),
        P(),
        P(),
        P(),
    )
    return jax.shard_map(shards, mesh=mesh, in_specs=in_specs, out_specs=out_specs, check_vma=False)
```

```python
import functools

import jax
import jax.numpy as jnp
import numpy as np
from jax import lax
from jax.experimental import pallas as pl
from jax.experimental.pallas import tpu as pltpu
from jax.sharding import PartitionSpec as P

EPS = 1e-06
THETA = 1000000.0
BF = jnp.bfloat16
F32 = jnp.float32
MESH = pl.DeviceIdType.MESH
IN_VMEM = pl.BlockSpec(memory_space=pltpu.VMEM)
VMEM_BYTES = 58 * 1024 * 1024

TOK = 128
D = 1152
HD = 256
HEADS = 4
ROWS = 2 * TOK
HID = 1728
HID_PAD = 1792
CUT = 768
HALF = 1408
STRIPE = TOK // 4
KEYS = 16 * STRIPE


class Place:
    def __init__(self):
        sp = lax.axis_index("sp")
        self.core = lax.rem(sp, 2)
        self.z = lax.rem(lax.div(sp, 2), 4)
        self.y = lax.div(sp, 16)
        self.x = lax.rem(lax.div(sp, 8), 2) * 2 + lax.axis_index("tp")

    def device(self, **moved):
        x, y, z, core = (moved.get(name, getattr(self, name)) for name in ("x", "y", "z", "core"))
        return (((y * 2 + lax.div(x, 2)) * 4 + z) * 2 + core, lax.rem(x, 2))

    def step(self, axis, by):
        return lax.rem(getattr(self, axis) + by, 4)

    def toward(self, axis, by):
        return self.device(**{axis: self.step(axis, by)})

    def partner(self):
        return self.device(core=1 - self.core)


class Net:
    def __init__(self, send, recv):
        self.send, self.recv, self.used, self.started = send, recv, 0, []

    def copy(self, source, target, device):
        at = self.used
        self.used += 1
        return pltpu.make_async_remote_copy(
            src_ref=source,
            dst_ref=target,
            send_sem=self.send.at[at],
            recv_sem=self.recv.at[at],
            device_id=device,
            device_id_type=MESH,
        )

    def go(self, copy):
        copy.start()
        self.started.append(copy)

    def settle(self, copy):
        copy.wait_send()
        self.started = [other for other in self.started if other is not copy]

    def drain(self):
        for copy in self.started:
            copy.wait_send()
        self.started = []


def greet(devices, meanwhile=None):
    barrier = pltpu.get_barrier_semaphore()
    for device in devices:
        pl.semaphore_signal(barrier, inc=1, device_id=device, device_id_type=MESH)
    if meanwhile is not None:
        meanwhile()
    pl.semaphore_wait(barrier, len(devices))


def ring(place, axis):
    return [place.toward(axis, 1), place.toward(axis, 3)]


class RingGather:
    def __init__(self, net, place, axis, view, lo, hi):
        self.net = net
        me, nxt, prev = getattr(place, axis), place.step(axis, 1), place.step(axis, 3)
        right, left = ring(place, axis)
        self.to_right = net.copy(view(me), view(me), right)
        self.to_left = net.copy(view(me), view(me), left)
        self.on_right = net.copy(lo(prev), lo(prev), right)
        self.on_left = net.copy(hi(nxt), hi(nxt), left)

    def start(self):
        self.net.go(self.to_right)
        self.net.go(self.to_left)

    def forward(self):
        self.to_right.wait_recv()
        self.net.go(self.on_right)
        self.to_left.wait_recv()
        self.net.go(self.on_left)

    def finish(self):
        self.on_right.wait_recv()
        self.on_left.wait_recv()


class Direct:
    def __init__(self, net, place, axis, source, landing):
        self.net = net
        self.copies = [
            net.copy(
                source(place.step(axis, by)), landing(getattr(place, axis)), place.toward(axis, by)
            )
            for by in (2, 1, 3)
        ]

    def start(self):
        for copy in self.copies:
            self.net.go(copy)

    def wait(self):
        for copy in self.copies:
            copy.wait_recv()


def by_rows(ref, act):
    *lead, rows, _ = ref.shape
    block = next(size for size in (64, 48, 32, 16) if rows % size == 0)
    for spot in np.ndindex(*lead):

        def one(i, carry, spot=spot):
            act(spot, pl.ds(pl.multiple_of(i * block, block), block))
            return carry

        lax.fori_loop(0, rows // block, one, 0)


def add_to(target, other):
    def act(spot, rows):
        at = (*spot, rows, slice(None))
        target[at] = (target[at].astype(F32) + other[at].astype(F32)).astype(target.dtype)

    by_rows(target, act)


def sum_to(target, others):
    def act(spot, rows):
        at = (*spot, rows, slice(None))
        total = others[0][at].astype(F32)
        for other in others[1:]:
            total = total + other[at].astype(F32)
        target[at] = total.astype(target.dtype)

    by_rows(target, act)


def stepped(place, axis, view):
    return lambda by: view(place.step(axis, by))


class RingScatter:
    def __init__(self, net, place, axis, lo, hi, room, lo_here=None, hi_here=None):
        self.net, self.lo, self.hi = net, lo_here or lo, hi_here or hi
        right, left = ring(place, axis)
        self.lo1, self.lo_l, self.lo_r, self.hi1, self.hi_l, self.hi_r = room
        self.a = net.copy(lo(2), self.lo1, right)
        self.b = net.copy(hi(2), self.hi1, left)
        self.c_hi = net.copy(hi(1), self.hi_l, right)
        self.d_lo = net.copy(lo(3), self.lo_r, left)
        self.c_lo = net.copy(self.lo1, self.lo_l, right)
        self.d_hi = net.copy(self.hi1, self.hi_r, left)

    def start_far(self):
        self.net.go(self.a)
        self.net.go(self.b)

    def start_right(self):
        self.net.go(self.c_hi)

    def start_left(self):
        self.net.go(self.d_lo)

    def start(self):
        self.start_far()
        self.start_right()
        self.start_left()

    def middle_right(self):
        self.a.wait_recv()
        add_to(self.lo1, self.lo(1))
        self.net.go(self.c_lo)

    def middle_left(self):
        self.b.wait_recv()
        add_to(self.hi1, self.hi(3))
        self.net.go(self.d_hi)

    def middle(self):
        self.middle_right()
        self.middle_left()

    def finish(self, lo_out, hi_out):
        self.c_hi.wait_recv()
        self.d_hi.wait_recv()
        sum_to(hi_out, [self.hi(0), self.hi_l, self.hi_r])
        self.d_lo.wait_recv()
        self.c_lo.wait_recv()
        sum_to(lo_out, [self.lo(0), self.lo_l, self.lo_r])

    @staticmethod
    def room_shapes(lo_shape, hi_shape):
        return [pltpu.VMEM(lo_shape, BF)] * 3 + [pltpu.VMEM(hi_shape, BF)] * 3


def params(call_id):
    return pltpu.CompilerParams(
        collective_id=call_id, has_side_effects=True, vmem_limit_bytes=VMEM_BYTES
    )


def sems(count):
    return [pltpu.SemaphoreType.DMA((count,)), pltpu.SemaphoreType.DMA((count,))]


class WeightSwap:
    def __init__(self, net, place, w_ref, other_ref):
        self.net = net
        quarter = w_ref.shape[0] // 4
        right, left = ring(place, "x")

        def rows(ref, side):
            return ref.at[pl.ds(pl.multiple_of((2 * side + place.core) * quarter, 16), quarter)]

        self.first = [
            net.copy(rows(w_ref, side), rows(other_ref, side), (left, right)[side])
            for side in (0, 1)
        ]
        self.trades = [
            net.copy(rows(other_ref, side), rows(other_ref, side), place.partner())
            for side in (0, 1)
        ]

    def start(self):
        for copy in self.first:
            self.net.go(copy)

    def forward(self):
        for copy, trade in zip(self.first, self.trades):
            copy.wait_recv()
            self.net.go(trade)

    def finish(self):
        for trade in self.trades:
            trade.wait_recv()


def key_lines(place, ref):
    def stage(axis, first, at):
        return (
            axis,
            lambda j: ref.at[(pl.ds(first, 2), *at(j))],
            lambda j: ref.at[(first, *at(j))],
            lambda j: ref.at[(first + 1, *at(j))],
        )

    every = slice(None)
    return (
        (stage("x", 0, lambda j: (place.z, j)), stage("z", 0, lambda j: (j,))),
        (stage("z", 2, lambda j: (j, place.x)), stage("x", 2, lambda j: (every, j))),
    )


def key_tokens():
    z, x, row = np.meshgrid(np.arange(4), np.arange(4), np.arange(STRIPE), indexing="ij")
    return ((x // 2) * 2048 + z * 512 + (x % 2) * 128 + row).reshape(1, KEYS).astype(np.int32)


KEY_TOKENS = key_tokens()


def first_key(place, y):
    return y * 4096 + place.core * 256 + STRIPE * place.y


def contract(left, right, left_dim, right_dim):
    return lax.dot_general(
        left, right, (((left_dim,), (right_dim,)), ((), ())), preferred_element_type=F32
    )


def turn(u, cosine, sine):
    half = HD // 2
    low, high = u[:, :half], u[:, half:]
    return jnp.concatenate([low * cosine - high * sine, high * cosine + low * sine], axis=1)


def row_bounds(place, segments, y):
    at = (y * 2 + lax.div(place.x, 2)) * 16 + place.z * 4 + lax.rem(place.x, 2)
    rows = jnp.concatenate([segments[pl.ds(at, 1)], segments[pl.ds(at + 2, 1)]], axis=1)
    every = segments[...]
    first = jnp.zeros((1, ROWS), jnp.int32)
    for k in range(1, 4):
        below = jnp.sum((every < k).astype(F32), axis=0, keepdims=True)
        below = jnp.sum(below, axis=1, keepdims=True).astype(jnp.int32)
        first = jnp.where(rows == k, below, first)
    lane = lax.broadcasted_iota(jnp.int32, (1, ROWS), 1)
    last = at * TOK + lane + jnp.where(lane < TOK, 0, TOK)
    return first, last


def down(row):
    return jnp.concatenate(
        [
            jnp.transpose(jnp.broadcast_to(row[:, 128 * i : 128 * i + 128], (128, 128)))
            for i in range(row.shape[1] // 128)
        ],
        axis=0,
    )


def across(ref):
    return ref[...].reshape(1, ref.shape[0])


def norm_scale(v):
    return lax.rsqrt(jnp.mean(v * v, axis=-1, keepdims=True) + EPS)


def norm_back(v, r, gain, e):
    eg = e * gain
    dv = r * eg - v * (r * r * r) * jnp.mean(eg * v, axis=-1, keepdims=True)
    return dv, jnp.sum(e * v * r, axis=0, keepdims=True)


def forward_kernel(
    x_ref,
    g_attn,
    g_query,
    g_key,
    wq_ref,
    wk_ref,
    wv_ref,
    w_hbm,
    cos_ref,
    sin_ref,
    segments,
    key_ref,
    kv_hbm,
    q_all,
    wq_other,
    w_other,
    o_out,
    inv_out,
    q_pre,
    k_pre,
    h_out,
    buf,
    kv_own,
    o_sum,
    l_sum,
    o_snd,
    o_part,
    o_got,
    o_done,
    l_mine,
    l_got,
    l_core,
    *rest,
):
    *room, send, recv, local = rest
    place, net = Place(), Net(send, recv)
    core = place.core
    partner = place.partner()
    mine = pl.ds(pl.multiple_of(core * TOK, TOK), TOK)
    theirs = pl.ds(pl.multiple_of((1 - core) * TOK, TOK), TOK)

    def keys_and_values():
        xf = x_ref[...].astype(F32)
        h = (xf * norm_scale(xf) * across(g_attn)).astype(BF)
        h_out[...] = h
        k = jnp.dot(h, wk_ref[...], preferred_element_type=F32)
        k_pre[...] = k
        k = turn(k * norm_scale(k) * across(g_key), cos_ref[...], sin_ref[...]).astype(BF)
        v = jnp.dot(h, wv_ref[...], preferred_element_type=F32).astype(BF)
        for j in range(4):
            kv_own[j, :, :HD] = k[STRIPE * j : STRIPE * j + STRIPE]
            kv_own[j, :, HD:] = v[STRIPE * j : STRIPE * j + STRIPE]
        buf[place.y, place.z, place.x] = kv_own[place.y]

    greet(
        ring(place, "x")
        + ring(place, "y")
        + ring(place, "z")
        + [partner, place.toward("y", 2)],
        keys_and_values,
    )
    swap_wq = WeightSwap(net, place, wq_ref, wq_other)
    swap_w = WeightSwap(net, place, w_hbm, w_other)
    stripes = Direct(
        net,
        place,
        "y",
        lambda j: kv_own.at[j],
        lambda j: buf.at[j, place.z, place.x],
    )
    stripes.start()
    swap_wq.start()
    (first_a, then_a), (first_b, then_b) = (
        [RingGather(net, place, *stage) for stage in part] for part in key_lines(place, buf)
    )
    q_ring = RingGather(
        net,
        place,
        "y",
        lambda j: q_all.at[j, :, mine],
        lambda j: q_all.at[j, pl.ds(0, 2), mine],
        lambda j: q_all.at[j, pl.ds(2, 2), mine],
    )

    def block_of(by):
        return q_all.at[place.step("y", by), :, mine]

    q_core = [net.copy(block_of(by), block_of(by), partner) for by in range(4)]

    def queries(which, w):
        q = jnp.dot(h_out[...], w[...], preferred_element_type=F32)
        for i in range(2):
            u = q[:, HD * i : HD * i + HD]
            q_pre[2 * which + i] = u
            u = turn(u * norm_scale(u) * across(g_query), cos_ref[...], sin_ref[...])
            q_all[place.y, 2 * which + i, mine] = (u.astype(BF).astype(F32) * HD**-0.5).astype(BF)

    queries(0, wq_ref)
    stripes.wait()
    first_a.start()
    first_b.start()
    swap_wq.forward()
    first_a.forward()
    first_b.forward()
    swap_wq.finish()
    queries(1, wq_other)
    q_ring.start()
    net.go(q_core[0])
    first_a.finish()
    then_a.start()
    first_b.finish()
    then_b.start()
    q_ring.forward()
    net.go(q_core[1])
    net.go(q_core[3])
    then_a.forward()
    then_b.forward()
    q_ring.finish()
    net.go(q_core[2])
    then_a.finish()
    then_b.finish()
    swap_w.start()
    store = pltpu.make_async_copy(buf, kv_hbm, local.at[0])
    store.start()

    o_core = [net.copy(o_snd.at[by], o_got.at[by], partner) for by in range(4)]

    def attend(by):
        y = place.step("y", by)
        q_core[by].wait_recv()
        first, last = (down(row) for row in row_bounds(place, segments, y))

        keys = buf[:, :, :, :, :HD].reshape(4 * KEYS, HD)
        values = buf[:, :, :, :, HD:].reshape(4 * KEYS, HD)
        token = jnp.concatenate([key_ref[...] + first_key(place, j) for j in range(4)], axis=1)
        allowed = jnp.concatenate(
            [
                (token[:, 128 * i : 128 * i + 128] <= last)
                & (token[:, 128 * i : 128 * i + 128] >= first)
                for i in range(4 * KEYS // 128)
            ],
            axis=1,
        )
        for h in range(HEADS):
            weights = jnp.exp(contract(q_all[y, h], keys, 1, 1))
            weights = jnp.where(allowed, weights, 0.0)
            l_sum[by, h] = sum(
                weights[:, 128 * i : 128 * i + 128] for i in range(4 * KEYS // 128)
            )
            o_sum[by, h] = jnp.dot(weights.astype(BF), values, preferred_element_type=F32)
        for h in range(HEADS):
            o_snd[by, h] = o_sum[by, h, theirs].astype(BF)
            o_part[by, h] = o_sum[by, h, mine].astype(BF)
            total = jnp.sum(l_sum[by, h], axis=1, keepdims=True)
            l_mine[y, h : h + 1] = jnp.transpose(jnp.broadcast_to(total, (ROWS, 128)))[:1]
        net.go(o_core[by])

    def both_cores(by):
        o_core[by].wait_recv()
        add_to(o_part.at[by], o_got.at[by])

    o_ring = RingScatter(
        net,
        place,
        "y",
        lambda by: o_part.at[by, pl.ds(0, 2)],
        lambda by: o_part.at[by, pl.ds(2, 2)],
        room,
    )
    attend(0)
    attend(2)
    attend(1)
    both_cores(2)
    o_ring.start_far()
    swap_w.forward()
    attend(3)
    l_swap = Direct(net, place, "y", lambda j: l_mine.at[j], lambda j: l_got.at[j])
    l_swap.start()
    l_got[place.y] = l_mine[place.y]
    both_cores(1)
    o_ring.start_right()
    o_ring.middle_right()
    both_cores(3)
    o_ring.start_left()
    o_ring.middle_left()
    both_cores(0)
    swap_w.finish()
    l_swap.wait()
    l_core[core] = (l_got[0] + l_got[1]) + (l_got[2] + l_got[3])
    l_over = net.copy(l_core.at[core], l_core.at[core], partner)
    net.go(l_over)
    l_over.wait_recv()
    total = l_core[0] + l_core[1]
    inverse = 1.0 / jnp.where(core == 0, total[:, :TOK], total[:, TOK:])
    o_ring.finish(o_done.at[pl.ds(0, 2)], o_done.at[pl.ds(2, 2)])
    for h in range(HEADS):
        scale = down(inverse[h : h + 1])
        o_out[h] = o_done[h] * jnp.concatenate([scale, scale], axis=1)
        inv_out[h] = scale
    store.wait()
    net.drain()


def attention_forward(args, call_id):
    shape = jax.ShapeDtypeStruct
    anywhere = pl.BlockSpec(memory_space=pl.ANY)
    halves = (2, TOK, HD)
    return pl.pallas_call(
        forward_kernel,
        out_shape=(
            shape((4, 4, 4, STRIPE, 2 * HD), BF),
            shape((4, HEADS, ROWS, HD), BF),
            shape((D, 2 * HD), BF),
            shape((2 * HD, D), BF),
            shape((HEADS, TOK, HD), F32),
            shape((HEADS, TOK, 128), F32),
            shape((HEADS, TOK, HD), F32),
            shape((TOK, HD), F32),
            shape((TOK, D), BF),
        ),
        in_specs=[IN_VMEM] * 7 + [anywhere] + [IN_VMEM] * 4,
        out_specs=[anywhere] + [IN_VMEM] * 2 + [anywhere] + [IN_VMEM] * 5,
        scratch_shapes=[
            pltpu.VMEM((4, 4, 4, STRIPE, 2 * HD), BF),
            pltpu.VMEM((4, STRIPE, 2 * HD), BF),
            pltpu.VMEM((4, HEADS, ROWS, HD), F32),
            pltpu.VMEM((4, HEADS, ROWS, 128), F32),
            pltpu.VMEM((4, HEADS, TOK, HD), BF),
            pltpu.VMEM((4, HEADS, TOK, HD), BF),
            pltpu.VMEM((4, HEADS, TOK, HD), BF),
            pltpu.VMEM((HEADS, TOK, HD), F32),
            pltpu.VMEM((4, 8, ROWS), F32),
            pltpu.VMEM((4, 8, ROWS), F32),
            pltpu.VMEM((2, 8, ROWS), F32),
            *RingScatter.room_shapes(halves, halves),
            *sems(64),
            pltpu.SemaphoreType.DMA((1,)),
        ],
        compiler_params=params(call_id),
    )(*args)


def kept_head(place, j):
    return jnp.where(lax.rem(j, 2) == lax.rem(place.x, 2), 0, 2) + lax.div(j, 2)


def turn_back(e, cosine, sine):
    half = HD // 2
    low, high = e[:, :half], e[:, half:]
    return jnp.concatenate([low * cosine + high * sine, high * cosine - low * sine], axis=1)


def backward_kernel(
    kv_hbm,
    q_hbm,
    do_hbm,
    sums_hbm,
    wq_hbm,
    wq2_hbm,
    wk_hbm,
    wv_hbm,
    delta_all,
    key_ref,
    segments,
    q_pre,
    k_pre,
    cos_ref,
    sin_ref,
    h_ref,
    da_ref,
    o_ref,
    x_ref,
    dmid_ref,
    g_attn,
    g_query,
    g_key,
    gains_ref,
    dx_out,
    home_out,
    late_out,
    w_top,
    w_low,
    gains_out,
    buf,
    q_all,
    do_all,
    wq,
    wq2,
    wk,
    wv,
    tokens,
    grads,
    fin,
    fin_got,
    dq_sum,
    dq_snd,
    dq_part,
    dq_got,
    dq_done,
    h_line,
    da_line,
    turned,
    o_line,
    dq_line,
    dq_own,
    o_own,
    late_all,
    late_got,
    late_y,
    late_z,
    gain_got,
    kv_own,
    kv_line,
    turned_other,
    w_got,
    w_y,
    w_z,
    *rest,
):
    rooms, dq_rooms, late_rooms, rest = rest[:24], rest[24:30], rest[30:42], rest[42:]
    *weight_refs, send, recv, send2, recv2, here = rest
    place, net = Place(), Net(send, recv)
    core, partner = place.core, place.partner()
    w_loads = [
        pltpu.make_async_copy(source, target, here.at[1 + i])
        for i, (source, target) in enumerate(
            (
                (kv_hbm, buf),
                (q_hbm, q_all),
                (do_hbm, do_all),
                (wq_hbm, wq),
                (wq2_hbm, wq2),
                (wk_hbm, wk),
                (wv_hbm, wv),
            )
        )
    ]
    for load in w_loads:
        load.start()
    weights = WeightSums(place, net, sums_hbm, late_z, weight_refs, (send2, recv2, here))
    across_x = [place.device(x=place.step("x", by), core=1 - core) for by in (1, 3)]
    greet(
        weights.friends
        + ring(place, "x")
        + ring(place, "y")
        + across_x
        + [place.toward("y", 2)]
    )
    mine = pl.ds(pl.multiple_of(core * TOK, TOK), TOK)
    theirs = pl.ds(pl.multiple_of((1 - core) * TOK, TOK), TOK)
    half = TOK // 2

    def line_of(rows):
        return RingGather(
            net,
            place,
            "x",
            lambda j: rows.at[j],
            lambda j: rows.at[j, pl.ds(0, half)],
            lambda j: rows.at[j, pl.ds(half, half)],
        )

    def head_of(j):
        return kept_head(place, j)

    h_line[place.x] = h_ref[...]
    da_line[place.x] = da_ref[...]
    for h in range(HEADS):
        o_own[h] = o_ref[h].astype(BF)
    o_line[place.x] = o_own[head_of(place.x)]
    line_h, line_da = line_of(h_line), line_of(da_line)
    o_swap = Direct(net, place, "x", lambda j: o_own.at[head_of(j)], lambda j: o_line.at[j])
    dq_swap = Direct(net, place, "x", lambda j: dq_own.at[head_of(j)], lambda j: dq_line.at[j])
    line_da.start()
    o_swap.start()
    key_rings = []
    for i, (inner, outer) in enumerate(key_lines(place, grads)):
        for k, (axis, _, lo, hi) in enumerate((outer, inner)):
            spot = 12 * i + 6 * k
            key_rings.append(
                RingScatter(
                    net,
                    place,
                    axis,
                    stepped(place, axis, lo),
                    stepped(place, axis, hi),
                    rooms[spot : spot + 6],
                )
            )
    first_a, then_a, first_b, then_b = key_rings
    fin_swap = Direct(net, place, "y", lambda j: fin.at[j], lambda j: fin_got.at[j])
    dq_core = net.copy(dq_snd, dq_got, partner)
    dq_ring = RingScatter(
        net,
        place,
        "y",
        stepped(place, "y", lambda j: dq_part.at[j, pl.ds(0, 2)]),
        stepped(place, "y", lambda j: dq_part.at[j, pl.ds(2, 2)]),
        dq_rooms,
    )
    late_first = RingScatter(
        net,
        place,
        "y",
        stepped(place, "y", lambda j: late_got.at[j, 0]),
        stepped(place, "y", lambda j: late_got.at[j, 1]),
        late_rooms[:6],
    )

    def late_spot(j):
        return late_y.at[lax.div(j, 2), lax.rem(j, 2)]

    late_second = RingScatter(
        net,
        place,
        "z",
        stepped(place, "z", lambda j: late_spot(j).at[pl.ds(0, 80)]),
        stepped(place, "z", lambda j: late_spot(j).at[pl.ds(80, 64)]),
        late_rooms[6:],
    )

    def late_term(c, turned, columns):
        term = jnp.dot(
            turned[...], columns[...].reshape(4 * TOK, HD), preferred_element_type=F32
        ).astype(BF)
        for k in range(8):
            for which in range(2):
                late_all[which, k // 2, k % 2, c] = term[
                    144 * k : 144 * k + 144, 128 * which : 128 * which + 128
                ]

    weights.first.begin()
    weights.first.go_on()
    tokens[...] = down(key_ref[...])
    bounds = [row_bounds(place, segments, y) for y in range(4)]
    for load in w_loads[:3]:
        load.wait()

    def differ(key_y):
        keys = buf[key_y, :, :, :, :HD].reshape(KEYS, HD)
        values = buf[key_y, :, :, :, HD:].reshape(KEYS, HD)
        token = tokens[...] + first_key(place, key_y)
        token = jnp.concatenate([token, token], axis=1)
        d_keys = d_values = None
        for y in range(key_y, 4):
            first, last = bounds[y]
            allowed = (token <= last) & (token >= first)
            for h in range(HEADS):
                probs = jnp.exp(contract(keys, q_all[y, h], 1, 1))
                probs = jnp.where(allowed, probs, 0.0)
                delta = jnp.concatenate(
                    [delta_all[y, 0, h : h + 1], delta_all[y, 1, h : h + 1]], axis=1
                )
                d_scores = (probs * (contract(values, do_all[y, h], 1, 1) - delta)).astype(BF)
                value_term = jnp.dot(probs.astype(BF), do_all[y, h], preferred_element_type=F32)
                key_term = jnp.dot(d_scores, q_all[y, h], preferred_element_type=F32)
                d_values = value_term if d_values is None else d_values + value_term
                d_keys = key_term if d_keys is None else d_keys + key_term
                query_term = contract(keys, d_scores, 0, 0)
                if y == key_y:
                    dq_sum[y, h] = query_term
                else:
                    dq_sum[y, h] += query_term
        grads[key_y, :, :, :, :HD] = d_keys.astype(BF).reshape(4, 4, STRIPE, HD)
        grads[key_y, :, :, :, HD:] = d_values.astype(BF).reshape(4, 4, STRIPE, HD)

    differ(3)
    differ(2)
    first_b.start()
    line_da.forward()
    line_h.start()
    differ(1)
    first_b.middle()
    weights.first.turn()
    differ(0)
    first_a.start()
    for y in range(4):
        for h in range(HEADS):
            dq_snd[y, h] = dq_sum[y, h, :, theirs].astype(BF)
            dq_part[y, h] = dq_sum[y, h, :, mine].astype(BF)
    net.go(dq_core)
    dq_core.wait_recv()
    for y in range(4):
        add_to(dq_part.at[y], dq_got.at[y])
    dq_ring.start()
    first_a.middle()
    first_b.finish(first_b.lo(0), first_b.hi(0))
    then_b.start()
    first_a.finish(first_a.lo(0), first_a.hi(0))
    then_a.start()
    weights.next()
    line_h.forward()
    line_da.finish()
    o_swap.wait()
    turned[...] = jnp.transpose(da_line[...].reshape(4 * TOK, D))
    late_term(0, turned, o_line)
    dq_ring.middle()
    then_b.middle()
    then_a.middle()
    then_b.finish(fin.at[2], fin.at[3])
    then_a.finish(fin.at[0], fin.at[1])
    fin_got[place.y] = fin[place.y]
    fin_swap.start()
    for load in w_loads[3:]:
        load.wait()

    dq_ring.finish(dq_done.at[pl.ds(0, 2)], dq_done.at[pl.ds(2, 2)])
    d_query = jnp.zeros((1, HD), F32)
    for h in range(HEADS):
        e = jnp.transpose(dq_done[h]) * HD**-0.5
        e = turn_back(e.astype(BF).astype(F32), cos_ref[...], sin_ref[...])
        u = q_pre[h]
        du, gain = norm_back(u, norm_scale(u), across(g_query), e)
        d_query = d_query + gain
        dq_own[h] = du.astype(BF)
    dq_line[place.x] = dq_own[head_of(place.x)]
    dq_swap.start()
    line_h.finish()
    turned[...] = jnp.transpose(h_line[...].reshape(4 * TOK, D))
    turned_swap = net.copy(
        turned.at[pl.ds(pl.multiple_of((1 - core) * 576, 16), 576)], turned_other, partner
    )
    net.go(turned_swap)
    fin_swap.wait()

    dkv = jnp.concatenate([fin_got[j] for j in range(4)], axis=0)
    e = turn_back(dkv[:, :HD].astype(BF).astype(F32), cos_ref[...], sin_ref[...])
    u = k_pre[...]
    dk, d_key = norm_back(u, norm_scale(u), across(g_key), e)
    dk, dv = dk.astype(BF), dkv[:, HD:].astype(BF)
    for i in range(2):
        kv_own[i] = dk[:, 128 * i : 128 * i + 128]
        kv_own[2 + i] = dv[:, 128 * i : 128 * i + 128]
    kv_line[core, place.x] = kv_own[place.x]
    kv_swap = Direct(net, place, "x", lambda j: kv_own.at[j], lambda j: kv_line.at[core, j])
    kv_swap.start()
    kv_across = []
    for by in range(4):
        j = place.step("x", by)
        device = place.device(x=j, core=1 - core)
        kv_across.append(net.copy(kv_own.at[j], kv_line.at[core, place.x], device))
        net.go(kv_across[by])
    weights.turn_again()
    dq_swap.wait()
    late_term(1, turned, dq_line)
    late_swap = net.copy(late_all.at[1 - core], late_got, partner)
    net.go(late_swap)
    d_h = contract(dk, wk[...], 1, 1) + contract(dv, wv[...], 1, 1)
    for h in range(HEADS):
        w = (wq, wq2)[h // 2]
        d_h = d_h + contract(dq_own[h], w[:, 256 * (h % 2) : 256 * (h % 2) + 256], 1, 1)
    xf = x_ref[...].astype(F32)
    dx, d_attn = norm_back(xf, norm_scale(xf), across(g_attn), d_h)
    dx_out[...] = (dmid_ref[...] + dx).astype(BF)
    def gain_swap(level, axis):
        return Direct(
            net, place, axis, lambda j: gain_got.at[level, at(axis)], lambda j: gain_got.at[level, j]
        )

    def at(axis):
        return getattr(place, axis)

    def gain_sum(level):
        return (gain_got[level, 0] + gain_got[level, 1]) + (gain_got[level, 2] + gain_got[level, 3])

    swaps = [gain_swap(0, "x"), gain_swap(1, "y"), gain_swap(2, "z")]
    norms = jnp.concatenate([d_query, d_key, jnp.zeros((1, D - 2 * HD), F32)], axis=1)
    gain_got[0, place.x] = jnp.concatenate(
        [d_attn, gains_ref[0:3], norms, jnp.zeros((3, D), F32)], axis=0
    )
    swaps[0].start()
    turned_swap.wait_recv()
    kv_swap.wait()
    for copy in kv_across:
        copy.wait_recv()
    term = jnp.dot(
        turned[pl.ds(pl.multiple_of(core * 576, 16), 576)],
        kv_line[core].reshape(4 * TOK, 128),
        preferred_element_type=F32,
    )
    term += jnp.dot(
        turned_other[...], kv_line[1 - core].reshape(4 * TOK, 128), preferred_element_type=F32
    )
    term = term.astype(BF)
    for k in range(4):
        w_got[k] = term[144 * k : 144 * k + 144]
    w_scatter = Direct(net, place, "y", lambda j: w_got.at[j], lambda j: w_y.at[j])
    w_scatter.start()
    w_y[place.y] = w_got[place.y]
    late_swap.wait_recv()
    for y in range(4):
        add_to(late_got.at[y], late_all.at[core, y])
    late_first.start()
    swaps[0].wait()
    gain_got[1, place.y] = gain_sum(0)
    swaps[1].start()
    weights.last()
    swaps[1].wait()
    gain_got[2, place.z] = gain_sum(1)
    swaps[2].start()
    w_scatter.wait()
    sum_to(w_z.at[place.z], [w_y.at[j] for j in range(4)])
    w_sums = Direct(net, place, "z", lambda j: w_z.at[place.z], lambda j: w_z.at[j])
    w_sums.start()
    late_first.middle()
    swaps[2].wait()
    gain_got[3, core] = gain_sum(2)
    gain_last = net.copy(gain_got.at[3, core], gain_got.at[3, core], partner)
    net.go(gain_last)
    w_sums.wait()
    upper, lower = w_top.at[core], w_low.at[core]
    sum_to(upper.at[place.x, place.y], [w_z.at[j, pl.ds(0, 80)] for j in range(4)])
    sum_to(lower.at[place.x, place.y], [w_z.at[j, pl.ds(80, 64)] for j in range(4)])

    def spread(axis, view):
        return Direct(net, place, axis, lambda j: view(at(axis)), view)

    first_way = [
        spread("y", lambda j: upper.at[place.x, j]),
        spread("x", lambda j: lower.at[j, place.y]),
    ]
    second_way = [spread("x", lambda j: upper.at[j]), spread("y", lambda j: lower.at[:, j])]
    for line in first_way:
        line.start()
    late_first.finish(late_y.at[0], late_y.at[1])
    late_second.start()
    for line, then in zip(first_way, second_way):
        line.wait()
        then.start()
    late_second.middle()
    gain_last.wait_recv()
    gains_out[...] = gain_got[3, 0] + gain_got[3, 1]
    over = [net.copy(upper, upper, partner), net.copy(lower, lower, partner)]
    for line, copy in zip(second_way, over):
        line.wait()
        net.go(copy)
    late_second.finish(late_z.at[pl.ds(0, 80)], late_z.at[pl.ds(80, 64)])
    weights.send_late()
    for copy in over:
        copy.wait_recv()
    weights.arrive()
    home_out[...] = weights.rcv[...]
    late_out[...] = weights.late_rcv[...]
    net.drain()


def attention_backward(hbm, small, call_id):
    shape = jax.ShapeDtypeStruct
    rooms = []
    for _ in range(2):
        rooms += RingScatter.room_shapes((4, STRIPE, 2 * HD), (4, STRIPE, 2 * HD))
        rooms += RingScatter.room_shapes((STRIPE, 2 * HD), (STRIPE, 2 * HD))
    rooms += RingScatter.room_shapes((2, HD, TOK), (2, HD, TOK))
    late_rooms = [
        *RingScatter.room_shapes((2, 144, 128), (2, 144, 128)),
        *RingScatter.room_shapes((80, 128), (64, 128)),
    ]
    return pl.pallas_call(
        backward_kernel,
        out_shape=(
            shape((TOK, D), BF),
            shape((8, 16, HALF + 256), BF),
            shape((8, 16, 256), BF),
            shape((2, 4, 4, 80, 128), BF),
            shape((2, 4, 4, 64, 128), BF),
            shape((8, D), F32),
        ),
        in_specs=[pl.BlockSpec(memory_space=pl.ANY)] * len(hbm) + [IN_VMEM] * len(small),
        out_specs=[IN_VMEM] * 6,
        scratch_shapes=[
            pltpu.VMEM((4, 4, 4, STRIPE, 2 * HD), BF),
            pltpu.VMEM((4, HEADS, ROWS, HD), BF),
            pltpu.VMEM((4, HEADS, ROWS, HD), BF),
            pltpu.VMEM((D, 2 * HD), BF),
            pltpu.VMEM((D, 2 * HD), BF),
            pltpu.VMEM((D, HD), BF),
            pltpu.VMEM((D, HD), BF),
            pltpu.VMEM((KEYS, 128), jnp.int32),
            pltpu.VMEM((4, 4, 4, STRIPE, 2 * HD), BF),
            pltpu.VMEM((4, STRIPE, 2 * HD), F32),
            pltpu.VMEM((4, STRIPE, 2 * HD), F32),
            pltpu.VMEM((4, HEADS, HD, ROWS), F32),
            pltpu.VMEM((4, HEADS, HD, TOK), BF),
            pltpu.VMEM((4, HEADS, HD, TOK), BF),
            pltpu.VMEM((4, HEADS, HD, TOK), BF),
            pltpu.VMEM((HEADS, HD, TOK), F32),
            pltpu.VMEM((4, TOK, D), BF),
            pltpu.VMEM((4, TOK, D), BF),
            pltpu.VMEM((D, 4 * TOK), BF),
            pltpu.VMEM((4, TOK, HD), BF),
            pltpu.VMEM((4, TOK, HD), BF),
            pltpu.VMEM((4, TOK, HD), BF),
            pltpu.VMEM((4, TOK, HD), BF),
            pltpu.VMEM((2, 4, 2, 2, 144, 128), BF),
            pltpu.VMEM((4, 2, 2, 144, 128), BF),
            pltpu.VMEM((2, 2, 144, 128), BF),
            pltpu.VMEM((144, 128), F32),
            pltpu.VMEM((4, 4, 8, D), F32),
            pltpu.VMEM((4, TOK, 128), BF),
            pltpu.VMEM((2, 4, TOK, 128), BF),
            pltpu.VMEM((576, 4 * TOK), BF),
            pltpu.VMEM((4, 144, 128), BF),
            pltpu.VMEM((4, 144, 128), BF),
            pltpu.VMEM((4, 144, 128), BF),
            *rooms,
            *late_rooms,
            *WeightSums.scratch(),
            *sems(160),
            *sems(16),
            pltpu.SemaphoreType.DMA((24,)),
        ],
        compiler_params=params(call_id),
    )(*hbm, *small)


def feed_kernel(
    x_ref,
    o_ref,
    inv_ref,
    wo_ref,
    wo2_ref,
    post_ref,
    ffn_ref,
    out_gain_ref,
    cot_ref,
    wg_hbm,
    wu_hbm,
    wd_hbm,
    out_ref,
    dmid_out,
    dattn_out,
    do_all,
    delta_all,
    dgains_out,
    sums_hbm,
    wg,
    wu,
    wd,
    h_line,
    f_line,
    h_turned,
    f_turned,
    gelu_kept,
    slope_kept,
    act,
    d_gate,
    d_up,
    f_terms,
    h_terms,
    snd,
    got,
    attn,
    mid,
    ffn,
    delta_rows,
    *rest,
):
    *room, send, recv, local = rest
    place, net = Place(), Net(send, recv)
    core, partner = place.core, place.partner()
    x_hi = lax.div(place.x, 2)
    first_unit = pl.multiple_of(x_hi * (2 * HID - HID_PAD), 128)
    window = pl.ds(first_unit, HID_PAD)
    loads = [
        pltpu.make_async_copy(source, target, local.at[i])
        for i, (source, target) in enumerate(
            ((wg_hbm.at[:, window], wg), (wu_hbm.at[:, window], wu), (wd_hbm.at[window], wd))
        )
    ]
    for load in loads:
        load.start()
    greet(
        ring(place, "x")
        + ring(place, "y")
        + ring(place, "z")
        + [partner, place.toward("y", 2)]
    )
    half, quarter = TOK // 2, TOK // 4
    top, bottom = pl.ds(0, quarter), pl.ds(quarter, quarter)
    g_post, g_ffn, g_out = (across(ref) for ref in (post_ref, ffn_ref, out_gain_ref))

    def rows_of(part):
        return slice(half * part, half * part + half)

    def lines_of(part):
        return slice(4 * half * part, 4 * half * part + 4 * half)

    def gather(lines):
        return RingGather(
            net,
            place,
            "x",
            lambda j: lines.at[j],
            lambda j: lines.at[j, top],
            lambda j: lines.at[j, bottom],
        )

    def scatter(terms, room):
        return RingScatter(
            net,
            place,
            "x",
            stepped(place, "x", lambda j: terms.at[j, top]),
            stepped(place, "x", lambda j: terms.at[j, bottom]),
            room,
        )

    def summed(line, part):
        at = half * part
        line.finish(ffn.at[pl.ds(at, quarter)], ffn.at[pl.ds(at + quarter, quarter)])

    o_cat = [o_ref[h].astype(BF) for h in range(HEADS)]
    a = jnp.dot(jnp.concatenate(o_cat[:2], axis=1), wo_ref[...], preferred_element_type=F32)
    a += jnp.dot(jnp.concatenate(o_cat[2:], axis=1), wo2_ref[...], preferred_element_type=F32)
    attn[...] = a
    mid[...] = x_ref[...].astype(F32) + a * norm_scale(a) * g_post
    m = mid[...]
    h = (m * norm_scale(m) * g_ffn).astype(BF)
    for part in range(2):
        h_line[part, place.x] = h[rows_of(part)]
    h_gathers = [gather(h_line.at[part]) for part in range(2)]
    f_gathers = [gather(f_line.at[part]) for part in range(2)]
    f_sums = [scatter(f_terms.at[part], room[6 * part : 6 * part + 6]) for part in range(2)]
    h_sums = [
        scatter(h_terms.at[part], room[12 + 6 * part : 18 + 6 * part]) for part in range(2)
    ]
    h_gathers[0].start()

    for load in loads:
        load.wait()
    low_unit, high_unit = jnp.where(x_hi == 0, 0, 64), jnp.where(x_hi == 0, HID, HID_PAD)

    def units(n):
        return pl.ds(pl.multiple_of(n * 256, 256), 256)

    def forward(part, n, carry):
        h = h_line[part].reshape(4 * half, D)
        gate = jnp.dot(h, wg[:, units(n)], preferred_element_type=F32)
        up = jnp.dot(h, wu[:, units(n)], preferred_element_type=F32)
        unit = n * 256 + lax.broadcasted_iota(jnp.int32, (1, 256), 1)
        own = jnp.where((unit >= low_unit) & (unit < high_unit), 1.0, 0.0)
        scale, cube = 0.7978845608028654, 0.044715
        square = gate * gate
        bent = jnp.tanh(scale * gate * (1.0 + cube * square))
        lifted = 0.5 * (1.0 + bent)
        gelu = gate * lifted * own
        slope = lifted + 0.5 * gate * (1.0 - bent * bent) * scale * (1.0 + 3.0 * cube * square)
        act[lines_of(part), units(n)] = (gelu * up).astype(BF)
        gelu_kept[lines_of(part), units(n)] = gelu.astype(BF)
        slope_kept[lines_of(part), units(n)] = (slope * up * own).astype(BF)
        return carry

    def columns(n):
        return pl.ds(pl.multiple_of(n * 384, 128), 384)

    def project(part, n, carry):
        term = jnp.dot(act[lines_of(part)], wd[:, columns(n)], preferred_element_type=F32)
        f_terms[part, :, :, columns(n)] = term.astype(BF).reshape(4, half, 384)
        return carry

    def backward(part, n, carry):
        d_act = contract(f_line[part].reshape(4 * half, D), wd[units(n)], 1, 1)
        rows = lines_of(part)
        d_gate[rows, units(n)] = (d_act * slope_kept[rows, units(n)].astype(F32)).astype(BF)
        d_up[rows, units(n)] = (d_act * gelu_kept[rows, units(n)].astype(F32)).astype(BF)
        return carry

    def back_project(part, n, carry):
        rows = lines_of(part)
        term = contract(d_gate[rows], wg[columns(n)], 1, 1)
        term += contract(d_up[rows], wu[columns(n)], 1, 1)
        h_terms[part, :, :, columns(n)] = term.astype(BF).reshape(4, half, 384)
        return carry

    def each(times, step, part):
        lax.fori_loop(0, times, functools.partial(step, part), 0)

    blocks = HID_PAD // 256

    def turn_round(part):
        rows = rows_of(part)
        summed(f_sums[part], part)
        f = ffn[rows]
        r = norm_scale(f)
        out_ref[rows] = (mid[rows] + f * r * g_out).astype(BF)
        df, gain = norm_back(f, r, g_out, cot_ref[rows].astype(F32))
        f_line[part, place.x] = df.astype(BF)
        f_gathers[part].start()
        return gain

    h_gathers[0].forward()
    h_gathers[1].start()
    h_gathers[0].finish()
    each(blocks, forward, 0)
    h_gathers[1].forward()
    each(3, project, 0)
    f_sums[0].start()
    h_gathers[1].finish()
    each(blocks, forward, 1)
    f_sums[0].middle()
    each(3, project, 1)
    f_sums[1].start()
    d_out = turn_round(0)
    f_sums[1].middle()
    h_turned[...] = jnp.transpose(h_line[...].reshape(8 * half, D))
    f_gathers[0].forward()
    d_out = d_out + turn_round(1)
    f_gathers[0].finish()
    each(blocks, backward, 0)
    f_gathers[1].forward()
    each(3, back_project, 0)
    h_sums[0].start()
    f_gathers[1].finish()

    def halves_of(which):
        return pl.ds(pl.multiple_of(which * 896, 128), 896)

    def fill(target, i, which, left, right, spans, add):
        term = jnp.dot(
            left[576 * i : 576 * i + 576], right[:, halves_of(which)], preferred_element_type=F32
        )
        for k in range(4):
            for half, low, high, start in spans:
                at = (2 * i + k // 2, k % 2, half, slice(None), slice(start, start + high - low))
                value = term[144 * k : 144 * k + 144, low:high]
                if add:
                    value = value + target[at].astype(F32)
                target[at] = value.astype(BF)

    down_spans = ((0, 0, 256, 0), (0, 256, 512, CUT), (1, 512, 768, 0), (1, 768, 896, CUT))

    def fill_down(target, i, which, add):
        fill(target, i, which, f_turned, act, down_spans, add)

    def fill_others(target, i, which, add):
        for c, right in enumerate((d_gate, d_up)):
            spans = ((c, 0, 512, 256), (c, 512, 896, CUT + 256))
            fill(target, i, which, h_turned, right, spans, add)

    for y in range(4):
        snd[y, :, 1, :, CUT + 128 : CUT + 256] = jnp.zeros((2, 144, 128), BF)
    swaps = [net.copy(snd.at[y], got.at[y], partner) for y in range(4)]
    each(blocks, backward, 1)
    h_sums[0].middle()
    each(3, back_project, 1)
    h_sums[1].start()
    def mine_of(part):
        return pl.ds(pl.multiple_of(core * TOK + half * part, half), half)

    def do_ring_of(part):
        mine = mine_of(part)
        return RingGather(
            net,
            place,
            "y",
            lambda j: do_all.at[j, :, mine],
            lambda j: do_all.at[j, pl.ds(0, 2), mine],
            lambda j: do_all.at[j, pl.ds(2, 2), mine],
        )

    def block_of(part, by):
        return do_all.at[place.step("y", by), :, mine_of(part)]

    do_rings = [do_ring_of(part) for part in range(2)]
    do_core = [
        [net.copy(block_of(part, by), block_of(part, by), partner) for by in range(4)]
        for part in range(2)
    ]
    delta_swap = Direct(
        net,
        place,
        "y",
        lambda j: delta_all.at[place.y, core],
        lambda j: delta_all.at[j, core],
    )
    delta_core = net.copy(delta_all.at[:, core], delta_all.at[:, core], partner)

    def heads_back(part):
        rows = rows_of(part)
        m, a = mid[rows], attn[rows]
        dm, d_ffn = norm_back(m, norm_scale(m), g_ffn, ffn[rows])
        d_mid = cot_ref[rows].astype(F32) + dm
        dmid_out[rows] = d_mid
        da, d_post = norm_back(a, norm_scale(a), g_post, d_mid)
        da = da.astype(BF)
        dattn_out[rows] = da
        for h in range(HEADS):
            w = (wo_ref, wo2_ref)[h // 2][256 * (h % 2) : 256 * (h % 2) + 256]
            d_o = contract(da, w, 1, 1).astype(BF).astype(F32)
            inverse = inv_ref[h, rows]
            scaled = d_o * jnp.concatenate([inverse, inverse], axis=1)
            do_all[place.y, h, mine_of(part)] = scaled.astype(BF)
            delta_rows[h, rows] = jnp.sum(d_o * o_ref[h, rows], axis=1, keepdims=True) * inverse
        do_rings[part].start()
        net.go(do_core[part][0])
        return d_post, d_ffn

    for i in range(2):
        fill_others(snd, i, 1 - core, False)
    h_sums[1].middle()
    summed(h_sums[0], 0)
    gains_top = heads_back(0)
    f_turned[...] = jnp.transpose(f_line[...].reshape(8 * half, D))
    for i in range(2):
        fill_down(snd, i, 1 - core, False)
        net.go(swaps[2 * i])
        net.go(swaps[2 * i + 1])
    summed(h_sums[1], 1)
    gains_low = heads_back(1)
    d_post, d_ffn = (top + low for top, low in zip(gains_top, gains_low))
    dgains_out[...] = jnp.concatenate([d_post, d_ffn, d_out, jnp.zeros((5, D), F32)], axis=0)
    delta_all[place.y, core] = jnp.concatenate(
        [jnp.transpose(delta_rows[h])[:1] for h in range(HEADS)] + [jnp.zeros((4, TOK), F32)],
        axis=0,
    )
    delta_swap.start()
    stores = [pltpu.make_async_copy(got.at[y], sums_hbm.at[y], local.at[3 + y]) for y in range(4)]

    def do_near(part):
        do_rings[part].forward()
        net.go(do_core[part][1])
        net.go(do_core[part][3])

    def do_far(part):
        do_rings[part].finish()
        net.go(do_core[part][2])

    do_near(0)
    for i in range(2):
        swaps[2 * i].wait_recv()
        swaps[2 * i + 1].wait_recv()
        fill_others(got, i, core, True)
        fill_down(got, i, core, True)
        stores[2 * i].start()
        stores[2 * i + 1].start()
        if i == 0:
            do_far(0)
            do_near(1)
    do_far(1)
    delta_swap.wait()
    net.go(delta_core)
    for copies in do_core:
        for copy in copies:
            copy.wait_recv()
    delta_core.wait_recv()
    for store in stores:
        store.wait()
    net.drain()


def feed_forward(args, call_id):
    quarter = (TOK // 4, D)
    shape = jax.ShapeDtypeStruct
    every = (4, 2, 2, 144, HALF)
    lines = 4 * TOK
    anywhere = pl.BlockSpec(memory_space=pl.ANY)
    unit_rows = [pltpu.VMEM((lines, HID_PAD), BF)] * 5
    return pl.pallas_call(
        feed_kernel,
        out_shape=(
            shape((TOK, D), BF),
            shape((TOK, D), F32),
            shape((TOK, D), BF),
            shape((4, HEADS, ROWS, HD), BF),
            shape((4, 2, 8, TOK), F32),
            shape((8, D), F32),
            shape(every, BF),
        ),
        in_specs=[IN_VMEM] * 9 + [anywhere] * 3,
        out_specs=[IN_VMEM] * 6 + [anywhere],
        scratch_shapes=[
            pltpu.VMEM((D, HID_PAD), BF),
            pltpu.VMEM((D, HID_PAD), BF),
            pltpu.VMEM((HID_PAD, D), BF),
            pltpu.VMEM((2, 4, TOK // 2, D), BF),
            pltpu.VMEM((2, 4, TOK // 2, D), BF),
            pltpu.VMEM((D, lines), BF),
            pltpu.VMEM((D, lines), BF),
            *unit_rows,
            pltpu.VMEM((2, 4, TOK // 2, D), BF),
            pltpu.VMEM((2, 4, TOK // 2, D), BF),
            pltpu.VMEM(every, BF),
            pltpu.VMEM(every, BF),
            pltpu.VMEM((TOK, D), F32),
            pltpu.VMEM((TOK, D), F32),
            pltpu.VMEM((TOK, D), F32),
            pltpu.VMEM((HEADS, TOK, TOK), F32),
            *(RingScatter.room_shapes(quarter, quarter) * 4),
            *sems(88),
            pltpu.SemaphoreType.DMA((7,)),
        ],
        compiler_params=params(call_id),
    )(*args)


class FirstSums:
    def __init__(self, net, place, sums, cut, rooms, here=None, marks=None):
        left, right = pl.ds(0, cut), pl.ds(cut, sums.shape[-1] - cut)

        def y_spot(half):
            return stepped(place, "y", lambda j: sums.at[j, half, :, :, left])

        def z_spot(half):
            return stepped(
                place,
                "z",
                lambda j: sums.at[pl.ds(2 * half, 2), lax.div(j, 2), lax.rem(j, 2), :, right],
            )

        self.loads = []
        self.lines = []
        for i, (axis, spot) in enumerate((("y", y_spot), ("z", z_spot))):
            near = (None, None)
            if here is not None:
                near = ({}, {})
                for k, (half, by) in enumerate(((0, 1), (1, 3), (0, 0), (1, 0))):
                    target = here[i].at[k]
                    near[half][by] = target
                    self.loads.append(
                        pltpu.make_async_copy(spot(half)(by), target, marks.at[8 + 4 * i + k])
                    )
                near = (near[0].get, near[1].get)
            room = rooms[6 * i : 6 * i + 6]
            self.lines.append(RingScatter(net, place, axis, spot(0), spot(1), room, *near))

    @staticmethod
    def room_shapes(cut, rest):
        return [
            *RingScatter.room_shapes((2, 144, cut), (2, 144, cut)),
            *RingScatter.room_shapes((2, 144, rest), (2, 144, rest)),
        ]

    def begin(self):
        for load in self.loads:
            load.start()
        for line in self.lines:
            line.start_far()

    def go_on(self):
        for line in self.lines:
            line.start_right()
            line.start_left()

    def turn(self):
        for load in self.loads:
            load.wait()
        for line in self.lines:
            line.middle()


class WeightSums:
    def __init__(self, place, net, sums, late, refs, marks):
        y_here, z_here, y1, z1, z2, y2, snd, late_snd, rcv, late_rcv, *rooms = refs
        self.late_snd, self.late_rcv = late_snd, late_rcv
        self.place, self.late, self.snd, self.rcv, self.marks = place, late, snd, rcv, marks
        self.y1, self.z1, self.y2, self.z2 = y1, z1, y2, z2
        self.x_hi, self.x_lo = lax.div(place.x, 2), lax.rem(place.x, 2)
        self.friends = []
        for k in range(1, 16):
            spot = lax.rem(self.x_hi * 8 + place.z * 2 + place.core + k, 16)
            x, z = lax.div(spot, 8) * 2 + self.x_lo, lax.rem(lax.div(spot, 2), 4)
            self.friends.append(place.device(x=x, z=z, core=lax.rem(spot, 2)))

        self.first = FirstSums(net, place, sums, CUT, rooms[:12], (y_here, z_here), marks[2])

        def then_z(j):
            return y1.at[lax.div(j, 2), lax.rem(j, 2)]

        self.z_second = RingScatter(
            net,
            place,
            "z",
            stepped(place, "z", lambda j: then_z(j).at[:, pl.ds(0, 384)]),
            stepped(place, "z", lambda j: then_z(j).at[:, pl.ds(384, 384)]),
            rooms[12:18],
        )
        self.y_second = RingScatter(
            net,
            place,
            "y",
            stepped(place, "y", lambda j: z1.at[j, :, pl.ds(0, 384)]),
            stepped(place, "y", lambda j: z1.at[j, :, pl.ds(384, 256)]),
            rooms[18:24],
        )

    @staticmethod
    def scratch():
        rest = HALF - CUT
        return [
            pltpu.VMEM((4, 2, 144, CUT), BF),
            pltpu.VMEM((4, 2, 144, rest), BF),
            pltpu.VMEM((2, 2, 144, CUT), BF),
            pltpu.VMEM((4, 144, rest), BF),
            pltpu.VMEM((144, CUT), F32),
            pltpu.VMEM((144, rest), F32),
            pltpu.VMEM((8, 16, HALF + 256), BF),
            pltpu.VMEM((8, 16, 256), BF),
            pltpu.VMEM((8, 16, HALF + 256), BF),
            pltpu.VMEM((8, 16, 256), BF),
            *FirstSums.room_shapes(CUT, rest),
            *RingScatter.room_shapes((144, 384), (144, 384)),
            *RingScatter.room_shapes((144, 384), (144, 256)),
        ]

    def next(self):
        y_line, z_line = self.first.lines
        y_line.finish(self.y1.at[0], self.y1.at[1])
        self.z_second.start()
        z_line.finish(self.z1.at[pl.ds(0, 2)], self.z1.at[pl.ds(2, 2)])
        self.y_second.start()

    def turn_again(self):
        self.z_second.middle()
        self.y_second.middle()

    def last(self):
        z2, y2 = self.z2, self.y2
        self.z_second.finish(z2.at[:, pl.ds(0, 384)], z2.at[:, pl.ds(384, 384)])
        self.y_second.finish(y2.at[:, pl.ds(0, 384)], y2.at[:, pl.ds(384, 256)])
        total = jnp.concatenate([z2[...], y2[...]], axis=1)
        self.pack(total, self.snd)
        self.exchange(self.snd, self.rcv, 0)

    def send_late(self):
        self.pack(self.late[...], self.late_snd)
        self.exchange(self.late_snd, self.late_rcv, 8)

    @staticmethod
    def pack(total, snd):
        width = total.shape[1]
        count = width // 128
        for k in range(8):
            extra = total[18 * k + 16 : 18 * k + 18]
            pieces = [extra[:, 128 * n : 128 * n + 128] for n in range(count)]
            snd[k, :, :width] = total[18 * k : 18 * k + 16].astype(BF)
            for n in range(0, count, 8):
                group = pieces[n : n + 8]
                if len(group) < 8:
                    group.append(jnp.zeros((16 - 2 * len(group), 128), F32))
                at = width + 16 * n
                snd[k, :, at : at + 128] = jnp.concatenate(group, axis=0).astype(BF)

    def exchange(self, snd, rcv, mark):
        place = self.place
        send, recv, here = self.marks
        row_half = lax.div(place.z, 2)
        self.slot = self.x_hi * 4 + place.core * 2 + lax.rem(place.z, 2)
        self.own = place.z * 2 + place.core
        self.stays = row_half == self.x_hi
        for k in range(8):
            copy = pltpu.make_async_remote_copy(
                src_ref=snd.at[k],
                dst_ref=rcv.at[self.slot],
                send_sem=send.at[mark + k],
                recv_sem=recv.at[mark + self.slot],
                device_id=place.device(x=row_half * 2 + self.x_lo, z=k // 2, core=k % 2),
                device_id_type=MESH,
            )
            is_here = self.stays & (self.own == k)

            @pl.when(jnp.logical_not(is_here))
            def _(copy=copy):
                copy.start()

            @pl.when(is_here)
            def _(k=k):
                keep = pltpu.make_async_copy(snd.at[k], rcv.at[self.slot], here.at[0])
                keep.start()
                keep.wait()

    def arrive(self):
        send, recv, _ = self.marks
        for mark, snd, rcv in ((0, self.snd, self.rcv), (8, self.late_snd, self.late_rcv)):
            for m in range(8):
                arrival = pltpu.make_async_remote_copy(
                    src_ref=snd.at[m],
                    dst_ref=rcv.at[m],
                    send_sem=send.at[mark + m],
                    recv_sem=recv.at[mark + m],
                    device_id=self.place.partner(),
                    device_id_type=MESH,
                )

                @pl.when(jnp.logical_not(self.stays & (self.slot == m)))
                def _(arrival=arrival):
                    arrival.wait_recv()

                @pl.when(jnp.logical_not(self.stays & (self.own == m)))
                def _(arrival=arrival):
                    arrival.wait_send()


def last_kernel(
    home_ref,
    late_ref,
    top_ref,
    low_ref,
    gains_ref,
    y_ref,
    dx_ref,
    y_out,
    dx_out,
    dwq_out,
    dwk_out,
    dwv_out,
    dwo_out,
    dwg_out,
    dwu_out,
    dwd_out,
    *gain_outs,
):
    y_out[...] = y_ref[...]
    dx_out[...] = dx_ref[...]

    def rows_at(ref, slot, n):
        spare = (HALF if ref is home_ref else 128) + 128 * (n // 8)
        more = ref[slot, :, spare : spare + 128].astype(F32)[2 * (n % 8) : 2 * (n % 8) + 2]
        return jnp.concatenate(
            [ref[slot, :, 128 * n : 128 * n + 128].astype(F32), more], axis=0
        )

    def tile(x_hi, which, n):
        core, n = n // 7, n % 7
        if which < 2:
            c, at = which, 256 + 128 * n if n < 4 else 512 + 128 * n
        else:
            c, n = n // 4, n % 4
            at = 128 * n if n < 2 else CUT + 128 * (n - 2)
        return rows_at(home_ref, x_hi * 4 + core * 2 + c, at // 128)

    for which, out in enumerate((dwg_out, dwu_out, dwd_out)):
        for n in range(27):
            value = None
            for x_hi in range(2):
                if 0 <= n - 13 * x_hi < 14:
                    term = tile(x_hi, which, n - 13 * x_hi)
                    value = term if value is None else value + term
            span = slice(128 * n, 128 * n + 128)
            out[:, span] = value
    for k in range(4):
        span = slice(128 * k, 128 * k + 128)
        dwo_out[:, span] = rows_at(late_ref, 2 * k, 0)
        dwq_out[:, span] = rows_at(late_ref, 2 * k + 1, 0)
    for which in range(2):
        for j in range(4):
            out = (dwk_out, dwv_out)[j // 2]
            for y in range(4):
                span = slice(128 * (j % 2), 128 * (j % 2) + 128)
                at = 576 * which + 144 * y
                out[at : at + 80, span] = top_ref[which, j, y].astype(F32)
                out[at + 80 : at + 144, span] = low_ref[which, j, y].astype(F32)
    for out, row, start in zip(gain_outs, (0, 4, 4, 1, 2, 3), (0, 0, HD, 0, 0, 0)):
        size = out.shape[0]
        out[...] = gains_ref[row : row + 1, start : start + size].reshape(size)


def last_layout(*args):
    shape = jax.ShapeDtypeStruct
    return pl.pallas_call(
        last_kernel,
        out_shape=(
            shape((TOK, D), BF),
            shape((TOK, D), BF),
            shape((18, 2 * HD), F32),
            shape((D, HD), F32),
            shape((D, HD), F32),
            shape((18, 2 * HD), F32),
            shape((18, 2 * HID), F32),
            shape((18, 2 * HID), F32),
            shape((18, 2 * HID), F32),
            *(shape((size,), F32) for size in (D, HD, HD, D, D, D)),
        ),
        in_specs=[IN_VMEM] * len(args),
        out_specs=[IN_VMEM] * 15,
        compiler_params=pltpu.CompilerParams(vmem_limit_bytes=VMEM_BYTES),
    )(*args)


def angles(token_pos):
    middle = HD // 2
    frequency = THETA ** (-2.0 * jnp.arange(middle, dtype=F32) / HD)
    turned = token_pos.astype(F32)[:, None] * frequency[None, :]
    return (jnp.cos(turned), jnp.sin(turned))


def shards(
    layer_input,
    segment_ids,
    positions,
    w_query,
    w_key,
    w_value,
    w_out,
    w_gate,
    w_up,
    w_down,
    norm_attn,
    norm_query,
    norm_key,
    norm_post,
    norm_ffn,
    norm_out,
    cotangent,
):
    sp, tp = lax.axis_index("sp"), lax.axis_index("tp")
    cosine, sine = angles(lax.dynamic_slice_in_dim(positions, (sp * 2 + tp) * TOK, TOK))
    segments = segment_ids.reshape(128, 128)
    key_rows = jnp.asarray(KEY_TOKENS)
    kv_all, q_all, wq_other, wo_other, o_heads, inverse, q_pre, k_pre, h_attn = attention_forward(
        (
            layer_input,
            norm_attn,
            norm_query,
            norm_key,
            w_query,
            w_key,
            w_value,
            w_out,
            cosine,
            sine,
            segments,
            key_rows,
        ),
        2,
    )
    (
        layer_output,
        d_mid,
        d_attn,
        d_heads,
        delta,
        d_gains,
        sums,
    ) = feed_forward(
        (
            layer_input,
            o_heads,
            inverse,
            w_out,
            wo_other,
            norm_post,
            norm_ffn,
            norm_out,
            cotangent,
            w_gate,
            w_up,
            w_down,
        ),
        6,
    )
    d_input, home, late, w_top, w_low, gains = attention_backward(
        (kv_all, q_all, d_heads, sums, w_query, wq_other, w_key, w_value),
        (
            delta,
            key_rows,
            segments,
            q_pre,
            k_pre,
            cosine,
            sine,
            h_attn,
            d_attn,
            o_heads,
            layer_input,
            d_mid,
            norm_attn,
            norm_query,
            norm_key,
            d_gains,
        ),
        8,
    )
    y, dx, d_wq, d_wk, d_wv, d_wo, d_wg, d_wu, d_wd, *d_norms = last_layout(
        home, late, w_top, w_low, gains, layer_output, d_input
    )
    return (y, dx, d_wq, d_wk, d_wv, d_wo.T, d_wg, d_wu, d_wd.T, *d_norms)


def solution(mesh):
    rows = P(("sp", "tp"), None)
    in_specs = (
        rows,
        P(),
        P(),
        P(None, "tp"),
        P(),
        P(),
        P("tp", None),
        P(None, "tp"),
        P(None, "tp"),
        P("tp", None),
        P(),
        P(),
        P(),
        P(),
        P(),
        P(),
        rows,
    )
    out_specs = (
        rows,
        rows,
        P("sp", "tp"),
        P(),
        P(),
        P("tp", "sp"),
        P("sp", "tp"),
        P("sp", "tp"),
        P("tp", "sp"),
        P(),
        P(),
        P(),
        P(),
        P(),
        P(),
    )
    return jax.shard_map(shards, mesh=mesh, in_specs=in_specs, out_specs=out_specs, check_vma=False)
```

```python
import functools

import jax
import jax.numpy as jnp
import numpy as np
from jax import lax
from jax.experimental import pallas as pl
from jax.experimental.pallas import tpu as pltpu
from jax.sharding import PartitionSpec as P

EPS = 1e-06
THETA = 1000000.0
BF = jnp.bfloat16
F32 = jnp.float32
MESH = pl.DeviceIdType.MESH
IN_VMEM = pl.BlockSpec(memory_space=pltpu.VMEM)
VMEM_BYTES = 58 * 1024 * 1024

TOK = 128
D = 1152
HD = 256
HEADS = 4
ROWS = 2 * TOK
HID = 1728
HID_PAD = 1792
CUT = 768
HALF = 1408
STRIPE = TOK // 4
KEYS = 16 * STRIPE


class Place:
    def __init__(self):
        sp = lax.axis_index("sp")
        self.core = lax.rem(sp, 2)
        self.z = lax.rem(lax.div(sp, 2), 4)
        self.y = lax.div(sp, 16)
        self.x = lax.rem(lax.div(sp, 8), 2) * 2 + lax.axis_index("tp")

    def device(self, **moved):
        x, y, z, core = (moved.get(name, getattr(self, name)) for name in ("x", "y", "z", "core"))
        return (((y * 2 + lax.div(x, 2)) * 4 + z) * 2 + core, lax.rem(x, 2))

    def step(self, axis, by):
        return lax.rem(getattr(self, axis) + by, 4)

    def toward(self, axis, by):
        return self.device(**{axis: self.step(axis, by)})

    def partner(self):
        return self.device(core=1 - self.core)


class Net:
    def __init__(self, send, recv):
        self.send, self.recv, self.used, self.started = send, recv, 0, []

    def copy(self, source, target, device):
        at = self.used
        self.used += 1
        return pltpu.make_async_remote_copy(
            src_ref=source,
            dst_ref=target,
            send_sem=self.send.at[at],
            recv_sem=self.recv.at[at],
            device_id=device,
            device_id_type=MESH,
        )

    def go(self, copy):
        copy.start()
        self.started.append(copy)

    def settle(self, copy):
        copy.wait_send()
        self.started = [other for other in self.started if other is not copy]

    def drain(self):
        for copy in self.started:
            copy.wait_send()
        self.started = []


def greet(devices, meanwhile=None):
    barrier = pltpu.get_barrier_semaphore()
    for device in devices:
        pl.semaphore_signal(barrier, inc=1, device_id=device, device_id_type=MESH)
    if meanwhile is not None:
        meanwhile()
    pl.semaphore_wait(barrier, len(devices))


def ring(place, axis):
    return [place.toward(axis, 1), place.toward(axis, 3)]


class RingGather:
    def __init__(self, net, place, axis, view, lo, hi):
        self.net = net
        me, nxt, prev = getattr(place, axis), place.step(axis, 1), place.step(axis, 3)
        right, left = ring(place, axis)
        self.to_right = net.copy(view(me), view(me), right)
        self.to_left = net.copy(view(me), view(me), left)
        self.on_right = net.copy(lo(prev), lo(prev), right)
        self.on_left = net.copy(hi(nxt), hi(nxt), left)

    def start(self):
        self.net.go(self.to_right)
        self.net.go(self.to_left)

    def forward(self):
        self.to_right.wait_recv()
        self.net.go(self.on_right)
        self.to_left.wait_recv()
        self.net.go(self.on_left)

    def finish(self):
        self.on_right.wait_recv()
        self.on_left.wait_recv()


class Direct:
    def __init__(self, net, place, axis, source, landing):
        self.net = net
        self.copies = [
            net.copy(
                source(place.step(axis, by)), landing(getattr(place, axis)), place.toward(axis, by)
            )
            for by in (2, 1, 3)
        ]

    def start(self):
        for copy in self.copies:
            self.net.go(copy)

    def wait(self):
        for copy in self.copies:
            copy.wait_recv()


def by_rows(ref, act):
    *lead, rows, _ = ref.shape
    block = next(size for size in (64, 48, 32, 16) if rows % size == 0)
    for spot in np.ndindex(*lead):

        def one(i, carry, spot=spot):
            act(spot, pl.ds(pl.multiple_of(i * block, block), block))
            return carry

        lax.fori_loop(0, rows // block, one, 0)


def add_to(target, other):
    def act(spot, rows):
        at = (*spot, rows, slice(None))
        target[at] = (target[at].astype(F32) + other[at].astype(F32)).astype(target.dtype)

    by_rows(target, act)


def sum_to(target, others):
    def act(spot, rows):
        at = (*spot, rows, slice(None))
        total = others[0][at].astype(F32)
        for other in others[1:]:
            total = total + other[at].astype(F32)
        target[at] = total.astype(target.dtype)

    by_rows(target, act)


def stepped(place, axis, view):
    return lambda by: view(place.step(axis, by))


class RingScatter:
    def __init__(self, net, place, axis, lo, hi, room, lo_here=None, hi_here=None):
        self.net, self.lo, self.hi = net, lo_here or lo, hi_here or hi
        right, left = ring(place, axis)
        self.lo1, self.lo_l, self.lo_r, self.hi1, self.hi_l, self.hi_r = room
        self.a = net.copy(lo(2), self.lo1, right)
        self.b = net.copy(hi(2), self.hi1, left)
        self.c_hi = net.copy(hi(1), self.hi_l, right)
        self.d_lo = net.copy(lo(3), self.lo_r, left)
        self.c_lo = net.copy(self.lo1, self.lo_l, right)
        self.d_hi = net.copy(self.hi1, self.hi_r, left)

    def start_far(self):
        self.net.go(self.a)
        self.net.go(self.b)

    def start_right(self):
        self.net.go(self.c_hi)

    def start_left(self):
        self.net.go(self.d_lo)

    def start(self):
        self.start_far()
        self.start_right()
        self.start_left()

    def middle_right(self):
        self.a.wait_recv()
        add_to(self.lo1, self.lo(1))
        self.net.go(self.c_lo)

    def middle_left(self):
        self.b.wait_recv()
        add_to(self.hi1, self.hi(3))
        self.net.go(self.d_hi)

    def middle(self):
        self.middle_right()
        self.middle_left()

    def finish(self, lo_out, hi_out):
        self.c_hi.wait_recv()
        self.d_hi.wait_recv()
        sum_to(hi_out, [self.hi(0), self.hi_l, self.hi_r])
        self.d_lo.wait_recv()
        self.c_lo.wait_recv()
        sum_to(lo_out, [self.lo(0), self.lo_l, self.lo_r])

    @staticmethod
    def room_shapes(lo_shape, hi_shape):
        return [pltpu.VMEM(lo_shape, BF)] * 3 + [pltpu.VMEM(hi_shape, BF)] * 3


def params(call_id):
    return pltpu.CompilerParams(
        collective_id=call_id, has_side_effects=True, vmem_limit_bytes=VMEM_BYTES
    )


def sems(count):
    return [pltpu.SemaphoreType.DMA((count,)), pltpu.SemaphoreType.DMA((count,))]


class WeightSwap:
    def __init__(self, net, place, w_ref, other_ref):
        self.net = net
        quarter = w_ref.shape[0] // 4
        right, left = ring(place, "x")

        def rows(ref, side):
            return ref.at[pl.ds(pl.multiple_of((2 * side + place.core) * quarter, 16), quarter)]

        self.first = [
            net.copy(rows(w_ref, side), rows(other_ref, side), (left, right)[side])
            for side in (0, 1)
        ]
        self.trades = [
            net.copy(rows(other_ref, side), rows(other_ref, side), place.partner())
            for side in (0, 1)
        ]

    def start(self):
        for copy in self.first:
            self.net.go(copy)

    def forward(self):
        for copy, trade in zip(self.first, self.trades):
            copy.wait_recv()
            self.net.go(trade)

    def finish(self):
        for trade in self.trades:
            trade.wait_recv()


def key_lines(place, ref):
    def stage(axis, first, at):
        return (
            axis,
            lambda j: ref.at[(pl.ds(first, 2), *at(j))],
            lambda j: ref.at[(first, *at(j))],
            lambda j: ref.at[(first + 1, *at(j))],
        )

    every = slice(None)
    return (
        (stage("x", 0, lambda j: (place.z, j)), stage("z", 0, lambda j: (j,))),
        (stage("z", 2, lambda j: (j, place.x)), stage("x", 2, lambda j: (every, j))),
    )


def key_tokens():
    z, x, row = np.meshgrid(np.arange(4), np.arange(4), np.arange(STRIPE), indexing="ij")
    return ((x // 2) * 2048 + z * 512 + (x % 2) * 128 + row).reshape(1, KEYS).astype(np.int32)


KEY_TOKENS = key_tokens()


def first_key(place, y):
    return y * 4096 + place.core * 256 + STRIPE * place.y


def contract(left, right, left_dim, right_dim):
    return lax.dot_general(
        left, right, (((left_dim,), (right_dim,)), ((), ())), preferred_element_type=F32
    )


def turn(u, cosine, sine):
    half = HD // 2
    low, high = u[:, :half], u[:, half:]
    return jnp.concatenate([low * cosine - high * sine, high * cosine + low * sine], axis=1)


def row_bounds(place, segments, y):
    at = (y * 2 + lax.div(place.x, 2)) * 16 + place.z * 4 + lax.rem(place.x, 2)
    rows = jnp.concatenate([segments[pl.ds(at, 1)], segments[pl.ds(at + 2, 1)]], axis=1)
    every = segments[...]
    first = jnp.zeros((1, ROWS), jnp.int32)
    for k in range(1, 4):
        below = jnp.sum((every < k).astype(F32), axis=0, keepdims=True)
        below = jnp.sum(below, axis=1, keepdims=True).astype(jnp.int32)
        first = jnp.where(rows == k, below, first)
    lane = lax.broadcasted_iota(jnp.int32, (1, ROWS), 1)
    last = at * TOK + lane + jnp.where(lane < TOK, 0, TOK)
    return first, last


def down(row):
    return jnp.concatenate(
        [
            jnp.transpose(jnp.broadcast_to(row[:, 128 * i : 128 * i + 128], (128, 128)))
            for i in range(row.shape[1] // 128)
        ],
        axis=0,
    )


def across(ref):
    return ref[...].reshape(1, ref.shape[0])


def norm_scale(v):
    return lax.rsqrt(jnp.mean(v * v, axis=-1, keepdims=True) + EPS)


def norm_back(v, r, gain, e):
    eg = e * gain
    dv = r * eg - v * (r * r * r) * jnp.mean(eg * v, axis=-1, keepdims=True)
    return dv, jnp.sum(e * v * r, axis=0, keepdims=True)


def forward_kernel(
    x_ref,
    g_attn,
    g_query,
    g_key,
    wq_ref,
    wk_ref,
    wv_ref,
    w_hbm,
    cos_ref,
    sin_ref,
    segments,
    key_ref,
    kv_hbm,
    q_hbm,
    wq_hbm,
    w_other,
    o_out,
    inv_out,
    q_pre,
    k_pre,
    h_out,
    buf,
    q_all,
    wq_other,
    kv_own,
    o_sum,
    l_sum,
    o_snd,
    o_part,
    o_got,
    o_done,
    l_mine,
    l_got,
    l_core,
    *rest,
):
    *room, send, recv, local = rest
    place, net = Place(), Net(send, recv)
    core = place.core
    partner = place.partner()
    mine = pl.ds(pl.multiple_of(core * TOK, TOK), TOK)
    theirs = pl.ds(pl.multiple_of((1 - core) * TOK, TOK), TOK)

    def keys_and_values():
        xf = x_ref[...].astype(F32)
        h = (xf * norm_scale(xf) * across(g_attn)).astype(BF)
        h_out[...] = h
        k = jnp.dot(h, wk_ref[...], preferred_element_type=F32)
        k_pre[...] = k
        k = turn(k * norm_scale(k) * across(g_key), cos_ref[...], sin_ref[...]).astype(BF)
        v = jnp.dot(h, wv_ref[...], preferred_element_type=F32).astype(BF)
        for j in range(4):
            kv_own[j, :, :HD] = k[STRIPE * j : STRIPE * j + STRIPE]
            kv_own[j, :, HD:] = v[STRIPE * j : STRIPE * j + STRIPE]
        buf[place.y, place.z, place.x] = kv_own[place.y]

    greet(
        ring(place, "x")
        + ring(place, "y")
        + ring(place, "z")
        + [partner, place.toward("y", 2)],
        keys_and_values,
    )
    swap_wq = WeightSwap(net, place, wq_ref, wq_other)
    swap_w = WeightSwap(net, place, w_hbm, w_other)
    stripes = Direct(
        net,
        place,
        "y",
        lambda j: kv_own.at[j],
        lambda j: buf.at[j, place.z, place.x],
    )
    stripes.start()
    swap_wq.start()
    (first_a, then_a), (first_b, then_b) = (
        [RingGather(net, place, *stage) for stage in part] for part in key_lines(place, buf)
    )
    q_ring = RingGather(
        net,
        place,
        "y",
        lambda j: q_all.at[j, :, mine],
        lambda j: q_all.at[j, pl.ds(0, 2), mine],
        lambda j: q_all.at[j, pl.ds(2, 2), mine],
    )

    def block_of(by):
        return q_all.at[place.step("y", by), :, mine]

    q_core = [net.copy(block_of(by), block_of(by), partner) for by in range(4)]

    def queries(which, w):
        q = jnp.dot(h_out[...], w[...], preferred_element_type=F32)
        for i in range(2):
            u = q[:, HD * i : HD * i + HD]
            q_pre[2 * which + i] = u
            u = turn(u * norm_scale(u) * across(g_query), cos_ref[...], sin_ref[...])
            q_all[place.y, 2 * which + i, mine] = (u.astype(BF).astype(F32) * HD**-0.5).astype(BF)

    queries(0, wq_ref)
    stripes.wait()
    first_a.start()
    first_b.start()
    swap_wq.forward()
    first_a.forward()
    first_b.forward()
    swap_wq.finish()
    wq_store = pltpu.make_async_copy(wq_other, wq_hbm, local.at[1])
    wq_store.start()
    queries(1, wq_other)
    q_ring.start()
    net.go(q_core[0])
    first_a.finish()
    then_a.start()
    first_b.finish()
    then_b.start()
    q_ring.forward()
    net.go(q_core[1])
    net.go(q_core[3])
    then_a.forward()
    then_b.forward()
    q_ring.finish()
    net.go(q_core[2])
    then_a.finish()
    then_b.finish()
    swap_w.start()
    store = pltpu.make_async_copy(buf, kv_hbm, local.at[0])
    store.start()

    o_core = [net.copy(o_snd.at[by], o_got.at[by], partner) for by in range(4)]

    def attend(by):
        y = place.step("y", by)
        q_core[by].wait_recv()
        first, last = (down(row) for row in row_bounds(place, segments, y))

        keys = buf[:, :, :, :, :HD].reshape(4 * KEYS, HD)
        values = buf[:, :, :, :, HD:].reshape(4 * KEYS, HD)
        token = jnp.concatenate([key_ref[...] + first_key(place, j) for j in range(4)], axis=1)
        allowed = jnp.concatenate(
            [
                (token[:, 128 * i : 128 * i + 128] <= last)
                & (token[:, 128 * i : 128 * i + 128] >= first)
                for i in range(4 * KEYS // 128)
            ],
            axis=1,
        )
        for h in range(HEADS):
            weights = jnp.exp(contract(q_all[y, h], keys, 1, 1))
            weights = jnp.where(allowed, weights, 0.0)
            l_sum[by, h] = sum(
                weights[:, 128 * i : 128 * i + 128] for i in range(4 * KEYS // 128)
            )
            o_sum[by, h] = jnp.dot(weights.astype(BF), values, preferred_element_type=F32)
        for h in range(HEADS):
            o_snd[by, h] = o_sum[by, h, theirs].astype(BF)
            o_part[by, h] = o_sum[by, h, mine].astype(BF)
            total = jnp.sum(l_sum[by, h], axis=1, keepdims=True)
            l_mine[y, h : h + 1] = jnp.transpose(jnp.broadcast_to(total, (ROWS, 128)))[:1]
        net.go(o_core[by])

    def both_cores(by):
        o_core[by].wait_recv()
        add_to(o_part.at[by], o_got.at[by])

    o_ring = RingScatter(
        net,
        place,
        "y",
        lambda by: o_part.at[by, pl.ds(0, 2)],
        lambda by: o_part.at[by, pl.ds(2, 2)],
        room,
    )
    attend(0)
    attend(2)
    attend(1)
    both_cores(2)
    o_ring.start_far()
    swap_w.forward()
    attend(3)
    l_swap = Direct(net, place, "y", lambda j: l_mine.at[j], lambda j: l_got.at[j])
    l_swap.start()
    l_got[place.y] = l_mine[place.y]
    both_cores(1)
    o_ring.start_right()
    both_cores(3)
    o_ring.middle_right()
    o_ring.start_left()
    o_ring.middle_left()
    both_cores(0)
    q_store = pltpu.make_async_copy(q_all, q_hbm, local.at[2])
    q_store.start()
    swap_w.finish()
    l_swap.wait()
    l_core[core] = (l_got[0] + l_got[1]) + (l_got[2] + l_got[3])
    l_over = net.copy(l_core.at[core], l_core.at[core], partner)
    net.go(l_over)
    l_over.wait_recv()
    total = l_core[0] + l_core[1]
    inverse = 1.0 / jnp.where(core == 0, total[:, :TOK], total[:, TOK:])
    o_ring.finish(o_done.at[pl.ds(0, 2)], o_done.at[pl.ds(2, 2)])
    for h in range(HEADS):
        scale = down(inverse[h : h + 1])
        o_out[h] = o_done[h] * jnp.concatenate([scale, scale], axis=1)
        inv_out[h] = scale
    for copy in (store, wq_store, q_store):
        copy.wait()
    net.drain()


def attention_forward(args, call_id):
    shape = jax.ShapeDtypeStruct
    anywhere = pl.BlockSpec(memory_space=pl.ANY)
    halves = (2, TOK, HD)
    return pl.pallas_call(
        forward_kernel,
        out_shape=(
            shape((4, 4, 4, STRIPE, 2 * HD), BF),
            shape((4, HEADS, ROWS, HD), BF),
            shape((D, 2 * HD), BF),
            shape((2 * HD, D), BF),
            shape((HEADS, TOK, HD), F32),
            shape((HEADS, TOK, 128), F32),
            shape((HEADS, TOK, HD), F32),
            shape((TOK, HD), F32),
            shape((TOK, D), BF),
        ),
        in_specs=[IN_VMEM] * 7 + [anywhere] + [IN_VMEM] * 4,
        out_specs=[anywhere] * 4 + [IN_VMEM] * 5,
        scratch_shapes=[
            pltpu.VMEM((4, 4, 4, STRIPE, 2 * HD), BF),
            pltpu.VMEM((4, HEADS, ROWS, HD), BF),
            pltpu.VMEM((D, 2 * HD), BF),
            pltpu.VMEM((4, STRIPE, 2 * HD), BF),
            pltpu.VMEM((4, HEADS, ROWS, HD), F32),
            pltpu.VMEM((4, HEADS, ROWS, 128), F32),
            pltpu.VMEM((4, HEADS, TOK, HD), BF),
            pltpu.VMEM((4, HEADS, TOK, HD), BF),
            pltpu.VMEM((4, HEADS, TOK, HD), BF),
            pltpu.VMEM((HEADS, TOK, HD), F32),
            pltpu.VMEM((4, 8, ROWS), F32),
            pltpu.VMEM((4, 8, ROWS), F32),
            pltpu.VMEM((2, 8, ROWS), F32),
            *RingScatter.room_shapes(halves, halves),
            *sems(64),
            pltpu.SemaphoreType.DMA((3,)),
        ],
        compiler_params=params(call_id),
    )(*args)


def kept_head(place, j):
    return jnp.where(lax.rem(j, 2) == lax.rem(place.x, 2), 0, 2) + lax.div(j, 2)


def turn_back(e, cosine, sine):
    half = HD // 2
    low, high = e[:, :half], e[:, half:]
    return jnp.concatenate([low * cosine + high * sine, high * cosine - low * sine], axis=1)


def backward_kernel(
    kv_hbm,
    q_hbm,
    do_hbm,
    sums_hbm,
    wq_hbm,
    wq2_hbm,
    wk_hbm,
    wv_hbm,
    delta_all,
    key_ref,
    segments,
    q_pre,
    k_pre,
    cos_ref,
    sin_ref,
    h_ref,
    da_ref,
    o_ref,
    x_ref,
    dmid_ref,
    g_attn,
    g_query,
    g_key,
    gains_ref,
    dx_out,
    home_out,
    late_out,
    w_top,
    w_low,
    gains_out,
    buf,
    q_all,
    do_all,
    wq,
    wq2,
    wk,
    wv,
    tokens,
    grads,
    fin,
    fin_got,
    dq_sum,
    dq_snd,
    dq_part,
    dq_got,
    dq_done,
    h_line,
    da_line,
    turned,
    o_line,
    dq_line,
    dq_own,
    o_own,
    late_all,
    late_got,
    late_y,
    late_z,
    gain_got,
    kv_own,
    kv_line,
    turned_other,
    w_got,
    w_y,
    w_z,
    *rest,
):
    rooms, dq_rooms, late_rooms, rest = rest[:24], rest[24:30], rest[30:42], rest[42:]
    *weight_refs, send, recv, send2, recv2, here = rest
    place, net = Place(), Net(send, recv)
    core, partner = place.core, place.partner()
    w_loads = [
        pltpu.make_async_copy(source, target, here.at[1 + i])
        for i, (source, target) in enumerate(
            (
                (kv_hbm, buf),
                (q_hbm, q_all),
                (do_hbm, do_all),
                (wq_hbm, wq),
                (wq2_hbm, wq2),
                (wk_hbm, wk),
                (wv_hbm, wv),
            )
        )
    ]
    for load in w_loads:
        load.start()
    weights = WeightSums(place, net, sums_hbm, late_z, weight_refs, (send2, recv2, here))
    across_x = [place.device(x=place.step("x", by), core=1 - core) for by in (1, 3)]
    greet(
        weights.friends
        + ring(place, "x")
        + ring(place, "y")
        + across_x
        + [place.toward("y", 2)]
    )
    mine = pl.ds(pl.multiple_of(core * TOK, TOK), TOK)
    theirs = pl.ds(pl.multiple_of((1 - core) * TOK, TOK), TOK)
    half = TOK // 2

    def line_of(rows):
        return RingGather(
            net,
            place,
            "x",
            lambda j: rows.at[j],
            lambda j: rows.at[j, pl.ds(0, half)],
            lambda j: rows.at[j, pl.ds(half, half)],
        )

    def head_of(j):
        return kept_head(place, j)

    h_line[place.x] = h_ref[...]
    da_line[place.x] = da_ref[...]
    for h in range(HEADS):
        o_own[h] = o_ref[h].astype(BF)
    o_line[place.x] = o_own[head_of(place.x)]
    line_h, line_da = line_of(h_line), line_of(da_line)
    o_swap = Direct(net, place, "x", lambda j: o_own.at[head_of(j)], lambda j: o_line.at[j])
    dq_swap = Direct(net, place, "x", lambda j: dq_own.at[head_of(j)], lambda j: dq_line.at[j])
    line_da.start()
    o_swap.start()
    key_rings = []
    for i, (inner, outer) in enumerate(key_lines(place, grads)):
        for k, (axis, _, lo, hi) in enumerate((outer, inner)):
            spot = 12 * i + 6 * k
            key_rings.append(
                RingScatter(
                    net,
                    place,
                    axis,
                    stepped(place, axis, lo),
                    stepped(place, axis, hi),
                    rooms[spot : spot + 6],
                )
            )
    first_a, then_a, first_b, then_b = key_rings
    fin_swap = Direct(net, place, "y", lambda j: fin.at[j], lambda j: fin_got.at[j])
    dq_core = net.copy(dq_snd, dq_got, partner)
    dq_ring = RingScatter(
        net,
        place,
        "y",
        stepped(place, "y", lambda j: dq_part.at[j, pl.ds(0, 2)]),
        stepped(place, "y", lambda j: dq_part.at[j, pl.ds(2, 2)]),
        dq_rooms,
    )
    late_first = RingScatter(
        net,
        place,
        "y",
        stepped(place, "y", lambda j: late_got.at[j, 0]),
        stepped(place, "y", lambda j: late_got.at[j, 1]),
        late_rooms[:6],
    )

    def late_spot(j):
        return late_y.at[lax.div(j, 2), lax.rem(j, 2)]

    late_second = RingScatter(
        net,
        place,
        "z",
        stepped(place, "z", lambda j: late_spot(j).at[pl.ds(0, 80)]),
        stepped(place, "z", lambda j: late_spot(j).at[pl.ds(80, 64)]),
        late_rooms[6:],
    )

    def late_term(c, turned, columns):
        term = jnp.dot(
            turned[...], columns[...].reshape(4 * TOK, HD), preferred_element_type=F32
        ).astype(BF)
        for k in range(8):
            for which in range(2):
                late_all[which, k // 2, k % 2, c] = term[
                    144 * k : 144 * k + 144, 128 * which : 128 * which + 128
                ]

    weights.first.begin()
    weights.first.go_on()
    tokens[...] = down(key_ref[...])
    bounds = [row_bounds(place, segments, y) for y in range(4)]
    for load in w_loads[:3]:
        load.wait()

    def differ(key_y):
        keys = buf[key_y, :, :, :, :HD].reshape(KEYS, HD)
        values = buf[key_y, :, :, :, HD:].reshape(KEYS, HD)
        token = tokens[...] + first_key(place, key_y)
        token = jnp.concatenate([token, token], axis=1)
        d_keys = d_values = None
        for y in range(key_y, 4):
            first, last = bounds[y]
            allowed = (token <= last) & (token >= first)
            for h in range(HEADS):
                probs = jnp.exp(contract(keys, q_all[y, h], 1, 1))
                probs = jnp.where(allowed, probs, 0.0)
                delta = jnp.concatenate(
                    [delta_all[y, 0, h : h + 1], delta_all[y, 1, h : h + 1]], axis=1
                )
                d_scores = (probs * (contract(values, do_all[y, h], 1, 1) - delta)).astype(BF)
                value_term = jnp.dot(probs.astype(BF), do_all[y, h], preferred_element_type=F32)
                key_term = jnp.dot(d_scores, q_all[y, h], preferred_element_type=F32)
                d_values = value_term if d_values is None else d_values + value_term
                d_keys = key_term if d_keys is None else d_keys + key_term
                query_term = contract(keys, d_scores, 0, 0)
                if y == key_y:
                    dq_sum[y, h] = query_term
                else:
                    dq_sum[y, h] += query_term
        grads[key_y, :, :, :, :HD] = d_keys.astype(BF).reshape(4, 4, STRIPE, HD)
        grads[key_y, :, :, :, HD:] = d_values.astype(BF).reshape(4, 4, STRIPE, HD)

    differ(3)
    differ(2)
    first_b.start()
    line_da.forward()
    line_h.start()
    differ(1)
    first_b.middle()
    weights.first.turn()
    differ(0)
    first_a.start()
    for y in range(4):
        for h in range(HEADS):
            dq_snd[y, h] = dq_sum[y, h, :, theirs].astype(BF)
            dq_part[y, h] = dq_sum[y, h, :, mine].astype(BF)
    net.go(dq_core)
    dq_core.wait_recv()
    for y in range(4):
        add_to(dq_part.at[y], dq_got.at[y])
    dq_ring.start()
    first_a.middle()
    first_b.finish(first_b.lo(0), first_b.hi(0))
    then_b.start()
    first_a.finish(first_a.lo(0), first_a.hi(0))
    then_a.start()
    weights.next()
    line_h.forward()
    line_da.finish()
    o_swap.wait()
    turned[...] = jnp.transpose(da_line[...].reshape(4 * TOK, D))
    late_term(0, turned, o_line)
    dq_ring.middle()
    then_b.middle()
    then_a.middle()
    then_b.finish(fin.at[2], fin.at[3])
    then_a.finish(fin.at[0], fin.at[1])
    fin_got[place.y] = fin[place.y]
    fin_swap.start()
    for load in w_loads[3:]:
        load.wait()

    dq_ring.finish(dq_done.at[pl.ds(0, 2)], dq_done.at[pl.ds(2, 2)])
    d_query = jnp.zeros((1, HD), F32)
    for h in range(HEADS):
        e = jnp.transpose(dq_done[h]) * HD**-0.5
        e = turn_back(e.astype(BF).astype(F32), cos_ref[...], sin_ref[...])
        u = q_pre[h]
        du, gain = norm_back(u, norm_scale(u), across(g_query), e)
        d_query = d_query + gain
        dq_own[h] = du.astype(BF)
    dq_line[place.x] = dq_own[head_of(place.x)]
    dq_swap.start()
    line_h.finish()
    turned[...] = jnp.transpose(h_line[...].reshape(4 * TOK, D))
    turned_swap = net.copy(
        turned.at[pl.ds(pl.multiple_of((1 - core) * 576, 16), 576)], turned_other, partner
    )
    net.go(turned_swap)
    fin_swap.wait()

    dkv = jnp.concatenate([fin_got[j] for j in range(4)], axis=0)
    e = turn_back(dkv[:, :HD].astype(BF).astype(F32), cos_ref[...], sin_ref[...])
    u = k_pre[...]
    dk, d_key = norm_back(u, norm_scale(u), across(g_key), e)
    dk, dv = dk.astype(BF), dkv[:, HD:].astype(BF)
    for i in range(2):
        kv_own[i] = dk[:, 128 * i : 128 * i + 128]
        kv_own[2 + i] = dv[:, 128 * i : 128 * i + 128]
    kv_line[core, place.x] = kv_own[place.x]
    kv_swap = Direct(net, place, "x", lambda j: kv_own.at[j], lambda j: kv_line.at[core, j])
    kv_swap.start()
    kv_across = []
    for by in range(4):
        j = place.step("x", by)
        device = place.device(x=j, core=1 - core)
        kv_across.append(net.copy(kv_own.at[j], kv_line.at[core, place.x], device))
        net.go(kv_across[by])
    weights.turn_again()
    dq_swap.wait()
    late_term(1, turned, dq_line)
    late_swap = net.copy(late_all.at[1 - core], late_got, partner)
    net.go(late_swap)
    d_h = contract(dk, wk[...], 1, 1) + contract(dv, wv[...], 1, 1)
    for h in range(HEADS):
        w = (wq, wq2)[h // 2]
        d_h = d_h + contract(dq_own[h], w[:, 256 * (h % 2) : 256 * (h % 2) + 256], 1, 1)
    xf = x_ref[...].astype(F32)
    dx, d_attn = norm_back(xf, norm_scale(xf), across(g_attn), d_h)
    dx_out[...] = (dmid_ref[...] + dx).astype(BF)
    def gain_swap(level, axis):
        return Direct(
            net, place, axis, lambda j: gain_got.at[level, at(axis)], lambda j: gain_got.at[level, j]
        )

    def at(axis):
        return getattr(place, axis)

    def gain_sum(level):
        return (gain_got[level, 0] + gain_got[level, 1]) + (gain_got[level, 2] + gain_got[level, 3])

    swaps = [gain_swap(0, "x"), gain_swap(1, "y"), gain_swap(2, "z")]
    norms = jnp.concatenate([d_query, d_key, jnp.zeros((1, D - 2 * HD), F32)], axis=1)
    gain_got[0, place.x] = jnp.concatenate(
        [d_attn, gains_ref[0:3], norms, jnp.zeros((3, D), F32)], axis=0
    )
    swaps[0].start()
    turned_swap.wait_recv()
    kv_swap.wait()
    for copy in kv_across:
        copy.wait_recv()
    term = jnp.dot(
        turned[pl.ds(pl.multiple_of(core * 576, 16), 576)],
        kv_line[core].reshape(4 * TOK, 128),
        preferred_element_type=F32,
    )
    term += jnp.dot(
        turned_other[...], kv_line[1 - core].reshape(4 * TOK, 128), preferred_element_type=F32
    )
    term = term.astype(BF)
    for k in range(4):
        w_got[k] = term[144 * k : 144 * k + 144]
    w_scatter = Direct(net, place, "y", lambda j: w_got.at[j], lambda j: w_y.at[j])
    w_scatter.start()
    w_y[place.y] = w_got[place.y]
    late_swap.wait_recv()
    for y in range(4):
        add_to(late_got.at[y], late_all.at[core, y])
    late_first.start()
    swaps[0].wait()
    gain_got[1, place.y] = gain_sum(0)
    swaps[1].start()
    weights.last()
    swaps[1].wait()
    gain_got[2, place.z] = gain_sum(1)
    swaps[2].start()
    w_scatter.wait()
    sum_to(w_z.at[place.z], [w_y.at[j] for j in range(4)])
    w_sums = Direct(net, place, "z", lambda j: w_z.at[place.z], lambda j: w_z.at[j])
    w_sums.start()
    late_first.middle()
    swaps[2].wait()
    gain_got[3, core] = gain_sum(2)
    gain_last = net.copy(gain_got.at[3, core], gain_got.at[3, core], partner)
    net.go(gain_last)
    w_sums.wait()
    upper, lower = w_top.at[core], w_low.at[core]
    sum_to(upper.at[place.x, place.y], [w_z.at[j, pl.ds(0, 80)] for j in range(4)])
    sum_to(lower.at[place.x, place.y], [w_z.at[j, pl.ds(80, 64)] for j in range(4)])

    def spread(axis, view):
        return Direct(net, place, axis, lambda j: view(at(axis)), view)

    first_way = [
        spread("y", lambda j: upper.at[place.x, j]),
        spread("x", lambda j: lower.at[j, place.y]),
    ]
    second_way = [spread("x", lambda j: upper.at[j]), spread("y", lambda j: lower.at[:, j])]
    for line in first_way:
        line.start()
    late_first.finish(late_y.at[0], late_y.at[1])
    late_second.start()
    for line, then in zip(first_way, second_way):
        line.wait()
        then.start()
    late_second.middle()
    gain_last.wait_recv()
    gains_out[...] = gain_got[3, 0] + gain_got[3, 1]
    over = [net.copy(upper, upper, partner), net.copy(lower, lower, partner)]
    for line, copy in zip(second_way, over):
        line.wait()
        net.go(copy)
    late_second.finish(late_z.at[pl.ds(0, 80)], late_z.at[pl.ds(80, 64)])
    weights.send_late()
    for copy in over:
        copy.wait_recv()
    weights.arrive()
    home_out[...] = weights.rcv[...]
    late_out[...] = weights.late_rcv[...]
    net.drain()


def attention_backward(hbm, small, call_id):
    shape = jax.ShapeDtypeStruct
    rooms = []
    for _ in range(2):
        rooms += RingScatter.room_shapes((4, STRIPE, 2 * HD), (4, STRIPE, 2 * HD))
        rooms += RingScatter.room_shapes((STRIPE, 2 * HD), (STRIPE, 2 * HD))
    rooms += RingScatter.room_shapes((2, HD, TOK), (2, HD, TOK))
    late_rooms = [
        *RingScatter.room_shapes((2, 144, 128), (2, 144, 128)),
        *RingScatter.room_shapes((80, 128), (64, 128)),
    ]
    return pl.pallas_call(
        backward_kernel,
        out_shape=(
            shape((TOK, D), BF),
            shape((8, 16, HALF + 256), BF),
            shape((8, 16, 256), BF),
            shape((2, 4, 4, 80, 128), BF),
            shape((2, 4, 4, 64, 128), BF),
            shape((8, D), F32),
        ),
        in_specs=[pl.BlockSpec(memory_space=pl.ANY)] * len(hbm) + [IN_VMEM] * len(small),
        out_specs=[IN_VMEM] * 6,
        scratch_shapes=[
            pltpu.VMEM((4, 4, 4, STRIPE, 2 * HD), BF),
            pltpu.VMEM((4, HEADS, ROWS, HD), BF),
            pltpu.VMEM((4, HEADS, ROWS, HD), BF),
            pltpu.VMEM((D, 2 * HD), BF),
            pltpu.VMEM((D, 2 * HD), BF),
            pltpu.VMEM((D, HD), BF),
            pltpu.VMEM((D, HD), BF),
            pltpu.VMEM((KEYS, 128), jnp.int32),
            pltpu.VMEM((4, 4, 4, STRIPE, 2 * HD), BF),
            pltpu.VMEM((4, STRIPE, 2 * HD), F32),
            pltpu.VMEM((4, STRIPE, 2 * HD), F32),
            pltpu.VMEM((4, HEADS, HD, ROWS), F32),
            pltpu.VMEM((4, HEADS, HD, TOK), BF),
            pltpu.VMEM((4, HEADS, HD, TOK), BF),
            pltpu.VMEM((4, HEADS, HD, TOK), BF),
            pltpu.VMEM((HEADS, HD, TOK), F32),
            pltpu.VMEM((4, TOK, D), BF),
            pltpu.VMEM((4, TOK, D), BF),
            pltpu.VMEM((D, 4 * TOK), BF),
            pltpu.VMEM((4, TOK, HD), BF),
            pltpu.VMEM((4, TOK, HD), BF),
            pltpu.VMEM((4, TOK, HD), BF),
            pltpu.VMEM((4, TOK, HD), BF),
            pltpu.VMEM((2, 4, 2, 2, 144, 128), BF),
            pltpu.VMEM((4, 2, 2, 144, 128), BF),
            pltpu.VMEM((2, 2, 144, 128), BF),
            pltpu.VMEM((144, 128), F32),
            pltpu.VMEM((4, 4, 8, D), F32),
            pltpu.VMEM((4, TOK, 128), BF),
            pltpu.VMEM((2, 4, TOK, 128), BF),
            pltpu.VMEM((576, 4 * TOK), BF),
            pltpu.VMEM((4, 144, 128), BF),
            pltpu.VMEM((4, 144, 128), BF),
            pltpu.VMEM((4, 144, 128), BF),
            *rooms,
            *late_rooms,
            *WeightSums.scratch(),
            *sems(160),
            *sems(16),
            pltpu.SemaphoreType.DMA((24,)),
        ],
        compiler_params=params(call_id),
    )(*hbm, *small)


def feed_kernel(
    x_ref,
    o_ref,
    inv_ref,
    wo_ref,
    wo2_ref,
    post_ref,
    ffn_ref,
    out_gain_ref,
    cot_ref,
    wg_hbm,
    wu_hbm,
    wd_hbm,
    out_ref,
    dmid_out,
    dattn_out,
    do_all,
    delta_all,
    dgains_out,
    sums_hbm,
    wg,
    wu,
    wd,
    h_line,
    f_line,
    h_turned,
    f_turned,
    gelu_kept,
    slope_kept,
    act,
    d_gate,
    d_up,
    f_terms,
    h_terms,
    snd,
    got,
    attn,
    mid,
    ffn,
    delta_rows,
    *rest,
):
    *room, send, recv, local = rest
    place, net = Place(), Net(send, recv)
    core, partner = place.core, place.partner()
    x_hi = lax.div(place.x, 2)
    first_unit = pl.multiple_of(x_hi * (2 * HID - HID_PAD), 128)
    window = pl.ds(first_unit, HID_PAD)
    loads = [
        pltpu.make_async_copy(source, target, local.at[i])
        for i, (source, target) in enumerate(
            ((wg_hbm.at[:, window], wg), (wu_hbm.at[:, window], wu), (wd_hbm.at[window], wd))
        )
    ]
    for load in loads:
        load.start()
    greet(
        ring(place, "x")
        + ring(place, "y")
        + ring(place, "z")
        + [partner, place.toward("y", 2)]
    )
    half, quarter = TOK // 2, TOK // 4
    top, bottom = pl.ds(0, quarter), pl.ds(quarter, quarter)
    g_post, g_ffn, g_out = (across(ref) for ref in (post_ref, ffn_ref, out_gain_ref))

    def rows_of(part):
        return slice(half * part, half * part + half)

    def lines_of(part):
        return slice(4 * half * part, 4 * half * part + 4 * half)

    def gather(lines):
        return RingGather(
            net,
            place,
            "x",
            lambda j: lines.at[j],
            lambda j: lines.at[j, top],
            lambda j: lines.at[j, bottom],
        )

    def scatter(terms, room):
        return RingScatter(
            net,
            place,
            "x",
            stepped(place, "x", lambda j: terms.at[j, top]),
            stepped(place, "x", lambda j: terms.at[j, bottom]),
            room,
        )

    def summed(line, part):
        at = half * part
        line.finish(ffn.at[pl.ds(at, quarter)], ffn.at[pl.ds(at + quarter, quarter)])

    o_cat = [o_ref[h].astype(BF) for h in range(HEADS)]
    a = jnp.dot(jnp.concatenate(o_cat[:2], axis=1), wo_ref[...], preferred_element_type=F32)
    a += jnp.dot(jnp.concatenate(o_cat[2:], axis=1), wo2_ref[...], preferred_element_type=F32)
    attn[...] = a
    mid[...] = x_ref[...].astype(F32) + a * norm_scale(a) * g_post
    m = mid[...]
    h = (m * norm_scale(m) * g_ffn).astype(BF)
    for part in range(2):
        h_line[part, place.x] = h[rows_of(part)]
    h_gathers = [gather(h_line.at[part]) for part in range(2)]
    f_gathers = [gather(f_line.at[part]) for part in range(2)]
    f_sums = [scatter(f_terms.at[part], room[6 * part : 6 * part + 6]) for part in range(2)]
    h_sums = [
        scatter(h_terms.at[part], room[12 + 6 * part : 18 + 6 * part]) for part in range(2)
    ]
    h_gathers[0].start()

    for load in loads:
        load.wait()
    low_unit, high_unit = jnp.where(x_hi == 0, 0, 64), jnp.where(x_hi == 0, HID, HID_PAD)

    def units(n):
        return pl.ds(pl.multiple_of(n * 256, 256), 256)

    def forward(part, n, carry):
        h = h_line[part].reshape(4 * half, D)
        gate = jnp.dot(h, wg[:, units(n)], preferred_element_type=F32)
        up = jnp.dot(h, wu[:, units(n)], preferred_element_type=F32)
        unit = n * 256 + lax.broadcasted_iota(jnp.int32, (1, 256), 1)
        own = jnp.where((unit >= low_unit) & (unit < high_unit), 1.0, 0.0)
        scale, cube = 0.7978845608028654, 0.044715
        square = gate * gate
        bent = jnp.tanh(scale * gate * (1.0 + cube * square))
        lifted = 0.5 * (1.0 + bent)
        gelu = gate * lifted * own
        slope = lifted + 0.5 * gate * (1.0 - bent * bent) * scale * (1.0 + 3.0 * cube * square)
        act[lines_of(part), units(n)] = (gelu * up).astype(BF)
        gelu_kept[lines_of(part), units(n)] = gelu.astype(BF)
        slope_kept[lines_of(part), units(n)] = (slope * up * own).astype(BF)
        return carry

    def columns(n):
        return pl.ds(pl.multiple_of(n * 384, 128), 384)

    def project(part, n, carry):
        term = jnp.dot(act[lines_of(part)], wd[:, columns(n)], preferred_element_type=F32)
        f_terms[part, :, :, columns(n)] = term.astype(BF).reshape(4, half, 384)
        return carry

    def backward(part, n, carry):
        d_act = contract(f_line[part].reshape(4 * half, D), wd[units(n)], 1, 1)
        rows = lines_of(part)
        d_gate[rows, units(n)] = (d_act * slope_kept[rows, units(n)].astype(F32)).astype(BF)
        d_up[rows, units(n)] = (d_act * gelu_kept[rows, units(n)].astype(F32)).astype(BF)
        return carry

    def back_project(part, n, carry):
        rows = lines_of(part)
        term = contract(d_gate[rows], wg[columns(n)], 1, 1)
        term += contract(d_up[rows], wu[columns(n)], 1, 1)
        h_terms[part, :, :, columns(n)] = term.astype(BF).reshape(4, half, 384)
        return carry

    def each(times, step, part):
        lax.fori_loop(0, times, functools.partial(step, part), 0)

    blocks = HID_PAD // 256

    def turn_round(part):
        rows = rows_of(part)
        summed(f_sums[part], part)
        f = ffn[rows]
        r = norm_scale(f)
        out_ref[rows] = (mid[rows] + f * r * g_out).astype(BF)
        df, gain = norm_back(f, r, g_out, cot_ref[rows].astype(F32))
        f_line[part, place.x] = df.astype(BF)
        f_gathers[part].start()
        return gain

    h_gathers[0].forward()
    h_gathers[1].start()
    h_gathers[0].finish()
    each(blocks, forward, 0)
    h_gathers[1].forward()
    each(3, project, 0)
    f_sums[0].start()
    h_gathers[1].finish()
    each(blocks, forward, 1)
    f_sums[0].middle()
    each(3, project, 1)
    f_sums[1].start()
    d_out = turn_round(0)
    f_sums[1].middle()
    h_turned[...] = jnp.transpose(h_line[...].reshape(8 * half, D))
    f_gathers[0].forward()
    d_out = d_out + turn_round(1)
    f_gathers[0].finish()
    each(blocks, backward, 0)
    f_gathers[1].forward()
    each(3, back_project, 0)
    h_sums[0].start()
    f_gathers[1].finish()

    def halves_of(which):
        return pl.ds(pl.multiple_of(which * 896, 128), 896)

    def fill(target, i, which, left, right, spans, add):
        term = jnp.dot(
            left[576 * i : 576 * i + 576], right[:, halves_of(which)], preferred_element_type=F32
        )
        for k in range(4):
            for half, low, high, start in spans:
                at = (2 * i + k // 2, k % 2, half, slice(None), slice(start, start + high - low))
                value = term[144 * k : 144 * k + 144, low:high]
                if add:
                    value = value + target[at].astype(F32)
                target[at] = value.astype(BF)

    down_spans = ((0, 0, 256, 0), (0, 256, 512, CUT), (1, 512, 768, 0), (1, 768, 896, CUT))

    def fill_down(target, i, which, add):
        fill(target, i, which, f_turned, act, down_spans, add)

    def fill_others(target, i, which, add):
        for c, right in enumerate((d_gate, d_up)):
            spans = ((c, 0, 512, 256), (c, 512, 896, CUT + 256))
            fill(target, i, which, h_turned, right, spans, add)

    for y in range(4):
        snd[y, :, 1, :, CUT + 128 : CUT + 256] = jnp.zeros((2, 144, 128), BF)
    swaps = [net.copy(snd.at[y], got.at[y], partner) for y in range(4)]
    each(blocks, backward, 1)
    h_sums[0].middle()
    each(3, back_project, 1)
    h_sums[1].start()
    def mine_of(part):
        return pl.ds(pl.multiple_of(core * TOK + half * part, half), half)

    def do_ring_of(part):
        mine = mine_of(part)
        return RingGather(
            net,
            place,
            "y",
            lambda j: do_all.at[j, :, mine],
            lambda j: do_all.at[j, pl.ds(0, 2), mine],
            lambda j: do_all.at[j, pl.ds(2, 2), mine],
        )

    def block_of(part, by):
        return do_all.at[place.step("y", by), :, mine_of(part)]

    do_rings = [do_ring_of(part) for part in range(2)]
    do_core = [
        [net.copy(block_of(part, by), block_of(part, by), partner) for by in range(4)]
        for part in range(2)
    ]
    delta_swap = Direct(
        net,
        place,
        "y",
        lambda j: delta_all.at[place.y, core],
        lambda j: delta_all.at[j, core],
    )
    delta_core = net.copy(delta_all.at[:, core], delta_all.at[:, core], partner)

    def heads_back(part):
        rows = rows_of(part)
        m, a = mid[rows], attn[rows]
        dm, d_ffn = norm_back(m, norm_scale(m), g_ffn, ffn[rows])
        d_mid = cot_ref[rows].astype(F32) + dm
        dmid_out[rows] = d_mid
        da, d_post = norm_back(a, norm_scale(a), g_post, d_mid)
        da = da.astype(BF)
        dattn_out[rows] = da
        for h in range(HEADS):
            w = (wo_ref, wo2_ref)[h // 2][256 * (h % 2) : 256 * (h % 2) + 256]
            d_o = contract(da, w, 1, 1).astype(BF).astype(F32)
            inverse = inv_ref[h, rows]
            scaled = d_o * jnp.concatenate([inverse, inverse], axis=1)
            do_all[place.y, h, mine_of(part)] = scaled.astype(BF)
            delta_rows[h, rows] = jnp.sum(d_o * o_ref[h, rows], axis=1, keepdims=True) * inverse
        do_rings[part].start()
        net.go(do_core[part][0])
        return d_post, d_ffn

    for i in range(2):
        fill_others(snd, i, 1 - core, False)
    h_sums[1].middle()
    summed(h_sums[0], 0)
    gains_top = heads_back(0)
    f_turned[...] = jnp.transpose(f_line[...].reshape(8 * half, D))
    for i in range(2):
        fill_down(snd, i, 1 - core, False)
        net.go(swaps[2 * i])
        net.go(swaps[2 * i + 1])
    summed(h_sums[1], 1)
    gains_low = heads_back(1)
    d_post, d_ffn = (top + low for top, low in zip(gains_top, gains_low))
    dgains_out[...] = jnp.concatenate([d_post, d_ffn, d_out, jnp.zeros((5, D), F32)], axis=0)
    delta_all[place.y, core] = jnp.concatenate(
        [jnp.transpose(delta_rows[h])[:1] for h in range(HEADS)] + [jnp.zeros((4, TOK), F32)],
        axis=0,
    )
    delta_swap.start()
    stores = [pltpu.make_async_copy(got.at[y], sums_hbm.at[y], local.at[3 + y]) for y in range(4)]

    def do_near(part):
        do_rings[part].forward()
        net.go(do_core[part][1])
        net.go(do_core[part][3])

    def do_far(part):
        do_rings[part].finish()
        net.go(do_core[part][2])

    do_near(0)
    for i in range(2):
        swaps[2 * i].wait_recv()
        swaps[2 * i + 1].wait_recv()
        fill_others(got, i, core, True)
        fill_down(got, i, core, True)
        stores[2 * i].start()
        stores[2 * i + 1].start()
        if i == 0:
            do_far(0)
            do_near(1)
    do_far(1)
    delta_swap.wait()
    net.go(delta_core)
    for copies in do_core:
        for copy in copies:
            copy.wait_recv()
    delta_core.wait_recv()
    for store in stores:
        store.wait()
    net.drain()


def feed_forward(args, call_id):
    quarter = (TOK // 4, D)
    shape = jax.ShapeDtypeStruct
    every = (4, 2, 2, 144, HALF)
    lines = 4 * TOK
    anywhere = pl.BlockSpec(memory_space=pl.ANY)
    unit_rows = [pltpu.VMEM((lines, HID_PAD), BF)] * 5
    return pl.pallas_call(
        feed_kernel,
        out_shape=(
            shape((TOK, D), BF),
            shape((TOK, D), F32),
            shape((TOK, D), BF),
            shape((4, HEADS, ROWS, HD), BF),
            shape((4, 2, 8, TOK), F32),
            shape((8, D), F32),
            shape(every, BF),
        ),
        in_specs=[IN_VMEM] * 9 + [anywhere] * 3,
        out_specs=[IN_VMEM] * 6 + [anywhere],
        scratch_shapes=[
            pltpu.VMEM((D, HID_PAD), BF),
            pltpu.VMEM((D, HID_PAD), BF),
            pltpu.VMEM((HID_PAD, D), BF),
            pltpu.VMEM((2, 4, TOK // 2, D), BF),
            pltpu.VMEM((2, 4, TOK // 2, D), BF),
            pltpu.VMEM((D, lines), BF),
            pltpu.VMEM((D, lines), BF),
            *unit_rows,
            pltpu.VMEM((2, 4, TOK // 2, D), BF),
            pltpu.VMEM((2, 4, TOK // 2, D), BF),
            pltpu.VMEM(every, BF),
            pltpu.VMEM(every, BF),
            pltpu.VMEM((TOK, D), F32),
            pltpu.VMEM((TOK, D), F32),
            pltpu.VMEM((TOK, D), F32),
            pltpu.VMEM((HEADS, TOK, TOK), F32),
            *(RingScatter.room_shapes(quarter, quarter) * 4),
            *sems(88),
            pltpu.SemaphoreType.DMA((7,)),
        ],
        compiler_params=params(call_id),
    )(*args)


class FirstSums:
    def __init__(self, net, place, sums, cut, rooms, here=None, marks=None):
        left, right = pl.ds(0, cut), pl.ds(cut, sums.shape[-1] - cut)

        def y_spot(half):
            return stepped(place, "y", lambda j: sums.at[j, half, :, :, left])

        def z_spot(half):
            return stepped(
                place,
                "z",
                lambda j: sums.at[pl.ds(2 * half, 2), lax.div(j, 2), lax.rem(j, 2), :, right],
            )

        self.loads = []
        self.lines = []
        for i, (axis, spot) in enumerate((("y", y_spot), ("z", z_spot))):
            near = (None, None)
            if here is not None:
                near = ({}, {})
                for k, (half, by) in enumerate(((0, 1), (1, 3), (0, 0), (1, 0))):
                    target = here[i].at[k]
                    near[half][by] = target
                    self.loads.append(
                        pltpu.make_async_copy(spot(half)(by), target, marks.at[8 + 4 * i + k])
                    )
                near = (near[0].get, near[1].get)
            room = rooms[6 * i : 6 * i + 6]
            self.lines.append(RingScatter(net, place, axis, spot(0), spot(1), room, *near))

    @staticmethod
    def room_shapes(cut, rest):
        return [
            *RingScatter.room_shapes((2, 144, cut), (2, 144, cut)),
            *RingScatter.room_shapes((2, 144, rest), (2, 144, rest)),
        ]

    def begin(self):
        for load in self.loads:
            load.start()
        for line in self.lines:
            line.start_far()

    def go_on(self):
        for line in self.lines:
            line.start_right()
            line.start_left()

    def turn(self):
        for load in self.loads:
            load.wait()
        for line in self.lines:
            line.middle()


class WeightSums:
    def __init__(self, place, net, sums, late, refs, marks):
        y_here, z_here, y1, z1, z2, y2, snd, late_snd, rcv, late_rcv, *rooms = refs
        self.late_snd, self.late_rcv = late_snd, late_rcv
        self.place, self.late, self.snd, self.rcv, self.marks = place, late, snd, rcv, marks
        self.y1, self.z1, self.y2, self.z2 = y1, z1, y2, z2
        self.x_hi, self.x_lo = lax.div(place.x, 2), lax.rem(place.x, 2)
        self.friends = []
        for k in range(1, 16):
            spot = lax.rem(self.x_hi * 8 + place.z * 2 + place.core + k, 16)
            x, z = lax.div(spot, 8) * 2 + self.x_lo, lax.rem(lax.div(spot, 2), 4)
            self.friends.append(place.device(x=x, z=z, core=lax.rem(spot, 2)))

        self.first = FirstSums(net, place, sums, CUT, rooms[:12], (y_here, z_here), marks[2])

        def then_z(j):
            return y1.at[lax.div(j, 2), lax.rem(j, 2)]

        self.z_second = RingScatter(
            net,
            place,
            "z",
            stepped(place, "z", lambda j: then_z(j).at[:, pl.ds(0, 384)]),
            stepped(place, "z", lambda j: then_z(j).at[:, pl.ds(384, 384)]),
            rooms[12:18],
        )
        self.y_second = RingScatter(
            net,
            place,
            "y",
            stepped(place, "y", lambda j: z1.at[j, :, pl.ds(0, 384)]),
            stepped(place, "y", lambda j: z1.at[j, :, pl.ds(384, 256)]),
            rooms[18:24],
        )

    @staticmethod
    def scratch():
        rest = HALF - CUT
        return [
            pltpu.VMEM((4, 2, 144, CUT), BF),
            pltpu.VMEM((4, 2, 144, rest), BF),
            pltpu.VMEM((2, 2, 144, CUT), BF),
            pltpu.VMEM((4, 144, rest), BF),
            pltpu.VMEM((144, CUT), F32),
            pltpu.VMEM((144, rest), F32),
            pltpu.VMEM((8, 16, HALF + 256), BF),
            pltpu.VMEM((8, 16, 256), BF),
            pltpu.VMEM((8, 16, HALF + 256), BF),
            pltpu.VMEM((8, 16, 256), BF),
            *FirstSums.room_shapes(CUT, rest),
            *RingScatter.room_shapes((144, 384), (144, 384)),
            *RingScatter.room_shapes((144, 384), (144, 256)),
        ]

    def next(self):
        y_line, z_line = self.first.lines
        y_line.finish(self.y1.at[0], self.y1.at[1])
        self.z_second.start()
        z_line.finish(self.z1.at[pl.ds(0, 2)], self.z1.at[pl.ds(2, 2)])
        self.y_second.start()

    def turn_again(self):
        self.z_second.middle()
        self.y_second.middle()

    def last(self):
        z2, y2 = self.z2, self.y2
        self.z_second.finish(z2.at[:, pl.ds(0, 384)], z2.at[:, pl.ds(384, 384)])
        self.y_second.finish(y2.at[:, pl.ds(0, 384)], y2.at[:, pl.ds(384, 256)])
        total = jnp.concatenate([z2[...], y2[...]], axis=1)
        self.pack(total, self.snd)
        self.exchange(self.snd, self.rcv, 0)

    def send_late(self):
        self.pack(self.late[...], self.late_snd)
        self.exchange(self.late_snd, self.late_rcv, 8)

    @staticmethod
    def pack(total, snd):
        width = total.shape[1]
        count = width // 128
        for k in range(8):
            extra = total[18 * k + 16 : 18 * k + 18]
            pieces = [extra[:, 128 * n : 128 * n + 128] for n in range(count)]
            snd[k, :, :width] = total[18 * k : 18 * k + 16].astype(BF)
            for n in range(0, count, 8):
                group = pieces[n : n + 8]
                if len(group) < 8:
                    group.append(jnp.zeros((16 - 2 * len(group), 128), F32))
                at = width + 16 * n
                snd[k, :, at : at + 128] = jnp.concatenate(group, axis=0).astype(BF)

    def exchange(self, snd, rcv, mark):
        place = self.place
        send, recv, here = self.marks
        row_half = lax.div(place.z, 2)
        self.slot = self.x_hi * 4 + place.core * 2 + lax.rem(place.z, 2)
        self.own = place.z * 2 + place.core
        self.stays = row_half == self.x_hi
        for k in range(8):
            copy = pltpu.make_async_remote_copy(
                src_ref=snd.at[k],
                dst_ref=rcv.at[self.slot],
                send_sem=send.at[mark + k],
                recv_sem=recv.at[mark + self.slot],
                device_id=place.device(x=row_half * 2 + self.x_lo, z=k // 2, core=k % 2),
                device_id_type=MESH,
            )
            is_here = self.stays & (self.own == k)

            @pl.when(jnp.logical_not(is_here))
            def _(copy=copy):
                copy.start()

            @pl.when(is_here)
            def _(k=k):
                keep = pltpu.make_async_copy(snd.at[k], rcv.at[self.slot], here.at[0])
                keep.start()
                keep.wait()

    def arrive(self):
        send, recv, _ = self.marks
        for mark, snd, rcv in ((0, self.snd, self.rcv), (8, self.late_snd, self.late_rcv)):
            for m in range(8):
                arrival = pltpu.make_async_remote_copy(
                    src_ref=snd.at[m],
                    dst_ref=rcv.at[m],
                    send_sem=send.at[mark + m],
                    recv_sem=recv.at[mark + m],
                    device_id=self.place.partner(),
                    device_id_type=MESH,
                )

                @pl.when(jnp.logical_not(self.stays & (self.slot == m)))
                def _(arrival=arrival):
                    arrival.wait_recv()

                @pl.when(jnp.logical_not(self.stays & (self.own == m)))
                def _(arrival=arrival):
                    arrival.wait_send()


def last_kernel(
    home_ref,
    late_ref,
    top_ref,
    low_ref,
    gains_ref,
    y_ref,
    dx_ref,
    y_out,
    dx_out,
    dwq_out,
    dwk_out,
    dwv_out,
    dwo_out,
    dwg_out,
    dwu_out,
    dwd_out,
    *gain_outs,
):
    y_out[...] = y_ref[...]
    dx_out[...] = dx_ref[...]

    def rows_at(ref, slot, n):
        spare = (HALF if ref is home_ref else 128) + 128 * (n // 8)
        more = ref[slot, :, spare : spare + 128].astype(F32)[2 * (n % 8) : 2 * (n % 8) + 2]
        return jnp.concatenate(
            [ref[slot, :, 128 * n : 128 * n + 128].astype(F32), more], axis=0
        )

    def tile(x_hi, which, n):
        core, n = n // 7, n % 7
        if which < 2:
            c, at = which, 256 + 128 * n if n < 4 else 512 + 128 * n
        else:
            c, n = n // 4, n % 4
            at = 128 * n if n < 2 else CUT + 128 * (n - 2)
        return rows_at(home_ref, x_hi * 4 + core * 2 + c, at // 128)

    for which, out in enumerate((dwg_out, dwu_out, dwd_out)):
        for n in range(27):
            value = None
            for x_hi in range(2):
                if 0 <= n - 13 * x_hi < 14:
                    term = tile(x_hi, which, n - 13 * x_hi)
                    value = term if value is None else value + term
            span = slice(128 * n, 128 * n + 128)
            out[:, span] = value
    for k in range(4):
        span = slice(128 * k, 128 * k + 128)
        dwo_out[:, span] = rows_at(late_ref, 2 * k, 0)
        dwq_out[:, span] = rows_at(late_ref, 2 * k + 1, 0)
    for which in range(2):
        for j in range(4):
            out = (dwk_out, dwv_out)[j // 2]
            for y in range(4):
                span = slice(128 * (j % 2), 128 * (j % 2) + 128)
                at = 576 * which + 144 * y
                out[at : at + 80, span] = top_ref[which, j, y].astype(F32)
                out[at + 80 : at + 144, span] = low_ref[which, j, y].astype(F32)
    for out, row, start in zip(gain_outs, (0, 4, 4, 1, 2, 3), (0, 0, HD, 0, 0, 0)):
        size = out.shape[0]
        out[...] = gains_ref[row : row + 1, start : start + size].reshape(size)


def last_layout(*args):
    shape = jax.ShapeDtypeStruct
    return pl.pallas_call(
        last_kernel,
        out_shape=(
            shape((TOK, D), BF),
            shape((TOK, D), BF),
            shape((18, 2 * HD), F32),
            shape((D, HD), F32),
            shape((D, HD), F32),
            shape((18, 2 * HD), F32),
            shape((18, 2 * HID), F32),
            shape((18, 2 * HID), F32),
            shape((18, 2 * HID), F32),
            *(shape((size,), F32) for size in (D, HD, HD, D, D, D)),
        ),
        in_specs=[IN_VMEM] * len(args),
        out_specs=[IN_VMEM] * 15,
        compiler_params=pltpu.CompilerParams(vmem_limit_bytes=VMEM_BYTES),
    )(*args)


def angles(token_pos):
    middle = HD // 2
    frequency = THETA ** (-2.0 * jnp.arange(middle, dtype=F32) / HD)
    turned = token_pos.astype(F32)[:, None] * frequency[None, :]
    return (jnp.cos(turned), jnp.sin(turned))


def shards(
    layer_input,
    segment_ids,
    positions,
    w_query,
    w_key,
    w_value,
    w_out,
    w_gate,
    w_up,
    w_down,
    norm_attn,
    norm_query,
    norm_key,
    norm_post,
    norm_ffn,
    norm_out,
    cotangent,
):
    sp, tp = lax.axis_index("sp"), lax.axis_index("tp")
    cosine, sine = angles(lax.dynamic_slice_in_dim(positions, (sp * 2 + tp) * TOK, TOK))
    segments = segment_ids.reshape(128, 128)
    key_rows = jnp.asarray(KEY_TOKENS)
    kv_all, q_all, wq_other, wo_other, o_heads, inverse, q_pre, k_pre, h_attn = attention_forward(
        (
            layer_input,
            norm_attn,
            norm_query,
            norm_key,
            w_query,
            w_key,
            w_value,
            w_out,
            cosine,
            sine,
            segments,
            key_rows,
        ),
        2,
    )
    (
        layer_output,
        d_mid,
        d_attn,
        d_heads,
        delta,
        d_gains,
        sums,
    ) = feed_forward(
        (
            layer_input,
            o_heads,
            inverse,
            w_out,
            wo_other,
            norm_post,
            norm_ffn,
            norm_out,
            cotangent,
            w_gate,
            w_up,
            w_down,
        ),
        6,
    )
    d_input, home, late, w_top, w_low, gains = attention_backward(
        (kv_all, q_all, d_heads, sums, w_query, wq_other, w_key, w_value),
        (
            delta,
            key_rows,
            segments,
            q_pre,
            k_pre,
            cosine,
            sine,
            h_attn,
            d_attn,
            o_heads,
            layer_input,
            d_mid,
            norm_attn,
            norm_query,
            norm_key,
            d_gains,
        ),
        8,
    )
    y, dx, d_wq, d_wk, d_wv, d_wo, d_wg, d_wu, d_wd, *d_norms = last_layout(
        home, late, w_top, w_low, gains, layer_output, d_input
    )
    return (y, dx, d_wq, d_wk, d_wv, d_wo.T, d_wg, d_wu, d_wd.T, *d_norms)


def solution(mesh):
    rows = P(("sp", "tp"), None)
    in_specs = (
        rows,
        P(),
        P(),
        P(None, "tp"),
        P(),
        P(),
        P("tp", None),
        P(None, "tp"),
        P(None, "tp"),
        P("tp", None),
        P(),
        P(),
        P(),
        P(),
        P(),
        P(),
        rows,
    )
    out_specs = (
        rows,
        rows,
        P("sp", "tp"),
        P(),
        P(),
        P("tp", "sp"),
        P("sp", "tp"),
        P("sp", "tp"),
        P("tp", "sp"),
        P(),
        P(),
        P(),
        P(),
        P(),
        P(),
    )
    return jax.shard_map(shards, mesh=mesh, in_specs=in_specs, out_specs=out_specs, check_vma=False)
```

```python
import functools

import jax
import jax.numpy as jnp
import numpy as np
from jax import lax
from jax.experimental import pallas as pl
from jax.experimental.pallas import tpu as pltpu
from jax.sharding import PartitionSpec as P

EPS = 1e-06
THETA = 1000000.0
BF = jnp.bfloat16
F32 = jnp.float32
MESH = pl.DeviceIdType.MESH
IN_VMEM = pl.BlockSpec(memory_space=pltpu.VMEM)
VMEM_BYTES = 58 * 1024 * 1024

TOK = 128
D = 1152
HD = 256
HEADS = 4
ROWS = 2 * TOK
HID = 1728
HID_PAD = 1792
CUT = 768
HALF = 1408
STRIPE = TOK // 4
KEYS = 16 * STRIPE


class Place:
    def __init__(self):
        sp = lax.axis_index("sp")
        self.core = lax.rem(sp, 2)
        self.z = lax.rem(lax.div(sp, 2), 4)
        self.y = lax.div(sp, 16)
        self.x = lax.rem(lax.div(sp, 8), 2) * 2 + lax.axis_index("tp")

    def device(self, **moved):
        x, y, z, core = (moved.get(name, getattr(self, name)) for name in ("x", "y", "z", "core"))
        return (((y * 2 + lax.div(x, 2)) * 4 + z) * 2 + core, lax.rem(x, 2))

    def step(self, axis, by):
        return lax.rem(getattr(self, axis) + by, 4)

    def toward(self, axis, by):
        return self.device(**{axis: self.step(axis, by)})

    def partner(self):
        return self.device(core=1 - self.core)


class Net:
    def __init__(self, send, recv):
        self.send, self.recv, self.used, self.started = send, recv, 0, []

    def copy(self, source, target, device):
        at = self.used
        self.used += 1
        return pltpu.make_async_remote_copy(
            src_ref=source,
            dst_ref=target,
            send_sem=self.send.at[at],
            recv_sem=self.recv.at[at],
            device_id=device,
            device_id_type=MESH,
        )

    def go(self, copy):
        copy.start()
        self.started.append(copy)

    def settle(self, copy):
        copy.wait_send()
        self.started = [other for other in self.started if other is not copy]

    def drain(self):
        for copy in self.started:
            copy.wait_send()
        self.started = []


def greet(devices, meanwhile=None):
    barrier = pltpu.get_barrier_semaphore()
    for device in devices:
        pl.semaphore_signal(barrier, inc=1, device_id=device, device_id_type=MESH)
    if meanwhile is not None:
        meanwhile()
    pl.semaphore_wait(barrier, len(devices))


def ring(place, axis):
    return [place.toward(axis, 1), place.toward(axis, 3)]


class RingGather:
    def __init__(self, net, place, axis, view, lo, hi):
        self.net = net
        me, nxt, prev = getattr(place, axis), place.step(axis, 1), place.step(axis, 3)
        right, left = ring(place, axis)
        self.to_right = net.copy(view(me), view(me), right)
        self.to_left = net.copy(view(me), view(me), left)
        self.on_right = net.copy(lo(prev), lo(prev), right)
        self.on_left = net.copy(hi(nxt), hi(nxt), left)

    def start(self):
        self.net.go(self.to_right)
        self.net.go(self.to_left)

    def forward(self):
        self.to_right.wait_recv()
        self.net.go(self.on_right)
        self.to_left.wait_recv()
        self.net.go(self.on_left)

    def finish(self):
        self.on_right.wait_recv()
        self.on_left.wait_recv()


class Direct:
    def __init__(self, net, place, axis, source, landing):
        self.net = net
        self.copies = [
            net.copy(
                source(place.step(axis, by)), landing(getattr(place, axis)), place.toward(axis, by)
            )
            for by in (2, 1, 3)
        ]

    def start(self):
        for copy in self.copies:
            self.net.go(copy)

    def wait(self):
        for copy in self.copies:
            copy.wait_recv()


def by_rows(ref, act):
    *lead, rows, _ = ref.shape
    block = next(size for size in (64, 48, 32, 16) if rows % size == 0)
    for spot in np.ndindex(*lead):

        def one(i, carry, spot=spot):
            act(spot, pl.ds(pl.multiple_of(i * block, block), block))
            return carry

        lax.fori_loop(0, rows // block, one, 0)


def add_to(target, other):
    def act(spot, rows):
        at = (*spot, rows, slice(None))
        target[at] = (target[at].astype(F32) + other[at].astype(F32)).astype(target.dtype)

    by_rows(target, act)


def sum_to(target, others):
    def act(spot, rows):
        at = (*spot, rows, slice(None))
        total = others[0][at].astype(F32)
        for other in others[1:]:
            total = total + other[at].astype(F32)
        target[at] = total.astype(target.dtype)

    by_rows(target, act)


def stepped(place, axis, view):
    return lambda by: view(place.step(axis, by))


class RingScatter:
    def __init__(self, net, place, axis, lo, hi, room, lo_here=None, hi_here=None):
        self.net, self.lo, self.hi = net, lo_here or lo, hi_here or hi
        right, left = ring(place, axis)
        self.lo1, self.lo_l, self.lo_r, self.hi1, self.hi_l, self.hi_r = room
        self.a = net.copy(lo(2), self.lo1, right)
        self.b = net.copy(hi(2), self.hi1, left)
        self.c_hi = net.copy(hi(1), self.hi_l, right)
        self.d_lo = net.copy(lo(3), self.lo_r, left)
        self.c_lo = net.copy(self.lo1, self.lo_l, right)
        self.d_hi = net.copy(self.hi1, self.hi_r, left)

    def start_far(self):
        self.net.go(self.a)
        self.net.go(self.b)

    def start_right(self):
        self.net.go(self.c_hi)

    def start_left(self):
        self.net.go(self.d_lo)

    def start(self):
        self.start_far()
        self.start_right()
        self.start_left()

    def middle_right(self):
        self.a.wait_recv()
        add_to(self.lo1, self.lo(1))
        self.net.go(self.c_lo)

    def middle_left(self):
        self.b.wait_recv()
        add_to(self.hi1, self.hi(3))
        self.net.go(self.d_hi)

    def middle(self):
        self.middle_right()
        self.middle_left()

    def finish(self, lo_out, hi_out):
        self.c_hi.wait_recv()
        self.d_hi.wait_recv()
        sum_to(hi_out, [self.hi(0), self.hi_l, self.hi_r])
        self.d_lo.wait_recv()
        self.c_lo.wait_recv()
        sum_to(lo_out, [self.lo(0), self.lo_l, self.lo_r])

    @staticmethod
    def room_shapes(lo_shape, hi_shape):
        return [pltpu.VMEM(lo_shape, BF)] * 3 + [pltpu.VMEM(hi_shape, BF)] * 3


def params(call_id):
    return pltpu.CompilerParams(
        collective_id=call_id, has_side_effects=True, vmem_limit_bytes=VMEM_BYTES
    )


def sems(count):
    return [pltpu.SemaphoreType.DMA((count,)), pltpu.SemaphoreType.DMA((count,))]


class WeightSwap:
    def __init__(self, net, place, w_ref, other_ref):
        self.net = net
        quarter = w_ref.shape[0] // 4
        right, left = ring(place, "x")

        def rows(ref, side):
            return ref.at[pl.ds(pl.multiple_of((2 * side + place.core) * quarter, 16), quarter)]

        self.first = [
            net.copy(rows(w_ref, side), rows(other_ref, side), (left, right)[side])
            for side in (0, 1)
        ]
        self.trades = [
            net.copy(rows(other_ref, side), rows(other_ref, side), place.partner())
            for side in (0, 1)
        ]

    def start(self):
        for copy in self.first:
            self.net.go(copy)

    def forward(self):
        for copy, trade in zip(self.first, self.trades):
            copy.wait_recv()
            self.net.go(trade)

    def finish(self):
        for trade in self.trades:
            trade.wait_recv()


def key_lines(place, ref):
    def stage(axis, first, at):
        return (
            axis,
            lambda j: ref.at[(pl.ds(first, 2), *at(j))],
            lambda j: ref.at[(first, *at(j))],
            lambda j: ref.at[(first + 1, *at(j))],
        )

    every = slice(None)
    return (
        (stage("x", 0, lambda j: (place.z, j)), stage("z", 0, lambda j: (j,))),
        (stage("z", 2, lambda j: (j, place.x)), stage("x", 2, lambda j: (every, j))),
    )


def key_tokens():
    z, x, row = np.meshgrid(np.arange(4), np.arange(4), np.arange(STRIPE), indexing="ij")
    return ((x // 2) * 2048 + z * 512 + (x % 2) * 128 + row).reshape(1, KEYS).astype(np.int32)


KEY_TOKENS = key_tokens()


def first_key(place, y):
    return y * 4096 + place.core * 256 + STRIPE * place.y


def contract(left, right, left_dim, right_dim):
    return lax.dot_general(
        left, right, (((left_dim,), (right_dim,)), ((), ())), preferred_element_type=F32
    )


def turn(u, cosine, sine):
    half = HD // 2
    low, high = u[:, :half], u[:, half:]
    return jnp.concatenate([low * cosine - high * sine, high * cosine + low * sine], axis=1)


def row_bounds(place, segments, y):
    at = (y * 2 + lax.div(place.x, 2)) * 16 + place.z * 4 + lax.rem(place.x, 2)
    rows = jnp.concatenate([segments[pl.ds(at, 1)], segments[pl.ds(at + 2, 1)]], axis=1)
    every = segments[...]
    first = jnp.zeros((1, ROWS), jnp.int32)
    for k in range(1, 4):
        below = jnp.sum((every < k).astype(F32), axis=0, keepdims=True)
        below = jnp.sum(below, axis=1, keepdims=True).astype(jnp.int32)
        first = jnp.where(rows == k, below, first)
    lane = lax.broadcasted_iota(jnp.int32, (1, ROWS), 1)
    last = at * TOK + lane + jnp.where(lane < TOK, 0, TOK)
    return first, last


def down(row):
    return jnp.concatenate(
        [
            jnp.transpose(jnp.broadcast_to(row[:, 128 * i : 128 * i + 128], (128, 128)))
            for i in range(row.shape[1] // 128)
        ],
        axis=0,
    )


def across(ref):
    return ref[...].reshape(1, ref.shape[0])


def norm_scale(v):
    return lax.rsqrt(jnp.mean(v * v, axis=-1, keepdims=True) + EPS)


def norm_back(v, r, gain, e):
    eg = e * gain
    dv = r * eg - v * (r * r * r) * jnp.mean(eg * v, axis=-1, keepdims=True)
    return dv, jnp.sum(e * v * r, axis=0, keepdims=True)


def forward_kernel(
    x_ref,
    g_attn,
    g_query,
    g_key,
    wq_ref,
    wk_ref,
    wv_ref,
    w_hbm,
    cos_ref,
    sin_ref,
    segments,
    key_ref,
    kv_hbm,
    q_all,
    wq_other,
    w_other,
    o_out,
    inv_out,
    q_pre,
    k_pre,
    h_out,
    buf,
    kv_own,
    o_sum,
    l_sum,
    o_snd,
    o_part,
    o_got,
    o_done,
    l_mine,
    l_got,
    l_core,
    *rest,
):
    *room, send, recv, local = rest
    place, net = Place(), Net(send, recv)
    core = place.core
    partner = place.partner()
    mine = pl.ds(pl.multiple_of(core * TOK, TOK), TOK)
    theirs = pl.ds(pl.multiple_of((1 - core) * TOK, TOK), TOK)

    def keys_and_values():
        xf = x_ref[...].astype(F32)
        h = (xf * norm_scale(xf) * across(g_attn)).astype(BF)
        h_out[...] = h
        k = jnp.dot(h, wk_ref[...], preferred_element_type=F32)
        k_pre[...] = k
        k = turn(k * norm_scale(k) * across(g_key), cos_ref[...], sin_ref[...]).astype(BF)
        v = jnp.dot(h, wv_ref[...], preferred_element_type=F32).astype(BF)
        for j in range(4):
            kv_own[j, :, :HD] = k[STRIPE * j : STRIPE * j + STRIPE]
            kv_own[j, :, HD:] = v[STRIPE * j : STRIPE * j + STRIPE]
        buf[place.y, place.z, place.x] = kv_own[place.y]

    greet(
        ring(place, "x")
        + ring(place, "y")
        + ring(place, "z")
        + [partner, place.toward("y", 2)],
        keys_and_values,
    )
    swap_wq = WeightSwap(net, place, wq_ref, wq_other)
    swap_w = WeightSwap(net, place, w_hbm, w_other)
    stripes = Direct(
        net,
        place,
        "y",
        lambda j: kv_own.at[j],
        lambda j: buf.at[j, place.z, place.x],
    )
    stripes.start()
    swap_wq.start()
    (first_a, then_a), (first_b, then_b) = (
        [RingGather(net, place, *stage) for stage in part] for part in key_lines(place, buf)
    )
    q_ring = RingGather(
        net,
        place,
        "y",
        lambda j: q_all.at[j, :, mine],
        lambda j: q_all.at[j, pl.ds(0, 2), mine],
        lambda j: q_all.at[j, pl.ds(2, 2), mine],
    )

    def block_of(by):
        return q_all.at[place.step("y", by), :, mine]

    q_core = [net.copy(block_of(by), block_of(by), partner) for by in range(4)]

    def queries(which, w):
        q = jnp.dot(h_out[...], w[...], preferred_element_type=F32)
        for i in range(2):
            u = q[:, HD * i : HD * i + HD]
            q_pre[2 * which + i] = u
            u = turn(u * norm_scale(u) * across(g_query), cos_ref[...], sin_ref[...])
            q_all[place.y, 2 * which + i, mine] = (u.astype(BF).astype(F32) * HD**-0.5).astype(BF)

    queries(0, wq_ref)
    stripes.wait()
    first_a.start()
    first_b.start()
    swap_wq.forward()
    first_a.forward()
    first_b.forward()
    swap_wq.finish()
    queries(1, wq_other)
    q_ring.start()
    net.go(q_core[0])
    first_a.finish()
    then_a.start()
    first_b.finish()
    then_b.start()
    q_ring.forward()
    net.go(q_core[1])
    net.go(q_core[3])
    then_a.forward()
    then_b.forward()
    q_ring.finish()
    net.go(q_core[2])
    then_a.finish()
    then_b.finish()
    swap_w.start()
    store = pltpu.make_async_copy(buf, kv_hbm, local.at[0])
    store.start()

    o_core = [net.copy(o_snd.at[by], o_got.at[by], partner) for by in range(4)]

    def attend(by):
        y = place.step("y", by)
        q_core[by].wait_recv()
        first, last = (down(row) for row in row_bounds(place, segments, y))

        keys = buf[:, :, :, :, :HD].reshape(4 * KEYS, HD)
        values = buf[:, :, :, :, HD:].reshape(4 * KEYS, HD)
        token = jnp.concatenate([key_ref[...] + first_key(place, j) for j in range(4)], axis=1)
        allowed = jnp.concatenate(
            [
                (token[:, 128 * i : 128 * i + 128] <= last)
                & (token[:, 128 * i : 128 * i + 128] >= first)
                for i in range(4 * KEYS // 128)
            ],
            axis=1,
        )
        for h in range(HEADS):
            weights = jnp.exp(contract(q_all[y, h], keys, 1, 1))
            weights = jnp.where(allowed, weights, 0.0)
            l_sum[by, h] = sum(
                weights[:, 128 * i : 128 * i + 128] for i in range(4 * KEYS // 128)
            )
            o_sum[by, h] = jnp.dot(weights.astype(BF), values, preferred_element_type=F32)
        for h in range(HEADS):
            o_snd[by, h] = o_sum[by, h, theirs].astype(BF)
            o_part[by, h] = o_sum[by, h, mine].astype(BF)
            total = jnp.sum(l_sum[by, h], axis=1, keepdims=True)
            l_mine[y, h : h + 1] = jnp.transpose(jnp.broadcast_to(total, (ROWS, 128)))[:1]
        net.go(o_core[by])

    def both_cores(by):
        o_core[by].wait_recv()
        add_to(o_part.at[by], o_got.at[by])

    o_ring = RingScatter(
        net,
        place,
        "y",
        lambda by: o_part.at[by, pl.ds(0, 2)],
        lambda by: o_part.at[by, pl.ds(2, 2)],
        room,
    )
    attend(0)
    attend(2)
    attend(1)
    both_cores(2)
    o_ring.start_far()
    swap_w.forward()
    attend(3)
    l_swap = Direct(net, place, "y", lambda j: l_mine.at[j], lambda j: l_got.at[j])
    l_swap.start()
    l_got[place.y] = l_mine[place.y]
    both_cores(1)
    o_ring.start_right()
    o_ring.middle_right()
    both_cores(3)
    o_ring.start_left()
    o_ring.middle_left()
    both_cores(0)
    swap_w.finish()
    l_swap.wait()
    l_core[core] = (l_got[0] + l_got[1]) + (l_got[2] + l_got[3])
    l_over = net.copy(l_core.at[core], l_core.at[core], partner)
    net.go(l_over)
    l_over.wait_recv()
    total = l_core[0] + l_core[1]
    inverse = 1.0 / jnp.where(core == 0, total[:, :TOK], total[:, TOK:])
    o_ring.finish(o_done.at[pl.ds(0, 2)], o_done.at[pl.ds(2, 2)])
    for h in range(HEADS):
        scale = down(inverse[h : h + 1])
        o_out[h] = o_done[h] * jnp.concatenate([scale, scale], axis=1)
        inv_out[h] = scale
    store.wait()
    net.drain()


def attention_forward(args, call_id):
    shape = jax.ShapeDtypeStruct
    anywhere = pl.BlockSpec(memory_space=pl.ANY)
    halves = (2, TOK, HD)
    return pl.pallas_call(
        forward_kernel,
        out_shape=(
            shape((4, 4, 4, STRIPE, 2 * HD), BF),
            shape((4, HEADS, ROWS, HD), BF),
            shape((D, 2 * HD), BF),
            shape((2 * HD, D), BF),
            shape((HEADS, TOK, HD), F32),
            shape((HEADS, TOK, 128), F32),
            shape((HEADS, TOK, HD), F32),
            shape((TOK, HD), F32),
            shape((TOK, D), BF),
        ),
        in_specs=[IN_VMEM] * 7 + [anywhere] + [IN_VMEM] * 4,
        out_specs=[anywhere] + [IN_VMEM] * 2 + [anywhere] + [IN_VMEM] * 5,
        scratch_shapes=[
            pltpu.VMEM((4, 4, 4, STRIPE, 2 * HD), BF),
            pltpu.VMEM((4, STRIPE, 2 * HD), BF),
            pltpu.VMEM((4, HEADS, ROWS, HD), F32),
            pltpu.VMEM((4, HEADS, ROWS, 128), F32),
            pltpu.VMEM((4, HEADS, TOK, HD), BF),
            pltpu.VMEM((4, HEADS, TOK, HD), BF),
            pltpu.VMEM((4, HEADS, TOK, HD), BF),
            pltpu.VMEM((HEADS, TOK, HD), F32),
            pltpu.VMEM((4, 8, ROWS), F32),
            pltpu.VMEM((4, 8, ROWS), F32),
            pltpu.VMEM((2, 8, ROWS), F32),
            *RingScatter.room_shapes(halves, halves),
            *sems(64),
            pltpu.SemaphoreType.DMA((1,)),
        ],
        compiler_params=params(call_id),
    )(*args)


def kept_head(place, j):
    return jnp.where(lax.rem(j, 2) == lax.rem(place.x, 2), 0, 2) + lax.div(j, 2)


def turn_back(e, cosine, sine):
    half = HD // 2
    low, high = e[:, :half], e[:, half:]
    return jnp.concatenate([low * cosine + high * sine, high * cosine - low * sine], axis=1)


def backward_kernel(
    kv_hbm,
    q_hbm,
    do_hbm,
    sums_hbm,
    wq_hbm,
    wq2_hbm,
    wk_hbm,
    wv_hbm,
    delta_all,
    key_ref,
    segments,
    q_pre,
    k_pre,
    cos_ref,
    sin_ref,
    h_ref,
    da_ref,
    o_ref,
    x_ref,
    dmid_ref,
    g_attn,
    g_query,
    g_key,
    gains_ref,
    dx_out,
    home_out,
    late_out,
    w_top,
    w_low,
    gains_out,
    buf,
    q_all,
    do_all,
    wq,
    wq2,
    wk,
    wv,
    tokens,
    grads,
    fin,
    fin_got,
    dq_sum,
    dq_snd,
    dq_part,
    dq_got,
    dq_done,
    h_line,
    da_line,
    turned,
    o_line,
    dq_line,
    dq_own,
    o_own,
    late_all,
    late_got,
    late_y,
    late_z,
    gain_got,
    kv_own,
    kv_line,
    turned_other,
    w_got,
    w_y,
    w_z,
    *rest,
):
    rooms, dq_rooms, late_rooms, rest = rest[:24], rest[24:30], rest[30:42], rest[42:]
    *weight_refs, send, recv, send2, recv2, here = rest
    place, net = Place(), Net(send, recv)
    core, partner = place.core, place.partner()
    w_loads = [
        pltpu.make_async_copy(source, target, here.at[1 + i])
        for i, (source, target) in enumerate(
            (
                (kv_hbm, buf),
                (q_hbm, q_all),
                (do_hbm, do_all),
                (wq_hbm, wq),
                (wq2_hbm, wq2),
                (wk_hbm, wk),
                (wv_hbm, wv),
            )
        )
    ]
    for load in w_loads:
        load.start()
    weights = WeightSums(place, net, sums_hbm, late_z, weight_refs, (send2, recv2, here))
    across_x = [place.device(x=place.step("x", by), core=1 - core) for by in (1, 3)]

    def prepare():
        h_line[place.x] = h_ref[...]
        da_line[place.x] = da_ref[...]
        for h in range(HEADS):
            o_own[h] = o_ref[h].astype(BF)
        o_line[place.x] = o_own[kept_head(place, place.x)]
        tokens[...] = down(key_ref[...])

    greet(
        weights.friends
        + ring(place, "x")
        + ring(place, "y")
        + across_x
        + [place.toward("y", 2)],
        prepare,
    )
    mine = pl.ds(pl.multiple_of(core * TOK, TOK), TOK)
    theirs = pl.ds(pl.multiple_of((1 - core) * TOK, TOK), TOK)
    half = TOK // 2

    def line_of(rows):
        return RingGather(
            net,
            place,
            "x",
            lambda j: rows.at[j],
            lambda j: rows.at[j, pl.ds(0, half)],
            lambda j: rows.at[j, pl.ds(half, half)],
        )

    def head_of(j):
        return kept_head(place, j)

    line_h, line_da = line_of(h_line), line_of(da_line)
    o_swap = Direct(net, place, "x", lambda j: o_own.at[head_of(j)], lambda j: o_line.at[j])
    dq_swap = Direct(net, place, "x", lambda j: dq_own.at[head_of(j)], lambda j: dq_line.at[j])
    line_da.start()
    o_swap.start()
    key_rings = []
    for i, (inner, outer) in enumerate(key_lines(place, grads)):
        for k, (axis, _, lo, hi) in enumerate((outer, inner)):
            spot = 12 * i + 6 * k
            key_rings.append(
                RingScatter(
                    net,
                    place,
                    axis,
                    stepped(place, axis, lo),
                    stepped(place, axis, hi),
                    rooms[spot : spot + 6],
                )
            )
    first_a, then_a, first_b, then_b = key_rings
    fin_swap = Direct(net, place, "y", lambda j: fin.at[j], lambda j: fin_got.at[j])
    dq_core = net.copy(dq_snd, dq_got, partner)
    dq_ring = RingScatter(
        net,
        place,
        "y",
        stepped(place, "y", lambda j: dq_part.at[j, pl.ds(0, 2)]),
        stepped(place, "y", lambda j: dq_part.at[j, pl.ds(2, 2)]),
        dq_rooms,
    )
    late_first = RingScatter(
        net,
        place,
        "y",
        stepped(place, "y", lambda j: late_got.at[j, 0]),
        stepped(place, "y", lambda j: late_got.at[j, 1]),
        late_rooms[:6],
    )

    def late_spot(j):
        return late_y.at[lax.div(j, 2), lax.rem(j, 2)]

    late_second = RingScatter(
        net,
        place,
        "z",
        stepped(place, "z", lambda j: late_spot(j).at[pl.ds(0, 80)]),
        stepped(place, "z", lambda j: late_spot(j).at[pl.ds(80, 64)]),
        late_rooms[6:],
    )

    def late_term(c, turned, columns):
        term = jnp.dot(
            turned[...], columns[...].reshape(4 * TOK, HD), preferred_element_type=F32
        ).astype(BF)
        for k in range(8):
            for which in range(2):
                late_all[which, k // 2, k % 2, c] = term[
                    144 * k : 144 * k + 144, 128 * which : 128 * which + 128
                ]

    weights.first.begin()
    weights.first.go_on()
    bounds = [row_bounds(place, segments, y) for y in range(4)]
    for load in w_loads[:3]:
        load.wait()

    def differ(key_y):
        keys = buf[key_y, :, :, :, :HD].reshape(KEYS, HD)
        values = buf[key_y, :, :, :, HD:].reshape(KEYS, HD)
        token = tokens[...] + first_key(place, key_y)
        token = jnp.concatenate([token, token], axis=1)
        d_keys = d_values = None
        for y in range(key_y, 4):
            first, last = bounds[y]
            allowed = (token <= last) & (token >= first)
            for h in range(HEADS):
                probs = jnp.exp(contract(keys, q_all[y, h], 1, 1))
                probs = jnp.where(allowed, probs, 0.0)
                delta = jnp.concatenate(
                    [delta_all[y, 0, h : h + 1], delta_all[y, 1, h : h + 1]], axis=1
                )
                d_scores = (probs * (contract(values, do_all[y, h], 1, 1) - delta)).astype(BF)
                value_term = jnp.dot(probs.astype(BF), do_all[y, h], preferred_element_type=F32)
                key_term = jnp.dot(d_scores, q_all[y, h], preferred_element_type=F32)
                d_values = value_term if d_values is None else d_values + value_term
                d_keys = key_term if d_keys is None else d_keys + key_term
                query_term = contract(keys, d_scores, 0, 0)
                if y == key_y:
                    dq_sum[y, h] = query_term
                else:
                    dq_sum[y, h] += query_term
        grads[key_y, :, :, :, :HD] = d_keys.astype(BF).reshape(4, 4, STRIPE, HD)
        grads[key_y, :, :, :, HD:] = d_values.astype(BF).reshape(4, 4, STRIPE, HD)

    differ(3)
    differ(2)
    first_b.start()
    line_da.forward()
    line_h.start()
    differ(1)
    first_b.middle()
    weights.first.turn()
    differ(0)
    first_a.start()
    for y in range(4):
        for h in range(HEADS):
            dq_snd[y, h] = dq_sum[y, h, :, theirs].astype(BF)
            dq_part[y, h] = dq_sum[y, h, :, mine].astype(BF)
    net.go(dq_core)
    dq_core.wait_recv()
    for y in range(4):
        add_to(dq_part.at[y], dq_got.at[y])
    dq_ring.start()
    first_a.middle()
    first_b.finish(first_b.lo(0), first_b.hi(0))
    then_b.start()
    first_a.finish(first_a.lo(0), first_a.hi(0))
    then_a.start()
    weights.next()
    line_h.forward()
    line_da.finish()
    o_swap.wait()
    turned[...] = jnp.transpose(da_line[...].reshape(4 * TOK, D))
    late_term(0, turned, o_line)
    dq_ring.middle()
    then_b.middle()
    then_a.middle()
    then_b.finish(fin.at[2], fin.at[3])
    then_a.finish(fin.at[0], fin.at[1])
    fin_got[place.y] = fin[place.y]
    fin_swap.start()
    for load in w_loads[3:]:
        load.wait()

    dq_ring.finish(dq_done.at[pl.ds(0, 2)], dq_done.at[pl.ds(2, 2)])
    d_query = jnp.zeros((1, HD), F32)
    for h in range(HEADS):
        e = jnp.transpose(dq_done[h]) * HD**-0.5
        e = turn_back(e.astype(BF).astype(F32), cos_ref[...], sin_ref[...])
        u = q_pre[h]
        du, gain = norm_back(u, norm_scale(u), across(g_query), e)
        d_query = d_query + gain
        dq_own[h] = du.astype(BF)
    dq_line[place.x] = dq_own[head_of(place.x)]
    dq_swap.start()
    line_h.finish()
    turned[...] = jnp.transpose(h_line[...].reshape(4 * TOK, D))
    turned_swap = net.copy(
        turned.at[pl.ds(pl.multiple_of((1 - core) * 576, 16), 576)], turned_other, partner
    )
    net.go(turned_swap)
    fin_swap.wait()

    dkv = jnp.concatenate([fin_got[j] for j in range(4)], axis=0)
    e = turn_back(dkv[:, :HD].astype(BF).astype(F32), cos_ref[...], sin_ref[...])
    u = k_pre[...]
    dk, d_key = norm_back(u, norm_scale(u), across(g_key), e)
    dk, dv = dk.astype(BF), dkv[:, HD:].astype(BF)
    for i in range(2):
        kv_own[i] = dk[:, 128 * i : 128 * i + 128]
        kv_own[2 + i] = dv[:, 128 * i : 128 * i + 128]
    kv_line[core, place.x] = kv_own[place.x]
    kv_swap = Direct(net, place, "x", lambda j: kv_own.at[j], lambda j: kv_line.at[core, j])
    kv_swap.start()
    kv_across = []
    for by in range(4):
        j = place.step("x", by)
        device = place.device(x=j, core=1 - core)
        kv_across.append(net.copy(kv_own.at[j], kv_line.at[core, place.x], device))
        net.go(kv_across[by])
    weights.turn_again()
    dq_swap.wait()
    late_term(1, turned, dq_line)
    late_swap = net.copy(late_all.at[1 - core], late_got, partner)
    net.go(late_swap)
    d_h = contract(dk, wk[...], 1, 1) + contract(dv, wv[...], 1, 1)
    for h in range(HEADS):
        w = (wq, wq2)[h // 2]
        d_h = d_h + contract(dq_own[h], w[:, 256 * (h % 2) : 256 * (h % 2) + 256], 1, 1)
    xf = x_ref[...].astype(F32)
    dx, d_attn = norm_back(xf, norm_scale(xf), across(g_attn), d_h)
    dx_out[...] = (dmid_ref[...] + dx).astype(BF)
    def gain_swap(level, axis):
        return Direct(
            net, place, axis, lambda j: gain_got.at[level, at(axis)], lambda j: gain_got.at[level, j]
        )

    def at(axis):
        return getattr(place, axis)

    def gain_sum(level):
        return (gain_got[level, 0] + gain_got[level, 1]) + (gain_got[level, 2] + gain_got[level, 3])

    swaps = [gain_swap(0, "x"), gain_swap(1, "y"), gain_swap(2, "z")]
    norms = jnp.concatenate([d_query, d_key, jnp.zeros((1, D - 2 * HD), F32)], axis=1)
    gain_got[0, place.x] = jnp.concatenate(
        [d_attn, gains_ref[0:3], norms, jnp.zeros((3, D), F32)], axis=0
    )
    swaps[0].start()
    turned_swap.wait_recv()
    kv_swap.wait()
    for copy in kv_across:
        copy.wait_recv()
    term = jnp.dot(
        turned[pl.ds(pl.multiple_of(core * 576, 16), 576)],
        kv_line[core].reshape(4 * TOK, 128),
        preferred_element_type=F32,
    )
    term += jnp.dot(
        turned_other[...], kv_line[1 - core].reshape(4 * TOK, 128), preferred_element_type=F32
    )
    term = term.astype(BF)
    for k in range(4):
        w_got[k] = term[144 * k : 144 * k + 144]
    w_scatter = Direct(net, place, "y", lambda j: w_got.at[j], lambda j: w_y.at[j])
    w_scatter.start()
    w_y[place.y] = w_got[place.y]
    late_swap.wait_recv()
    for y in range(4):
        add_to(late_got.at[y], late_all.at[core, y])
    late_first.start()
    swaps[0].wait()
    gain_got[1, place.y] = gain_sum(0)
    swaps[1].start()
    weights.last()
    swaps[1].wait()
    gain_got[2, place.z] = gain_sum(1)
    swaps[2].start()
    w_scatter.wait()
    sum_to(w_z.at[place.z], [w_y.at[j] for j in range(4)])
    w_sums = Direct(net, place, "z", lambda j: w_z.at[place.z], lambda j: w_z.at[j])
    w_sums.start()
    late_first.middle()
    swaps[2].wait()
    gain_got[3, core] = gain_sum(2)
    gain_last = net.copy(gain_got.at[3, core], gain_got.at[3, core], partner)
    net.go(gain_last)
    w_sums.wait()
    upper, lower = w_top.at[core], w_low.at[core]
    sum_to(upper.at[place.x, place.y], [w_z.at[j, pl.ds(0, 80)] for j in range(4)])
    sum_to(lower.at[place.x, place.y], [w_z.at[j, pl.ds(80, 64)] for j in range(4)])

    def spread(axis, view):
        return Direct(net, place, axis, lambda j: view(at(axis)), view)

    first_way = [
        spread("y", lambda j: upper.at[place.x, j]),
        spread("x", lambda j: lower.at[j, place.y]),
    ]
    second_way = [spread("x", lambda j: upper.at[j]), spread("y", lambda j: lower.at[:, j])]
    for line in first_way:
        line.start()
    late_first.finish(late_y.at[0], late_y.at[1])
    late_second.start()
    for line, then in zip(first_way, second_way):
        line.wait()
        then.start()
    late_second.middle()
    gain_last.wait_recv()
    gains_out[...] = gain_got[3, 0] + gain_got[3, 1]
    over = [net.copy(upper, upper, partner), net.copy(lower, lower, partner)]
    for line, copy in zip(second_way, over):
        line.wait()
        net.go(copy)
    late_second.finish(late_z.at[pl.ds(0, 80)], late_z.at[pl.ds(80, 64)])
    weights.send_late()
    for copy in over:
        copy.wait_recv()
    weights.arrive()
    home_out[...] = weights.rcv[...]
    late_out[...] = weights.late_rcv[...]
    net.drain()


def attention_backward(hbm, small, call_id):
    shape = jax.ShapeDtypeStruct
    rooms = []
    for _ in range(2):
        rooms += RingScatter.room_shapes((4, STRIPE, 2 * HD), (4, STRIPE, 2 * HD))
        rooms += RingScatter.room_shapes((STRIPE, 2 * HD), (STRIPE, 2 * HD))
    rooms += RingScatter.room_shapes((2, HD, TOK), (2, HD, TOK))
    late_rooms = [
        *RingScatter.room_shapes((2, 144, 128), (2, 144, 128)),
        *RingScatter.room_shapes((80, 128), (64, 128)),
    ]
    return pl.pallas_call(
        backward_kernel,
        out_shape=(
            shape((TOK, D), BF),
            shape((8, 16, HALF + 256), BF),
            shape((8, 16, 256), BF),
            shape((2, 4, 4, 80, 128), BF),
            shape((2, 4, 4, 64, 128), BF),
            shape((8, D), F32),
        ),
        in_specs=[pl.BlockSpec(memory_space=pl.ANY)] * len(hbm) + [IN_VMEM] * len(small),
        out_specs=[IN_VMEM] * 6,
        scratch_shapes=[
            pltpu.VMEM((4, 4, 4, STRIPE, 2 * HD), BF),
            pltpu.VMEM((4, HEADS, ROWS, HD), BF),
            pltpu.VMEM((4, HEADS, ROWS, HD), BF),
            pltpu.VMEM((D, 2 * HD), BF),
            pltpu.VMEM((D, 2 * HD), BF),
            pltpu.VMEM((D, HD), BF),
            pltpu.VMEM((D, HD), BF),
            pltpu.VMEM((KEYS, 128), jnp.int32),
            pltpu.VMEM((4, 4, 4, STRIPE, 2 * HD), BF),
            pltpu.VMEM((4, STRIPE, 2 * HD), F32),
            pltpu.VMEM((4, STRIPE, 2 * HD), F32),
            pltpu.VMEM((4, HEADS, HD, ROWS), F32),
            pltpu.VMEM((4, HEADS, HD, TOK), BF),
            pltpu.VMEM((4, HEADS, HD, TOK), BF),
            pltpu.VMEM((4, HEADS, HD, TOK), BF),
            pltpu.VMEM((HEADS, HD, TOK), F32),
            pltpu.VMEM((4, TOK, D), BF),
            pltpu.VMEM((4, TOK, D), BF),
            pltpu.VMEM((D, 4 * TOK), BF),
            pltpu.VMEM((4, TOK, HD), BF),
            pltpu.VMEM((4, TOK, HD), BF),
            pltpu.VMEM((4, TOK, HD), BF),
            pltpu.VMEM((4, TOK, HD), BF),
            pltpu.VMEM((2, 4, 2, 2, 144, 128), BF),
            pltpu.VMEM((4, 2, 2, 144, 128), BF),
            pltpu.VMEM((2, 2, 144, 128), BF),
            pltpu.VMEM((144, 128), F32),
            pltpu.VMEM((4, 4, 8, D), F32),
            pltpu.VMEM((4, TOK, 128), BF),
            pltpu.VMEM((2, 4, TOK, 128), BF),
            pltpu.VMEM((576, 4 * TOK), BF),
            pltpu.VMEM((4, 144, 128), BF),
            pltpu.VMEM((4, 144, 128), BF),
            pltpu.VMEM((4, 144, 128), BF),
            *rooms,
            *late_rooms,
            *WeightSums.scratch(),
            *sems(160),
            *sems(16),
            pltpu.SemaphoreType.DMA((24,)),
        ],
        compiler_params=params(call_id),
    )(*hbm, *small)


def feed_kernel(
    x_ref,
    o_ref,
    inv_ref,
    wo_ref,
    wo2_ref,
    post_ref,
    ffn_ref,
    out_gain_ref,
    cot_ref,
    wg_hbm,
    wu_hbm,
    wd_hbm,
    out_ref,
    dmid_out,
    dattn_out,
    do_all,
    delta_all,
    dgains_out,
    sums_hbm,
    wg,
    wu,
    wd,
    h_line,
    f_line,
    h_turned,
    f_turned,
    gelu_kept,
    slope_kept,
    act,
    d_gate,
    d_up,
    f_terms,
    h_terms,
    snd,
    got,
    attn,
    mid,
    ffn,
    delta_rows,
    *rest,
):
    *room, send, recv, local = rest
    place, net = Place(), Net(send, recv)
    core, partner = place.core, place.partner()
    x_hi = lax.div(place.x, 2)
    first_unit = pl.multiple_of(x_hi * (2 * HID - HID_PAD), 128)
    window = pl.ds(first_unit, HID_PAD)
    loads = [
        pltpu.make_async_copy(source, target, local.at[i])
        for i, (source, target) in enumerate(
            ((wg_hbm.at[:, window], wg), (wu_hbm.at[:, window], wu), (wd_hbm.at[window], wd))
        )
    ]
    for load in loads:
        load.start()
    half, quarter = TOK // 2, TOK // 4
    top, bottom = pl.ds(0, quarter), pl.ds(quarter, quarter)
    g_post, g_ffn, g_out = (across(ref) for ref in (post_ref, ffn_ref, out_gain_ref))

    def rows_of(part):
        return slice(half * part, half * part + half)

    def lines_of(part):
        return slice(4 * half * part, 4 * half * part + 4 * half)

    def gather(lines):
        return RingGather(
            net,
            place,
            "x",
            lambda j: lines.at[j],
            lambda j: lines.at[j, top],
            lambda j: lines.at[j, bottom],
        )

    def scatter(terms, room):
        return RingScatter(
            net,
            place,
            "x",
            stepped(place, "x", lambda j: terms.at[j, top]),
            stepped(place, "x", lambda j: terms.at[j, bottom]),
            room,
        )

    def summed(line, part):
        at = half * part
        line.finish(ffn.at[pl.ds(at, quarter)], ffn.at[pl.ds(at + quarter, quarter)])

    def heads_out():
        o_cat = [o_ref[h].astype(BF) for h in range(HEADS)]
        a = jnp.dot(jnp.concatenate(o_cat[:2], axis=1), wo_ref[...], preferred_element_type=F32)
        a += jnp.dot(jnp.concatenate(o_cat[2:], axis=1), wo2_ref[...], preferred_element_type=F32)
        attn[...] = a
        mid[...] = x_ref[...].astype(F32) + a * norm_scale(a) * g_post
        m = mid[...]
        h = (m * norm_scale(m) * g_ffn).astype(BF)
        for part in range(2):
            h_line[part, place.x] = h[rows_of(part)]

    greet(
        ring(place, "x")
        + ring(place, "y")
        + ring(place, "z")
        + [partner, place.toward("y", 2)],
        heads_out,
    )
    h_gathers = [gather(h_line.at[part]) for part in range(2)]
    f_gathers = [gather(f_line.at[part]) for part in range(2)]
    f_sums = [scatter(f_terms.at[part], room[6 * part : 6 * part + 6]) for part in range(2)]
    h_sums = [
        scatter(h_terms.at[part], room[12 + 6 * part : 18 + 6 * part]) for part in range(2)
    ]
    h_gathers[0].start()

    for load in loads:
        load.wait()
    low_unit, high_unit = jnp.where(x_hi == 0, 0, 64), jnp.where(x_hi == 0, HID, HID_PAD)

    def units(n):
        return pl.ds(pl.multiple_of(n * 256, 256), 256)

    def forward(part, n, carry):
        h = h_line[part].reshape(4 * half, D)
        gate = jnp.dot(h, wg[:, units(n)], preferred_element_type=F32)
        up = jnp.dot(h, wu[:, units(n)], preferred_element_type=F32)
        unit = n * 256 + lax.broadcasted_iota(jnp.int32, (1, 256), 1)
        own = jnp.where((unit >= low_unit) & (unit < high_unit), 1.0, 0.0)
        scale, cube = 0.7978845608028654, 0.044715
        square = gate * gate
        bent = jnp.tanh(scale * gate * (1.0 + cube * square))
        lifted = 0.5 * (1.0 + bent)
        gelu = gate * lifted * own
        slope = lifted + 0.5 * gate * (1.0 - bent * bent) * scale * (1.0 + 3.0 * cube * square)
        act[lines_of(part), units(n)] = (gelu * up).astype(BF)
        gelu_kept[lines_of(part), units(n)] = gelu.astype(BF)
        slope_kept[lines_of(part), units(n)] = (slope * up * own).astype(BF)
        return carry

    def columns(n):
        return pl.ds(pl.multiple_of(n * 384, 128), 384)

    def project(part, n, carry):
        term = jnp.dot(act[lines_of(part)], wd[:, columns(n)], preferred_element_type=F32)
        f_terms[part, :, :, columns(n)] = term.astype(BF).reshape(4, half, 384)
        return carry

    def backward(part, n, carry):
        d_act = contract(f_line[part].reshape(4 * half, D), wd[units(n)], 1, 1)
        rows = lines_of(part)
        d_gate[rows, units(n)] = (d_act * slope_kept[rows, units(n)].astype(F32)).astype(BF)
        d_up[rows, units(n)] = (d_act * gelu_kept[rows, units(n)].astype(F32)).astype(BF)
        return carry

    def back_project(part, n, carry):
        rows = lines_of(part)
        term = contract(d_gate[rows], wg[columns(n)], 1, 1)
        term += contract(d_up[rows], wu[columns(n)], 1, 1)
        h_terms[part, :, :, columns(n)] = term.astype(BF).reshape(4, half, 384)
        return carry

    def each(times, step, part):
        lax.fori_loop(0, times, functools.partial(step, part), 0)

    blocks = HID_PAD // 256

    def turn_round(part):
        rows = rows_of(part)
        summed(f_sums[part], part)
        f = ffn[rows]
        r = norm_scale(f)
        out_ref[rows] = (mid[rows] + f * r * g_out).astype(BF)
        df, gain = norm_back(f, r, g_out, cot_ref[rows].astype(F32))
        f_line[part, place.x] = df.astype(BF)
        f_gathers[part].start()
        return gain

    h_gathers[0].forward()
    h_gathers[1].start()
    h_gathers[0].finish()
    each(blocks, forward, 0)
    h_gathers[1].forward()
    each(3, project, 0)
    f_sums[0].start()
    h_gathers[1].finish()
    each(blocks, forward, 1)
    f_sums[0].middle()
    each(3, project, 1)
    f_sums[1].start()
    d_out = turn_round(0)
    f_sums[1].middle()
    h_turned[...] = jnp.transpose(h_line[...].reshape(8 * half, D))
    f_gathers[0].forward()
    d_out = d_out + turn_round(1)
    f_gathers[0].finish()
    each(blocks, backward, 0)
    f_gathers[1].forward()
    each(3, back_project, 0)
    h_sums[0].start()
    f_gathers[1].finish()

    def halves_of(which):
        return pl.ds(pl.multiple_of(which * 896, 128), 896)

    def fill(target, i, which, left, right, spans, add):
        term = jnp.dot(
            left[576 * i : 576 * i + 576], right[:, halves_of(which)], preferred_element_type=F32
        )
        for k in range(4):
            for half, low, high, start in spans:
                at = (2 * i + k // 2, k % 2, half, slice(None), slice(start, start + high - low))
                value = term[144 * k : 144 * k + 144, low:high]
                if add:
                    value = value + target[at].astype(F32)
                target[at] = value.astype(BF)

    down_spans = ((0, 0, 256, 0), (0, 256, 512, CUT), (1, 512, 768, 0), (1, 768, 896, CUT))

    def fill_down(target, i, which, add):
        fill(target, i, which, f_turned, act, down_spans, add)

    def fill_others(target, i, which, add):
        for c, right in enumerate((d_gate, d_up)):
            spans = ((c, 0, 512, 256), (c, 512, 896, CUT + 256))
            fill(target, i, which, h_turned, right, spans, add)

    for y in range(4):
        snd[y, :, 1, :, CUT + 128 : CUT + 256] = jnp.zeros((2, 144, 128), BF)
    swaps = [net.copy(snd.at[y], got.at[y], partner) for y in range(4)]
    each(blocks, backward, 1)
    h_sums[0].middle()
    each(3, back_project, 1)
    h_sums[1].start()
    def mine_of(part):
        return pl.ds(pl.multiple_of(core * TOK + half * part, half), half)

    def do_ring_of(part):
        mine = mine_of(part)
        return RingGather(
            net,
            place,
            "y",
            lambda j: do_all.at[j, :, mine],
            lambda j: do_all.at[j, pl.ds(0, 2), mine],
            lambda j: do_all.at[j, pl.ds(2, 2), mine],
        )

    def block_of(part, by):
        return do_all.at[place.step("y", by), :, mine_of(part)]

    do_rings = [do_ring_of(part) for part in range(2)]
    do_core = [
        [net.copy(block_of(part, by), block_of(part, by), partner) for by in range(4)]
        for part in range(2)
    ]
    delta_swap = Direct(
        net,
        place,
        "y",
        lambda j: delta_all.at[place.y, core],
        lambda j: delta_all.at[j, core],
    )
    delta_core = net.copy(delta_all.at[:, core], delta_all.at[:, core], partner)

    def heads_back(part):
        rows = rows_of(part)
        m, a = mid[rows], attn[rows]
        dm, d_ffn = norm_back(m, norm_scale(m), g_ffn, ffn[rows])
        d_mid = cot_ref[rows].astype(F32) + dm
        dmid_out[rows] = d_mid
        da, d_post = norm_back(a, norm_scale(a), g_post, d_mid)
        da = da.astype(BF)
        dattn_out[rows] = da
        for h in range(HEADS):
            w = (wo_ref, wo2_ref)[h // 2][256 * (h % 2) : 256 * (h % 2) + 256]
            d_o = contract(da, w, 1, 1).astype(BF).astype(F32)
            inverse = inv_ref[h, rows]
            scaled = d_o * jnp.concatenate([inverse, inverse], axis=1)
            do_all[place.y, h, mine_of(part)] = scaled.astype(BF)
            delta_rows[h, rows] = jnp.sum(d_o * o_ref[h, rows], axis=1, keepdims=True) * inverse
        do_rings[part].start()
        net.go(do_core[part][0])
        return d_post, d_ffn

    for i in range(2):
        fill_others(snd, i, 1 - core, False)
    h_sums[1].middle()
    summed(h_sums[0], 0)
    gains_top = heads_back(0)
    f_turned[...] = jnp.transpose(f_line[...].reshape(8 * half, D))
    for i in range(2):
        fill_down(snd, i, 1 - core, False)
        net.go(swaps[2 * i])
        net.go(swaps[2 * i + 1])
    summed(h_sums[1], 1)
    gains_low = heads_back(1)
    d_post, d_ffn = (top + low for top, low in zip(gains_top, gains_low))
    dgains_out[...] = jnp.concatenate([d_post, d_ffn, d_out, jnp.zeros((5, D), F32)], axis=0)
    delta_all[place.y, core] = jnp.concatenate(
        [jnp.transpose(delta_rows[h])[:1] for h in range(HEADS)] + [jnp.zeros((4, TOK), F32)],
        axis=0,
    )
    delta_swap.start()
    stores = [pltpu.make_async_copy(got.at[y], sums_hbm.at[y], local.at[3 + y]) for y in range(4)]

    def do_near(part):
        do_rings[part].forward()
        net.go(do_core[part][1])
        net.go(do_core[part][3])

    def do_far(part):
        do_rings[part].finish()
        net.go(do_core[part][2])

    do_near(0)
    for i in range(2):
        swaps[2 * i].wait_recv()
        swaps[2 * i + 1].wait_recv()
        fill_others(got, i, core, True)
        fill_down(got, i, core, True)
        stores[2 * i].start()
        stores[2 * i + 1].start()
        if i == 0:
            do_far(0)
            do_near(1)
    do_far(1)
    delta_swap.wait()
    net.go(delta_core)
    for copies in do_core:
        for copy in copies:
            copy.wait_recv()
    delta_core.wait_recv()
    for store in stores:
        store.wait()
    net.drain()


def feed_forward(args, call_id):
    quarter = (TOK // 4, D)
    shape = jax.ShapeDtypeStruct
    every = (4, 2, 2, 144, HALF)
    lines = 4 * TOK
    anywhere = pl.BlockSpec(memory_space=pl.ANY)
    unit_rows = [pltpu.VMEM((lines, HID_PAD), BF)] * 5
    return pl.pallas_call(
        feed_kernel,
        out_shape=(
            shape((TOK, D), BF),
            shape((TOK, D), F32),
            shape((TOK, D), BF),
            shape((4, HEADS, ROWS, HD), BF),
            shape((4, 2, 8, TOK), F32),
            shape((8, D), F32),
            shape(every, BF),
        ),
        in_specs=[IN_VMEM] * 9 + [anywhere] * 3,
        out_specs=[IN_VMEM] * 6 + [anywhere],
        scratch_shapes=[
            pltpu.VMEM((D, HID_PAD), BF),
            pltpu.VMEM((D, HID_PAD), BF),
            pltpu.VMEM((HID_PAD, D), BF),
            pltpu.VMEM((2, 4, TOK // 2, D), BF),
            pltpu.VMEM((2, 4, TOK // 2, D), BF),
            pltpu.VMEM((D, lines), BF),
            pltpu.VMEM((D, lines), BF),
            *unit_rows,
            pltpu.VMEM((2, 4, TOK // 2, D), BF),
            pltpu.VMEM((2, 4, TOK // 2, D), BF),
            pltpu.VMEM(every, BF),
            pltpu.VMEM(every, BF),
            pltpu.VMEM((TOK, D), F32),
            pltpu.VMEM((TOK, D), F32),
            pltpu.VMEM((TOK, D), F32),
            pltpu.VMEM((HEADS, TOK, TOK), F32),
            *(RingScatter.room_shapes(quarter, quarter) * 4),
            *sems(88),
            pltpu.SemaphoreType.DMA((7,)),
        ],
        compiler_params=params(call_id),
    )(*args)


class FirstSums:
    def __init__(self, net, place, sums, cut, rooms, here=None, marks=None):
        left, right = pl.ds(0, cut), pl.ds(cut, sums.shape[-1] - cut)

        def y_spot(half):
            return stepped(place, "y", lambda j: sums.at[j, half, :, :, left])

        def z_spot(half):
            return stepped(
                place,
                "z",
                lambda j: sums.at[pl.ds(2 * half, 2), lax.div(j, 2), lax.rem(j, 2), :, right],
            )

        self.loads = []
        self.lines = []
        for i, (axis, spot) in enumerate((("y", y_spot), ("z", z_spot))):
            near = (None, None)
            if here is not None:
                near = ({}, {})
                for k, (half, by) in enumerate(((0, 1), (1, 3), (0, 0), (1, 0))):
                    target = here[i].at[k]
                    near[half][by] = target
                    self.loads.append(
                        pltpu.make_async_copy(spot(half)(by), target, marks.at[8 + 4 * i + k])
                    )
                near = (near[0].get, near[1].get)
            room = rooms[6 * i : 6 * i + 6]
            self.lines.append(RingScatter(net, place, axis, spot(0), spot(1), room, *near))

    @staticmethod
    def room_shapes(cut, rest):
        return [
            *RingScatter.room_shapes((2, 144, cut), (2, 144, cut)),
            *RingScatter.room_shapes((2, 144, rest), (2, 144, rest)),
        ]

    def begin(self):
        for load in self.loads:
            load.start()
        for line in self.lines:
            line.start_far()

    def go_on(self):
        for line in self.lines:
            line.start_right()
            line.start_left()

    def turn(self):
        for load in self.loads:
            load.wait()
        for line in self.lines:
            line.middle()


class WeightSums:
    def __init__(self, place, net, sums, late, refs, marks):
        y_here, z_here, y1, z1, z2, y2, snd, late_snd, rcv, late_rcv, *rooms = refs
        self.late_snd, self.late_rcv = late_snd, late_rcv
        self.place, self.late, self.snd, self.rcv, self.marks = place, late, snd, rcv, marks
        self.y1, self.z1, self.y2, self.z2 = y1, z1, y2, z2
        self.x_hi, self.x_lo = lax.div(place.x, 2), lax.rem(place.x, 2)
        self.friends = []
        for k in range(1, 16):
            spot = lax.rem(self.x_hi * 8 + place.z * 2 + place.core + k, 16)
            x, z = lax.div(spot, 8) * 2 + self.x_lo, lax.rem(lax.div(spot, 2), 4)
            self.friends.append(place.device(x=x, z=z, core=lax.rem(spot, 2)))

        self.first = FirstSums(net, place, sums, CUT, rooms[:12], (y_here, z_here), marks[2])

        def then_z(j):
            return y1.at[lax.div(j, 2), lax.rem(j, 2)]

        self.z_second = RingScatter(
            net,
            place,
            "z",
            stepped(place, "z", lambda j: then_z(j).at[:, pl.ds(0, 384)]),
            stepped(place, "z", lambda j: then_z(j).at[:, pl.ds(384, 384)]),
            rooms[12:18],
        )
        self.y_second = RingScatter(
            net,
            place,
            "y",
            stepped(place, "y", lambda j: z1.at[j, :, pl.ds(0, 384)]),
            stepped(place, "y", lambda j: z1.at[j, :, pl.ds(384, 256)]),
            rooms[18:24],
        )

    @staticmethod
    def scratch():
        rest = HALF - CUT
        return [
            pltpu.VMEM((4, 2, 144, CUT), BF),
            pltpu.VMEM((4, 2, 144, rest), BF),
            pltpu.VMEM((2, 2, 144, CUT), BF),
            pltpu.VMEM((4, 144, rest), BF),
            pltpu.VMEM((144, CUT), F32),
            pltpu.VMEM((144, rest), F32),
            pltpu.VMEM((8, 16, HALF + 256), BF),
            pltpu.VMEM((8, 16, 256), BF),
            pltpu.VMEM((8, 16, HALF + 256), BF),
            pltpu.VMEM((8, 16, 256), BF),
            *FirstSums.room_shapes(CUT, rest),
            *RingScatter.room_shapes((144, 384), (144, 384)),
            *RingScatter.room_shapes((144, 384), (144, 256)),
        ]

    def next(self):
        y_line, z_line = self.first.lines
        y_line.finish(self.y1.at[0], self.y1.at[1])
        self.z_second.start()
        z_line.finish(self.z1.at[pl.ds(0, 2)], self.z1.at[pl.ds(2, 2)])
        self.y_second.start()

    def turn_again(self):
        self.z_second.middle()
        self.y_second.middle()

    def last(self):
        z2, y2 = self.z2, self.y2
        self.z_second.finish(z2.at[:, pl.ds(0, 384)], z2.at[:, pl.ds(384, 384)])
        self.y_second.finish(y2.at[:, pl.ds(0, 384)], y2.at[:, pl.ds(384, 256)])
        total = jnp.concatenate([z2[...], y2[...]], axis=1)
        self.pack(total, self.snd)
        self.exchange(self.snd, self.rcv, 0)

    def send_late(self):
        self.pack(self.late[...], self.late_snd)
        self.exchange(self.late_snd, self.late_rcv, 8)

    @staticmethod
    def pack(total, snd):
        width = total.shape[1]
        count = width // 128
        for k in range(8):
            extra = total[18 * k + 16 : 18 * k + 18]
            pieces = [extra[:, 128 * n : 128 * n + 128] for n in range(count)]
            snd[k, :, :width] = total[18 * k : 18 * k + 16].astype(BF)
            for n in range(0, count, 8):
                group = pieces[n : n + 8]
                if len(group) < 8:
                    group.append(jnp.zeros((16 - 2 * len(group), 128), F32))
                at = width + 16 * n
                snd[k, :, at : at + 128] = jnp.concatenate(group, axis=0).astype(BF)

    def exchange(self, snd, rcv, mark):
        place = self.place
        send, recv, here = self.marks
        row_half = lax.div(place.z, 2)
        self.slot = self.x_hi * 4 + place.core * 2 + lax.rem(place.z, 2)
        self.own = place.z * 2 + place.core
        self.stays = row_half == self.x_hi
        for k in range(8):
            copy = pltpu.make_async_remote_copy(
                src_ref=snd.at[k],
                dst_ref=rcv.at[self.slot],
                send_sem=send.at[mark + k],
                recv_sem=recv.at[mark + self.slot],
                device_id=place.device(x=row_half * 2 + self.x_lo, z=k // 2, core=k % 2),
                device_id_type=MESH,
            )
            is_here = self.stays & (self.own == k)

            @pl.when(jnp.logical_not(is_here))
            def _(copy=copy):
                copy.start()

            @pl.when(is_here)
            def _(k=k):
                keep = pltpu.make_async_copy(snd.at[k], rcv.at[self.slot], here.at[0])
                keep.start()
                keep.wait()

    def arrive(self):
        send, recv, _ = self.marks
        for mark, snd, rcv in ((0, self.snd, self.rcv), (8, self.late_snd, self.late_rcv)):
            for m in range(8):
                arrival = pltpu.make_async_remote_copy(
                    src_ref=snd.at[m],
                    dst_ref=rcv.at[m],
                    send_sem=send.at[mark + m],
                    recv_sem=recv.at[mark + m],
                    device_id=self.place.partner(),
                    device_id_type=MESH,
                )

                @pl.when(jnp.logical_not(self.stays & (self.slot == m)))
                def _(arrival=arrival):
                    arrival.wait_recv()

                @pl.when(jnp.logical_not(self.stays & (self.own == m)))
                def _(arrival=arrival):
                    arrival.wait_send()


def last_kernel(
    home_ref,
    late_ref,
    top_ref,
    low_ref,
    gains_ref,
    y_ref,
    dx_ref,
    y_out,
    dx_out,
    dwq_out,
    dwk_out,
    dwv_out,
    dwo_out,
    dwg_out,
    dwu_out,
    dwd_out,
    *gain_outs,
):
    y_out[...] = y_ref[...]
    dx_out[...] = dx_ref[...]

    def rows_at(ref, slot, n):
        spare = (HALF if ref is home_ref else 128) + 128 * (n // 8)
        more = ref[slot, :, spare : spare + 128].astype(F32)[2 * (n % 8) : 2 * (n % 8) + 2]
        return jnp.concatenate(
            [ref[slot, :, 128 * n : 128 * n + 128].astype(F32), more], axis=0
        )

    def tile(x_hi, which, n):
        core, n = n // 7, n % 7
        if which < 2:
            c, at = which, 256 + 128 * n if n < 4 else 512 + 128 * n
        else:
            c, n = n // 4, n % 4
            at = 128 * n if n < 2 else CUT + 128 * (n - 2)
        return rows_at(home_ref, x_hi * 4 + core * 2 + c, at // 128)

    for which, out in enumerate((dwg_out, dwu_out, dwd_out)):
        for n in range(27):
            value = None
            for x_hi in range(2):
                if 0 <= n - 13 * x_hi < 14:
                    term = tile(x_hi, which, n - 13 * x_hi)
                    value = term if value is None else value + term
            span = slice(128 * n, 128 * n + 128)
            out[:, span] = value
    for k in range(4):
        span = slice(128 * k, 128 * k + 128)
        dwo_out[:, span] = rows_at(late_ref, 2 * k, 0)
        dwq_out[:, span] = rows_at(late_ref, 2 * k + 1, 0)
    for which in range(2):
        for j in range(4):
            out = (dwk_out, dwv_out)[j // 2]
            for y in range(4):
                span = slice(128 * (j % 2), 128 * (j % 2) + 128)
                at = 576 * which + 144 * y
                out[at : at + 80, span] = top_ref[which, j, y].astype(F32)
                out[at + 80 : at + 144, span] = low_ref[which, j, y].astype(F32)
    for out, row, start in zip(gain_outs, (0, 4, 4, 1, 2, 3), (0, 0, HD, 0, 0, 0)):
        size = out.shape[0]
        out[...] = gains_ref[row : row + 1, start : start + size].reshape(size)


def last_layout(*args):
    shape = jax.ShapeDtypeStruct
    return pl.pallas_call(
        last_kernel,
        out_shape=(
            shape((TOK, D), BF),
            shape((TOK, D), BF),
            shape((18, 2 * HD), F32),
            shape((D, HD), F32),
            shape((D, HD), F32),
            shape((18, 2 * HD), F32),
            shape((18, 2 * HID), F32),
            shape((18, 2 * HID), F32),
            shape((18, 2 * HID), F32),
            *(shape((size,), F32) for size in (D, HD, HD, D, D, D)),
        ),
        in_specs=[IN_VMEM] * len(args),
        out_specs=[IN_VMEM] * 15,
        compiler_params=pltpu.CompilerParams(vmem_limit_bytes=VMEM_BYTES),
    )(*args)


def angles(token_pos):
    middle = HD // 2
    frequency = THETA ** (-2.0 * jnp.arange(middle, dtype=F32) / HD)
    turned = token_pos.astype(F32)[:, None] * frequency[None, :]
    return (jnp.cos(turned), jnp.sin(turned))


def shards(
    layer_input,
    segment_ids,
    positions,
    w_query,
    w_key,
    w_value,
    w_out,
    w_gate,
    w_up,
    w_down,
    norm_attn,
    norm_query,
    norm_key,
    norm_post,
    norm_ffn,
    norm_out,
    cotangent,
):
    sp, tp = lax.axis_index("sp"), lax.axis_index("tp")
    cosine, sine = angles(lax.dynamic_slice_in_dim(positions, (sp * 2 + tp) * TOK, TOK))
    segments = segment_ids.reshape(128, 128)
    key_rows = jnp.asarray(KEY_TOKENS)
    kv_all, q_all, wq_other, wo_other, o_heads, inverse, q_pre, k_pre, h_attn = attention_forward(
        (
            layer_input,
            norm_attn,
            norm_query,
            norm_key,
            w_query,
            w_key,
            w_value,
            w_out,
            cosine,
            sine,
            segments,
            key_rows,
        ),
        2,
    )
    (
        layer_output,
        d_mid,
        d_attn,
        d_heads,
        delta,
        d_gains,
        sums,
    ) = feed_forward(
        (
            layer_input,
            o_heads,
            inverse,
            w_out,
            wo_other,
            norm_post,
            norm_ffn,
            norm_out,
            cotangent,
            w_gate,
            w_up,
            w_down,
        ),
        6,
    )
    d_input, home, late, w_top, w_low, gains = attention_backward(
        (kv_all, q_all, d_heads, sums, w_query, wq_other, w_key, w_value),
        (
            delta,
            key_rows,
            segments,
            q_pre,
            k_pre,
            cosine,
            sine,
            h_attn,
            d_attn,
            o_heads,
            layer_input,
            d_mid,
            norm_attn,
            norm_query,
            norm_key,
            d_gains,
        ),
        8,
    )
    y, dx, d_wq, d_wk, d_wv, d_wo, d_wg, d_wu, d_wd, *d_norms = last_layout(
        home, late, w_top, w_low, gains, layer_output, d_input
    )
    return (y, dx, d_wq, d_wk, d_wv, d_wo.T, d_wg, d_wu, d_wd.T, *d_norms)


def solution(mesh):
    rows = P(("sp", "tp"), None)
    in_specs = (
        rows,
        P(),
        P(),
        P(None, "tp"),
        P(),
        P(),
        P("tp", None),
        P(None, "tp"),
        P(None, "tp"),
        P("tp", None),
        P(),
        P(),
        P(),
        P(),
        P(),
        P(),
        rows,
    )
    out_specs = (
        rows,
        rows,
        P("sp", "tp"),
        P(),
        P(),
        P("tp", "sp"),
        P("sp", "tp"),
        P("sp", "tp"),
        P("tp", "sp"),
        P(),
        P(),
        P(),
        P(),
        P(),
        P(),
    )
    return jax.shard_map(shards, mesh=mesh, in_specs=in_specs, out_specs=out_specs, check_vma=False)
```
